32 devices in a mesh: groups: 2 (over x), shard: 16 (over z, y, core).
Axes of the slice: x: 2, y: 2, z: 4, core: 2. Of those that a mesh axis runs over, the one named last changes fastest.
Arguments:
- query_grads: bfloat16 [32, 16, 4096], P(('groups', 'shard')), parts along dimension 0, may hold values from -6 to 6
- cand_grads: bfloat16 [64, 16, 4096], P(('groups', 'shard')), parts along dimension 0, may hold values from -0.0234375 to 0.0234375
- basis_out: bfloat16 [16, 64, 64], P('shard'), may hold values from -0.75 to 0.75
- basis_in: bfloat16 [16, 64, 64], P('shard'), may hold values from -0.75 to 0.75
- eigvals: float32 [16, 4096], P('shard'), may hold values from 0.1 to 10
- layer_map: int32 [16], replicated, may hold values from 0 to 15, each once
- cand_rows: int32 [64], P('groups'), parts along dimension 0, may hold values from 0 to 31, each once
- cand_lists: int32 [32, 384], P(('groups', 'shard')), parts along dimension 0, may hold values from 0 to 31
- list_lengths: int32 [32], P(('groups', 'shard')), parts along dimension 0, may hold values from 1 to 384, 2048 in all
Outputs:
- preconditioned: bfloat16 [32, 16, 4096], P(('groups', 'shard')), parts along dimension 0
- scores: float32 [32, 384], P(('groups', 'shard')), parts along dimension 0
The draws below stay inside these ranges and needn't reach their ends.
There are 2 independent parts, one for each index of `groups`. The reference program is written for one: setup_inputs(seed, part) draws one part's arguments, and reference() takes and returns one part's arrays. A program takes and returns all parts, laid end to end along the dimension named above; an argument that names none is the same for every part. Nothing has to cross between parts.
Inputs may be any that keep to these rules, and one draw needn't show every extreme that they name: Slot s of basis_out, basis_in and eigvals holds module layer_map[s]; slot s lies on index s // 1 of shard; each module once. cand_grads row cand_rows[c] holds candidate c, on index cand_rows[c] // 2 of shard; each row once. `cand_lists`: A candidate may be named several times in one list; entries at positions list_lengths[q] and beyond are padding. `list_lengths`: within each attribution job (each index of groups) the 16 lengths sum to 2048, a mean of 128; the whole array, holding all jobs, sums to that times the number of jobs.
All inputs are finite; a program needn't handle non-finite values.
Results may differ from the reference program's by a relative error of at most 0.013.
Values may be sent and summed in bfloat16 or wider, within the bound.
No kernel may reach another device: no remote copies, remote signals or barrier semaphores. Data moves between devices by JAX's collectives and lax.ppermute only.
A program may use at most 64 MiB of HBM per device.

```python
import math
import jax
import jax.numpy as jnp
import numpy as np
from jax import lax

D_O = 64
D_I = 64
FLAT = 4096
MODULES = 16
QUERIES = 16
CANDS = 32
LISTMAX = 384


def plant(entries, key, low, high):
    shape = entries.shape
    spot = [jax.random.randint(jax.random.fold_in(key, axis), (), 0, shape[axis]) for axis in range(len(shape))]
    entries = entries.at[tuple(spot)].set(low)
    longest = shape.index(max(shape))
    spot[longest] = (spot[longest] + 1) % shape[longest]
    return entries.at[tuple(spot)].set(high)


def block_scale(own_key, dims, shards, least, high):
    loudness, own = 1.0, jax.random.fold_in(own_key, 6)
    for dim, shards_of in shards:
        draws = jnp.exp(jax.random.uniform(jax.random.fold_in(own, dim), (shards_of,), jnp.float32, least / len(shards), high / len(shards)))
        loudness = loudness * jnp.repeat(draws, dims[dim] // shards_of).reshape([-1 if axis == dim else 1 for axis in range(len(dims))])
    return loudness


def length_profile(amount, total, reach, slope):
    portions = [(1 << 20) // math.isqrt(rank ** slope) + 1 for rank in range(2, amount + 1)]
    surplus, counts = total - reach - (amount - 1), [1] * (amount - 1)
    while surplus > 0:
        free = [i for i in range(amount - 1) if counts[i] < reach]
        mass, remaining = sum([portions[i] for i in free]), surplus
        for i in free:
            more = min(reach - counts[i], max(1, remaining * portions[i] // mass), surplus)
            counts[i] = counts[i] + more
            surplus = surplus - more
    return np.array([reach] + counts)


def uneven(key, amount, total, most, lean):
    if amount == 2:
        one = jax.random.randint(key, (), max(1, total - most), min(most, total - 1) + 1)
        return jnp.stack([one, total - one])
    lengths = jnp.asarray(length_profile(amount, total, most, lean), jnp.int32)
    twos = (amount - 1) // 2
    giver, sink = lengths[1:1 + 2 * twos:2], lengths[2:2 + 2 * twos:2]
    slack = jnp.minimum(giver - 1, most - sink)
    moved = jax.random.randint(jax.random.fold_in(key, 1), (twos,), 0, 1 << 20) % (slack + 1)
    lengths = lengths.at[1:1 + 2 * twos:2].set(giver - moved).at[2:2 + 2 * twos:2].set(sink + moved)
    return lengths[jax.random.permutation(jax.random.fold_in(key, 2), amount)]


def normal_values(key, shape, spread, most, shards=(), kind=jnp.bfloat16):
    result = spread * jax.random.normal(key, shape, jnp.float32)
    if shards:
        result = result * block_scale(key, shape, shards, -0.22, 0.18)
    return jnp.clip(result, -most, most).astype(kind)


def setup_inputs(seed: int = 0, part: int = 0) -> dict:
    key_of = jax.random.split(jax.random.key(seed), 10)
    own_keys = jax.random.split(jax.random.fold_in(key_of[9], part), 10)
    query_grads = normal_values(own_keys[0], (QUERIES, MODULES, FLAT), 1.0, 6.0, ((0, 16),))
    cand_grads = normal_values(own_keys[1], (CANDS, MODULES, FLAT), (MODULES * FLAT) ** -0.5, 0.0234375, ((0, 16),))
    basis_out = normal_values(key_of[2], (MODULES, D_O, D_O), D_O ** -0.5, 0.75, ((0, 16),))
    basis_in = normal_values(key_of[3], (MODULES, D_I, D_I), D_I ** -0.5, 0.75, ((0, 16),))
    eigvals = jnp.clip(jnp.exp(math.log(10.0) - 4.6051702 * jax.random.uniform(key_of[4], (MODULES, FLAT), jnp.float32) ** block_scale(key_of[4], (MODULES, FLAT), ((0, 16),), -0.2, 0.2)), 0.1, 10.0)
    layer_map = jax.random.permutation(key_of[5], MODULES).astype(jnp.int32)
    cand_rows = jax.random.permutation(own_keys[6], CANDS).astype(jnp.int32)
    cand_lists = plant(jax.random.randint(own_keys[7], (QUERIES, LISTMAX), 0, CANDS), jax.random.fold_in(own_keys[7], 1), 0, CANDS - 1).astype(jnp.int32)
    list_lengths = uneven(own_keys[8], QUERIES, QUERIES * LISTMAX // 3, LISTMAX, 2).astype(jnp.int32)
    return {"query_grads": query_grads, "cand_grads": cand_grads, "basis_out": basis_out, "basis_in": basis_in, "eigvals": eigvals, "layer_map": layer_map, "cand_rows": cand_rows, "cand_lists": cand_lists, "list_lengths": list_lengths}


damping = 0.1


def rounded(values):
    return lax.optimization_barrier(values.astype(jnp.bfloat16)).astype(jnp.float32)


def precondition(matrices, out_basis, in_basis, eigen):
    highest = lax.Precision.HIGHEST
    applied = rounded(jnp.einsum('roi,ij->roj', matrices, in_basis, precision=highest))
    rotated = jnp.einsum('op,roj->rpj', out_basis, applied, precision=highest)
    scaled = rounded(rotated / (eigen + damping))
    returned = rounded(jnp.einsum('rpj,ij->rpi', scaled, in_basis, precision=highest))
    return jnp.einsum('op,rpi->roi', out_basis, returned, precision=highest).astype(jnp.bfloat16)


def reference(query_grads, cand_grads, basis_out, basis_in, eigvals, layer_map, cand_rows, cand_lists, list_lengths):
    def one_slot(totals, slot):
        module = layer_map[slot].astype(jnp.int32)
        matrices = lax.dynamic_index_in_dim(query_grads, module, 1, keepdims=False)
        matrices = matrices.astype(jnp.float32).reshape(QUERIES, D_O, D_I)
        out_basis = lax.dynamic_index_in_dim(basis_out, slot, 0, keepdims=False).astype(jnp.float32)
        in_basis = lax.dynamic_index_in_dim(basis_in, slot, 0, keepdims=False).astype(jnp.float32)
        eigen = lax.dynamic_index_in_dim(eigvals, slot, 0, keepdims=False).reshape(D_O, D_I)
        precond = precondition(matrices, out_basis, in_basis, eigen).reshape(QUERIES, FLAT)
        candidates = lax.dynamic_index_in_dim(cand_grads, module, 1, keepdims=False)
        totals = totals + jnp.dot(precond, candidates.T, preferred_element_type=jnp.float32)
        return totals, precond

    totals, stacked = lax.scan(one_slot, jnp.zeros((QUERIES, CANDS), jnp.float32), jnp.arange(MODULES, dtype=jnp.int32))
    inverse = jnp.argsort(layer_map).astype(jnp.int32)
    preconditioned = jnp.transpose(jnp.take(stacked, inverse, axis=0), (1, 0, 2))
    positions = jnp.take(cand_rows, cand_lists).astype(jnp.int32)
    picked = jnp.take_along_axis(totals, positions, axis=1)
    live = jnp.arange(LISTMAX, dtype=jnp.int32)[None, :] < list_lengths[:, None]
    scores = jnp.where(live, picked, jnp.zeros_like(picked))
    return preconditioned, scores
```

```python
import functools

import jax
import jax.numpy as jnp
from jax import lax
from jax.experimental import pallas as pl
from jax.experimental.pallas import tpu as pltpu
from jax.sharding import PartitionSpec as P

damping = 0.1
LANES = 128
PIECES = 3
f32, bf16 = jnp.float32, jnp.bfloat16


def iota(shape, axis):
    return lax.broadcasted_iota(jnp.int32, shape, axis)


def dot(a, b, dims=((1,), (0,))):
    return lax.dot_general(a, b, (dims, ((), ())), preferred_element_type=f32)


def holds(layer_row, modules):
    slots = layer_row.shape[1]
    return (iota((modules, slots), 0) == layer_row).astype(f32).astype(bf16)


def pack(layer_ref, query_ref, cand_ref, out_ref, wide):
    modules, flat = query_ref.shape[1:]
    slots, height, _ = out_ref.shape
    tall = flat // LANES
    one_hot = holds(layer_ref[...], modules)
    sources = [query_ref[r] for r in range(query_ref.shape[0])]
    sources += [cand_ref[r] for r in range(cand_ref.shape[0])]
    for r, rows in enumerate(sources):
        by_slot = dot(one_hot, rows, ((0,), (0,)))
        for j in range(tall):
            wide[pl.ds(r * tall + j, slots, stride=height), :] = by_slot[:, j * LANES : (j + 1) * LANES]
    out_ref[...] = wide[...].reshape(out_ref.shape).astype(bf16)


def half(left, right):
    return jnp.where(iota(left.shape, 1) < LANES // 2, left, right)


def swap(block):
    return pltpu.roll(block, LANES // 2, 1)


def work(moved_ref, out_basis_ref, in_basis_ref, eigen_ref, out_ref, cands, homes):
    sources, height, _ = moved_ref.shape
    _, send, _ = out_ref.shape
    side = out_basis_ref.shape[0]
    tall = side // 2
    per = height // tall - 1
    count = sources * per
    out_basis = out_basis_ref[...]
    in_basis = in_basis_ref[...]

    order = (iota((side, side), 1) == 2 * (iota((side, side), 0) % tall) + iota((side, side), 0) // tall)
    order = order.astype(f32).astype(bf16)
    basis = dot(dot(order, out_basis).astype(bf16), order, ((1,), (1,))).astype(bf16)
    twice = (iota((LANES, side), 0) % side == iota((LANES, side), 1)).astype(f32).astype(bf16)
    spread = dot(dot(twice, in_basis).astype(bf16), twice, ((1,), (1,)))
    same = iota((LANES, LANES), 0) // side == iota((LANES, LANES), 1) // side
    inner = jnp.where(same, spread, 0.0).astype(bf16)
    eigen = eigen_ref[...]
    turned = swap(eigen)
    factor = 1.0 / (jnp.concatenate([half(eigen, turned), half(turned, eigen)], axis=0) + damping)

    pairs = []
    for p in range(sources // 2):
        a = moved_ref[2 * p, :tall, :].astype(f32)
        b = moved_ref[2 * p + 1, :tall, :].astype(f32)
        pairs.append(jnp.concatenate([half(a, swap(b)), half(swap(a), b)], axis=0).astype(bf16))

    def stack(wide):
        return jnp.concatenate([wide[:, p * LANES : (p + 1) * LANES] for p in range(len(pairs))], axis=0)

    def spread_out(rows):
        return jnp.concatenate([rows[p * side : (p + 1) * side] for p in range(len(pairs))], axis=1)

    applied = spread_out(dot(jnp.concatenate(pairs, axis=0), inner).astype(bf16))
    rotated = stack(dot(basis, applied, ((0,), (0,))))
    scaled = (rotated.reshape(len(pairs), side, LANES) * factor[None]).reshape(rotated.shape).astype(bf16)
    returned = spread_out(dot(scaled, inner, ((1,), (1,))).astype(bf16))
    precond = dot(basis, returned).astype(bf16).astype(f32)
    for p in range(len(pairs)):
        top = precond[:tall, p * LANES : (p + 1) * LANES]
        low = precond[tall:, p * LANES : (p + 1) * LANES]
        homes[pl.ds(2 * p * send, tall), :] = half(top, swap(low))
        homes[pl.ds((2 * p + 1) * send, tall), :] = half(swap(top), low)

    for d in range(sources):
        cands[pl.ds(d * per * tall, per * tall), :] = moved_ref[d, tall:, :].astype(f32)
    queries_flat = jnp.concatenate(
        [homes[pl.ds(j, sources, stride=send), :].astype(bf16) for j in range(tall)], axis=1
    )
    cands_flat = jnp.concatenate(
        [cands[pl.ds(j, count, stride=tall), :].astype(bf16) for j in range(tall)], axis=1
    )
    rest = dot(queries_flat, cands_flat, ((1,), (1,)))
    wide = -(-count // LANES)
    if wide * LANES > count:
        rest = jnp.concatenate([rest, jnp.zeros((sources, wide * LANES - count), f32)], axis=1)
    for k in range(PIECES):
        piece = rest.astype(bf16).astype(f32)
        rest = rest - piece
        for t in range(wide):
            homes[pl.ds(tall + k * wide + t, sources, stride=send), :] = piece[:, t * LANES : (t + 1) * LANES]
    for row in range(tall + PIECES * wide, send):
        homes[pl.ds(row, sources, stride=send), :] = jnp.zeros((sources, LANES), f32)
    out_ref[...] = homes[...].reshape(out_ref.shape).astype(bf16)


def upright(row):
    n = row.shape[1]
    return jnp.sum(jnp.where(iota((n, n), 0) == iota((n, n), 1), row, 0.0), axis=1, keepdims=True)


def finish(length_ref, layer_ref, rows_ref, lists_ref, home_ref, precond_ref, scores_ref, wide):
    slots, send, _ = home_ref.shape
    modules, flat = precond_ref.shape[1:]
    count = rows_ref.shape[1]
    tall = flat // LANES
    wide[...] = home_ref[...].reshape(wide.shape).astype(f32)
    by_slot = jnp.concatenate([wide[pl.ds(j, slots, stride=send), :].astype(bf16) for j in range(tall)], axis=1)
    precond_ref[0] = dot(holds(layer_ref[...], modules), by_slot).astype(bf16)
    groups = -(-count // LANES)
    parts = []
    for t in range(groups):
        pieces = [wide[pl.ds(tall + k * groups + t, slots, stride=send), :] for k in range(PIECES)]
        parts.append(jnp.sum((pieces[2] + pieces[1]) + pieces[0], axis=0, keepdims=True))
    dense = parts[0] if groups == 1 else jnp.concatenate(parts, axis=1)
    dense = dense[:, :count]
    by_cand = jnp.sum(
        jnp.where(iota((count, count), 0) == rows_ref[...], upright(dense), 0.0), axis=0, keepdims=True
    )
    lists = lists_ref[...]
    longest = lists.shape[1]
    picked = jnp.sum(
        jnp.where(iota((count, longest), 0) == lists, upright(by_cand), 0.0), axis=0, keepdims=True
    )
    scores_ref[...] = jnp.where(iota((1, longest), 1) < length_ref[0], picked, 0.0)


VMEM = pl.BlockSpec(memory_space=pltpu.VMEM)
SMEM = pl.BlockSpec(memory_space=pltpu.SMEM)
PARAMS = pltpu.CompilerParams(vmem_limit_bytes=40 * 1024 * 1024)


def body(
    query_grads,
    cand_grads,
    basis_out,
    basis_in,
    eigvals,
    layer_map,
    cand_rows,
    cand_lists,
    list_lengths,
):
    own, modules, flat = query_grads.shape
    per = cand_grads.shape[0]
    slots = layer_map.shape[0]
    tall = flat // LANES
    count = cand_rows.shape[0]
    layer_row = layer_map.reshape(1, slots)
    height = (own + per) * tall
    send = tall + -(-PIECES * -(-count // LANES) // 16) * 16

    packed = pl.pallas_call(
        pack,
        out_shape=jax.ShapeDtypeStruct((slots, height, LANES), bf16),
        in_specs=[VMEM] * 3,
        out_specs=VMEM,
        scratch_shapes=[pltpu.VMEM((slots * height, LANES), f32)],
        compiler_params=PARAMS,
        name="pack",
    )(layer_row, query_grads, cand_grads)
    moved = lax.all_to_all(packed, "shard", split_axis=0, concat_axis=0, tiled=True)
    sources = moved.shape[0]
    homes = pl.pallas_call(
        work,
        out_shape=jax.ShapeDtypeStruct((sources, send, LANES), bf16),
        in_specs=[VMEM] * 4,
        out_specs=VMEM,
        scratch_shapes=[pltpu.VMEM((sources * per * tall, LANES), f32), pltpu.VMEM((sources * send, LANES), f32)],
        compiler_params=PARAMS,
        name="work",
    )(
        moved,
        basis_out.reshape(basis_out.shape[1:]),
        basis_in.reshape(basis_in.shape[1:]),
        eigvals.reshape(tall, LANES),
    )
    home = lax.all_to_all(homes, "shard", split_axis=0, concat_axis=0, tiled=True)
    return pl.pallas_call(
        finish,
        out_shape=(
            jax.ShapeDtypeStruct(query_grads.shape, bf16),
            jax.ShapeDtypeStruct(cand_lists.shape, f32),
        ),
        in_specs=[SMEM] + [VMEM] * 4,
        out_specs=(VMEM, VMEM),
        scratch_shapes=[pltpu.VMEM((slots * send, LANES), f32)],
        compiler_params=PARAMS,
        name="finish",
    )(list_lengths, layer_row, cand_rows.reshape(1, count), cand_lists, home)


def solution(mesh):
    return jax.shard_map(
        body,
        mesh=mesh,
        in_specs=(
            P(("groups", "shard"), None, None),
            P(("groups", "shard"), None, None),
            P("shard", None, None),
            P("shard", None, None),
            P("shard", None),
            P(),
            P("groups"),
            P(("groups", "shard"), None),
            P(("groups", "shard")),
        ),
        out_specs=(P(("groups", "shard"), None, None), P(("groups", "shard"), None)),
        check_vma=False,
    )
```

```python
import functools

import jax
import jax.numpy as jnp
from jax import lax
from jax.experimental import pallas as pl
from jax.experimental.pallas import tpu as pltpu
from jax.sharding import PartitionSpec as P

damping = 0.1
LANES = 128
PIECES = 3
f32, bf16 = jnp.float32, jnp.bfloat16


def iota(shape, axis):
    return lax.broadcasted_iota(jnp.int32, shape, axis)


def dot(a, b, dims=((1,), (0,))):
    return lax.dot_general(a, b, (dims, ((), ())), preferred_element_type=f32)


def holds(layer_row, modules):
    slots = layer_row.shape[1]
    return (iota((modules, slots), 0) == layer_row).astype(f32).astype(bf16)


def pack(layer_hbm, query_hbm, cand_hbm, out_ref, layer_ref, query_ref, cand_ref, wide, sems):
    arrivals = [
        pltpu.make_async_copy(source, target, sems.at[i])
        for i, (source, target) in enumerate(
            ((layer_hbm, layer_ref), (query_hbm, query_ref), (cand_hbm, cand_ref))
        )
    ]
    for arrival in arrivals:
        arrival.start()
    for arrival in arrivals:
        arrival.wait()
    modules, flat = query_ref.shape[1:]
    slots, height, _ = out_ref.shape
    tall = flat // LANES
    one_hot = holds(layer_ref[...], modules)
    sources = [query_ref[r] for r in range(query_ref.shape[0])]
    sources += [cand_ref[r] for r in range(cand_ref.shape[0])]
    for r, rows in enumerate(sources):
        by_slot = dot(one_hot, rows, ((0,), (0,)))
        for j in range(tall):
            wide[pl.ds(r * tall + j, slots, stride=height), :] = by_slot[:, j * LANES : (j + 1) * LANES]
    out_ref[...] = wide[...].reshape(out_ref.shape).astype(bf16)


def half(left, right):
    return jnp.where(iota(left.shape, 1) < LANES // 2, left, right)


def swap(block):
    return pltpu.roll(block, LANES // 2, 1)


def work(moved_ref, out_basis_ref, in_basis_ref, eigen_ref, out_ref, cands, homes):
    sources, height, _ = moved_ref.shape
    _, send, _ = out_ref.shape
    side = out_basis_ref.shape[0]
    tall = side // 2
    per = height // tall - 1
    count = sources * per
    out_basis = out_basis_ref[...]
    in_basis = in_basis_ref[...]

    order = (iota((side, side), 1) == 2 * (iota((side, side), 0) % tall) + iota((side, side), 0) // tall)
    order = order.astype(f32).astype(bf16)
    basis = dot(dot(order, out_basis).astype(bf16), order, ((1,), (1,))).astype(bf16)
    twice = (iota((LANES, side), 0) % side == iota((LANES, side), 1)).astype(f32).astype(bf16)
    spread = dot(dot(twice, in_basis).astype(bf16), twice, ((1,), (1,)))
    same = iota((LANES, LANES), 0) // side == iota((LANES, LANES), 1) // side
    inner = jnp.where(same, spread, 0.0).astype(bf16)
    eigen = eigen_ref[...]
    turned = swap(eigen)
    factor = 1.0 / (jnp.concatenate([half(eigen, turned), half(turned, eigen)], axis=0) + damping)

    pairs = []
    for p in range(sources // 2):
        a = moved_ref[2 * p, :tall, :].astype(f32)
        b = moved_ref[2 * p + 1, :tall, :].astype(f32)
        pairs.append(jnp.concatenate([half(a, swap(b)), half(swap(a), b)], axis=0).astype(bf16))

    def stack(wide):
        return jnp.concatenate([wide[:, p * LANES : (p + 1) * LANES] for p in range(len(pairs))], axis=0)

    def spread_out(rows):
        return jnp.concatenate([rows[p * side : (p + 1) * side] for p in range(len(pairs))], axis=1)

    applied = spread_out(dot(jnp.concatenate(pairs, axis=0), inner).astype(bf16))
    rotated = stack(dot(basis, applied, ((0,), (0,))))
    scaled = (rotated.reshape(len(pairs), side, LANES) * factor[None]).reshape(rotated.shape).astype(bf16)
    returned = spread_out(dot(scaled, inner, ((1,), (1,))).astype(bf16))
    precond = dot(basis, returned).astype(bf16).astype(f32)
    for p in range(len(pairs)):
        top = precond[:tall, p * LANES : (p + 1) * LANES]
        low = precond[tall:, p * LANES : (p + 1) * LANES]
        homes[pl.ds(2 * p * send, tall), :] = half(top, swap(low))
        homes[pl.ds((2 * p + 1) * send, tall), :] = half(swap(top), low)

    for d in range(sources):
        cands[pl.ds(d * per * tall, per * tall), :] = moved_ref[d, tall:, :].astype(f32)
    queries_flat = jnp.concatenate(
        [homes[pl.ds(j, sources, stride=send), :].astype(bf16) for j in range(tall)], axis=1
    )
    cands_flat = jnp.concatenate(
        [cands[pl.ds(j, count, stride=tall), :].astype(bf16) for j in range(tall)], axis=1
    )
    rest = dot(queries_flat, cands_flat, ((1,), (1,)))
    wide = -(-count // LANES)
    if wide * LANES > count:
        rest = jnp.concatenate([rest, jnp.zeros((sources, wide * LANES - count), f32)], axis=1)
    for k in range(PIECES):
        piece = rest.astype(bf16).astype(f32)
        rest = rest - piece
        for t in range(wide):
            homes[pl.ds(tall + k * wide + t, sources, stride=send), :] = piece[:, t * LANES : (t + 1) * LANES]
    for row in range(tall + PIECES * wide, send):
        homes[pl.ds(row, sources, stride=send), :] = jnp.zeros((sources, LANES), f32)
    out_ref[...] = homes[...].reshape(out_ref.shape).astype(bf16)


def upright(row):
    n = row.shape[1]
    return jnp.sum(jnp.where(iota((n, n), 0) == iota((n, n), 1), row, 0.0), axis=1, keepdims=True)


def finish(length_ref, layer_ref, rows_ref, lists_ref, home_ref, precond_ref, scores_ref, wide):
    slots, send, _ = home_ref.shape
    modules, flat = precond_ref.shape[1:]
    count = rows_ref.shape[1]
    tall = flat // LANES
    wide[...] = home_ref[...].reshape(wide.shape).astype(f32)
    by_slot = jnp.concatenate([wide[pl.ds(j, slots, stride=send), :].astype(bf16) for j in range(tall)], axis=1)
    precond_ref[0] = dot(holds(layer_ref[...], modules), by_slot).astype(bf16)
    groups = -(-count // LANES)
    parts = []
    for t in range(groups):
        pieces = [wide[pl.ds(tall + k * groups + t, slots, stride=send), :] for k in range(PIECES)]
        parts.append(jnp.sum((pieces[2] + pieces[1]) + pieces[0], axis=0, keepdims=True))
    dense = parts[0] if groups == 1 else jnp.concatenate(parts, axis=1)
    dense = dense[:, :count]
    by_cand = jnp.sum(
        jnp.where(iota((count, count), 0) == rows_ref[...], upright(dense), 0.0), axis=0, keepdims=True
    )
    lists = lists_ref[...]
    longest = lists.shape[1]
    picked = jnp.sum(
        jnp.where(iota((count, longest), 0) == lists, upright(by_cand), 0.0), axis=0, keepdims=True
    )
    scores_ref[...] = jnp.where(iota((1, longest), 1) < length_ref[0], picked, 0.0)


VMEM = pl.BlockSpec(memory_space=pltpu.VMEM)
HBM = pl.BlockSpec(memory_space=pltpu.HBM)
SMEM = pl.BlockSpec(memory_space=pltpu.SMEM)
PARAMS = pltpu.CompilerParams(vmem_limit_bytes=40 * 1024 * 1024)
FULL = pltpu.CompilerParams(vmem_limit_bytes=56 * 1024 * 1024)


def body(
    query_grads,
    cand_grads,
    basis_out,
    basis_in,
    eigvals,
    layer_map,
    cand_rows,
    cand_lists,
    list_lengths,
):
    own, modules, flat = query_grads.shape
    per = cand_grads.shape[0]
    slots = layer_map.shape[0]
    tall = flat // LANES
    count = cand_rows.shape[0]
    layer_row = layer_map.reshape(1, slots)
    height = (own + per) * tall
    send = tall + -(-PIECES * -(-count // LANES) // 16) * 16

    packed = pl.pallas_call(
        pack,
        out_shape=jax.ShapeDtypeStruct((slots, height, LANES), bf16),
        in_specs=[HBM] * 3,
        out_specs=VMEM,
        scratch_shapes=[
            pltpu.VMEM(layer_row.shape, jnp.int32),
            pltpu.VMEM(query_grads.shape, bf16),
            pltpu.VMEM(cand_grads.shape, bf16),
            pltpu.VMEM((slots * height, LANES), f32),
            pltpu.SemaphoreType.DMA((3,)),
        ],
        compiler_params=FULL,
        name="pack",
    )(layer_row, query_grads, cand_grads)
    moved = lax.all_to_all(packed, "shard", split_axis=0, concat_axis=0, tiled=True)
    sources = moved.shape[0]
    homes = pl.pallas_call(
        work,
        out_shape=jax.ShapeDtypeStruct((sources, send, LANES), bf16),
        in_specs=[VMEM] * 4,
        out_specs=VMEM,
        scratch_shapes=[pltpu.VMEM((sources * per * tall, LANES), f32), pltpu.VMEM((sources * send, LANES), f32)],
        compiler_params=PARAMS,
        name="work",
    )(
        moved,
        basis_out.reshape(basis_out.shape[1:]),
        basis_in.reshape(basis_in.shape[1:]),
        eigvals.reshape(tall, LANES),
    )
    home = lax.all_to_all(homes, "shard", split_axis=0, concat_axis=0, tiled=True)
    return pl.pallas_call(
        finish,
        out_shape=(
            jax.ShapeDtypeStruct(query_grads.shape, bf16),
            jax.ShapeDtypeStruct(cand_lists.shape, f32),
        ),
        in_specs=[SMEM] + [VMEM] * 4,
        out_specs=(VMEM, VMEM),
        scratch_shapes=[pltpu.VMEM((slots * send, LANES), f32)],
        compiler_params=PARAMS,
        name="finish",
    )(list_lengths, layer_row, cand_rows.reshape(1, count), cand_lists, home)


def solution(mesh):
    return jax.shard_map(
        body,
        mesh=mesh,
        in_specs=(
            P(("groups", "shard"), None, None),
            P(("groups", "shard"), None, None),
            P("shard", None, None),
            P("shard", None, None),
            P("shard", None),
            P(),
            P("groups"),
            P(("groups", "shard"), None),
            P(("groups", "shard")),
        ),
        out_specs=(P(("groups", "shard"), None, None), P(("groups", "shard"), None)),
        check_vma=False,
    )
```

```python
import functools

import jax
import jax.numpy as jnp
from jax import lax
from jax.experimental import pallas as pl
from jax.experimental.pallas import tpu as pltpu
from jax.sharding import PartitionSpec as P

damping = 0.1
LANES = 128
EIGEN_PIECES = 2
f32, bf16 = jnp.float32, jnp.bfloat16


def iota(shape, axis):
    return lax.broadcasted_iota(jnp.int32, shape, axis)


def dot(a, b, dims=((1,), (0,))):
    return lax.dot_general(a, b, (dims, ((), ())), preferred_element_type=f32)


def holds(layer_row, modules):
    slots = layer_row.shape[1]
    return (iota((modules, slots), 0) == layer_row).astype(f32).astype(bf16)


def half(left, right):
    return jnp.where(iota(left.shape, 1) < LANES // 2, left, right)


def swap(block):
    return pltpu.roll(block, LANES // 2, 1)


def paired(a, b):
    return jnp.concatenate([half(a, swap(b)), half(swap(a), b)], axis=0)


def unpaired(block):
    tall = block.shape[0] // 2
    top, low = block[:tall], block[tall:]
    return half(top, swap(low)), half(swap(top), low)


def reorder(out_basis):
    side = out_basis.shape[0]
    tall = side // 2
    order = iota((side, side), 1) == 2 * (iota((side, side), 0) % tall) + iota((side, side), 0) // tall
    order = order.astype(f32).astype(bf16)
    return dot(dot(order, out_basis).astype(bf16), order, ((1,), (1,)))


def widen(basis, where):
    side = basis.shape[0]
    spot = (iota((side, LANES), 0) + where * side == iota((side, LANES), 1)).astype(f32).astype(bf16)
    return dot(basis, spot)


def pack(
    layer_hbm, query_hbm, cand_hbm, out_basis_ref, in_basis_ref, eigen_ref,
    out_ref, shared_ref, layer_ref, query_ref, cand_ref, wide, sems,
):
    arrivals = [
        pltpu.make_async_copy(source, target, sems.at[i])
        for i, (source, target) in enumerate(
            ((layer_hbm, layer_ref), (query_hbm, query_ref), (cand_hbm, cand_ref))
        )
    ]
    for arrival in arrivals:
        arrival.start()
    side = out_basis_ref.shape[0]
    tall = side // 2
    eigen = eigen_ref[...]
    shared_ref[:side, :] = (
        widen(reorder(out_basis_ref[...]).astype(bf16), 0) + widen(in_basis_ref[...], 1)
    ).astype(bf16)
    for k in range(EIGEN_PIECES):
        piece = eigen.astype(bf16)
        eigen = eigen - piece.astype(f32)
        shared_ref[side + k * tall : side + (k + 1) * tall, :] = piece
    for arrival in arrivals:
        arrival.wait()
    modules, flat = query_ref.shape[1:]
    slots, height, _ = out_ref.shape
    one_hot = holds(layer_ref[...], modules)
    sources = [query_ref[r] for r in range(query_ref.shape[0])]
    sources += [cand_ref[r] for r in range(cand_ref.shape[0])]
    for r, rows in enumerate(sources):
        by_slot = dot(one_hot, rows, ((0,), (0,)))
        for j in range(tall):
            wide[pl.ds(r * tall + j, slots, stride=height), :] = by_slot[:, j * LANES : (j + 1) * LANES]
    out_ref[...] = wide[...].reshape(out_ref.shape).astype(bf16)


def at_home(packed_ref, gathered_ref, layer_ref, precond_ref, wide):
    slots = packed_ref.shape[0]
    modules, flat = precond_ref.shape[1:]
    tall = flat // LANES
    side = 2 * tall
    for p in range(slots // 2):
        a, b = 2 * p, 2 * p + 1
        basis_a, basis_b = gathered_ref[a, :side, :].astype(f32), gathered_ref[b, :side, :].astype(f32)
        zero = jnp.zeros_like(basis_a)
        turned_b = swap(basis_b)
        inner = jnp.concatenate([half(swap(basis_a), zero), half(zero, basis_b)], axis=0).astype(bf16)
        tower = jnp.concatenate([basis_a[:, :side], basis_b[:, :side]], axis=0).astype(bf16)
        beside = half(basis_a, turned_b).astype(bf16)
        eigens = []
        for s in (a, b):
            pieces = [
                gathered_ref[s, side + k * tall : side + (k + 1) * tall, :].astype(f32)
                for k in range(EIGEN_PIECES)
            ]
            eigens.append(sum(pieces[1:], pieces[0]))
        divisor = paired(*eigens) + damping
        query = paired(packed_ref[a, :tall, :].astype(f32), packed_ref[b, :tall, :].astype(f32)).astype(bf16)

        def apart(block):
            return jnp.concatenate([half(block, zero), half(zero, block)], axis=0).astype(bf16)

        applied = dot(query, inner).astype(bf16).astype(f32)
        rotated = dot(tower, apart(applied), ((0,), (0,)))
        scaled = (rotated / divisor).astype(bf16)
        returned = dot(scaled, inner, ((1,), (1,))).astype(bf16).astype(f32)
        precond_a, precond_b = unpaired(dot(beside, apart(returned)))
        wide[pl.ds(a * tall, tall), :] = precond_a
        wide[pl.ds(b * tall, tall), :] = precond_b
    by_slot = jnp.concatenate([wide[pl.ds(j, slots, stride=tall), :].astype(bf16) for j in range(tall)], axis=1)
    precond_ref[0] = dot(holds(layer_ref[...], modules), by_slot).astype(bf16)


def work(moved_ref, out_basis_ref, in_basis_ref, eigen_ref, out_ref, cands, queries):
    sources, height, _ = moved_ref.shape
    side = out_basis_ref.shape[0]
    tall = side // 2
    per = height // tall - 1
    count = sources * per
    basis = reorder(out_basis_ref[...]).astype(bf16)
    in_basis = in_basis_ref[...]
    inner = jnp.concatenate([widen(in_basis, 0), widen(in_basis, 1)], axis=0).astype(bf16)
    eigen = eigen_ref[...]
    factor = 1.0 / (paired(eigen, eigen) + damping)
    pairs = [
        paired(moved_ref[2 * p, :tall, :].astype(f32), moved_ref[2 * p + 1, :tall, :].astype(f32)).astype(bf16)
        for p in range(sources // 2)
    ]

    def stack(wide):
        return jnp.concatenate([wide[:, p * LANES : (p + 1) * LANES] for p in range(len(pairs))], axis=0)

    def spread_out(rows):
        return jnp.concatenate([rows[p * side : (p + 1) * side] for p in range(len(pairs))], axis=1)

    applied = spread_out(dot(jnp.concatenate(pairs, axis=0), inner).astype(bf16))
    rotated = stack(dot(basis, applied, ((0,), (0,))))
    scaled = (rotated.reshape(len(pairs), side, LANES) * factor[None]).reshape(rotated.shape).astype(bf16)
    returned = spread_out(dot(scaled, inner, ((1,), (1,))).astype(bf16))
    precond = dot(basis, returned).astype(bf16).astype(f32)
    for p in range(len(pairs)):
        a, b = unpaired(precond[:, p * LANES : (p + 1) * LANES])
        queries[pl.ds(2 * p * tall, tall), :] = a
        queries[pl.ds((2 * p + 1) * tall, tall), :] = b

    for d in range(sources):
        cands[pl.ds(d * per * tall, per * tall), :] = moved_ref[d, tall:, :].astype(f32)
    queries_flat = jnp.concatenate(
        [queries[pl.ds(j, sources, stride=tall), :].astype(bf16) for j in range(tall)], axis=1
    )
    cands_flat = jnp.concatenate(
        [cands[pl.ds(j, count, stride=tall), :].astype(bf16) for j in range(tall)], axis=1
    )
    partial = dot(queries_flat, cands_flat, ((1,), (1,)))
    width = out_ref.shape[2]
    if width > count:
        partial = jnp.concatenate([partial, jnp.zeros((sources, width - count), f32)], axis=1)
    out_ref[...] = partial.reshape(out_ref.shape)


def upright(row):
    n = row.shape[1]
    return jnp.sum(jnp.where(iota((n, n), 0) == iota((n, n), 1), row, 0.0), axis=1, keepdims=True)


def finish(length_ref, rows_ref, lists_ref, partial_ref, scores_ref):
    count = rows_ref.shape[1]
    dense = jnp.sum(partial_ref[...], axis=0)[:, :count]
    by_cand = jnp.sum(
        jnp.where(iota((count, count), 0) == rows_ref[...], upright(dense), 0.0), axis=0, keepdims=True
    )
    lists = lists_ref[...]
    longest = lists.shape[1]
    picked = jnp.sum(
        jnp.where(iota((count, longest), 0) == lists, upright(by_cand), 0.0), axis=0, keepdims=True
    )
    scores_ref[...] = jnp.where(iota((1, longest), 1) < length_ref[0], picked, 0.0)


VMEM = pl.BlockSpec(memory_space=pltpu.VMEM)
HBM = pl.BlockSpec(memory_space=pltpu.HBM)
SMEM = pl.BlockSpec(memory_space=pltpu.SMEM)
PARAMS = pltpu.CompilerParams(vmem_limit_bytes=40 * 1024 * 1024)
FULL = pltpu.CompilerParams(vmem_limit_bytes=56 * 1024 * 1024)


def body(
    query_grads,
    cand_grads,
    basis_out,
    basis_in,
    eigvals,
    layer_map,
    cand_rows,
    cand_lists,
    list_lengths,
):
    own, modules, flat = query_grads.shape
    per = cand_grads.shape[0]
    slots = layer_map.shape[0]
    tall = flat // LANES
    count = cand_rows.shape[0]
    layer_row = layer_map.reshape(1, slots)
    height = (own + per) * tall
    side = basis_out.shape[1]
    width = -(-count // LANES) * LANES
    out_basis = basis_out.reshape(basis_out.shape[1:])
    in_basis = basis_in.reshape(basis_in.shape[1:])
    eigen = eigvals.reshape(tall, LANES)

    packed, shared = pl.pallas_call(
        pack,
        out_shape=(
            jax.ShapeDtypeStruct((slots, height, LANES), bf16),
            jax.ShapeDtypeStruct((side + EIGEN_PIECES * tall, LANES), bf16),
        ),
        in_specs=[HBM] * 3 + [VMEM] * 3,
        out_specs=(VMEM, VMEM),
        scratch_shapes=[
            pltpu.VMEM(layer_row.shape, jnp.int32),
            pltpu.VMEM(query_grads.shape, bf16),
            pltpu.VMEM(cand_grads.shape, bf16),
            pltpu.VMEM((slots * height, LANES), f32),
            pltpu.SemaphoreType.DMA((3,)),
        ],
        compiler_params=FULL,
        name="pack",
    )(layer_row, query_grads, cand_grads, out_basis, in_basis, eigen)
    gathered = lax.all_gather(shared, "shard", axis=0, tiled=False)
    moved = lax.all_to_all(packed, "shard", split_axis=0, concat_axis=0, tiled=True)
    sources = moved.shape[0]
    partial = pl.pallas_call(
        work,
        out_shape=jax.ShapeDtypeStruct((sources, 1, width), f32),
        in_specs=[VMEM] * 4,
        out_specs=VMEM,
        scratch_shapes=[pltpu.VMEM((sources * per * tall, LANES), f32), pltpu.VMEM((sources * tall, LANES), f32)],
        compiler_params=PARAMS,
        name="work",
    )(moved, out_basis, in_basis, eigen)
    partials = lax.all_to_all(partial, "shard", split_axis=0, concat_axis=0, tiled=True)
    precond = pl.pallas_call(
        at_home,
        out_shape=jax.ShapeDtypeStruct(query_grads.shape, bf16),
        in_specs=[VMEM] * 3,
        out_specs=VMEM,
        scratch_shapes=[pltpu.VMEM((slots * tall, LANES), f32)],
        compiler_params=PARAMS,
        cost_estimate=pl.CostEstimate(
            flops=8 * slots * side * LANES * LANES, bytes_accessed=4 * slots * height * LANES, transcendentals=0
        ),
        name="at_home",
    )(packed, gathered, layer_row)
    scores = pl.pallas_call(
        finish,
        out_shape=jax.ShapeDtypeStruct(cand_lists.shape, f32),
        in_specs=[SMEM] + [VMEM] * 3,
        out_specs=VMEM,
        compiler_params=PARAMS,
        name="finish",
    )(list_lengths, cand_rows.reshape(1, count), cand_lists, partials)
    return precond, scores


def solution(mesh):
    return jax.shard_map(
        body,
        mesh=mesh,
        in_specs=(
            P(("groups", "shard"), None, None),
            P(("groups", "shard"), None, None),
            P("shard", None, None),
            P("shard", None, None),
            P("shard", None),
            P(),
            P("groups"),
            P(("groups", "shard"), None),
            P(("groups", "shard")),
        ),
        out_specs=(P(("groups", "shard"), None, None), P(("groups", "shard"), None)),
        check_vma=False,
    )
```

```python
import functools

import jax
import jax.numpy as jnp
from jax import lax
from jax.experimental import pallas as pl
from jax.experimental.pallas import tpu as pltpu
from jax.sharding import PartitionSpec as P

damping = 0.1
LANES = 128
PIECES = 3
f32, bf16 = jnp.float32, jnp.bfloat16


def iota(shape, axis):
    return lax.broadcasted_iota(jnp.int32, shape, axis)


def dot(a, b, dims=((1,), (0,))):
    return lax.dot_general(a, b, (dims, ((), ())), preferred_element_type=f32)


def holds(layer_row, modules):
    slots = layer_row.shape[1]
    return (iota((modules, slots), 0) == layer_row).astype(f32).astype(bf16)


def pack(direct, layer_hbm, query_hbm, cand_hbm, *refs):
    *out_refs, layer_ref, query_ref, cand_ref, wide, sems = refs
    arrivals = [
        pltpu.make_async_copy(source, target, sems.at[i])
        for i, (source, target) in enumerate(
            ((layer_hbm, layer_ref), (query_hbm, query_ref), (cand_hbm, cand_ref))
        )
    ]
    for arrival in arrivals:
        arrival.start()
    for arrival in arrivals:
        arrival.wait()
    modules, flat = query_ref.shape[1:]
    slots = layer_ref.shape[1]
    height = out_refs[0].shape[-2]
    tall = flat // LANES
    one_hot = holds(layer_ref[...], modules)
    if direct:
        me = lax.axis_index("shard")
        partner = iota((slots, slots), 0) == (iota((slots, slots), 1) ^ me)
        one_hot = dot(one_hot, partner.astype(f32).astype(bf16)).astype(bf16)
    sources = [query_ref[r] for r in range(query_ref.shape[0])]
    sources += [cand_ref[r] for r in range(cand_ref.shape[0])]
    for r, rows in enumerate(sources):
        by_slot = dot(one_hot, rows, ((0,), (0,)))
        for j in range(tall):
            wide[pl.ds(r * tall + j, slots, stride=height), :] = by_slot[:, j * LANES : (j + 1) * LANES]
    for k in range(slots):
        block = wide[pl.ds(k * height, height), :].astype(bf16)
        if direct:
            out_refs[k][...] = block
        else:
            out_refs[0][k] = block


def half(left, right):
    return jnp.where(iota(left.shape, 1) < LANES // 2, left, right)


def swap(block):
    return pltpu.roll(block, LANES // 2, 1)


def work(direct, *refs):
    *moved_refs, out_basis_ref, in_basis_ref, eigen_ref, out_ref, cands, homes = refs
    sources = out_ref.shape[0]
    height = moved_refs[0].shape[-2]
    me = lax.axis_index("shard") if direct else 0

    def arrived(k, rows):
        return (moved_refs[k][rows, :] if direct else moved_refs[0][k, rows, :]).astype(f32)

    def place(k, size):
        return pl.multiple_of((k ^ me) * size, 8) if direct else k * size

    _, send, _ = out_ref.shape
    side = out_basis_ref.shape[0]
    tall = side // 2
    per = height // tall - 1
    count = sources * per
    out_basis = out_basis_ref[...]
    in_basis = in_basis_ref[...]

    order = (iota((side, side), 1) == 2 * (iota((side, side), 0) % tall) + iota((side, side), 0) // tall)
    order = order.astype(f32).astype(bf16)
    basis = dot(dot(order, out_basis).astype(bf16), order, ((1,), (1,))).astype(bf16)
    twice = (iota((LANES, side), 0) % side == iota((LANES, side), 1)).astype(f32).astype(bf16)
    spread = dot(dot(twice, in_basis).astype(bf16), twice, ((1,), (1,)))
    same = iota((LANES, LANES), 0) // side == iota((LANES, LANES), 1) // side
    inner = jnp.where(same, spread, 0.0).astype(bf16)
    eigen = eigen_ref[...]
    turned = swap(eigen)
    factor = 1.0 / (jnp.concatenate([half(eigen, turned), half(turned, eigen)], axis=0) + damping)

    pairs = []
    for p in range(sources // 2):
        a = arrived(2 * p, slice(0, tall))
        b = arrived(2 * p + 1, slice(0, tall))
        pairs.append(jnp.concatenate([half(a, swap(b)), half(swap(a), b)], axis=0).astype(bf16))

    def stack(wide):
        return jnp.concatenate([wide[:, p * LANES : (p + 1) * LANES] for p in range(len(pairs))], axis=0)

    def spread_out(rows):
        return jnp.concatenate([rows[p * side : (p + 1) * side] for p in range(len(pairs))], axis=1)

    applied = spread_out(dot(jnp.concatenate(pairs, axis=0), inner).astype(bf16))
    rotated = stack(dot(basis, applied, ((0,), (0,))))
    scaled = (rotated.reshape(len(pairs), side, LANES) * factor[None]).reshape(rotated.shape).astype(bf16)
    returned = spread_out(dot(scaled, inner, ((1,), (1,))).astype(bf16))
    precond = dot(basis, returned).astype(bf16).astype(f32)
    for p in range(len(pairs)):
        top = precond[:tall, p * LANES : (p + 1) * LANES]
        low = precond[tall:, p * LANES : (p + 1) * LANES]
        homes[pl.ds(place(2 * p, send), tall), :] = half(top, swap(low))
        homes[pl.ds(place(2 * p + 1, send), tall), :] = half(swap(top), low)

    for d in range(sources):
        cands[pl.ds(place(d, per * tall), per * tall), :] = arrived(d, slice(tall, height))
    queries_flat = jnp.concatenate(
        [homes[pl.ds(j, sources, stride=send), :].astype(bf16) for j in range(tall)], axis=1
    )
    cands_flat = jnp.concatenate(
        [cands[pl.ds(j, count, stride=tall), :].astype(bf16) for j in range(tall)], axis=1
    )
    rest = dot(queries_flat, cands_flat, ((1,), (1,)))
    wide = -(-count // LANES)
    if wide * LANES > count:
        rest = jnp.concatenate([rest, jnp.zeros((sources, wide * LANES - count), f32)], axis=1)
    for k in range(PIECES):
        piece = rest.astype(bf16).astype(f32)
        rest = rest - piece
        for t in range(wide):
            homes[pl.ds(tall + k * wide + t, sources, stride=send), :] = piece[:, t * LANES : (t + 1) * LANES]
    for row in range(tall + PIECES * wide, send):
        homes[pl.ds(row, sources, stride=send), :] = jnp.zeros((sources, LANES), f32)
    out_ref[...] = homes[...].reshape(out_ref.shape).astype(bf16)


def upright(row):
    n = row.shape[1]
    return jnp.sum(jnp.where(iota((n, n), 0) == iota((n, n), 1), row, 0.0), axis=1, keepdims=True)


def finish(length_ref, layer_ref, rows_ref, lists_ref, home_ref, precond_ref, scores_ref, wide):
    slots, send, _ = home_ref.shape
    modules, flat = precond_ref.shape[1:]
    count = rows_ref.shape[1]
    tall = flat // LANES
    wide[...] = home_ref[...].reshape(wide.shape).astype(f32)
    by_slot = jnp.concatenate([wide[pl.ds(j, slots, stride=send), :].astype(bf16) for j in range(tall)], axis=1)
    precond_ref[0] = dot(holds(layer_ref[...], modules), by_slot).astype(bf16)
    groups = -(-count // LANES)
    parts = []
    for t in range(groups):
        pieces = [wide[pl.ds(tall + k * groups + t, slots, stride=send), :] for k in range(PIECES)]
        parts.append(jnp.sum((pieces[2] + pieces[1]) + pieces[0], axis=0, keepdims=True))
    dense = parts[0] if groups == 1 else jnp.concatenate(parts, axis=1)
    dense = dense[:, :count]
    by_cand = jnp.sum(
        jnp.where(iota((count, count), 0) == rows_ref[...], upright(dense), 0.0), axis=0, keepdims=True
    )
    lists = lists_ref[...]
    longest = lists.shape[1]
    picked = jnp.sum(
        jnp.where(iota((count, longest), 0) == lists, upright(by_cand), 0.0), axis=0, keepdims=True
    )
    scores_ref[...] = jnp.where(iota((1, longest), 1) < length_ref[0], picked, 0.0)


VMEM = pl.BlockSpec(memory_space=pltpu.VMEM)
HBM = pl.BlockSpec(memory_space=pltpu.HBM)
SMEM = pl.BlockSpec(memory_space=pltpu.SMEM)
PARAMS = pltpu.CompilerParams(vmem_limit_bytes=40 * 1024 * 1024)
FULL = pltpu.CompilerParams(vmem_limit_bytes=56 * 1024 * 1024)


def body(
    query_grads,
    cand_grads,
    basis_out,
    basis_in,
    eigvals,
    layer_map,
    cand_rows,
    cand_lists,
    list_lengths,
):
    own, modules, flat = query_grads.shape
    per = cand_grads.shape[0]
    slots = layer_map.shape[0]
    tall = flat // LANES
    count = cand_rows.shape[0]
    layer_row = layer_map.reshape(1, slots)
    height = (own + per) * tall
    send = tall + -(-PIECES * -(-count // LANES) // 16) * 16

    sources = lax.axis_size("shard")
    direct = sources <= 16
    block = jax.ShapeDtypeStruct((height, LANES), bf16)
    blocks = [block] * slots if direct else [jax.ShapeDtypeStruct((slots, height, LANES), bf16)]

    packed = pl.pallas_call(
        functools.partial(pack, direct),
        out_shape=blocks,
        in_specs=[HBM] * 3,
        out_specs=[VMEM] * len(blocks),
        scratch_shapes=[
            pltpu.VMEM(layer_row.shape, jnp.int32),
            pltpu.VMEM(query_grads.shape, bf16),
            pltpu.VMEM(cand_grads.shape, bf16),
            pltpu.VMEM((slots * height, LANES), f32),
            pltpu.SemaphoreType.DMA((3,)),
        ],
        compiler_params=FULL,
        name="pack",
    )(layer_row, query_grads, cand_grads)
    if direct:
        moved = [packed[0]] + [
            lax.ppermute(packed[k], "shard", [(i, i ^ k) for i in range(sources)]) for k in range(1, sources)
        ]
    else:
        moved = [lax.all_to_all(packed[0], "shard", split_axis=0, concat_axis=0, tiled=True)]
    homes = pl.pallas_call(
        functools.partial(work, direct),
        out_shape=jax.ShapeDtypeStruct((sources, send, LANES), bf16),
        in_specs=[VMEM] * (len(moved) + 3),
        out_specs=VMEM,
        scratch_shapes=[pltpu.VMEM((sources * per * tall, LANES), f32), pltpu.VMEM((sources * send, LANES), f32)],
        compiler_params=PARAMS,
        name="work",
    )(
        *moved,
        basis_out.reshape(basis_out.shape[1:]),
        basis_in.reshape(basis_in.shape[1:]),
        eigvals.reshape(tall, LANES),
    )
    home = lax.all_to_all(homes, "shard", split_axis=0, concat_axis=0, tiled=True)
    return pl.pallas_call(
        finish,
        out_shape=(
            jax.ShapeDtypeStruct(query_grads.shape, bf16),
            jax.ShapeDtypeStruct(cand_lists.shape, f32),
        ),
        in_specs=[SMEM] + [VMEM] * 4,
        out_specs=(VMEM, VMEM),
        scratch_shapes=[pltpu.VMEM((slots * send, LANES), f32)],
        compiler_params=PARAMS,
        name="finish",
    )(list_lengths, layer_row, cand_rows.reshape(1, count), cand_lists, home)


def solution(mesh):
    return jax.shard_map(
        body,
        mesh=mesh,
        in_specs=(
            P(("groups", "shard"), None, None),
            P(("groups", "shard"), None, None),
            P("shard", None, None),
            P("shard", None, None),
            P("shard", None),
            P(),
            P("groups"),
            P(("groups", "shard"), None),
            P(("groups", "shard")),
        ),
        out_specs=(P(("groups", "shard"), None, None), P(("groups", "shard"), None)),
        check_vma=False,
    )
```

```python
import functools

import jax
import jax.numpy as jnp
from jax import lax
from jax.experimental import pallas as pl
from jax.experimental.pallas import tpu as pltpu
from jax.sharding import PartitionSpec as P

damping = 0.1
LANES = 128
TALL = 32
f32, bf16 = jnp.float32, jnp.bfloat16


def iota(shape, axis):
    return lax.broadcasted_iota(jnp.int32, shape, axis)


def dot(a, b, dims=((1,), (0,))):
    return lax.dot_general(a, b, (dims, ((), ())), preferred_element_type=f32)


def holds(layer_row, modules):
    slots = layer_row.shape[1]
    return (iota((modules, slots), 0) == layer_row).astype(f32).astype(bf16)


def lay_out(layer_row, sources, out_ref, wide):
    modules, flat = sources[0].shape
    slots, height, _ = out_ref.shape
    tall = flat // LANES
    one_hot = holds(layer_row, modules)
    for r, rows in enumerate(sources):
        by_slot = dot(one_hot, rows, ((0,), (0,)))
        for j in range(tall):
            wide[pl.ds(r * tall + j, slots, stride=height), :] = by_slot[:, j * LANES : (j + 1) * LANES]
    out_ref[...] = wide[...].reshape(out_ref.shape).astype(bf16)


def pack_queries(layer_hbm, query_hbm, out_ref, layer_ref, query_ref, wide, sems):
    arrivals = [
        pltpu.make_async_copy(source, target, sems.at[i])
        for i, (source, target) in enumerate(((layer_hbm, layer_ref), (query_hbm, query_ref)))
    ]
    for arrival in arrivals:
        arrival.start()
    for arrival in arrivals:
        arrival.wait()
    lay_out(layer_ref[...], [query_ref[r] for r in range(query_ref.shape[0])], out_ref, wide)


def pack_cands(layer_ref, cand_ref, out_ref, wide):
    lay_out(layer_ref[...], [cand_ref[r] for r in range(cand_ref.shape[0])], out_ref, wide)


def half(left, right):
    return jnp.where(iota(left.shape, 1) < LANES // 2, left, right)


def swap(block):
    return pltpu.roll(block, LANES // 2, 1)


def work(moved_ref, out_basis_ref, in_basis_ref, eigen_ref, out_ref):
    sources, tall, _ = moved_ref.shape
    side = out_basis_ref.shape[0]
    out_basis = out_basis_ref[...]
    in_basis = in_basis_ref[...]

    order = (iota((side, side), 1) == 2 * (iota((side, side), 0) % tall) + iota((side, side), 0) // tall)
    order = order.astype(f32).astype(bf16)
    basis = dot(dot(order, out_basis).astype(bf16), order, ((1,), (1,))).astype(bf16)
    twice = (iota((LANES, side), 0) % side == iota((LANES, side), 1)).astype(f32).astype(bf16)
    spread = dot(dot(twice, in_basis).astype(bf16), twice, ((1,), (1,)))
    same = iota((LANES, LANES), 0) // side == iota((LANES, LANES), 1) // side
    inner = jnp.where(same, spread, 0.0).astype(bf16)
    eigen = eigen_ref[...]
    turned = swap(eigen)
    factor = 1.0 / (jnp.concatenate([half(eigen, turned), half(turned, eigen)], axis=0) + damping)

    pairs = []
    for p in range(sources // 2):
        a = moved_ref[2 * p].astype(f32)
        b = moved_ref[2 * p + 1].astype(f32)
        pairs.append(jnp.concatenate([half(a, swap(b)), half(swap(a), b)], axis=0).astype(bf16))

    def stack(wide):
        return jnp.concatenate([wide[:, p * LANES : (p + 1) * LANES] for p in range(len(pairs))], axis=0)

    def spread_out(rows):
        return jnp.concatenate([rows[p * side : (p + 1) * side] for p in range(len(pairs))], axis=1)

    applied = spread_out(dot(jnp.concatenate(pairs, axis=0), inner).astype(bf16))
    rotated = stack(dot(basis, applied, ((0,), (0,))))
    scaled = (rotated.reshape(len(pairs), side, LANES) * factor[None]).reshape(rotated.shape).astype(bf16)
    returned = spread_out(dot(scaled, inner, ((1,), (1,))).astype(bf16))
    precond = dot(basis, returned).astype(bf16).astype(f32)
    for p in range(len(pairs)):
        top = precond[:tall, p * LANES : (p + 1) * LANES]
        low = precond[tall:, p * LANES : (p + 1) * LANES]
        out_ref[2 * p] = half(top, swap(low)).astype(bf16)
        out_ref[2 * p + 1] = half(swap(top), low).astype(bf16)


def flatten(block_ref, wide):
    wide[...] = block_ref[...].reshape(wide.shape).astype(f32)
    count = wide.shape[0] // TALL
    return jnp.concatenate(
        [wide[pl.ds(j, count, stride=TALL), :].astype(bf16) for j in range(TALL)], axis=1
    )


def compare(precond_ref, moved_ref, out_ref, queries, cands):
    partial = dot(flatten(precond_ref, queries), flatten(moved_ref, cands), ((1,), (1,)))
    sources, count = partial.shape
    width = out_ref.shape[2]
    if width > count:
        partial = jnp.concatenate([partial, jnp.zeros((sources, width - count), f32)], axis=1)
    out_ref[...] = partial.reshape(out_ref.shape)


def come_home(layer_ref, home_ref, precond_ref, wide):
    precond_ref[0] = dot(holds(layer_ref[...], precond_ref.shape[1]), flatten(home_ref, wide)).astype(bf16)


def upright(row):
    n = row.shape[1]
    return jnp.sum(jnp.where(iota((n, n), 0) == iota((n, n), 1), row, 0.0), axis=1, keepdims=True)


def finish(length_ref, rows_ref, lists_ref, partial_ref, scores_ref):
    count = rows_ref.shape[1]
    dense = jnp.sum(partial_ref[...], axis=0)[:, :count]
    by_cand = jnp.sum(
        jnp.where(iota((count, count), 0) == rows_ref[...], upright(dense), 0.0), axis=0, keepdims=True
    )
    lists = lists_ref[...]
    longest = lists.shape[1]
    picked = jnp.sum(
        jnp.where(iota((count, longest), 0) == lists, upright(by_cand), 0.0), axis=0, keepdims=True
    )
    scores_ref[...] = jnp.where(iota((1, longest), 1) < length_ref[0], picked, 0.0)


VMEM = pl.BlockSpec(memory_space=pltpu.VMEM)
HBM = pl.BlockSpec(memory_space=pltpu.HBM)
SMEM = pl.BlockSpec(memory_space=pltpu.SMEM)
PARAMS = pltpu.CompilerParams(vmem_limit_bytes=40 * 1024 * 1024)
FULL = pltpu.CompilerParams(vmem_limit_bytes=56 * 1024 * 1024)


def body(
    query_grads,
    cand_grads,
    basis_out,
    basis_in,
    eigvals,
    layer_map,
    cand_rows,
    cand_lists,
    list_lengths,
):
    own, modules, flat = query_grads.shape
    per = cand_grads.shape[0]
    slots = layer_map.shape[0]
    tall = flat // LANES
    count = cand_rows.shape[0]
    layer_row = layer_map.reshape(1, slots)
    width = -(-count // LANES) * LANES

    def swap_over(x):
        return lax.all_to_all(x, "shard", split_axis=0, concat_axis=0, tiled=True)

    def scratch(rows):
        return pltpu.VMEM((rows * tall, LANES), f32)

    packed_queries = pl.pallas_call(
        pack_queries,
        out_shape=jax.ShapeDtypeStruct((slots, own * tall, LANES), bf16),
        in_specs=[HBM] * 2,
        out_specs=VMEM,
        scratch_shapes=[
            pltpu.VMEM(layer_row.shape, jnp.int32),
            pltpu.VMEM(query_grads.shape, bf16),
            scratch(slots * own),
            pltpu.SemaphoreType.DMA((2,)),
        ],
        compiler_params=FULL,
        name="pack_queries",
    )(layer_row, query_grads)
    moved_queries = swap_over(packed_queries)
    packed_cands = pl.pallas_call(
        pack_cands,
        out_shape=jax.ShapeDtypeStruct((slots, per * tall, LANES), bf16),
        in_specs=[VMEM] * 2,
        out_specs=VMEM,
        scratch_shapes=[scratch(slots * per)],
        compiler_params=PARAMS,
        name="pack_cands",
    )(layer_row, cand_grads)
    moved_cands = swap_over(packed_cands)
    sources = moved_queries.shape[0]
    precond = pl.pallas_call(
        work,
        out_shape=jax.ShapeDtypeStruct(moved_queries.shape, bf16),
        in_specs=[VMEM] * 4,
        out_specs=VMEM,
        compiler_params=PARAMS,
        name="work",
    )(
        moved_queries,
        basis_out.reshape(basis_out.shape[1:]),
        basis_in.reshape(basis_in.shape[1:]),
        eigvals.reshape(tall, LANES),
    )
    home = swap_over(precond)
    partial = pl.pallas_call(
        compare,
        out_shape=jax.ShapeDtypeStruct((sources, 1, width), f32),
        in_specs=[VMEM] * 2,
        out_specs=VMEM,
        scratch_shapes=[scratch(sources * own), scratch(sources * per)],
        compiler_params=PARAMS,
        name="compare",
    )(precond, moved_cands)
    partials = swap_over(partial)
    preconditioned = pl.pallas_call(
        come_home,
        out_shape=jax.ShapeDtypeStruct(query_grads.shape, bf16),
        in_specs=[VMEM] * 2,
        out_specs=VMEM,
        scratch_shapes=[scratch(slots * own)],
        compiler_params=PARAMS,
        name="come_home",
    )(layer_row, home)
    scores = pl.pallas_call(
        finish,
        out_shape=jax.ShapeDtypeStruct(cand_lists.shape, f32),
        in_specs=[SMEM] + [VMEM] * 3,
        out_specs=VMEM,
        compiler_params=PARAMS,
        name="finish",
    )(list_lengths, cand_rows.reshape(1, count), cand_lists, partials)
    return preconditioned, scores


def solution(mesh):
    return jax.shard_map(
        body,
        mesh=mesh,
        in_specs=(
            P(("groups", "shard"), None, None),
            P(("groups", "shard"), None, None),
            P("shard", None, None),
            P("shard", None, None),
            P("shard", None),
            P(),
            P("groups"),
            P(("groups", "shard"), None),
            P(("groups", "shard")),
        ),
        out_specs=(P(("groups", "shard"), None, None), P(("groups", "shard"), None)),
        check_vma=False,
    )
```

```python
import functools

import jax
import jax.numpy as jnp
from jax import lax
from jax.experimental import pallas as pl
from jax.experimental.pallas import tpu as pltpu
from jax.sharding import PartitionSpec as P

damping = 0.1
LANES = 128
PIECES = 3
f32, bf16 = jnp.float32, jnp.bfloat16


def iota(shape, axis):
    return lax.broadcasted_iota(jnp.int32, shape, axis)


def dot(a, b, dims=((1,), (0,))):
    return lax.dot_general(a, b, (dims, ((), ())), preferred_element_type=f32)


def first_of(slots):
    return slots // 4


def holds(layer_row, modules):
    slots = layer_row.shape[1]
    first = first_of(slots)
    layer_row = jnp.concatenate([layer_row[:, first:], layer_row[:, :first]], axis=1)
    return (iota((modules, slots), 0) == layer_row).astype(f32).astype(bf16)


def pack(layer_hbm, query_hbm, cand_hbm, out_ref, layer_ref, query_ref, cand_ref, wide, sems):
    arrivals = [
        pltpu.make_async_copy(source, target, sems.at[i])
        for i, (source, target) in enumerate(
            ((layer_hbm, layer_ref), (query_hbm, query_ref), (cand_hbm, cand_ref))
        )
    ]
    for arrival in arrivals:
        arrival.start()
    for arrival in arrivals:
        arrival.wait()
    modules, flat = query_ref.shape[1:]
    slots, height, _ = out_ref.shape
    tall = flat // LANES
    one_hot = holds(layer_ref[...], modules)
    sources = [query_ref[r] for r in range(query_ref.shape[0])]
    sources += [cand_ref[r] for r in range(cand_ref.shape[0])]
    for r, rows in enumerate(sources):
        by_slot = dot(one_hot, rows, ((0,), (0,)))
        for j in range(tall):
            wide[pl.ds(r * tall + j, slots, stride=height), :] = by_slot[:, j * LANES : (j + 1) * LANES]
    out_ref[...] = wide[...].reshape(out_ref.shape).astype(bf16)


def half(left, right):
    return jnp.where(iota(left.shape, 1) < LANES // 2, left, right)


def swap(block):
    return pltpu.roll(block, LANES // 2, 1)


def work(moved_ref, out_basis_ref, in_basis_ref, eigen_ref, out_ref, cands, homes):
    sources, height, _ = moved_ref.shape
    _, send, _ = out_ref.shape
    side = out_basis_ref.shape[0]
    tall = side // 2
    per = height // tall - 1
    count = sources * per
    out_basis = out_basis_ref[...]
    in_basis = in_basis_ref[...]

    order = (iota((side, side), 1) == 2 * (iota((side, side), 0) % tall) + iota((side, side), 0) // tall)
    order = order.astype(f32).astype(bf16)
    basis = dot(dot(order, out_basis).astype(bf16), order, ((1,), (1,))).astype(bf16)
    twice = (iota((LANES, side), 0) % side == iota((LANES, side), 1)).astype(f32).astype(bf16)
    spread = dot(dot(twice, in_basis).astype(bf16), twice, ((1,), (1,)))
    same = iota((LANES, LANES), 0) // side == iota((LANES, LANES), 1) // side
    inner = jnp.where(same, spread, 0.0).astype(bf16)
    eigen = eigen_ref[...]
    turned = swap(eigen)
    factor = 1.0 / (jnp.concatenate([half(eigen, turned), half(turned, eigen)], axis=0) + damping)

    pairs = []
    for p in range(sources // 2):
        a = moved_ref[2 * p, :tall, :].astype(f32)
        b = moved_ref[2 * p + 1, :tall, :].astype(f32)
        pairs.append(jnp.concatenate([half(a, swap(b)), half(swap(a), b)], axis=0).astype(bf16))

    def stack(wide):
        return jnp.concatenate([wide[:, p * LANES : (p + 1) * LANES] for p in range(len(pairs))], axis=0)

    def spread_out(rows):
        return jnp.concatenate([rows[p * side : (p + 1) * side] for p in range(len(pairs))], axis=1)

    applied = spread_out(dot(jnp.concatenate(pairs, axis=0), inner).astype(bf16))
    rotated = stack(dot(basis, applied, ((0,), (0,))))
    scaled = (rotated.reshape(len(pairs), side, LANES) * factor[None]).reshape(rotated.shape).astype(bf16)
    returned = spread_out(dot(scaled, inner, ((1,), (1,))).astype(bf16))
    precond = dot(basis, returned).astype(bf16).astype(f32)
    for p in range(len(pairs)):
        top = precond[:tall, p * LANES : (p + 1) * LANES]
        low = precond[tall:, p * LANES : (p + 1) * LANES]
        homes[pl.ds(2 * p * send, tall), :] = half(top, swap(low))
        homes[pl.ds((2 * p + 1) * send, tall), :] = half(swap(top), low)

    for d in range(sources):
        cands[pl.ds(d * per * tall, per * tall), :] = moved_ref[d, tall:, :].astype(f32)
    queries_flat = jnp.concatenate(
        [homes[pl.ds(j, sources, stride=send), :].astype(bf16) for j in range(tall)], axis=1
    )
    cands_flat = jnp.concatenate(
        [cands[pl.ds(j, count, stride=tall), :].astype(bf16) for j in range(tall)], axis=1
    )
    rest = dot(queries_flat, cands_flat, ((1,), (1,)))
    wide = -(-count // LANES)
    if wide * LANES > count:
        rest = jnp.concatenate([rest, jnp.zeros((sources, wide * LANES - count), f32)], axis=1)
    for k in range(PIECES):
        piece = rest.astype(bf16).astype(f32)
        rest = rest - piece
        for t in range(wide):
            homes[pl.ds(tall + k * wide + t, sources, stride=send), :] = piece[:, t * LANES : (t + 1) * LANES]
    for row in range(tall + PIECES * wide, send):
        homes[pl.ds(row, sources, stride=send), :] = jnp.zeros((sources, LANES), f32)
    out_ref[...] = homes[...].reshape(out_ref.shape).astype(bf16)


def upright(row):
    n = row.shape[1]
    return jnp.sum(jnp.where(iota((n, n), 0) == iota((n, n), 1), row, 0.0), axis=1, keepdims=True)


def finish(length_ref, layer_ref, rows_ref, lists_ref, home_ref, precond_ref, scores_ref, wide):
    slots, send, _ = home_ref.shape
    modules, flat = precond_ref.shape[1:]
    count = rows_ref.shape[1]
    tall = flat // LANES
    wide[...] = home_ref[...].reshape(wide.shape).astype(f32)
    by_slot = jnp.concatenate([wide[pl.ds(j, slots, stride=send), :].astype(bf16) for j in range(tall)], axis=1)
    precond_ref[0] = dot(holds(layer_ref[...], modules), by_slot).astype(bf16)
    groups = -(-count // LANES)
    parts = []
    for t in range(groups):
        pieces = [wide[pl.ds(tall + k * groups + t, slots, stride=send), :] for k in range(PIECES)]
        parts.append(jnp.sum((pieces[2] + pieces[1]) + pieces[0], axis=0, keepdims=True))
    dense = parts[0] if groups == 1 else jnp.concatenate(parts, axis=1)
    dense = dense[:, :count]
    ahead = first_of(slots) * (count // slots)
    place = rows_ref[...] - ahead
    place = jnp.where(place < 0, place + count, place)
    by_cand = jnp.sum(
        jnp.where(iota((count, count), 0) == place, upright(dense), 0.0), axis=0, keepdims=True
    )
    lists = lists_ref[...]
    longest = lists.shape[1]
    picked = jnp.sum(
        jnp.where(iota((count, longest), 0) == lists, upright(by_cand), 0.0), axis=0, keepdims=True
    )
    scores_ref[...] = jnp.where(iota((1, longest), 1) < length_ref[0], picked, 0.0)


VMEM = pl.BlockSpec(memory_space=pltpu.VMEM)
HBM = pl.BlockSpec(memory_space=pltpu.HBM)
SMEM = pl.BlockSpec(memory_space=pltpu.SMEM)
PARAMS = pltpu.CompilerParams(vmem_limit_bytes=40 * 1024 * 1024)
FULL = pltpu.CompilerParams(vmem_limit_bytes=56 * 1024 * 1024)


def body(
    query_grads,
    cand_grads,
    basis_out,
    basis_in,
    eigvals,
    layer_map,
    cand_rows,
    cand_lists,
    list_lengths,
):
    own, modules, flat = query_grads.shape
    per = cand_grads.shape[0]
    slots = layer_map.shape[0]
    tall = flat // LANES
    count = cand_rows.shape[0]
    layer_row = layer_map.reshape(1, slots)
    height = (own + per) * tall
    send = tall + -(-PIECES * -(-count // LANES) // 8) * 8
    order = [(first_of(slots) + k) % slots for k in range(slots)]

    def swap_over(x):
        return lax.all_to_all(
            x, "shard", split_axis=0, concat_axis=0, tiled=True, axis_index_groups=[order]
        )


    packed = pl.pallas_call(
        pack,
        out_shape=jax.ShapeDtypeStruct((slots, height, LANES), bf16),
        in_specs=[HBM] * 3,
        out_specs=VMEM,
        scratch_shapes=[
            pltpu.VMEM(layer_row.shape, jnp.int32),
            pltpu.VMEM(query_grads.shape, bf16),
            pltpu.VMEM(cand_grads.shape, bf16),
            pltpu.VMEM((slots * height, LANES), f32),
            pltpu.SemaphoreType.DMA((3,)),
        ],
        compiler_params=FULL,
        name="pack",
    )(layer_row, query_grads, cand_grads)
    moved = swap_over(packed)
    sources = moved.shape[0]
    homes = pl.pallas_call(
        work,
        out_shape=jax.ShapeDtypeStruct((sources, send, LANES), bf16),
        in_specs=[VMEM] * 4,
        out_specs=VMEM,
        scratch_shapes=[pltpu.VMEM((sources * per * tall, LANES), f32), pltpu.VMEM((sources * send, LANES), f32)],
        compiler_params=PARAMS,
        name="work",
    )(
        moved,
        basis_out.reshape(basis_out.shape[1:]),
        basis_in.reshape(basis_in.shape[1:]),
        eigvals.reshape(tall, LANES),
    )
    home = swap_over(homes)
    return pl.pallas_call(
        finish,
        out_shape=(
            jax.ShapeDtypeStruct(query_grads.shape, bf16),
            jax.ShapeDtypeStruct(cand_lists.shape, f32),
        ),
        in_specs=[SMEM] + [VMEM] * 4,
        out_specs=(VMEM, VMEM),
        scratch_shapes=[pltpu.VMEM((slots * send, LANES), f32)],
        compiler_params=PARAMS,
        name="finish",
    )(list_lengths, layer_row, cand_rows.reshape(1, count), cand_lists, home)


def solution(mesh):
    return jax.shard_map(
        body,
        mesh=mesh,
        in_specs=(
            P(("groups", "shard"), None, None),
            P(("groups", "shard"), None, None),
            P("shard", None, None),
            P("shard", None, None),
            P("shard", None),
            P(),
            P("groups"),
            P(("groups", "shard"), None),
            P(("groups", "shard")),
        ),
        out_specs=(P(("groups", "shard"), None, None), P(("groups", "shard"), None)),
        check_vma=False,
    )
```

```python
import functools

import jax
import jax.numpy as jnp
from jax import lax
from jax.experimental import pallas as pl
from jax.experimental.pallas import tpu as pltpu
from jax.sharding import PartitionSpec as P

damping = 0.1
LANES = 128
PIECES = 3
f32, bf16 = jnp.float32, jnp.bfloat16


def iota(shape, axis):
    return lax.broadcasted_iota(jnp.int32, shape, axis)


def dot(a, b, dims=((1,), (0,))):
    return lax.dot_general(a, b, (dims, ((), ())), preferred_element_type=f32)


def first_of(slots):
    return slots - 2


def holds(layer_row, modules):
    slots = layer_row.shape[1]
    first = first_of(slots)
    layer_row = jnp.concatenate([layer_row[:, first:], layer_row[:, :first]], axis=1)
    return (iota((modules, slots), 0) == layer_row).astype(f32).astype(bf16)


def pack(layer_hbm, query_hbm, cand_hbm, out_ref, layer_ref, query_ref, cand_ref, wide, sems):
    arrivals = [
        pltpu.make_async_copy(source, target, sems.at[i])
        for i, (source, target) in enumerate(
            ((layer_hbm, layer_ref), (query_hbm, query_ref), (cand_hbm, cand_ref))
        )
    ]
    for arrival in arrivals:
        arrival.start()
    for arrival in arrivals:
        arrival.wait()
    modules, flat = query_ref.shape[1:]
    slots, height, _ = out_ref.shape
    tall = flat // LANES
    one_hot = holds(layer_ref[...], modules)
    sources = [query_ref[r] for r in range(query_ref.shape[0])]
    sources += [cand_ref[r] for r in range(cand_ref.shape[0])]
    for r, rows in enumerate(sources):
        by_slot = dot(one_hot, rows, ((0,), (0,)))
        for j in range(tall):
            wide[pl.ds(r * tall + j, slots, stride=height), :] = by_slot[:, j * LANES : (j + 1) * LANES]
    out_ref[...] = wide[...].reshape(out_ref.shape).astype(bf16)


def half(left, right):
    return jnp.where(iota(left.shape, 1) < LANES // 2, left, right)


def swap(block):
    return pltpu.roll(block, LANES // 2, 1)


def work(moved_ref, out_basis_ref, in_basis_ref, eigen_ref, out_ref, cands, homes):
    sources, height, _ = moved_ref.shape
    _, send, _ = out_ref.shape
    side = out_basis_ref.shape[0]
    tall = side // 2
    per = height // tall - 1
    count = sources * per
    out_basis = out_basis_ref[...]
    in_basis = in_basis_ref[...]

    order = (iota((side, side), 1) == 2 * (iota((side, side), 0) % tall) + iota((side, side), 0) // tall)
    order = order.astype(f32).astype(bf16)
    basis = dot(dot(order, out_basis).astype(bf16), order, ((1,), (1,))).astype(bf16)
    twice = (iota((LANES, side), 0) % side == iota((LANES, side), 1)).astype(f32).astype(bf16)
    spread = dot(dot(twice, in_basis).astype(bf16), twice, ((1,), (1,)))
    same = iota((LANES, LANES), 0) // side == iota((LANES, LANES), 1) // side
    inner = jnp.where(same, spread, 0.0).astype(bf16)
    eigen = eigen_ref[...]
    turned = swap(eigen)
    factor = 1.0 / (jnp.concatenate([half(eigen, turned), half(turned, eigen)], axis=0) + damping)

    pairs = []
    for p in range(sources // 2):
        a = moved_ref[2 * p, :tall, :].astype(f32)
        b = moved_ref[2 * p + 1, :tall, :].astype(f32)
        pairs.append(jnp.concatenate([half(a, swap(b)), half(swap(a), b)], axis=0).astype(bf16))

    def stack(wide):
        return jnp.concatenate([wide[:, p * LANES : (p + 1) * LANES] for p in range(len(pairs))], axis=0)

    def spread_out(rows):
        return jnp.concatenate([rows[p * side : (p + 1) * side] for p in range(len(pairs))], axis=1)

    applied = spread_out(dot(jnp.concatenate(pairs, axis=0), inner).astype(bf16))
    rotated = stack(dot(basis, applied, ((0,), (0,))))
    scaled = (rotated.reshape(len(pairs), side, LANES) * factor[None]).reshape(rotated.shape).astype(bf16)
    returned = spread_out(dot(scaled, inner, ((1,), (1,))).astype(bf16))
    precond = dot(basis, returned).astype(bf16).astype(f32)
    for p in range(len(pairs)):
        top = precond[:tall, p * LANES : (p + 1) * LANES]
        low = precond[tall:, p * LANES : (p + 1) * LANES]
        homes[pl.ds(2 * p * send, tall), :] = half(top, swap(low))
        homes[pl.ds((2 * p + 1) * send, tall), :] = half(swap(top), low)

    for d in range(sources):
        cands[pl.ds(d * per * tall, per * tall), :] = moved_ref[d, tall:, :].astype(f32)
    queries_flat = jnp.concatenate(
        [homes[pl.ds(j, sources, stride=send), :].astype(bf16) for j in range(tall)], axis=1
    )
    cands_flat = jnp.concatenate(
        [cands[pl.ds(j, count, stride=tall), :].astype(bf16) for j in range(tall)], axis=1
    )
    rest = dot(queries_flat, cands_flat, ((1,), (1,)))
    wide = -(-count // LANES)
    if wide * LANES > count:
        rest = jnp.concatenate([rest, jnp.zeros((sources, wide * LANES - count), f32)], axis=1)
    for k in range(PIECES):
        piece = rest.astype(bf16).astype(f32)
        rest = rest - piece
        for t in range(wide):
            homes[pl.ds(tall + k * wide + t, sources, stride=send), :] = piece[:, t * LANES : (t + 1) * LANES]
    for row in range(tall + PIECES * wide, send):
        homes[pl.ds(row, sources, stride=send), :] = jnp.zeros((sources, LANES), f32)
    out_ref[...] = homes[...].reshape(out_ref.shape).astype(bf16)


def upright(row):
    n = row.shape[1]
    return jnp.sum(jnp.where(iota((n, n), 0) == iota((n, n), 1), row, 0.0), axis=1, keepdims=True)


def finish(length_ref, layer_ref, rows_ref, lists_ref, home_ref, precond_ref, scores_ref, wide):
    slots, send, _ = home_ref.shape
    modules, flat = precond_ref.shape[1:]
    count = rows_ref.shape[1]
    tall = flat // LANES
    wide[...] = home_ref[...].reshape(wide.shape).astype(f32)
    by_slot = jnp.concatenate([wide[pl.ds(j, slots, stride=send), :].astype(bf16) for j in range(tall)], axis=1)
    precond_ref[0] = dot(holds(layer_ref[...], modules), by_slot).astype(bf16)
    groups = -(-count // LANES)
    parts = []
    for t in range(groups):
        pieces = [wide[pl.ds(tall + k * groups + t, slots, stride=send), :] for k in range(PIECES)]
        parts.append(jnp.sum((pieces[2] + pieces[1]) + pieces[0], axis=0, keepdims=True))
    dense = parts[0] if groups == 1 else jnp.concatenate(parts, axis=1)
    dense = dense[:, :count]
    ahead = first_of(slots) * (count // slots)
    place = rows_ref[...] - ahead
    place = jnp.where(place < 0, place + count, place)
    by_cand = jnp.sum(
        jnp.where(iota((count, count), 0) == place, upright(dense), 0.0), axis=0, keepdims=True
    )
    lists = lists_ref[...]
    longest = lists.shape[1]
    picked = jnp.sum(
        jnp.where(iota((count, longest), 0) == lists, upright(by_cand), 0.0), axis=0, keepdims=True
    )
    scores_ref[...] = jnp.where(iota((1, longest), 1) < length_ref[0], picked, 0.0)


VMEM = pl.BlockSpec(memory_space=pltpu.VMEM)
HBM = pl.BlockSpec(memory_space=pltpu.HBM)
SMEM = pl.BlockSpec(memory_space=pltpu.SMEM)
PARAMS = pltpu.CompilerParams(vmem_limit_bytes=40 * 1024 * 1024)
FULL = pltpu.CompilerParams(vmem_limit_bytes=56 * 1024 * 1024)


def body(
    query_grads,
    cand_grads,
    basis_out,
    basis_in,
    eigvals,
    layer_map,
    cand_rows,
    cand_lists,
    list_lengths,
):
    own, modules, flat = query_grads.shape
    per = cand_grads.shape[0]
    slots = layer_map.shape[0]
    tall = flat // LANES
    count = cand_rows.shape[0]
    layer_row = layer_map.reshape(1, slots)
    height = (own + per) * tall
    send = tall + -(-PIECES * -(-count // LANES) // 8) * 8
    order = [(first_of(slots) + k) % slots for k in range(slots)]

    def swap_over(x):
        return lax.all_to_all(
            x, "shard", split_axis=0, concat_axis=0, tiled=True, axis_index_groups=[order]
        )


    packed = pl.pallas_call(
        pack,
        out_shape=jax.ShapeDtypeStruct((slots, height, LANES), bf16),
        in_specs=[HBM] * 3,
        out_specs=VMEM,
        scratch_shapes=[
            pltpu.VMEM(layer_row.shape, jnp.int32),
            pltpu.VMEM(query_grads.shape, bf16),
            pltpu.VMEM(cand_grads.shape, bf16),
            pltpu.VMEM((slots * height, LANES), f32),
            pltpu.SemaphoreType.DMA((3,)),
        ],
        compiler_params=FULL,
        name="pack",
    )(layer_row, query_grads, cand_grads)
    moved = swap_over(packed)
    sources = moved.shape[0]
    homes = pl.pallas_call(
        work,
        out_shape=jax.ShapeDtypeStruct((sources, send, LANES), bf16),
        in_specs=[VMEM] * 4,
        out_specs=VMEM,
        scratch_shapes=[pltpu.VMEM((sources * per * tall, LANES), f32), pltpu.VMEM((sources * send, LANES), f32)],
        compiler_params=PARAMS,
        name="work",
    )(
        moved,
        basis_out.reshape(basis_out.shape[1:]),
        basis_in.reshape(basis_in.shape[1:]),
        eigvals.reshape(tall, LANES),
    )
    home = swap_over(homes)
    return pl.pallas_call(
        finish,
        out_shape=(
            jax.ShapeDtypeStruct(query_grads.shape, bf16),
            jax.ShapeDtypeStruct(cand_lists.shape, f32),
        ),
        in_specs=[SMEM] + [VMEM] * 4,
        out_specs=(VMEM, VMEM),
        scratch_shapes=[pltpu.VMEM((slots * send, LANES), f32)],
        compiler_params=PARAMS,
        name="finish",
    )(list_lengths, layer_row, cand_rows.reshape(1, count), cand_lists, home)


def solution(mesh):
    return jax.shard_map(
        body,
        mesh=mesh,
        in_specs=(
            P(("groups", "shard"), None, None),
            P(("groups", "shard"), None, None),
            P("shard", None, None),
            P("shard", None, None),
            P("shard", None),
            P(),
            P("groups"),
            P(("groups", "shard"), None),
            P(("groups", "shard")),
        ),
        out_specs=(P(("groups", "shard"), None, None), P(("groups", "shard"), None)),
        check_vma=False,
    )
```

```python
import functools

import jax
import jax.numpy as jnp
from jax import lax
from jax.experimental import pallas as pl
from jax.experimental.pallas import tpu as pltpu
from jax.sharding import PartitionSpec as P

damping = 0.1
LANES = 128
PIECES = 3
f32, bf16 = jnp.float32, jnp.bfloat16


def iota(shape, axis):
    return lax.broadcasted_iota(jnp.int32, shape, axis)


def dot(a, b, dims=((1,), (0,))):
    return lax.dot_general(a, b, (dims, ((), ())), preferred_element_type=f32)


def order_of(slots, first):
    return [(first + k) % slots for k in range(slots)]


def firsts(slots):
    return slots // 4, slots - 2


def holds(layer_row, modules, first):
    slots = layer_row.shape[1]
    if first:
        layer_row = jnp.concatenate([layer_row[:, first:], layer_row[:, :first]], axis=1)
    return (iota((modules, slots), 0) == layer_row).astype(f32).astype(bf16)


def pack(layer_hbm, query_hbm, cand_hbm, out_ref, layer_ref, query_ref, cand_ref, wide, sems):
    arrivals = [
        pltpu.make_async_copy(source, target, sems.at[i])
        for i, (source, target) in enumerate(
            ((layer_hbm, layer_ref), (query_hbm, query_ref), (cand_hbm, cand_ref))
        )
    ]
    for arrival in arrivals:
        arrival.start()
    arrivals[0].wait()
    modules, flat = query_ref.shape[1:]
    slots, height, _ = out_ref.shape
    tall = flat // LANES
    one_hot = holds(layer_ref[...], modules, firsts(slots)[0])
    sources = [(query_ref, r) for r in range(query_ref.shape[0])] + [(cand_ref, r) for r in range(cand_ref.shape[0])]
    for r, (ref, row) in enumerate(sources):
        if row == 0:
            arrivals[1 if ref is query_ref else 2].wait()
        by_slot = dot(one_hot, ref[row], ((0,), (0,)))
        for j in range(tall):
            wide[pl.ds(r * tall + j, slots, stride=height), :] = by_slot[:, j * LANES : (j + 1) * LANES]
    out_ref[...] = wide[...].reshape(out_ref.shape).astype(bf16)


def half(left, right):
    return jnp.where(iota(left.shape, 1) < LANES // 2, left, right)


def swap(block):
    return pltpu.roll(block, LANES // 2, 1)


def work(moved_ref, out_basis_ref, in_basis_ref, eigen_ref, out_ref, cands, homes):
    sources, height, _ = moved_ref.shape
    _, send, _ = out_ref.shape
    side = out_basis_ref.shape[0]
    tall = side // 2
    per = height // tall - 1
    count = sources * per
    arrive, leave = firsts(sources)
    devices = order_of(sources, arrive)
    places = [(d - leave) % sources for d in devices]
    out_basis = out_basis_ref[...]
    in_basis = in_basis_ref[...]

    order = (iota((side, side), 1) == 2 * (iota((side, side), 0) % tall) + iota((side, side), 0) // tall)
    order = order.astype(f32).astype(bf16)
    basis = dot(dot(order, out_basis).astype(bf16), order, ((1,), (1,))).astype(bf16)
    twice = (iota((LANES, side), 0) % side == iota((LANES, side), 1)).astype(f32).astype(bf16)
    spread = dot(dot(twice, in_basis).astype(bf16), twice, ((1,), (1,)))
    same = iota((LANES, LANES), 0) // side == iota((LANES, LANES), 1) // side
    inner = jnp.where(same, spread, 0.0).astype(bf16)
    eigen = eigen_ref[...]
    turned = swap(eigen)
    factor = 1.0 / (jnp.concatenate([half(eigen, turned), half(turned, eigen)], axis=0) + damping)

    pairs = []
    for p in range(sources // 2):
        a = moved_ref[2 * p, :tall, :].astype(f32)
        b = moved_ref[2 * p + 1, :tall, :].astype(f32)
        pairs.append(jnp.concatenate([half(a, swap(b)), half(swap(a), b)], axis=0).astype(bf16))

    def stack(wide):
        return jnp.concatenate([wide[:, p * LANES : (p + 1) * LANES] for p in range(len(pairs))], axis=0)

    def spread_out(rows):
        return jnp.concatenate([rows[p * side : (p + 1) * side] for p in range(len(pairs))], axis=1)

    applied = spread_out(dot(jnp.concatenate(pairs, axis=0), inner).astype(bf16))
    rotated = stack(dot(basis, applied, ((0,), (0,))))
    scaled = (rotated.reshape(len(pairs), side, LANES) * factor[None]).reshape(rotated.shape).astype(bf16)
    returned = spread_out(dot(scaled, inner, ((1,), (1,))).astype(bf16))
    precond = dot(basis, returned).astype(bf16).astype(f32)
    for p in range(len(pairs)):
        top = precond[:tall, p * LANES : (p + 1) * LANES]
        low = precond[tall:, p * LANES : (p + 1) * LANES]
        homes[pl.ds(places[2 * p] * send, tall), :] = half(top, swap(low))
        homes[pl.ds(places[2 * p + 1] * send, tall), :] = half(swap(top), low)

    for k, d in enumerate(devices):
        cands[pl.ds(d * per * tall, per * tall), :] = moved_ref[k, tall:, :].astype(f32)
    queries_flat = jnp.concatenate(
        [homes[pl.ds(j, sources, stride=send), :].astype(bf16) for j in range(tall)], axis=1
    )
    cands_flat = jnp.concatenate(
        [cands[pl.ds(j, count, stride=tall), :].astype(bf16) for j in range(tall)], axis=1
    )
    rest = dot(queries_flat, cands_flat, ((1,), (1,)))
    wide = -(-count // LANES)
    if wide * LANES > count:
        rest = jnp.concatenate([rest, jnp.zeros((sources, wide * LANES - count), f32)], axis=1)
    for k in range(PIECES):
        piece = rest.astype(bf16).astype(f32)
        rest = rest - piece
        for t in range(wide):
            homes[pl.ds(tall + k * wide + t, sources, stride=send), :] = piece[:, t * LANES : (t + 1) * LANES]
    for row in range(tall + PIECES * wide, send):
        homes[pl.ds(row, sources, stride=send), :] = jnp.zeros((sources, LANES), f32)
    out_ref[...] = homes[...].reshape(out_ref.shape).astype(bf16)


def upright(row):
    n = row.shape[1]
    return jnp.sum(jnp.where(iota((n, n), 0) == iota((n, n), 1), row, 0.0), axis=1, keepdims=True)


def finish(length_ref, layer_ref, rows_ref, lists_ref, home_ref, precond_ref, scores_ref, wide):
    slots, send, _ = home_ref.shape
    modules, flat = precond_ref.shape[1:]
    count = rows_ref.shape[1]
    tall = flat // LANES
    wide[...] = home_ref[...].reshape(wide.shape).astype(f32)
    by_slot = jnp.concatenate([wide[pl.ds(j, slots, stride=send), :].astype(bf16) for j in range(tall)], axis=1)
    precond_ref[0] = dot(holds(layer_ref[...], modules, firsts(slots)[1]), by_slot).astype(bf16)
    groups = -(-count // LANES)
    parts = []
    for t in range(groups):
        pieces = [wide[pl.ds(tall + k * groups + t, slots, stride=send), :] for k in range(PIECES)]
        parts.append(jnp.sum((pieces[2] + pieces[1]) + pieces[0], axis=0, keepdims=True))
    dense = parts[0] if groups == 1 else jnp.concatenate(parts, axis=1)
    dense = dense[:, :count]
    by_cand = jnp.sum(
        jnp.where(iota((count, count), 0) == rows_ref[...], upright(dense), 0.0), axis=0, keepdims=True
    )
    lists = lists_ref[...]
    longest = lists.shape[1]
    picked = jnp.sum(
        jnp.where(iota((count, longest), 0) == lists, upright(by_cand), 0.0), axis=0, keepdims=True
    )
    scores_ref[...] = jnp.where(iota((1, longest), 1) < length_ref[0], picked, 0.0)


VMEM = pl.BlockSpec(memory_space=pltpu.VMEM)
HBM = pl.BlockSpec(memory_space=pltpu.HBM)
SMEM = pl.BlockSpec(memory_space=pltpu.SMEM)
PARAMS = pltpu.CompilerParams(vmem_limit_bytes=40 * 1024 * 1024)


def body(
    query_grads,
    cand_grads,
    basis_out,
    basis_in,
    eigvals,
    layer_map,
    cand_rows,
    cand_lists,
    list_lengths,
):
    own, modules, flat = query_grads.shape
    per = cand_grads.shape[0]
    slots = layer_map.shape[0]
    tall = flat // LANES
    count = cand_rows.shape[0]
    layer_row = layer_map.reshape(1, slots)
    height = (own + per) * tall
    send = tall + -(-PIECES * -(-count // LANES) // 8) * 8

    def in_hbm(x):
        return pltpu.with_memory_space_constraint(x, pltpu.HBM)

    def swap_over(x, first):
        groups = [order_of(slots, first)]
        return lax.all_to_all(x, "shard", split_axis=0, concat_axis=0, tiled=True, axis_index_groups=groups)


    packed = pl.pallas_call(
        pack,
        out_shape=pltpu.VMEM((slots, height, LANES), bf16),
        in_specs=[HBM] * 3,
        out_specs=VMEM,
        scratch_shapes=[
            pltpu.VMEM(layer_row.shape, jnp.int32),
            pltpu.VMEM(query_grads.shape, bf16),
            pltpu.VMEM(cand_grads.shape, bf16),
            pltpu.VMEM((slots * height, LANES), f32),
            pltpu.SemaphoreType.DMA((3,)),
        ],
        compiler_params=PARAMS,
        name="pack",
    )(in_hbm(layer_row), in_hbm(query_grads), in_hbm(cand_grads))
    moved = swap_over(packed, firsts(slots)[0])
    sources = moved.shape[0]
    homes = pl.pallas_call(
        work,
        out_shape=jax.ShapeDtypeStruct((sources, send, LANES), bf16),
        in_specs=[VMEM] * 4,
        out_specs=VMEM,
        scratch_shapes=[pltpu.VMEM((sources * per * tall, LANES), f32), pltpu.VMEM((sources * send, LANES), f32)],
        compiler_params=PARAMS,
        name="work",
    )(
        moved,
        basis_out.reshape(basis_out.shape[1:]),
        basis_in.reshape(basis_in.shape[1:]),
        eigvals.reshape(tall, LANES),
    )
    home = swap_over(homes, firsts(slots)[1])
    return pl.pallas_call(
        finish,
        out_shape=(
            jax.ShapeDtypeStruct(query_grads.shape, bf16),
            jax.ShapeDtypeStruct(cand_lists.shape, f32),
        ),
        in_specs=[SMEM] + [VMEM] * 4,
        out_specs=(VMEM, VMEM),
        scratch_shapes=[pltpu.VMEM((slots * send, LANES), f32)],
        compiler_params=PARAMS,
        name="finish",
    )(list_lengths, layer_row, cand_rows.reshape(1, count), cand_lists, home)


def solution(mesh):
    return jax.shard_map(
        body,
        mesh=mesh,
        in_specs=(
            P(("groups", "shard"), None, None),
            P(("groups", "shard"), None, None),
            P("shard", None, None),
            P("shard", None, None),
            P("shard", None),
            P(),
            P("groups"),
            P(("groups", "shard"), None),
            P(("groups", "shard")),
        ),
        out_specs=(P(("groups", "shard"), None, None), P(("groups", "shard"), None)),
        check_vma=False,
    )
```

```python
import jax
import jax.numpy as jnp
from jax import lax
from jax.experimental import pallas as pl
from jax.experimental.pallas import tpu as pltpu
from jax.sharding import PartitionSpec as P

damping = 0.1
LANES = 128
SUBLANES = 8
PIECES = 3
f32, bf16 = jnp.float32, jnp.bfloat16


def iota(shape, axis):
    return lax.broadcasted_iota(jnp.int32, shape, axis)


def dot(a, b, dims=((1,), (0,))):
    return lax.dot_general(a, b, (dims, ((), ())), preferred_element_type=f32)


def mask(condition):
    return condition.astype(f32).astype(bf16)


def order_of(slots, first):
    return [(first + k) % slots for k in range(slots)]


def firsts(slots):
    return slots // 4, slots - 2


def gather_rows(tall):
    size = SUBLANES * tall
    row = iota((size, size), 0)
    return mask(row // SUBLANES + tall * (row % SUBLANES) == iota((size, size), 1))


def scatter_rows(tall):
    size = SUBLANES * tall
    row = iota((size, size), 0)
    return mask(row // tall + SUBLANES * (row % tall) == iota((size, size), 1))


def half(left, right):
    return jnp.where(iota(left.shape, 1) < LANES // 2, left, right)


def swap(block):
    return pltpu.roll(block, LANES // 2, 1)


def unpaired(block):
    tall = block.shape[0] // 2
    top, low = block[:tall], block[tall:]
    return half(top, swap(low)), half(swap(top), low)


def pack(layer_hbm, query_hbm, cand_hbm, out_ref, layer_ref, query_ref, cand_ref, by_module, sems):
    arrivals = [
        pltpu.make_async_copy(source, target, sems.at[i])
        for i, (source, target) in enumerate(
            ((query_hbm, query_ref), (cand_hbm, cand_ref), (layer_hbm, layer_ref))
        )
    ]
    for arrival in arrivals:
        arrival.start()
    modules, flat = query_ref.shape[1:]
    slots = out_ref.shape[0]
    tall = flat // LANES
    scatter = scatter_rows(tall)
    sources = [(query_ref, r) for r in range(query_ref.shape[0])] + [(cand_ref, r) for r in range(cand_ref.shape[0])]
    for r, (ref, row) in enumerate(sources):
        if row == 0:
            arrivals[0 if ref is query_ref else 1].wait()
        rows = ref[row].astype(f32)
        columns = []
        for m in range(0, modules, SUBLANES):
            tiles = [rows[m : m + SUBLANES, j * LANES : (j + 1) * LANES] for j in range(tall)]
            columns.append(jnp.concatenate(tiles, axis=0).astype(bf16))
        blocks = dot(scatter, jnp.concatenate(columns, axis=1)).astype(bf16)
        for m in range(modules):
            c, g = m % SUBLANES, m // SUBLANES
            by_module[m, r * tall : (r + 1) * tall, :] = blocks[c * tall : (c + 1) * tall, g * LANES : (g + 1) * LANES]
    arrivals[2].wait()
    for k, s in enumerate(order_of(slots, firsts(slots)[0])):
        out_ref[k] = by_module[layer_ref[s]]


def upright(row, count):
    shape = (count, row.shape[1])
    return jnp.sum(jnp.where(iota(shape, 0) == iota(shape, 1), row, 0.0), axis=1, keepdims=True)


def prepare(
    length_ref, out_basis_ref, in_basis_ref, eigen_ref, rows_ref, lists_ref, after_ref,
    enter_ref, outer_ref, inner_ref, factor_ref, gather_ref, chosen_ref,
):
    del after_ref
    out_basis, in_basis = out_basis_ref[...], in_basis_ref[...]
    side = out_basis.shape[0]
    tall = side // 2
    size = enter_ref.shape[0]
    order = mask(iota((side, side), 1) == 2 * (iota((side, side), 0) % tall) + iota((side, side), 0) // tall)
    basis = dot(dot(order, out_basis).astype(bf16), order, ((1,), (1,))).astype(bf16)
    spread = mask(iota((size, side), 0) % side == iota((size, side), 1))
    row, column = iota((size, size), 0) // side, iota((size, size), 1) // side
    outer = dot(dot(spread, basis).astype(bf16), spread, ((1,), (1,)))
    inner = dot(dot(spread, in_basis).astype(bf16), spread, ((1,), (1,)))
    outer_ref[...] = jnp.where(row == column, outer, 0.0).astype(bf16)
    inner_ref[...] = jnp.where(row == column, inner, 0.0).astype(bf16)
    enter_ref[...] = jnp.where(row == 2 * (column % 2) + column // 2, inner, 0.0).astype(bf16)
    eigen = eigen_ref[...]
    turned = swap(eigen)
    factor_ref[...] = 1.0 / (jnp.concatenate([half(eigen, turned), half(turned, eigen)], axis=0) + damping)
    gather_ref[...] = gather_rows(tall)

    count = rows_ref.shape[1]
    lists = lists_ref[...]
    longest = lists.shape[1]
    rows = upright(rows_ref[...].astype(f32), count)
    place = jnp.sum(jnp.where(iota((count, longest), 0) == lists, rows, 0.0), axis=0, keepdims=True)
    place = jnp.where(iota((1, longest), 1) < length_ref[0], place.astype(jnp.int32), -1)
    chosen_ref[...] = (iota((count, longest), 0) == place).astype(f32)


def work(moved_ref, enter_ref, outer_ref, inner_ref, factor_ref, gather_ref, out_ref, tails):
    sources, height, _ = moved_ref.shape
    _, send, _ = out_ref.shape
    size = enter_ref.shape[0]
    side, tall = size // 4, size // SUBLANES
    per = height // tall - 1
    count = sources * per
    pairs = sources // 2
    stacks = pairs // 4
    arrive, leave = firsts(sources)
    places = [(d - leave) % sources for d in order_of(sources, arrive)]
    outer, inner, gather = outer_ref[...], inner_ref[...], gather_ref[...]
    factor = factor_ref[...]

    queries = [jnp.concatenate([moved_ref[2 * p, :tall, :], moved_ref[2 * p + 1, :tall, :]], axis=1) for p in range(pairs)]
    entered = dot(jnp.concatenate(queries, axis=0), enter_ref[...]).astype(bf16)
    columns = []
    for t in range(stacks):
        tiles = []
        for p in range(4 * t, 4 * t + 4):
            rows = entered[p * tall : (p + 1) * tall]
            tiles += [rows[:, :LANES], rows[:, LANES:]]
        columns.append(jnp.concatenate(tiles, axis=0))
    rotated = dot(outer, jnp.concatenate(columns, axis=1), ((0,), (0,)))
    tile = jnp.concatenate([jnp.concatenate([factor] * 4, axis=0)] * 2, axis=1)
    scaled = [
        (rotated[:, t * LANES : (t + 2) * LANES] * tile).astype(bf16) for t in range(0, stacks, 2)
    ]
    returned = dot(jnp.concatenate(scaled, axis=0), inner, ((1,), (1,))).astype(bf16)
    returned = jnp.concatenate([returned[t * size : (t + 1) * size] for t in range(stacks // 2)], axis=1)
    precond = dot(outer, returned).astype(bf16).astype(f32)

    homes = [None] * sources
    for p in range(pairs):
        t, u = p // 4, p % 4
        block = precond[u * side : (u + 1) * side, t * LANES : (t + 1) * LANES]
        homes[places[2 * p]], homes[places[2 * p + 1]] = unpaired(block)

    def flat(blocks):
        groups = [
            jnp.concatenate(blocks[g : g + SUBLANES], axis=0).astype(bf16) for g in range(0, len(blocks), SUBLANES)
        ]
        turned = dot(gather, jnp.concatenate(groups, axis=1))
        return jnp.concatenate(
            [
                jnp.concatenate(
                    [
                        turned[j * SUBLANES : (j + 1) * SUBLANES, g * LANES : (g + 1) * LANES]
                        for g in range(len(groups))
                    ],
                    axis=0,
                ).astype(bf16)
                for j in range(tall)
            ],
            axis=1,
        )

    cands = [
        moved_ref[(d - arrive) % sources, (1 + c) * tall : (2 + c) * tall, :]
        for d in range(sources)
        for c in range(per)
    ]
    rest = dot(flat(homes), flat(cands), ((1,), (1,)))
    wide = -(-count // LANES)
    if wide * LANES > count:
        rest = jnp.concatenate([rest, jnp.zeros((sources, wide * LANES - count), f32)], axis=1)
    tail = send - tall
    tails[...] = jnp.zeros_like(tails)
    for k in range(PIECES):
        piece = rest.astype(bf16).astype(f32)
        rest = rest - piece
        for t in range(wide):
            tails[pl.ds(k * wide + t, sources, stride=tail), :] = piece[:, t * LANES : (t + 1) * LANES]
    for k in range(sources):
        out_ref[k] = jnp.concatenate([homes[k], tails[k * tail : (k + 1) * tail, :]], axis=0).astype(bf16)


def finish(layer_ref, home_ref, gather_ref, chosen_ref, precond_ref, scores_ref, by_module):
    slots, send, _ = home_ref.shape
    modules, flat = precond_ref.shape[1:]
    count = chosen_ref.shape[0]
    tall = flat // LANES
    totals = None
    for k, s in enumerate(order_of(slots, firsts(slots)[1])):
        block = home_ref[k].astype(f32)
        by_module[layer_ref[s]] = block[:tall].astype(bf16)
        totals = block[tall:] if totals is None else totals + block[tall:]
    groups = [
        jnp.concatenate([by_module[m + c] for c in range(SUBLANES)], axis=0) for m in range(0, modules, SUBLANES)
    ]
    turned = dot(gather_ref[...], jnp.concatenate(groups, axis=1))
    for j in range(tall):
        tiles = [turned[j * SUBLANES : (j + 1) * SUBLANES, g * LANES : (g + 1) * LANES] for g in range(len(groups))]
        precond_ref[0, :, j * LANES : (j + 1) * LANES] = jnp.concatenate(tiles, axis=0).astype(bf16)
    wide = -(-count // LANES)
    parts = [
        sum((totals[k * wide + t : k * wide + t + 1] for k in range(1, PIECES)), totals[t : t + 1]) for t in range(wide)
    ]
    dense = parts[0] if wide == 1 else jnp.concatenate(parts, axis=1)
    scores_ref[...] = jnp.sum(
        jnp.where(chosen_ref[...] > 0.0, upright(dense, count), 0.0), axis=0, keepdims=True
    )


HBM = pl.BlockSpec(memory_space=pltpu.HBM)
ANY = pl.BlockSpec(memory_space=pl.ANY)
SMEM = pl.BlockSpec(memory_space=pltpu.SMEM)
VMEM = pl.BlockSpec(memory_space=pltpu.VMEM)
PARAMS = pltpu.CompilerParams(vmem_limit_bytes=40 * 1024 * 1024)


def body(
    query_grads,
    cand_grads,
    basis_out,
    basis_in,
    eigvals,
    layer_map,
    cand_rows,
    cand_lists,
    list_lengths,
):
    own, modules, flat = query_grads.shape
    per = cand_grads.shape[0]
    slots = layer_map.shape[0]
    tall = flat // LANES
    side = basis_out.shape[1]
    size = SUBLANES * tall
    count = cand_rows.shape[0]
    height = (own + per) * tall
    send = tall + -(-PIECES * -(-count // LANES) // SUBLANES) * SUBLANES

    def in_hbm(x):
        return pltpu.with_memory_space_constraint(x, pltpu.HBM)

    def swap_over(x, first):
        groups = [order_of(slots, first)]
        return lax.all_to_all(x, "shard", split_axis=0, concat_axis=0, tiled=True, axis_index_groups=groups)

    packed = pl.pallas_call(
        pack,
        out_shape=pltpu.VMEM((slots, height, LANES), bf16),
        in_specs=[HBM] * 3,
        out_specs=VMEM,
        scratch_shapes=[
            pltpu.SMEM(layer_map.shape, jnp.int32),
            pltpu.VMEM(query_grads.shape, bf16),
            pltpu.VMEM(cand_grads.shape, bf16),
            pltpu.VMEM((modules, height, LANES), bf16),
            pltpu.SemaphoreType.DMA((3,)),
        ],
        compiler_params=PARAMS,
        name="pack",
    )(in_hbm(layer_map), in_hbm(query_grads), in_hbm(cand_grads))
    square = jax.ShapeDtypeStruct((size, size), bf16)
    enter, outer, inner, factor, gather, chosen = pl.pallas_call(
        prepare,
        out_shape=(
            square,
            square,
            square,
            jax.ShapeDtypeStruct((side, LANES), f32),
            square,
            jax.ShapeDtypeStruct((count, cand_lists.shape[1]), f32),
        ),
        in_specs=[SMEM] + [VMEM] * 5 + [ANY],
        out_specs=[VMEM] * 6,
        compiler_params=PARAMS,
        name="prepare",
    )(
        list_lengths,
        basis_out.reshape(basis_out.shape[1:]),
        basis_in.reshape(basis_in.shape[1:]),
        eigvals.reshape(tall, LANES),
        cand_rows.reshape(1, count),
        cand_lists,
        packed,
    )
    moved = swap_over(packed, firsts(slots)[0])
    homes = pl.pallas_call(
        work,
        out_shape=jax.ShapeDtypeStruct((slots, send, LANES), bf16),
        in_specs=[VMEM] * 6,
        out_specs=VMEM,
        scratch_shapes=[pltpu.VMEM((slots * (send - tall), LANES), f32)],
        compiler_params=PARAMS,
        name="work",
    )(moved, enter, outer, inner, factor, gather)
    home = swap_over(homes, firsts(slots)[1])
    return pl.pallas_call(
        finish,
        out_shape=(
            jax.ShapeDtypeStruct(query_grads.shape, bf16),
            jax.ShapeDtypeStruct(cand_lists.shape, f32),
        ),
        in_specs=[SMEM] + [VMEM] * 3,
        out_specs=(VMEM, VMEM),
        scratch_shapes=[pltpu.VMEM((modules, tall, LANES), bf16)],
        compiler_params=PARAMS,
        name="finish",
    )(layer_map, home, gather, chosen)


def solution(mesh):
    return jax.shard_map(
        body,
        mesh=mesh,
        in_specs=(
            P(("groups", "shard"), None, None),
            P(("groups", "shard"), None, None),
            P("shard", None, None),
            P("shard", None, None),
            P("shard", None),
            P(),
            P("groups"),
            P(("groups", "shard"), None),
            P(("groups", "shard")),
        ),
        out_specs=(P(("groups", "shard"), None, None), P(("groups", "shard"), None)),
        check_vma=False,
    )
```

```python
import jax
import jax.numpy as jnp
from jax import lax
from jax.experimental import pallas as pl
from jax.experimental.pallas import tpu as pltpu
from jax.sharding import PartitionSpec as P

damping = 0.1
LANES = 128
SUBLANES = 8
PIECES = 3
f32, bf16 = jnp.float32, jnp.bfloat16


def iota(shape, axis):
    return lax.broadcasted_iota(jnp.int32, shape, axis)


def dot(a, b, dims=((1,), (0,))):
    return lax.dot_general(a, b, (dims, ((), ())), preferred_element_type=f32)


def mask(condition):
    return condition.astype(f32).astype(bf16)


def order_of(slots, first):
    return [(first + k) % slots for k in range(slots)]


def firsts(slots):
    return slots // 4, slots - 2


def gather_rows(tall):
    size = SUBLANES * tall
    row = iota((size, size), 0)
    return mask(row // SUBLANES + tall * (row % SUBLANES) == iota((size, size), 1))


def half(left, right):
    return jnp.where(iota(left.shape, 1) < LANES // 2, left, right)


def swap(block):
    return pltpu.roll(block, LANES // 2, 1)


def unpaired(block):
    tall = block.shape[0] // 2
    top, low = block[:tall], block[tall:]
    return half(top, swap(low)), half(swap(top), low)


def holds(layer_row, modules, first):
    slots = layer_row.shape[1]
    if first:
        layer_row = jnp.concatenate([layer_row[:, first:], layer_row[:, :first]], axis=1)
    return mask(iota((modules, slots), 0) == layer_row)


def pack(layer_hbm, query_hbm, cand_hbm, out_ref, layer_ref, query_ref, cand_ref, wide, sems):
    arrivals = [
        pltpu.make_async_copy(source, target, sems.at[i])
        for i, (source, target) in enumerate(
            ((layer_hbm, layer_ref), (query_hbm, query_ref), (cand_hbm, cand_ref))
        )
    ]
    for arrival in arrivals:
        arrival.start()
    arrivals[0].wait()
    modules, flat = query_ref.shape[1:]
    slots, height, _ = out_ref.shape
    tall = flat // LANES
    step = height + 1
    one_hot = holds(layer_ref[...], modules, firsts(slots)[0])
    sources = [(query_ref, r) for r in range(query_ref.shape[0])] + [(cand_ref, r) for r in range(cand_ref.shape[0])]
    for r, (ref, row) in enumerate(sources):
        if row == 0:
            arrivals[1 if ref is query_ref else 2].wait()
        by_slot = dot(one_hot, ref[row], ((0,), (0,)))
        for j in range(tall):
            wide[pl.ds(r * tall + j, slots, stride=step), :] = by_slot[:, j * LANES : (j + 1) * LANES]
    for k in range(slots):
        out_ref[k] = wide[pl.ds(k * step, height), :].astype(bf16)


def upright(row, count):
    shape = (count, row.shape[1])
    return jnp.sum(jnp.where(iota(shape, 0) == iota(shape, 1), row, 0.0), axis=1, keepdims=True)


def prepare(
    length_ref, layer_ref, out_basis_ref, in_basis_ref, eigen_ref, rows_ref, lists_ref, after_ref,
    enter_ref, outer_ref, inner_ref, factor_ref, gather_ref, holds_ref, chosen_ref,
):
    del after_ref
    out_basis, in_basis = out_basis_ref[...], in_basis_ref[...]
    side = out_basis.shape[0]
    tall = side // 2
    size = enter_ref.shape[0]
    order = mask(iota((side, side), 1) == 2 * (iota((side, side), 0) % tall) + iota((side, side), 0) // tall)
    basis = dot(dot(order, out_basis).astype(bf16), order, ((1,), (1,))).astype(bf16)
    spread = mask(iota((size, side), 0) % side == iota((size, side), 1))
    row, column = iota((size, size), 0) // side, iota((size, size), 1) // side
    outer = dot(dot(spread, basis).astype(bf16), spread, ((1,), (1,)))
    inner = dot(dot(spread, in_basis).astype(bf16), spread, ((1,), (1,)))
    outer_ref[...] = jnp.where(row == column, outer, 0.0).astype(bf16)
    inner_ref[...] = jnp.where(row == column, inner, 0.0).astype(bf16)
    enter_ref[...] = jnp.where(row == 2 * (column % 2) + column // 2, inner, 0.0).astype(bf16)
    eigen = eigen_ref[...]
    turned = swap(eigen)
    factor_ref[...] = 1.0 / (jnp.concatenate([half(eigen, turned), half(turned, eigen)], axis=0) + damping)
    gather_ref[...] = gather_rows(tall)
    modules, slots = holds_ref.shape
    holds_ref[...] = holds(layer_ref[...], modules, firsts(slots)[1])

    count = rows_ref.shape[1]
    lists = lists_ref[...]
    longest = lists.shape[1]
    rows = upright(rows_ref[...].astype(f32), count)
    place = jnp.sum(jnp.where(iota((count, longest), 0) == lists, rows, 0.0), axis=0, keepdims=True)
    place = jnp.where(iota((1, longest), 1) < length_ref[0], place.astype(jnp.int32), -1)
    chosen_ref[...] = (iota((count, longest), 0) == place).astype(f32)


def work(moved_ref, enter_ref, outer_ref, inner_ref, factor_ref, gather_ref, out_ref, tails):
    sources, height, _ = moved_ref.shape
    _, send, _ = out_ref.shape
    size = enter_ref.shape[0]
    side, tall = size // 4, size // SUBLANES
    per = height // tall - 1
    count = sources * per
    pairs = sources // 2
    stacks = pairs // 4
    arrive, leave = firsts(sources)
    places = [(d - leave) % sources for d in order_of(sources, arrive)]
    outer, inner, gather = outer_ref[...], inner_ref[...], gather_ref[...]
    factor = factor_ref[...]

    queries = [jnp.concatenate([moved_ref[2 * p, :tall, :], moved_ref[2 * p + 1, :tall, :]], axis=1) for p in range(pairs)]
    entered = dot(jnp.concatenate(queries, axis=0), enter_ref[...]).astype(bf16)
    columns = []
    for t in range(stacks):
        tiles = []
        for p in range(4 * t, 4 * t + 4):
            rows = entered[p * tall : (p + 1) * tall]
            tiles += [rows[:, :LANES], rows[:, LANES:]]
        columns.append(jnp.concatenate(tiles, axis=0))
    rotated = dot(outer, jnp.concatenate(columns, axis=1), ((0,), (0,)))
    tile = jnp.concatenate([jnp.concatenate([factor] * 4, axis=0)] * 2, axis=1)
    scaled = [
        (rotated[:, t * LANES : (t + 2) * LANES] * tile).astype(bf16) for t in range(0, stacks, 2)
    ]
    returned = dot(jnp.concatenate(scaled, axis=0), inner, ((1,), (1,))).astype(bf16)
    returned = jnp.concatenate([returned[t * size : (t + 1) * size] for t in range(stacks // 2)], axis=1)
    precond = dot(outer, returned).astype(bf16).astype(f32)

    homes = [None] * sources
    for p in range(pairs):
        t, u = p // 4, p % 4
        block = precond[u * side : (u + 1) * side, t * LANES : (t + 1) * LANES]
        homes[places[2 * p]], homes[places[2 * p + 1]] = unpaired(block)

    def flat(blocks):
        groups = [
            jnp.concatenate(blocks[g : g + SUBLANES], axis=0).astype(bf16) for g in range(0, len(blocks), SUBLANES)
        ]
        turned = dot(gather, jnp.concatenate(groups, axis=1))
        return jnp.concatenate(
            [
                jnp.concatenate(
                    [
                        turned[j * SUBLANES : (j + 1) * SUBLANES, g * LANES : (g + 1) * LANES]
                        for g in range(len(groups))
                    ],
                    axis=0,
                ).astype(bf16)
                for j in range(tall)
            ],
            axis=1,
        )

    cands = [
        moved_ref[(d - arrive) % sources, (1 + c) * tall : (2 + c) * tall, :]
        for d in range(sources)
        for c in range(per)
    ]
    rest = dot(flat(homes), flat(cands), ((1,), (1,)))
    wide = -(-count // LANES)
    if wide * LANES > count:
        rest = jnp.concatenate([rest, jnp.zeros((sources, wide * LANES - count), f32)], axis=1)
    tail = send - tall
    tails[...] = jnp.zeros_like(tails)
    for k in range(PIECES):
        piece = rest.astype(bf16).astype(f32)
        rest = rest - piece
        for t in range(wide):
            tails[pl.ds(k * wide + t, sources, stride=tail), :] = piece[:, t * LANES : (t + 1) * LANES]
    for k in range(sources):
        out_ref[k] = jnp.concatenate([homes[k], tails[k * tail : (k + 1) * tail, :]], axis=0).astype(bf16)


def finish(home_ref, holds_ref, chosen_ref, precond_ref, scores_ref, wide):
    slots, send, _ = home_ref.shape
    _, flat = precond_ref.shape[1:]
    count = chosen_ref.shape[0]
    tall = flat // LANES
    step = send + 1
    for k in range(slots):
        wide[pl.ds(k * step, send), :] = home_ref[k].astype(f32)
    by_slot = jnp.concatenate([wide[pl.ds(j, slots, stride=step), :].astype(bf16) for j in range(tall)], axis=1)
    precond_ref[0] = dot(holds_ref[...], by_slot).astype(bf16)
    groups = -(-count // LANES)
    parts = []
    for t in range(groups):
        pieces = [wide[pl.ds(tall + k * groups + t, slots, stride=step), :] for k in range(PIECES)]
        parts.append(jnp.sum((pieces[2] + pieces[1]) + pieces[0], axis=0, keepdims=True))
    dense = parts[0] if groups == 1 else jnp.concatenate(parts, axis=1)
    scores_ref[...] = jnp.sum(
        jnp.where(chosen_ref[...] > 0.0, upright(dense, count), 0.0), axis=0, keepdims=True
    )


HBM = pl.BlockSpec(memory_space=pltpu.HBM)
ANY = pl.BlockSpec(memory_space=pl.ANY)
SMEM = pl.BlockSpec(memory_space=pltpu.SMEM)
VMEM = pl.BlockSpec(memory_space=pltpu.VMEM)
PARAMS = pltpu.CompilerParams(vmem_limit_bytes=40 * 1024 * 1024)


def body(
    query_grads,
    cand_grads,
    basis_out,
    basis_in,
    eigvals,
    layer_map,
    cand_rows,
    cand_lists,
    list_lengths,
):
    own, modules, flat = query_grads.shape
    per = cand_grads.shape[0]
    slots = layer_map.shape[0]
    layer_row = layer_map.reshape(1, slots)
    tall = flat // LANES
    side = basis_out.shape[1]
    size = SUBLANES * tall
    count = cand_rows.shape[0]
    height = (own + per) * tall
    send = tall + -(-PIECES * -(-count // LANES) // SUBLANES) * SUBLANES

    def in_hbm(x):
        return pltpu.with_memory_space_constraint(x, pltpu.HBM)

    def swap_over(x, first):
        groups = [order_of(slots, first)]
        return lax.all_to_all(x, "shard", split_axis=0, concat_axis=0, tiled=True, axis_index_groups=groups)

    packed = pl.pallas_call(
        pack,
        out_shape=pltpu.VMEM((slots, height, LANES), bf16),
        in_specs=[HBM] * 3,
        out_specs=VMEM,
        scratch_shapes=[
            pltpu.VMEM(layer_row.shape, jnp.int32),
            pltpu.VMEM(query_grads.shape, bf16),
            pltpu.VMEM(cand_grads.shape, bf16),
            pltpu.VMEM((slots * (height + 1), LANES), f32),
            pltpu.SemaphoreType.DMA((3,)),
        ],
        compiler_params=PARAMS,
        name="pack",
    )(in_hbm(layer_row), in_hbm(query_grads), in_hbm(cand_grads))
    square = jax.ShapeDtypeStruct((size, size), bf16)
    enter, outer, inner, factor, gather, held, chosen = pl.pallas_call(
        prepare,
        out_shape=(
            square,
            square,
            square,
            jax.ShapeDtypeStruct((side, LANES), f32),
            square,
            jax.ShapeDtypeStruct((modules, slots), bf16),
            jax.ShapeDtypeStruct((count, cand_lists.shape[1]), f32),
        ),
        in_specs=[SMEM] + [VMEM] * 6 + [ANY],
        out_specs=[VMEM] * 7,
        compiler_params=PARAMS,
        name="prepare",
    )(
        list_lengths,
        layer_row,
        basis_out.reshape(basis_out.shape[1:]),
        basis_in.reshape(basis_in.shape[1:]),
        eigvals.reshape(tall, LANES),
        cand_rows.reshape(1, count),
        cand_lists,
        packed,
    )
    moved = swap_over(packed, firsts(slots)[0])
    homes = pl.pallas_call(
        work,
        out_shape=jax.ShapeDtypeStruct((slots, send, LANES), bf16),
        in_specs=[VMEM] * 6,
        out_specs=VMEM,
        scratch_shapes=[pltpu.VMEM((slots * (send - tall), LANES), f32)],
        compiler_params=PARAMS,
        name="work",
    )(moved, enter, outer, inner, factor, gather)
    home = swap_over(homes, firsts(slots)[1])
    return pl.pallas_call(
        finish,
        out_shape=(
            jax.ShapeDtypeStruct(query_grads.shape, bf16),
            jax.ShapeDtypeStruct(cand_lists.shape, f32),
        ),
        in_specs=[VMEM] * 3,
        out_specs=(VMEM, VMEM),
        scratch_shapes=[pltpu.VMEM((slots * (send + 1), LANES), f32)],
        compiler_params=PARAMS,
        name="finish",
    )(home, held, chosen)


def solution(mesh):
    return jax.shard_map(
        body,
        mesh=mesh,
        in_specs=(
            P(("groups", "shard"), None, None),
            P(("groups", "shard"), None, None),
            P("shard", None, None),
            P("shard", None, None),
            P("shard", None),
            P(),
            P("groups"),
            P(("groups", "shard"), None),
            P(("groups", "shard")),
        ),
        out_specs=(P(("groups", "shard"), None, None), P(("groups", "shard"), None)),
        check_vma=False,
    )
```

```python
import jax
import jax.numpy as jnp
from jax import lax
from jax.experimental import pallas as pl
from jax.experimental.pallas import tpu as pltpu
from jax.sharding import PartitionSpec as P

damping = 0.1
LANES = 128
SUBLANES = 8
PIECES = 3
f32, bf16 = jnp.float32, jnp.bfloat16


def iota(shape, axis):
    return lax.broadcasted_iota(jnp.int32, shape, axis)


def dot(a, b, dims=((1,), (0,))):
    return lax.dot_general(a, b, (dims, ((), ())), preferred_element_type=f32)


def mask(condition):
    return condition.astype(f32).astype(bf16)


def order_of(slots, first):
    return [(first + k) % slots for k in range(slots)]


def firsts(slots):
    return slots * 5 // 8, slots * 5 // 8


def gather_rows(tall):
    size = SUBLANES * tall
    row = iota((size, size), 0)
    return mask(row // SUBLANES + tall * (row % SUBLANES) == iota((size, size), 1))


def half(left, right):
    return jnp.where(iota(left.shape, 1) < LANES // 2, left, right)


def swap(block):
    return pltpu.roll(block, LANES // 2, 1)


def unpaired(block):
    tall = block.shape[0] // 2
    top, low = block[:tall], block[tall:]
    return half(top, swap(low)), half(swap(top), low)


def holds(layer_row, modules, first):
    slots = layer_row.shape[1]
    if first:
        layer_row = jnp.concatenate([layer_row[:, first:], layer_row[:, :first]], axis=1)
    return mask(iota((modules, slots), 0) == layer_row)


def pack(layer_hbm, query_hbm, cand_hbm, out_hbm, layer_ref, query_ref, cand_ref, wide, ready, sems):
    arrivals = [
        pltpu.make_async_copy(source, target, sems.at[i])
        for i, (source, target) in enumerate(
            ((layer_hbm, layer_ref), (query_hbm, query_ref), (cand_hbm, cand_ref))
        )
    ]
    for arrival in arrivals:
        arrival.start()
    arrivals[0].wait()
    modules, flat = query_ref.shape[1:]
    slots = out_hbm.shape[0]
    tall = flat // LANES
    step = tall + 1
    one_hot = holds(layer_ref[...], modules, firsts(slots)[0])
    sources = [(query_ref, r) for r in range(query_ref.shape[0])] + [(cand_ref, r) for r in range(cand_ref.shape[0])]
    departures = []
    for r, (ref, row) in enumerate(sources):
        if row == 0:
            arrivals[1 if ref is query_ref else 2].wait()
        by_slot = dot(one_hot, ref[row], ((0,), (0,)))
        base = r * slots * step
        for j in range(tall):
            wide[pl.ds(base + j, slots, stride=step), :] = by_slot[:, j * LANES : (j + 1) * LANES]
        part = pl.ds(r * tall, tall)
        for k in range(slots):
            ready[k, part, :] = wide[pl.ds(base + k * step, tall), :].astype(bf16)
        departures.append(
            pltpu.make_async_copy(ready.at[:, part, :], out_hbm.at[:, part, :], sems.at[len(arrivals) + r])
        )
        departures[-1].start()
    for departure in departures:
        departure.wait()


def upright(row, count):
    shape = (count, row.shape[1])
    return jnp.sum(jnp.where(iota(shape, 0) == iota(shape, 1), row, 0.0), axis=1, keepdims=True)


def prepare(
    length_ref, layer_ref, out_basis_ref, in_basis_ref, eigen_ref, rows_ref, lists_ref, after_ref,
    enter_ref, outer_ref, inner_ref, factor_ref, gather_ref, holds_ref, chosen_ref,
):
    del after_ref
    out_basis, in_basis = out_basis_ref[...], in_basis_ref[...]
    side = out_basis.shape[0]
    tall = side // 2
    size = enter_ref.shape[0]
    order = mask(iota((side, side), 1) == 2 * (iota((side, side), 0) % tall) + iota((side, side), 0) // tall)
    basis = dot(dot(order, out_basis).astype(bf16), order, ((1,), (1,))).astype(bf16)
    spread = mask(iota((size, side), 0) % side == iota((size, side), 1))
    row, column = iota((size, size), 0) // side, iota((size, size), 1) // side
    outer = dot(dot(spread, basis).astype(bf16), spread, ((1,), (1,)))
    inner = dot(dot(spread, in_basis).astype(bf16), spread, ((1,), (1,)))
    outer_ref[...] = jnp.where(row == column, outer, 0.0).astype(bf16)
    inner_ref[...] = jnp.where(row == column, inner, 0.0).astype(bf16)
    enter_ref[...] = jnp.where(row == 2 * (column % 2) + column // 2, inner, 0.0).astype(bf16)
    eigen = eigen_ref[...]
    turned = swap(eigen)
    factor_ref[...] = 1.0 / (jnp.concatenate([half(eigen, turned), half(turned, eigen)], axis=0) + damping)
    gather_ref[...] = gather_rows(tall)
    modules, slots = holds_ref.shape
    holds_ref[...] = holds(layer_ref[...], modules, firsts(slots)[1])

    count = rows_ref.shape[1]
    lists = lists_ref[...]
    longest = lists.shape[1]
    rows = upright(rows_ref[...].astype(f32), count)
    place = jnp.sum(jnp.where(iota((count, longest), 0) == lists, rows, 0.0), axis=0, keepdims=True)
    place = jnp.where(iota((1, longest), 1) < length_ref[0], place.astype(jnp.int32), -1)
    chosen_ref[...] = (iota((count, longest), 0) == place).astype(f32)


def work(moved_ref, enter_ref, outer_ref, inner_ref, factor_ref, gather_ref, out_ref, tails):
    sources, height, _ = moved_ref.shape
    _, send, _ = out_ref.shape
    size = enter_ref.shape[0]
    side, tall = size // 4, size // SUBLANES
    per = height // tall - 1
    count = sources * per
    pairs = sources // 2
    stacks = pairs // 4
    arrive, leave = firsts(sources)
    places = [(d - leave) % sources for d in order_of(sources, arrive)]
    outer, inner, gather = outer_ref[...], inner_ref[...], gather_ref[...]
    factor = factor_ref[...]

    queries = [jnp.concatenate([moved_ref[2 * p, :tall, :], moved_ref[2 * p + 1, :tall, :]], axis=1) for p in range(pairs)]
    entered = dot(jnp.concatenate(queries, axis=0), enter_ref[...]).astype(bf16)
    columns = []
    for t in range(stacks):
        tiles = []
        for p in range(4 * t, 4 * t + 4):
            rows = entered[p * tall : (p + 1) * tall]
            tiles += [rows[:, :LANES], rows[:, LANES:]]
        columns.append(jnp.concatenate(tiles, axis=0))
    rotated = dot(outer, jnp.concatenate(columns, axis=1), ((0,), (0,)))
    tile = jnp.concatenate([jnp.concatenate([factor] * 4, axis=0)] * 2, axis=1)
    scaled = [
        (rotated[:, t * LANES : (t + 2) * LANES] * tile).astype(bf16) for t in range(0, stacks, 2)
    ]
    returned = dot(jnp.concatenate(scaled, axis=0), inner, ((1,), (1,))).astype(bf16)
    returned = jnp.concatenate([returned[t * size : (t + 1) * size] for t in range(stacks // 2)], axis=1)
    precond = dot(outer, returned).astype(bf16).astype(f32)

    homes = [None] * sources
    for p in range(pairs):
        t, u = p // 4, p % 4
        block = precond[u * side : (u + 1) * side, t * LANES : (t + 1) * LANES]
        homes[places[2 * p]], homes[places[2 * p + 1]] = unpaired(block)

    def flat(blocks):
        groups = [
            jnp.concatenate(blocks[g : g + SUBLANES], axis=0).astype(bf16) for g in range(0, len(blocks), SUBLANES)
        ]
        turned = dot(gather, jnp.concatenate(groups, axis=1))
        return jnp.concatenate(
            [
                jnp.concatenate(
                    [
                        turned[j * SUBLANES : (j + 1) * SUBLANES, g * LANES : (g + 1) * LANES]
                        for g in range(len(groups))
                    ],
                    axis=0,
                ).astype(bf16)
                for j in range(tall)
            ],
            axis=1,
        )

    cands = [
        moved_ref[(d - arrive) % sources, (1 + c) * tall : (2 + c) * tall, :]
        for d in range(sources)
        for c in range(per)
    ]
    rest = dot(flat(homes), flat(cands), ((1,), (1,)))
    wide = -(-count // LANES)
    if wide * LANES > count:
        rest = jnp.concatenate([rest, jnp.zeros((sources, wide * LANES - count), f32)], axis=1)
    tail = send - tall
    tails[...] = jnp.zeros_like(tails)
    for k in range(PIECES):
        piece = rest.astype(bf16).astype(f32)
        rest = rest - piece
        for t in range(wide):
            tails[pl.ds(k * wide + t, sources, stride=tail), :] = piece[:, t * LANES : (t + 1) * LANES]
    for k in range(sources):
        out_ref[k] = jnp.concatenate([homes[k], tails[k * tail : (k + 1) * tail, :]], axis=0).astype(bf16)


def finish(home_ref, holds_ref, chosen_ref, precond_hbm, scores_ref, wide, precond_ref, sem):
    slots, send, _ = home_ref.shape
    _, flat = precond_ref.shape[1:]
    count = chosen_ref.shape[0]
    tall = flat // LANES
    step = send + 1
    for k in range(slots):
        wide[pl.ds(k * step, send), :] = home_ref[k].astype(f32)
    by_slot = jnp.concatenate([wide[pl.ds(j, slots, stride=step), :].astype(bf16) for j in range(tall)], axis=1)
    precond_ref[0] = dot(holds_ref[...], by_slot).astype(bf16)
    departure = pltpu.make_async_copy(precond_ref, precond_hbm, sem)
    departure.start()
    groups = -(-count // LANES)
    parts = []
    for t in range(groups):
        pieces = [wide[pl.ds(tall + k * groups + t, slots, stride=step), :] for k in range(PIECES)]
        parts.append(jnp.sum((pieces[2] + pieces[1]) + pieces[0], axis=0, keepdims=True))
    dense = parts[0] if groups == 1 else jnp.concatenate(parts, axis=1)
    scores_ref[...] = jnp.sum(
        jnp.where(chosen_ref[...] > 0.0, upright(dense, count), 0.0), axis=0, keepdims=True
    )
    departure.wait()


HBM = pl.BlockSpec(memory_space=pltpu.HBM)
ANY = pl.BlockSpec(memory_space=pl.ANY)
SMEM = pl.BlockSpec(memory_space=pltpu.SMEM)
VMEM = pl.BlockSpec(memory_space=pltpu.VMEM)
PARAMS = pltpu.CompilerParams(vmem_limit_bytes=40 * 1024 * 1024)


def body(
    query_grads,
    cand_grads,
    basis_out,
    basis_in,
    eigvals,
    layer_map,
    cand_rows,
    cand_lists,
    list_lengths,
):
    own, modules, flat = query_grads.shape
    per = cand_grads.shape[0]
    slots = layer_map.shape[0]
    layer_row = layer_map.reshape(1, slots)
    tall = flat // LANES
    side = basis_out.shape[1]
    size = SUBLANES * tall
    count = cand_rows.shape[0]
    height = (own + per) * tall
    send = tall + -(-PIECES * -(-count // LANES) // SUBLANES) * SUBLANES

    def in_hbm(x):
        return pltpu.with_memory_space_constraint(x, pltpu.HBM)

    def swap_over(x, first):
        groups = [order_of(slots, first)]
        return lax.all_to_all(x, "shard", split_axis=0, concat_axis=0, tiled=True, axis_index_groups=groups)

    packed = pl.pallas_call(
        pack,
        out_shape=jax.ShapeDtypeStruct((slots, height, LANES), bf16),
        in_specs=[HBM] * 3,
        out_specs=HBM,
        scratch_shapes=[
            pltpu.VMEM(layer_row.shape, jnp.int32),
            pltpu.VMEM(query_grads.shape, bf16),
            pltpu.VMEM(cand_grads.shape, bf16),
            pltpu.VMEM(((own + per) * slots * (tall + 1), LANES), f32),
            pltpu.VMEM((slots, height, LANES), bf16),
            pltpu.SemaphoreType.DMA((3 + own + per,)),
        ],
        compiler_params=PARAMS,
        name="pack",
    )(in_hbm(layer_row), in_hbm(query_grads), in_hbm(cand_grads))
    square = jax.ShapeDtypeStruct((size, size), bf16)
    enter, outer, inner, factor, gather, held, chosen = pl.pallas_call(
        prepare,
        out_shape=(
            square,
            square,
            square,
            jax.ShapeDtypeStruct((side, LANES), f32),
            square,
            jax.ShapeDtypeStruct((modules, slots), bf16),
            jax.ShapeDtypeStruct((count, cand_lists.shape[1]), f32),
        ),
        in_specs=[SMEM] + [VMEM] * 6 + [ANY],
        out_specs=[VMEM] * 7,
        compiler_params=PARAMS,
        name="prepare",
    )(
        list_lengths,
        layer_row,
        basis_out.reshape(basis_out.shape[1:]),
        basis_in.reshape(basis_in.shape[1:]),
        eigvals.reshape(tall, LANES),
        cand_rows.reshape(1, count),
        cand_lists,
        packed,
    )
    moved = swap_over(packed, firsts(slots)[0])
    homes = pl.pallas_call(
        work,
        out_shape=jax.ShapeDtypeStruct((slots, send, LANES), bf16),
        in_specs=[VMEM] * 6,
        out_specs=VMEM,
        scratch_shapes=[pltpu.VMEM((slots * (send - tall), LANES), f32)],
        compiler_params=PARAMS,
        name="work",
    )(moved, enter, outer, inner, factor, gather)
    home = swap_over(homes, firsts(slots)[1])
    return pl.pallas_call(
        finish,
        out_shape=(
            jax.ShapeDtypeStruct(query_grads.shape, bf16),
            jax.ShapeDtypeStruct(cand_lists.shape, f32),
        ),
        in_specs=[VMEM] * 3,
        out_specs=(HBM, VMEM),
        scratch_shapes=[
            pltpu.VMEM((slots * (send + 1), LANES), f32),
            pltpu.VMEM(query_grads.shape, bf16),
            pltpu.SemaphoreType.DMA,
        ],
        compiler_params=PARAMS,
        name="finish",
    )(home, held, chosen)


def solution(mesh):
    return jax.shard_map(
        body,
        mesh=mesh,
        in_specs=(
            P(("groups", "shard"), None, None),
            P(("groups", "shard"), None, None),
            P("shard", None, None),
            P("shard", None, None),
            P("shard", None),
            P(),
            P("groups"),
            P(("groups", "shard"), None),
            P(("groups", "shard")),
        ),
        out_specs=(P(("groups", "shard"), None, None), P(("groups", "shard"), None)),
        check_vma=False,
    )
```

```python
import jax
import jax.numpy as jnp
from jax import lax
from jax.experimental import pallas as pl
from jax.experimental.pallas import tpu as pltpu
from jax.sharding import PartitionSpec as P

damping = 0.1
LANES = 128
SUBLANES = 8
PIECES = 3
f32, bf16 = jnp.float32, jnp.bfloat16


def iota(shape, axis):
    return lax.broadcasted_iota(jnp.int32, shape, axis)


def dot(a, b, dims=((1,), (0,))):
    return lax.dot_general(a, b, (dims, ((), ())), preferred_element_type=f32)


def mask(condition):
    return condition.astype(f32).astype(bf16)


def order_of(slots, first):
    return [(first + k) % slots for k in range(slots)]


def firsts(slots):
    return slots * 5 // 8, slots * 5 // 8


def gather_rows(tall):
    size = SUBLANES * tall
    row = iota((size, size), 0)
    return mask(row // SUBLANES + tall * (row % SUBLANES) == iota((size, size), 1))


def half(left, right):
    return jnp.where(iota(left.shape, 1) < LANES // 2, left, right)


def swap(block):
    return pltpu.roll(block, LANES // 2, 1)


def unpaired(block):
    tall = block.shape[0] // 2
    top, low = block[:tall], block[tall:]
    return half(top, swap(low)), half(swap(top), low)


def holds(layer_row, modules, first):
    slots = layer_row.shape[1]
    if first:
        layer_row = jnp.concatenate([layer_row[:, first:], layer_row[:, :first]], axis=1)
    return mask(iota((modules, slots), 0) == layer_row)


def pack(layer_ref, query_ref, cand_ref, out_ref, wide):
    modules, flat = query_ref.shape[1:]
    slots, height, _ = out_ref.shape
    tall = flat // LANES
    step = height + 1
    one_hot = holds(layer_ref[...], modules, firsts(slots)[0])
    sources = [query_ref[r] for r in range(query_ref.shape[0])]
    sources += [cand_ref[r] for r in range(cand_ref.shape[0])]
    for r, rows in enumerate(sources):
        by_slot = dot(one_hot, rows, ((0,), (0,)))
        for j in range(tall):
            wide[pl.ds(r * tall + j, slots, stride=step), :] = by_slot[:, j * LANES : (j + 1) * LANES]
    for k in range(slots):
        out_ref[k] = wide[pl.ds(k * step, height), :].astype(bf16)


def upright(row, count):
    shape = (count, row.shape[1])
    return jnp.sum(jnp.where(iota(shape, 0) == iota(shape, 1), row, 0.0), axis=1, keepdims=True)


def prepare(
    length_ref, layer_ref, out_basis_ref, in_basis_ref, eigen_ref, rows_ref, lists_ref, after_ref,
    enter_ref, outer_ref, inner_ref, factor_ref, gather_ref, holds_ref, chosen_ref,
):
    del after_ref
    out_basis, in_basis = out_basis_ref[...], in_basis_ref[...]
    side = out_basis.shape[0]
    tall = side // 2
    size = enter_ref.shape[0]
    order = mask(iota((side, side), 1) == 2 * (iota((side, side), 0) % tall) + iota((side, side), 0) // tall)
    basis = dot(dot(order, out_basis).astype(bf16), order, ((1,), (1,))).astype(bf16)
    spread = mask(iota((size, side), 0) % side == iota((size, side), 1))
    row, column = iota((size, size), 0) // side, iota((size, size), 1) // side
    outer = dot(dot(spread, basis).astype(bf16), spread, ((1,), (1,)))
    inner = dot(dot(spread, in_basis).astype(bf16), spread, ((1,), (1,)))
    outer_ref[...] = jnp.where(row == column, outer, 0.0).astype(bf16)
    inner_ref[...] = jnp.where(row == column, inner, 0.0).astype(bf16)
    enter_ref[...] = jnp.where(row == 2 * (column % 2) + column // 2, inner, 0.0).astype(bf16)
    eigen = eigen_ref[...]
    turned = swap(eigen)
    factor_ref[...] = 1.0 / (jnp.concatenate([half(eigen, turned), half(turned, eigen)], axis=0) + damping)
    gather_ref[...] = gather_rows(tall)
    modules, slots = holds_ref.shape
    holds_ref[...] = holds(layer_ref[...], modules, firsts(slots)[1])

    count = rows_ref.shape[1]
    lists = lists_ref[...]
    longest = lists.shape[1]
    rows = upright(rows_ref[...].astype(f32), count)
    place = jnp.sum(jnp.where(iota((count, longest), 0) == lists, rows, 0.0), axis=0, keepdims=True)
    place = jnp.where(iota((1, longest), 1) < length_ref[0], place.astype(jnp.int32), -1)
    chosen_ref[...] = (iota((count, longest), 0) == place).astype(f32)


def work(moved_ref, enter_ref, outer_ref, inner_ref, factor_ref, gather_ref, out_ref, tails):
    sources, height, _ = moved_ref.shape
    _, send, _ = out_ref.shape
    size = enter_ref.shape[0]
    side, tall = size // 4, size // SUBLANES
    per = height // tall - 1
    count = sources * per
    pairs = sources // 2
    stacks = pairs // 4
    arrive, leave = firsts(sources)
    places = [(d - leave) % sources for d in order_of(sources, arrive)]
    outer, inner, gather = outer_ref[...], inner_ref[...], gather_ref[...]
    factor = factor_ref[...]

    queries = [jnp.concatenate([moved_ref[2 * p, :tall, :], moved_ref[2 * p + 1, :tall, :]], axis=1) for p in range(pairs)]
    entered = dot(jnp.concatenate(queries, axis=0), enter_ref[...]).astype(bf16)
    columns = []
    for t in range(stacks):
        tiles = []
        for p in range(4 * t, 4 * t + 4):
            rows = entered[p * tall : (p + 1) * tall]
            tiles += [rows[:, :LANES], rows[:, LANES:]]
        columns.append(jnp.concatenate(tiles, axis=0))
    rotated = dot(outer, jnp.concatenate(columns, axis=1), ((0,), (0,)))
    tile = jnp.concatenate([jnp.concatenate([factor] * 4, axis=0)] * 2, axis=1)
    scaled = [
        (rotated[:, t * LANES : (t + 2) * LANES] * tile).astype(bf16) for t in range(0, stacks, 2)
    ]
    returned = dot(jnp.concatenate(scaled, axis=0), inner, ((1,), (1,))).astype(bf16)
    returned = jnp.concatenate([returned[t * size : (t + 1) * size] for t in range(stacks // 2)], axis=1)
    precond = dot(outer, returned).astype(bf16).astype(f32)

    homes = [None] * sources
    for p in range(pairs):
        t, u = p // 4, p % 4
        block = precond[u * side : (u + 1) * side, t * LANES : (t + 1) * LANES]
        homes[places[2 * p]], homes[places[2 * p + 1]] = unpaired(block)

    def flat(blocks):
        groups = [
            jnp.concatenate(blocks[g : g + SUBLANES], axis=0).astype(bf16) for g in range(0, len(blocks), SUBLANES)
        ]
        turned = dot(gather, jnp.concatenate(groups, axis=1))
        return jnp.concatenate(
            [
                jnp.concatenate(
                    [
                        turned[j * SUBLANES : (j + 1) * SUBLANES, g * LANES : (g + 1) * LANES]
                        for g in range(len(groups))
                    ],
                    axis=0,
                ).astype(bf16)
                for j in range(tall)
            ],
            axis=1,
        )

    cands = [
        moved_ref[(d - arrive) % sources, (1 + c) * tall : (2 + c) * tall, :]
        for d in range(sources)
        for c in range(per)
    ]
    rest = dot(flat(homes), flat(cands), ((1,), (1,)))
    wide = -(-count // LANES)
    if wide * LANES > count:
        rest = jnp.concatenate([rest, jnp.zeros((sources, wide * LANES - count), f32)], axis=1)
    tail = send - tall
    tails[...] = jnp.zeros_like(tails)
    for k in range(PIECES):
        piece = rest.astype(bf16).astype(f32)
        rest = rest - piece
        for t in range(wide):
            tails[pl.ds(k * wide + t, sources, stride=tail), :] = piece[:, t * LANES : (t + 1) * LANES]
    for k in range(sources):
        out_ref[k] = jnp.concatenate([homes[k], tails[k * tail : (k + 1) * tail, :]], axis=0).astype(bf16)


def finish(home_ref, holds_ref, chosen_ref, precond_ref, scores_ref, wide):
    slots, send, _ = home_ref.shape
    _, flat = precond_ref.shape[1:]
    count = chosen_ref.shape[0]
    tall = flat // LANES
    step = send + 1
    for k in range(slots):
        wide[pl.ds(k * step, send), :] = home_ref[k].astype(f32)
    by_slot = jnp.concatenate([wide[pl.ds(j, slots, stride=step), :].astype(bf16) for j in range(tall)], axis=1)
    precond_ref[0] = dot(holds_ref[...], by_slot).astype(bf16)
    groups = -(-count // LANES)
    parts = []
    for t in range(groups):
        pieces = [wide[pl.ds(tall + k * groups + t, slots, stride=step), :] for k in range(PIECES)]
        parts.append(jnp.sum((pieces[2] + pieces[1]) + pieces[0], axis=0, keepdims=True))
    dense = parts[0] if groups == 1 else jnp.concatenate(parts, axis=1)
    scores_ref[...] = jnp.sum(
        jnp.where(chosen_ref[...] > 0.0, upright(dense, count), 0.0), axis=0, keepdims=True
    )


ANY = pl.BlockSpec(memory_space=pl.ANY)
SMEM = pl.BlockSpec(memory_space=pltpu.SMEM)
VMEM = pl.BlockSpec(memory_space=pltpu.VMEM)
PARAMS = pltpu.CompilerParams(vmem_limit_bytes=40 * 1024 * 1024)


def body(
    query_grads,
    cand_grads,
    basis_out,
    basis_in,
    eigvals,
    layer_map,
    cand_rows,
    cand_lists,
    list_lengths,
):
    own, modules, flat = query_grads.shape
    per = cand_grads.shape[0]
    slots = layer_map.shape[0]
    layer_row = layer_map.reshape(1, slots)
    tall = flat // LANES
    side = basis_out.shape[1]
    size = SUBLANES * tall
    count = cand_rows.shape[0]
    height = (own + per) * tall
    send = tall + -(-PIECES * -(-count // LANES) // SUBLANES) * SUBLANES

    def in_hbm(x):
        return pltpu.with_memory_space_constraint(x, pltpu.HBM)

    def swap_over(x, first):
        groups = [order_of(slots, first)]
        return lax.all_to_all(x, "shard", split_axis=0, concat_axis=0, tiled=True, axis_index_groups=groups)

    packed = pl.pallas_call(
        pack,
        out_shape=jax.ShapeDtypeStruct((slots, height, LANES), bf16),
        in_specs=[VMEM] * 3,
        out_specs=VMEM,
        scratch_shapes=[pltpu.VMEM((slots * (height + 1), LANES), f32)],
        compiler_params=PARAMS,
        name="pack",
    )(in_hbm(layer_row), in_hbm(query_grads), in_hbm(cand_grads))
    square = jax.ShapeDtypeStruct((size, size), bf16)
    enter, outer, inner, factor, gather, held, chosen = pl.pallas_call(
        prepare,
        out_shape=(
            square,
            square,
            square,
            jax.ShapeDtypeStruct((side, LANES), f32),
            square,
            jax.ShapeDtypeStruct((modules, slots), bf16),
            jax.ShapeDtypeStruct((count, cand_lists.shape[1]), f32),
        ),
        in_specs=[SMEM] + [VMEM] * 6 + [ANY],
        out_specs=[VMEM] * 7,
        compiler_params=PARAMS,
        name="prepare",
    )(
        list_lengths,
        layer_row,
        basis_out.reshape(basis_out.shape[1:]),
        basis_in.reshape(basis_in.shape[1:]),
        eigvals.reshape(tall, LANES),
        cand_rows.reshape(1, count),
        cand_lists,
        packed,
    )
    moved = swap_over(packed, firsts(slots)[0])
    homes = pl.pallas_call(
        work,
        out_shape=jax.ShapeDtypeStruct((slots, send, LANES), bf16),
        in_specs=[VMEM] * 6,
        out_specs=VMEM,
        scratch_shapes=[pltpu.VMEM((slots * (send - tall), LANES), f32)],
        compiler_params=PARAMS,
        name="work",
    )(moved, enter, outer, inner, factor, gather)
    home = swap_over(homes, firsts(slots)[1])
    return pl.pallas_call(
        finish,
        out_shape=(
            jax.ShapeDtypeStruct(query_grads.shape, bf16),
            jax.ShapeDtypeStruct(cand_lists.shape, f32),
        ),
        in_specs=[VMEM] * 3,
        out_specs=(VMEM, VMEM),
        scratch_shapes=[pltpu.VMEM((slots * (send + 1), LANES), f32)],
        compiler_params=PARAMS,
        name="finish",
    )(home, held, chosen)


def solution(mesh):
    return jax.shard_map(
        body,
        mesh=mesh,
        in_specs=(
            P(("groups", "shard"), None, None),
            P(("groups", "shard"), None, None),
            P("shard", None, None),
            P("shard", None, None),
            P("shard", None),
            P(),
            P("groups"),
            P(("groups", "shard"), None),
            P(("groups", "shard")),
        ),
        out_specs=(P(("groups", "shard"), None, None), P(("groups", "shard"), None)),
        check_vma=False,
    )
```

```python
import jax
import jax.numpy as jnp
from jax import lax
from jax.experimental import pallas as pl
from jax.experimental.pallas import tpu as pltpu
from jax.sharding import PartitionSpec as P

damping = 0.1
LANES = 128
SUBLANES = 8
PIECES = 3
PARTS = 4
f32, bf16 = jnp.float32, jnp.bfloat16


def iota(shape, axis):
    return lax.broadcasted_iota(jnp.int32, shape, axis)


def dot(a, b, dims=((1,), (0,))):
    return lax.dot_general(a, b, (dims, ((), ())), preferred_element_type=f32)


def mask(condition):
    return condition.astype(f32).astype(bf16)


def reversed_bits(k, slots):
    bits = (slots - 1).bit_length()
    return sum(((k >> b) & 1) << (bits - 1 - b) for b in range(bits))


def centre(slots):
    return slots * 5 // 8


def order_of(slots):
    return [reversed_bits(k, slots) ^ centre(slots) for k in range(slots)]


def gather_rows(tall):
    size = SUBLANES * tall
    row = iota((size, size), 0)
    return mask(row // SUBLANES + tall * (row % SUBLANES) == iota((size, size), 1))


def half(left, right):
    return jnp.where(iota(left.shape, 1) < LANES // 2, left, right)


def swap(block):
    return pltpu.roll(block, LANES // 2, 1)


def unpaired(block):
    tall = block.shape[0] // 2
    top, low = block[:tall], block[tall:]
    return half(top, swap(low)), half(swap(top), low)


def holds(layer_row, modules):
    slots = layer_row.shape[1]
    order = reversed_bits(iota((slots, slots), 1), slots) ^ centre(slots)
    placed = mask(iota((slots, slots), 0) == order)
    return dot(mask(iota((modules, slots), 0) == layer_row), placed).astype(bf16)


def pack(layer_hbm, query_hbm, cand_hbm, out_ref, layer_ref, query_ref, cand_ref, wide, sems):
    modules, flat = query_ref.shape[1:]
    slots, height, _ = out_ref.shape
    tall = flat // LANES
    step = height + 1
    first = pltpu.make_async_copy(layer_hbm, layer_ref, sems.at[2 * PARTS])
    first.start()
    arrivals = []
    for g in range(PARTS):
        part = pl.ds(g * flat // PARTS, flat // PARTS)
        arrivals.append(
            [
                pltpu.make_async_copy(source.at[:, :, part], target.at[:, :, part], sems.at[2 * g + i])
                for i, (source, target) in enumerate(((query_hbm, query_ref), (cand_hbm, cand_ref)))
            ]
        )
        for arrival in arrivals[-1]:
            arrival.start()
    first.wait()
    one_hot = holds(layer_ref[...], modules)
    for g in range(PARTS):
        part = slice(g * flat // PARTS, (g + 1) * flat // PARTS)
        r = 0
        for arrival, ref in zip(arrivals[g], (query_ref, cand_ref)):
            arrival.wait()
            for row in range(ref.shape[0]):
                by_slot = dot(one_hot, ref[row, :, part], ((0,), (0,)))
                for j in range(tall // PARTS):
                    place = r * tall + g * tall // PARTS + j
                    wide[pl.ds(place, slots, stride=step), :] = by_slot[:, j * LANES : (j + 1) * LANES]
                r += 1
    for k in range(slots):
        out_ref[k] = wide[pl.ds(k * step, height), :].astype(bf16)


def upright(row, count):
    shape = (count, row.shape[1])
    return jnp.sum(jnp.where(iota(shape, 0) == iota(shape, 1), row, 0.0), axis=1, keepdims=True)


def prepare(
    length_ref, layer_ref, out_basis_ref, in_basis_ref, eigen_ref, rows_ref, lists_ref, after_ref,
    enter_ref, outer_ref, inner_ref, factor_ref, gather_ref, holds_ref, chosen_ref,
):
    del after_ref
    out_basis, in_basis = out_basis_ref[...], in_basis_ref[...]
    side = out_basis.shape[0]
    tall = side // 2
    size = enter_ref.shape[0]
    order = mask(iota((side, side), 1) == 2 * (iota((side, side), 0) % tall) + iota((side, side), 0) // tall)
    basis = dot(dot(order, out_basis).astype(bf16), order, ((1,), (1,))).astype(bf16)
    spread = mask(iota((size, side), 0) % side == iota((size, side), 1))
    row, column = iota((size, size), 0) // side, iota((size, size), 1) // side
    outer = dot(dot(spread, basis).astype(bf16), spread, ((1,), (1,)))
    inner = dot(dot(spread, in_basis).astype(bf16), spread, ((1,), (1,)))
    outer_ref[...] = jnp.where(row == column, outer, 0.0).astype(bf16)
    inner_ref[...] = jnp.where(row == column, inner, 0.0).astype(bf16)
    enter_ref[...] = jnp.where(row == 2 * (column % 2) + column // 2, inner, 0.0).astype(bf16)
    eigen = eigen_ref[...]
    turned = swap(eigen)
    factor_ref[...] = 1.0 / (jnp.concatenate([half(eigen, turned), half(turned, eigen)], axis=0) + damping)
    gather_ref[...] = gather_rows(tall)
    modules, slots = holds_ref.shape
    holds_ref[...] = holds(layer_ref[...], modules)

    count = rows_ref.shape[1]
    lists = lists_ref[...]
    longest = lists.shape[1]
    rows = upright(rows_ref[...].astype(f32), count)
    place = jnp.sum(jnp.where(iota((count, longest), 0) == lists, rows, 0.0), axis=0, keepdims=True)
    place = jnp.where(iota((1, longest), 1) < length_ref[0], place.astype(jnp.int32), -1)
    chosen_ref[...] = (iota((count, longest), 0) == place).astype(f32)


def work(moved_ref, enter_ref, outer_ref, inner_ref, factor_ref, gather_ref, out_ref, tails):
    sources, height, _ = moved_ref.shape
    _, send, _ = out_ref.shape
    size = enter_ref.shape[0]
    side, tall = size // 4, size // SUBLANES
    per = height // tall - 1
    count = sources * per
    pairs = sources // 2
    stacks = pairs // 4
    order = order_of(sources)
    outer, inner, gather = outer_ref[...], inner_ref[...], gather_ref[...]
    factor = factor_ref[...]

    queries = [jnp.concatenate([moved_ref[2 * p, :tall, :], moved_ref[2 * p + 1, :tall, :]], axis=1) for p in range(pairs)]
    entered = dot(jnp.concatenate(queries, axis=0), enter_ref[...]).astype(bf16)
    columns = []
    for t in range(stacks):
        tiles = []
        for p in range(4 * t, 4 * t + 4):
            rows = entered[p * tall : (p + 1) * tall]
            tiles += [rows[:, :LANES], rows[:, LANES:]]
        columns.append(jnp.concatenate(tiles, axis=0))
    rotated = dot(outer, jnp.concatenate(columns, axis=1), ((0,), (0,)))
    tile = jnp.concatenate([jnp.concatenate([factor] * 4, axis=0)] * 2, axis=1)
    scaled = [
        (rotated[:, t * LANES : (t + 2) * LANES] * tile).astype(bf16) for t in range(0, stacks, 2)
    ]
    returned = dot(jnp.concatenate(scaled, axis=0), inner, ((1,), (1,))).astype(bf16)
    returned = jnp.concatenate([returned[t * size : (t + 1) * size] for t in range(stacks // 2)], axis=1)
    precond = dot(outer, returned).astype(bf16).astype(f32)

    homes = [None] * sources
    for p in range(pairs):
        t, u = p // 4, p % 4
        block = precond[u * side : (u + 1) * side, t * LANES : (t + 1) * LANES]
        homes[2 * p], homes[2 * p + 1] = unpaired(block)

    def flat(blocks):
        groups = [
            jnp.concatenate(blocks[g : g + SUBLANES], axis=0).astype(bf16) for g in range(0, len(blocks), SUBLANES)
        ]
        turned = dot(gather, jnp.concatenate(groups, axis=1))
        return jnp.concatenate(
            [
                jnp.concatenate(
                    [
                        turned[j * SUBLANES : (j + 1) * SUBLANES, g * LANES : (g + 1) * LANES]
                        for g in range(len(groups))
                    ],
                    axis=0,
                ).astype(bf16)
                for j in range(tall)
            ],
            axis=1,
        )

    cands = [
        moved_ref[order.index(d), (1 + c) * tall : (2 + c) * tall, :]
        for d in range(sources)
        for c in range(per)
    ]
    rest = dot(flat(homes), flat(cands), ((1,), (1,)))
    wide = -(-count // LANES)
    if wide * LANES > count:
        rest = jnp.concatenate([rest, jnp.zeros((sources, wide * LANES - count), f32)], axis=1)
    tail = send - tall
    tails[...] = jnp.zeros_like(tails)
    for k in range(PIECES):
        piece = rest.astype(bf16).astype(f32)
        rest = rest - piece
        for t in range(wide):
            tails[pl.ds(k * wide + t, sources, stride=tail), :] = piece[:, t * LANES : (t + 1) * LANES]
    for k in range(sources):
        out_ref[k] = jnp.concatenate([homes[k], tails[k * tail : (k + 1) * tail, :]], axis=0).astype(bf16)


def finish(home_ref, holds_ref, chosen_ref, precond_ref, scores_ref, wide):
    slots, send, _ = home_ref.shape
    _, flat = precond_ref.shape[1:]
    count = chosen_ref.shape[0]
    tall = flat // LANES
    step = send + 1
    for k in range(slots):
        wide[pl.ds(k * step, send), :] = home_ref[k].astype(f32)
    by_slot = jnp.concatenate([wide[pl.ds(j, slots, stride=step), :].astype(bf16) for j in range(tall)], axis=1)
    precond_ref[0] = dot(holds_ref[...], by_slot).astype(bf16)
    groups = -(-count // LANES)
    parts = []
    for t in range(groups):
        pieces = [wide[pl.ds(tall + k * groups + t, slots, stride=step), :] for k in range(PIECES)]
        parts.append(jnp.sum((pieces[2] + pieces[1]) + pieces[0], axis=0, keepdims=True))
    dense = parts[0] if groups == 1 else jnp.concatenate(parts, axis=1)
    scores_ref[...] = jnp.sum(
        jnp.where(chosen_ref[...] > 0.0, upright(dense, count), 0.0), axis=0, keepdims=True
    )


HBM = pl.BlockSpec(memory_space=pltpu.HBM)
ANY = pl.BlockSpec(memory_space=pl.ANY)
SMEM = pl.BlockSpec(memory_space=pltpu.SMEM)
VMEM = pl.BlockSpec(memory_space=pltpu.VMEM)
PARAMS = pltpu.CompilerParams(vmem_limit_bytes=40 * 1024 * 1024)


def body(
    query_grads,
    cand_grads,
    basis_out,
    basis_in,
    eigvals,
    layer_map,
    cand_rows,
    cand_lists,
    list_lengths,
):
    own, modules, flat = query_grads.shape
    per = cand_grads.shape[0]
    slots = layer_map.shape[0]
    layer_row = layer_map.reshape(1, slots)
    tall = flat // LANES
    side = basis_out.shape[1]
    size = SUBLANES * tall
    count = cand_rows.shape[0]
    height = (own + per) * tall
    send = tall + -(-PIECES * -(-count // LANES) // SUBLANES) * SUBLANES

    def in_hbm(x):
        return pltpu.with_memory_space_constraint(x, pltpu.HBM)

    def swap_over(x):
        groups = [order_of(slots)]
        return lax.all_to_all(x, "shard", split_axis=0, concat_axis=0, tiled=True, axis_index_groups=groups)

    packed = pl.pallas_call(
        pack,
        out_shape=jax.ShapeDtypeStruct((slots, height, LANES), bf16),
        in_specs=[HBM] * 3,
        out_specs=VMEM,
        scratch_shapes=[
            pltpu.VMEM(layer_row.shape, jnp.int32),
            pltpu.VMEM(query_grads.shape, bf16),
            pltpu.VMEM(cand_grads.shape, bf16),
            pltpu.VMEM((slots * (height + 1), LANES), f32),
            pltpu.SemaphoreType.DMA((2 * PARTS + 1,)),
        ],
        compiler_params=PARAMS,
        name="pack",
    )(in_hbm(layer_row), in_hbm(query_grads), in_hbm(cand_grads))
    square = jax.ShapeDtypeStruct((size, size), bf16)
    enter, outer, inner, factor, gather, held, chosen = pl.pallas_call(
        prepare,
        out_shape=(
            square,
            square,
            square,
            jax.ShapeDtypeStruct((side, LANES), f32),
            square,
            jax.ShapeDtypeStruct((modules, slots), bf16),
            jax.ShapeDtypeStruct((count, cand_lists.shape[1]), f32),
        ),
        in_specs=[SMEM] + [VMEM] * 6 + [ANY],
        out_specs=[VMEM] * 7,
        compiler_params=PARAMS,
        name="prepare",
    )(
        list_lengths,
        layer_row,
        basis_out.reshape(basis_out.shape[1:]),
        basis_in.reshape(basis_in.shape[1:]),
        eigvals.reshape(tall, LANES),
        cand_rows.reshape(1, count),
        cand_lists,
        packed,
    )
    moved = swap_over(packed)
    homes = pl.pallas_call(
        work,
        out_shape=jax.ShapeDtypeStruct((slots, send, LANES), bf16),
        in_specs=[VMEM] * 6,
        out_specs=VMEM,
        scratch_shapes=[pltpu.VMEM((slots * (send - tall), LANES), f32)],
        compiler_params=PARAMS,
        name="work",
    )(moved, enter, outer, inner, factor, gather)
    home = swap_over(homes)
    return pl.pallas_call(
        finish,
        out_shape=(
            jax.ShapeDtypeStruct(query_grads.shape, bf16),
            jax.ShapeDtypeStruct(cand_lists.shape, f32),
        ),
        in_specs=[VMEM] * 3,
        out_specs=(VMEM, VMEM),
        scratch_shapes=[pltpu.VMEM((slots * (send + 1), LANES), f32)],
        compiler_params=PARAMS,
        name="finish",
    )(home, held, chosen)


def solution(mesh):
    return jax.shard_map(
        body,
        mesh=mesh,
        in_specs=(
            P(("groups", "shard"), None, None),
            P(("groups", "shard"), None, None),
            P("shard", None, None),
            P("shard", None, None),
            P("shard", None),
            P(),
            P("groups"),
            P(("groups", "shard"), None),
            P(("groups", "shard")),
        ),
        out_specs=(P(("groups", "shard"), None, None), P(("groups", "shard"), None)),
        check_vma=False,
    )
```

```python
import jax
import jax.numpy as jnp
from jax import lax
from jax.experimental import pallas as pl
from jax.experimental.pallas import tpu as pltpu
from jax.sharding import PartitionSpec as P

damping = 0.1
LANES = 128
SUBLANES = 8
PIECES = 3
f32, bf16 = jnp.float32, jnp.bfloat16


def iota(shape, axis):
    return lax.broadcasted_iota(jnp.int32, shape, axis)


def dot(a, b, dims=((1,), (0,))):
    return lax.dot_general(a, b, (dims, ((), ())), preferred_element_type=f32)


def mask(condition):
    return condition.astype(f32).astype(bf16)


def order_of(slots, first):
    return [(first + k) % slots for k in range(slots)]


def firsts(slots):
    return slots * 5 // 8, slots * 5 // 8


def gather_rows(tall):
    size = SUBLANES * tall
    row = iota((size, size), 0)
    return mask(row // SUBLANES + tall * (row % SUBLANES) == iota((size, size), 1))


def scatter_rows(tall):
    size = SUBLANES * tall
    row = iota((size, size), 0)
    return mask(row // tall + SUBLANES * (row % tall) == iota((size, size), 1))


def half(left, right):
    return jnp.where(iota(left.shape, 1) < LANES // 2, left, right)


def swap(block):
    return pltpu.roll(block, LANES // 2, 1)


def unpaired(block):
    tall = block.shape[0] // 2
    top, low = block[:tall], block[tall:]
    return half(top, swap(low)), half(swap(top), low)


def holds(layer_row, modules, first):
    slots = layer_row.shape[1]
    if first:
        layer_row = jnp.concatenate([layer_row[:, first:], layer_row[:, :first]], axis=1)
    return mask(iota((modules, slots), 0) == layer_row)


def spread_bases(out_basis, in_basis, eigen, enter_ref, outer_ref, inner_ref, factor_ref):
    side = out_basis.shape[0]
    tall = side // 2
    size = enter_ref.shape[0]
    order = mask(iota((side, side), 1) == 2 * (iota((side, side), 0) % tall) + iota((side, side), 0) // tall)
    basis = dot(dot(order, out_basis).astype(bf16), order, ((1,), (1,))).astype(bf16)
    spread = mask(iota((size, side), 0) % side == iota((size, side), 1))
    row, column = iota((size, size), 0) // side, iota((size, size), 1) // side
    outer = dot(dot(spread, basis).astype(bf16), spread, ((1,), (1,)))
    inner = dot(dot(spread, in_basis).astype(bf16), spread, ((1,), (1,)))
    outer_ref[...] = jnp.where(row == column, outer, 0.0).astype(bf16)
    inner_ref[...] = jnp.where(row == column, inner, 0.0).astype(bf16)
    enter_ref[...] = jnp.where(row == 2 * (column % 2) + column // 2, inner, 0.0).astype(bf16)
    turned = swap(eigen)
    factor_ref[...] = 1.0 / (jnp.concatenate([half(eigen, turned), half(turned, eigen)], axis=0) + damping)


def pack(
    layer_hbm, out_basis_hbm, in_basis_hbm, eigen_hbm, query_hbm, cand_hbm,
    out_ref, enter_ref, outer_ref, inner_ref, factor_ref, gather_ref,
    layer_ref, out_basis_ref, in_basis_ref, eigen_ref, query_ref, cand_ref, by_module, sems,
):
    arrivals = [
        pltpu.make_async_copy(source, target, sems.at[i])
        for i, (source, target) in enumerate(
            (
                (layer_hbm, layer_ref),
                (out_basis_hbm, out_basis_ref),
                (in_basis_hbm, in_basis_ref),
                (eigen_hbm, eigen_ref),
                (query_hbm, query_ref),
                (cand_hbm, cand_ref),
            )
        )
    ]
    for arrival in arrivals:
        arrival.start()
    modules, flat = query_ref.shape[1:]
    slots = out_ref.shape[0]
    tall = flat // LANES
    order = order_of(slots, firsts(slots)[0])
    gather_ref[...] = gather_rows(tall)
    for arrival in arrivals[:4]:
        arrival.wait()
    spread_bases(
        out_basis_ref[...], in_basis_ref[...], eigen_ref[...], enter_ref, outer_ref, inner_ref, factor_ref
    )
    at_once = slots * tall <= 512
    if at_once:
        shape = (tall, tall * modules)
        offset = iota(shape, 1) - modules * iota(shape, 0)
        place = jnp.concatenate([mask(offset == layer_ref[s]) for s in order], axis=0)
    else:
        place = scatter_rows(tall)
    r = 0
    for arrival, ref in zip(arrivals[4:], (query_ref, cand_ref)):
        arrival.wait()
        many = ref.shape[0]
        if at_once:
            tiles = [
                jnp.concatenate([ref[i, :, j * LANES : (j + 1) * LANES] for j in range(tall)], axis=0)
                for i in range(many)
            ]
            blocks = dot(place, jnp.concatenate(tiles, axis=1)).astype(bf16)
            for k in range(slots):
                for i in range(many):
                    part = blocks[k * tall : (k + 1) * tall, i * LANES : (i + 1) * LANES]
                    out_ref[k, (r + i) * tall : (r + i + 1) * tall, :] = part
        else:
            for i in range(many):
                rows = ref[i].astype(f32)
                columns = []
                for m in range(0, modules, SUBLANES):
                    tiles = [rows[m : m + SUBLANES, j * LANES : (j + 1) * LANES] for j in range(tall)]
                    columns.append(jnp.concatenate(tiles, axis=0).astype(bf16))
                blocks = dot(place, jnp.concatenate(columns, axis=1)).astype(bf16)
                for m in range(modules):
                    c, g = m % SUBLANES, m // SUBLANES
                    part = blocks[c * tall : (c + 1) * tall, g * LANES : (g + 1) * LANES]
                    by_module[m, (r + i) * tall : (r + i + 1) * tall, :] = part
        r += many
    if not at_once:
        for k, s in enumerate(order):
            out_ref[k] = by_module[layer_ref[s]]


def upright(row, count):
    shape = (count, row.shape[1])
    return jnp.sum(jnp.where(iota(shape, 0) == iota(shape, 1), row, 0.0), axis=1, keepdims=True)


def work(moved_ref, enter_ref, outer_ref, inner_ref, factor_ref, gather_ref, out_ref, tails):
    sources, height, _ = moved_ref.shape
    _, send, _ = out_ref.shape
    size = enter_ref.shape[0]
    side, tall = size // 4, size // SUBLANES
    per = height // tall - 1
    count = sources * per
    pairs = sources // 2
    stacks = pairs // 4
    arrive, leave = firsts(sources)
    places = [(d - leave) % sources for d in order_of(sources, arrive)]
    outer, inner, gather = outer_ref[...], inner_ref[...], gather_ref[...]
    factor = factor_ref[...]

    queries = [jnp.concatenate([moved_ref[2 * p, :tall, :], moved_ref[2 * p + 1, :tall, :]], axis=1) for p in range(pairs)]
    entered = dot(jnp.concatenate(queries, axis=0), enter_ref[...]).astype(bf16)
    columns = []
    for t in range(stacks):
        tiles = []
        for p in range(4 * t, 4 * t + 4):
            rows = entered[p * tall : (p + 1) * tall]
            tiles += [rows[:, :LANES], rows[:, LANES:]]
        columns.append(jnp.concatenate(tiles, axis=0))
    rotated = dot(outer, jnp.concatenate(columns, axis=1), ((0,), (0,)))
    tile = jnp.concatenate([jnp.concatenate([factor] * 4, axis=0)] * 2, axis=1)
    scaled = [
        (rotated[:, t * LANES : (t + 2) * LANES] * tile).astype(bf16) for t in range(0, stacks, 2)
    ]
    returned = dot(jnp.concatenate(scaled, axis=0), inner, ((1,), (1,))).astype(bf16)
    returned = jnp.concatenate([returned[t * size : (t + 1) * size] for t in range(stacks // 2)], axis=1)
    precond = dot(outer, returned).astype(bf16).astype(f32)

    homes = [None] * sources
    for p in range(pairs):
        t, u = p // 4, p % 4
        block = precond[u * side : (u + 1) * side, t * LANES : (t + 1) * LANES]
        homes[places[2 * p]], homes[places[2 * p + 1]] = unpaired(block)

    def flat(blocks):
        groups = [
            jnp.concatenate(blocks[g : g + SUBLANES], axis=0).astype(bf16) for g in range(0, len(blocks), SUBLANES)
        ]
        turned = dot(gather, jnp.concatenate(groups, axis=1))
        return jnp.concatenate(
            [
                jnp.concatenate(
                    [
                        turned[j * SUBLANES : (j + 1) * SUBLANES, g * LANES : (g + 1) * LANES]
                        for g in range(len(groups))
                    ],
                    axis=0,
                ).astype(bf16)
                for j in range(tall)
            ],
            axis=1,
        )

    cands = [
        moved_ref[(d - arrive) % sources, (1 + c) * tall : (2 + c) * tall, :]
        for d in range(sources)
        for c in range(per)
    ]
    rest = dot(flat(homes), flat(cands), ((1,), (1,)))
    wide = -(-count // LANES)
    if wide * LANES > count:
        rest = jnp.concatenate([rest, jnp.zeros((sources, wide * LANES - count), f32)], axis=1)
    tail = send - tall
    tails[...] = jnp.zeros_like(tails)
    for k in range(PIECES):
        piece = rest.astype(bf16).astype(f32)
        rest = rest - piece
        for t in range(wide):
            tails[pl.ds(k * wide + t, sources, stride=tail), :] = piece[:, t * LANES : (t + 1) * LANES]
    for k in range(sources):
        out_ref[k] = jnp.concatenate([homes[k], tails[k * tail : (k + 1) * tail, :]], axis=0).astype(bf16)


def finish(length_ref, layer_ref, rows_ref, lists_ref, home_ref, precond_ref, scores_ref, wide):
    slots, send, _ = home_ref.shape
    modules, flat = precond_ref.shape[1:]
    tall = flat // LANES
    step = send + 1
    for k in range(slots):
        wide[pl.ds(k * step, send), :] = home_ref[k].astype(f32)
    by_slot = jnp.concatenate([wide[pl.ds(j, slots, stride=step), :].astype(bf16) for j in range(tall)], axis=1)
    precond_ref[0] = dot(holds(layer_ref[...], modules, firsts(slots)[1]), by_slot).astype(bf16)

    count = rows_ref.shape[1]
    lists = lists_ref[...]
    longest = lists.shape[1]
    rows = upright(rows_ref[...].astype(f32), count)
    place = jnp.sum(jnp.where(iota((count, longest), 0) == lists, rows, 0.0), axis=0, keepdims=True)
    place = jnp.where(iota((1, longest), 1) < length_ref[...], place.astype(jnp.int32), -1)
    groups = -(-count // LANES)
    parts = []
    for t in range(groups):
        pieces = [wide[pl.ds(tall + k * groups + t, slots, stride=step), :] for k in range(PIECES)]
        parts.append(jnp.sum((pieces[2] + pieces[1]) + pieces[0], axis=0, keepdims=True))
    dense = parts[0] if groups == 1 else jnp.concatenate(parts, axis=1)
    scores_ref[...] = jnp.sum(
        jnp.where(iota((count, longest), 0) == place, upright(dense, count), 0.0), axis=0, keepdims=True
    )


HBM = pl.BlockSpec(memory_space=pltpu.HBM)
VMEM = pl.BlockSpec(memory_space=pltpu.VMEM)
PARAMS = pltpu.CompilerParams(vmem_limit_bytes=40 * 1024 * 1024)


def body(
    query_grads,
    cand_grads,
    basis_out,
    basis_in,
    eigvals,
    layer_map,
    cand_rows,
    cand_lists,
    list_lengths,
):
    own, modules, flat = query_grads.shape
    per = cand_grads.shape[0]
    slots = layer_map.shape[0]
    layer_row = layer_map.reshape(1, slots)
    tall = flat // LANES
    side = basis_out.shape[1]
    size = SUBLANES * tall
    count = cand_rows.shape[0]
    height = (own + per) * tall
    send = tall + -(-PIECES * -(-count // LANES) // SUBLANES) * SUBLANES

    def in_hbm(x):
        return pltpu.with_memory_space_constraint(x, pltpu.HBM)

    def swap_over(x, first):
        groups = [order_of(slots, first)]
        return lax.all_to_all(x, "shard", split_axis=0, concat_axis=0, tiled=True, axis_index_groups=groups)

    square = pltpu.VMEM((size, size), bf16)
    operands = (
        layer_map,
        basis_out.reshape(basis_out.shape[1:]),
        basis_in.reshape(basis_in.shape[1:]),
        eigvals.reshape(tall, LANES),
        query_grads,
        cand_grads,
    )
    packed, enter, outer, inner, factor, gather = pl.pallas_call(
        pack,
        out_shape=(
            pltpu.VMEM((slots, height, LANES), bf16),
            square,
            square,
            square,
            pltpu.VMEM((side, LANES), f32),
            square,
        ),
        in_specs=[HBM] * len(operands),
        out_specs=[VMEM] * 6,
        scratch_shapes=[pltpu.SMEM(layer_map.shape, jnp.int32)]
        + [pltpu.VMEM(x.shape, x.dtype) for x in operands[1:]]
        + [pltpu.VMEM((modules, height, LANES), bf16), pltpu.SemaphoreType.DMA((len(operands),))],
        compiler_params=PARAMS,
        name="pack",
    )(*(in_hbm(x) for x in operands))
    moved = swap_over(packed, firsts(slots)[0])
    homes = pl.pallas_call(
        work,
        out_shape=jax.ShapeDtypeStruct((slots, send, LANES), bf16),
        in_specs=[VMEM] * 6,
        out_specs=VMEM,
        scratch_shapes=[pltpu.VMEM((slots * (send - tall), LANES), f32)],
        compiler_params=PARAMS,
        name="work",
    )(moved, enter, outer, inner, factor, gather)
    home = swap_over(homes, firsts(slots)[1])
    return pl.pallas_call(
        finish,
        out_shape=(
            jax.ShapeDtypeStruct(query_grads.shape, bf16),
            jax.ShapeDtypeStruct(cand_lists.shape, f32),
        ),
        in_specs=[VMEM] * 5,
        out_specs=(VMEM, VMEM),
        scratch_shapes=[pltpu.VMEM((slots * (send + 1), LANES), f32)],
        compiler_params=PARAMS,
        name="finish",
    )(list_lengths.reshape(1, 1), layer_row, cand_rows.reshape(1, count), cand_lists, home)


def solution(mesh):
    return jax.shard_map(
        body,
        mesh=mesh,
        in_specs=(
            P(("groups", "shard"), None, None),
            P(("groups", "shard"), None, None),
            P("shard", None, None),
            P("shard", None, None),
            P("shard", None),
            P(),
            P("groups"),
            P(("groups", "shard"), None),
            P(("groups", "shard")),
        ),
        out_specs=(P(("groups", "shard"), None, None), P(("groups", "shard"), None)),
        check_vma=False,
    )
```

```python
import jax
import jax.numpy as jnp
from jax import lax
from jax.experimental import pallas as pl
from jax.experimental.pallas import tpu as pltpu
from jax.sharding import PartitionSpec as P

damping = 0.1
LANES = 128
SUBLANES = 8
PIECES = 3
f32, bf16 = jnp.float32, jnp.bfloat16


def iota(shape, axis):
    return lax.broadcasted_iota(jnp.int32, shape, axis)


def dot(a, b, dims=((1,), (0,))):
    return lax.dot_general(a, b, (dims, ((), ())), preferred_element_type=f32)


def mask(condition):
    return condition.astype(f32).astype(bf16)


def order_of(slots, first):
    return [(first + k) % slots for k in range(slots)]


def firsts(slots):
    return slots * 5 // 8, slots * 5 // 8


def gather_rows(tall):
    size = SUBLANES * tall
    row = iota((size, size), 0)
    return mask(row // SUBLANES + tall * (row % SUBLANES) == iota((size, size), 1))


def scatter_rows(tall):
    size = SUBLANES * tall
    row = iota((size, size), 0)
    return mask(row // tall + SUBLANES * (row % tall) == iota((size, size), 1))


def half(left, right):
    return jnp.where(iota(left.shape, 1) < LANES // 2, left, right)


def swap(block):
    return pltpu.roll(block, LANES // 2, 1)


def unpaired(block):
    tall = block.shape[0] // 2
    top, low = block[:tall], block[tall:]
    return half(top, swap(low)), half(swap(top), low)


def pack(layer_hbm, query_hbm, cand_hbm, out_ref, holds_ref, layer_ref, query_ref, cand_ref, by_module, sems):
    arrivals = [
        pltpu.make_async_copy(source, target, sems.at[i])
        for i, (source, target) in enumerate(
            ((layer_hbm, layer_ref), (query_hbm, query_ref), (cand_hbm, cand_ref))
        )
    ]
    for arrival in arrivals:
        arrival.start()
    modules, flat = query_ref.shape[1:]
    slots = out_ref.shape[0]
    tall = flat // LANES
    order = order_of(slots, firsts(slots)[0])
    arrivals[0].wait()
    module, slot = iota((modules, slots), 0), iota((modules, slots), 1)
    held = jnp.zeros((modules, slots), f32)
    for k, s in enumerate(order_of(slots, firsts(slots)[1])):
        held = jnp.where((slot == k) & (module == layer_ref[s]), 1.0, held)
    holds_ref[...] = held.astype(bf16)
    at_once = slots * tall <= 512
    if at_once:
        shape = (tall, tall * modules)
        offset = iota(shape, 1) - modules * iota(shape, 0)
        place = jnp.concatenate([mask(offset == layer_ref[s]) for s in order], axis=0)
    else:
        place = scatter_rows(tall)
    r = 0
    for arrival, ref in zip(arrivals[1:], (query_ref, cand_ref)):
        arrival.wait()
        many = ref.shape[0]
        if at_once:
            tiles = [
                jnp.concatenate([ref[i, :, j * LANES : (j + 1) * LANES] for j in range(tall)], axis=0)
                for i in range(many)
            ]
            blocks = dot(place, jnp.concatenate(tiles, axis=1)).astype(bf16)
            for k in range(slots):
                for i in range(many):
                    part = blocks[k * tall : (k + 1) * tall, i * LANES : (i + 1) * LANES]
                    out_ref[k, (r + i) * tall : (r + i + 1) * tall, :] = part
        else:
            for i in range(many):
                rows = ref[i].astype(f32)
                columns = []
                for m in range(0, modules, SUBLANES):
                    tiles = [rows[m : m + SUBLANES, j * LANES : (j + 1) * LANES] for j in range(tall)]
                    columns.append(jnp.concatenate(tiles, axis=0).astype(bf16))
                blocks = dot(place, jnp.concatenate(columns, axis=1)).astype(bf16)
                for m in range(modules):
                    c, g = m % SUBLANES, m // SUBLANES
                    part = blocks[c * tall : (c + 1) * tall, g * LANES : (g + 1) * LANES]
                    by_module[m, (r + i) * tall : (r + i + 1) * tall, :] = part
        r += many
    if not at_once:
        for k, s in enumerate(order):
            out_ref[k] = by_module[layer_ref[s]]


def upright(row, count):
    shape = (count, row.shape[1])
    return jnp.sum(jnp.where(iota(shape, 0) == iota(shape, 1), row, 0.0), axis=1, keepdims=True)


def work(
    moved_ref, out_basis_ref, in_basis_ref, eigen_ref, length_ref, rows_hbm, lists_hbm,
    out_ref, chosen_ref, tails, rows_ref, lists_ref, sems,
):
    arrivals = [
        pltpu.make_async_copy(source, target, sems.at[i])
        for i, (source, target) in enumerate(
            ((rows_hbm, rows_ref), (lists_hbm, lists_ref))
        )
    ]
    for arrival in arrivals:
        arrival.start()
    sources, height, _ = moved_ref.shape
    _, send, _ = out_ref.shape
    side = out_basis_ref.shape[0]
    tall = side // 2
    size = SUBLANES * tall
    per = height // tall - 1
    count = sources * per
    pairs = sources // 2
    stacks = pairs // 4
    arrive, leave = firsts(sources)
    places = [(d - leave) % sources for d in order_of(sources, arrive)]

    def spread(basis):
        wide = jnp.concatenate([basis] * 4, axis=1)
        return jnp.concatenate([wide] * 4, axis=0)

    row, column = iota((size, size), 0) // side, iota((size, size), 1) // side
    bases = spread(in_basis_ref[...].astype(f32))
    enter = jnp.where(row == 2 * (column % 2) + column // 2, bases, 0.0).astype(bf16)
    inner = jnp.where(row == column, bases, 0.0).astype(bf16)
    turn = mask(iota((side, side), 1) == 2 * (iota((side, side), 0) % tall) + iota((side, side), 0) // tall)
    bases = spread(dot(dot(turn, out_basis_ref[...]).astype(bf16), turn, ((1,), (1,))))
    outer = jnp.where(row == column, bases, 0.0).astype(bf16)
    eigen = eigen_ref[...]
    turned = swap(eigen)
    factor = 1.0 / (jnp.concatenate([half(eigen, turned), half(turned, eigen)], axis=0) + damping)
    gather = gather_rows(tall)


    queries = [jnp.concatenate([moved_ref[2 * p, :tall, :], moved_ref[2 * p + 1, :tall, :]], axis=1) for p in range(pairs)]
    entered = dot(jnp.concatenate(queries, axis=0), enter).astype(bf16)
    columns = []
    for t in range(stacks):
        tiles = []
        for p in range(4 * t, 4 * t + 4):
            rows = entered[p * tall : (p + 1) * tall]
            tiles += [rows[:, :LANES], rows[:, LANES:]]
        columns.append(jnp.concatenate(tiles, axis=0))
    rotated = dot(outer, jnp.concatenate(columns, axis=1), ((0,), (0,)))
    tile = jnp.concatenate([jnp.concatenate([factor] * 4, axis=0)] * 2, axis=1)
    scaled = [
        (rotated[:, t * LANES : (t + 2) * LANES] * tile).astype(bf16) for t in range(0, stacks, 2)
    ]
    returned = dot(jnp.concatenate(scaled, axis=0), inner, ((1,), (1,))).astype(bf16)
    returned = jnp.concatenate([returned[t * size : (t + 1) * size] for t in range(stacks // 2)], axis=1)
    precond = dot(outer, returned).astype(bf16).astype(f32)

    homes = [None] * sources
    for p in range(pairs):
        t, u = p // 4, p % 4
        block = precond[u * side : (u + 1) * side, t * LANES : (t + 1) * LANES]
        homes[places[2 * p]], homes[places[2 * p + 1]] = unpaired(block)

    def flat(blocks):
        groups = [
            jnp.concatenate(blocks[g : g + SUBLANES], axis=0).astype(bf16) for g in range(0, len(blocks), SUBLANES)
        ]
        turned = dot(gather, jnp.concatenate(groups, axis=1))
        return jnp.concatenate(
            [
                jnp.concatenate(
                    [
                        turned[j * SUBLANES : (j + 1) * SUBLANES, g * LANES : (g + 1) * LANES]
                        for g in range(len(groups))
                    ],
                    axis=0,
                ).astype(bf16)
                for j in range(tall)
            ],
            axis=1,
        )

    cands = [
        moved_ref[(d - arrive) % sources, (1 + c) * tall : (2 + c) * tall, :]
        for d in range(sources)
        for c in range(per)
    ]
    rest = dot(flat(homes), flat(cands), ((1,), (1,)))
    wide = -(-count // LANES)
    if wide * LANES > count:
        rest = jnp.concatenate([rest, jnp.zeros((sources, wide * LANES - count), f32)], axis=1)
    tail = send - tall
    tails[...] = jnp.zeros_like(tails)
    for k in range(PIECES):
        piece = rest.astype(bf16).astype(f32)
        rest = rest - piece
        for t in range(wide):
            tails[pl.ds(k * wide + t, sources, stride=tail), :] = piece[:, t * LANES : (t + 1) * LANES]
    for k in range(sources):
        out_ref[k] = jnp.concatenate([homes[k], tails[k * tail : (k + 1) * tail, :]], axis=0).astype(bf16)

    for arrival in arrivals:
        arrival.wait()
    lists = lists_ref[...]
    longest = lists.shape[1]
    rows = upright(rows_ref[...].astype(f32), count)
    place = jnp.sum(jnp.where(iota((count, longest), 0) == lists, rows, 0.0), axis=0, keepdims=True)
    place = jnp.where(iota((1, longest), 1) < length_ref[0], place.astype(jnp.int32), -1)
    chosen_ref[...] = (iota((count, longest), 0) == place).astype(f32)


def finish(home_ref, holds_ref, chosen_ref, precond_ref, scores_ref, wide):
    slots, send, _ = home_ref.shape
    _, flat = precond_ref.shape[1:]
    count = chosen_ref.shape[0]
    tall = flat // LANES
    step = send + 1
    for k in range(slots):
        wide[pl.ds(k * step, send), :] = home_ref[k].astype(f32)
    by_slot = jnp.concatenate([wide[pl.ds(j, slots, stride=step), :].astype(bf16) for j in range(tall)], axis=1)
    precond_ref[0] = dot(holds_ref[...], by_slot).astype(bf16)
    groups = -(-count // LANES)
    parts = []
    for t in range(groups):
        pieces = [wide[pl.ds(tall + k * groups + t, slots, stride=step), :] for k in range(PIECES)]
        parts.append(jnp.sum((pieces[2] + pieces[1]) + pieces[0], axis=0, keepdims=True))
    dense = parts[0] if groups == 1 else jnp.concatenate(parts, axis=1)
    scores_ref[...] = jnp.sum(
        jnp.where(chosen_ref[...] > 0.0, upright(dense, count), 0.0), axis=0, keepdims=True
    )


SMEM = pl.BlockSpec(memory_space=pltpu.SMEM)
HBM = pl.BlockSpec(memory_space=pltpu.HBM)
VMEM = pl.BlockSpec(memory_space=pltpu.VMEM)
PARAMS = pltpu.CompilerParams(vmem_limit_bytes=40 * 1024 * 1024)


def body(
    query_grads,
    cand_grads,
    basis_out,
    basis_in,
    eigvals,
    layer_map,
    cand_rows,
    cand_lists,
    list_lengths,
):
    own, modules, flat = query_grads.shape
    per = cand_grads.shape[0]
    slots = layer_map.shape[0]
    tall = flat // LANES
    count = cand_rows.shape[0]
    height = (own + per) * tall
    send = tall + -(-PIECES * -(-count // LANES) // SUBLANES) * SUBLANES

    def in_hbm(x):
        return pltpu.with_memory_space_constraint(x, pltpu.HBM)

    def swap_over(x, first):
        groups = [order_of(slots, first)]
        return lax.all_to_all(x, "shard", split_axis=0, concat_axis=0, tiled=True, axis_index_groups=groups)

    operands = (layer_map, query_grads, cand_grads)
    packed, held = pl.pallas_call(
        pack,
        out_shape=(pltpu.VMEM((slots, height, LANES), bf16), pltpu.VMEM((modules, slots), bf16)),
        in_specs=[HBM] * 3,
        out_specs=(VMEM, VMEM),
        scratch_shapes=[
            pltpu.SMEM(layer_map.shape, jnp.int32),
            pltpu.VMEM(query_grads.shape, bf16),
            pltpu.VMEM(cand_grads.shape, bf16),
            pltpu.VMEM((modules, height, LANES), bf16),
            pltpu.SemaphoreType.DMA((3,)),
        ],
        compiler_params=PARAMS,
        name="pack",
    )(*(in_hbm(x) for x in operands))
    moved = swap_over(packed, firsts(slots)[0])
    small = (cand_rows.reshape(1, count), cand_lists)
    homes, chosen = pl.pallas_call(
        work,
        out_shape=(
            jax.ShapeDtypeStruct((slots, send, LANES), bf16),
            jax.ShapeDtypeStruct((count, cand_lists.shape[1]), f32),
        ),
        in_specs=[VMEM] * 4 + [SMEM] + [HBM] * 2,
        out_specs=[VMEM] * 2,
        scratch_shapes=[pltpu.VMEM((slots * (send - tall), LANES), f32)]
        + [pltpu.VMEM(x.shape, jnp.int32) for x in small]
        + [pltpu.SemaphoreType.DMA((2,))],
        compiler_params=PARAMS,
        name="work",
    )(
        moved,
        basis_out.reshape(basis_out.shape[1:]),
        basis_in.reshape(basis_in.shape[1:]),
        eigvals.reshape(tall, LANES),
        list_lengths,
        *(in_hbm(x) for x in small),
    )
    home = swap_over(homes, firsts(slots)[1])
    return pl.pallas_call(
        finish,
        out_shape=(
            jax.ShapeDtypeStruct(query_grads.shape, bf16),
            jax.ShapeDtypeStruct(cand_lists.shape, f32),
        ),
        in_specs=[VMEM] * 3,
        out_specs=(VMEM, VMEM),
        scratch_shapes=[pltpu.VMEM((slots * (send + 1), LANES), f32)],
        compiler_params=PARAMS,
        name="finish",
    )(home, held, chosen)


def solution(mesh):
    return jax.shard_map(
        body,
        mesh=mesh,
        in_specs=(
            P(("groups", "shard"), None, None),
            P(("groups", "shard"), None, None),
            P("shard", None, None),
            P("shard", None, None),
            P("shard", None),
            P(),
            P("groups"),
            P(("groups", "shard"), None),
            P(("groups", "shard")),
        ),
        out_specs=(P(("groups", "shard"), None, None), P(("groups", "shard"), None)),
        check_vma=False,
    )
```

```python
import jax
import jax.numpy as jnp
from jax import lax
from jax.experimental import pallas as pl
from jax.experimental.pallas import tpu as pltpu
from jax.sharding import PartitionSpec as P

damping = 0.1
LANES = 128
SUBLANES = 8
PIECES = 3
f32, bf16 = jnp.float32, jnp.bfloat16


def iota(shape, axis):
    return lax.broadcasted_iota(jnp.int32, shape, axis)


def dot(a, b, dims=((1,), (0,))):
    return lax.dot_general(a, b, (dims, ((), ())), preferred_element_type=f32)


def mask(condition):
    return condition.astype(f32).astype(bf16)


def order_of(slots, first):
    return [(first + k) % slots for k in range(slots)]


def firsts(slots):
    return slots * 3 // 4, slots * 3 // 4


def gather_rows(tall):
    size = SUBLANES * tall
    row = iota((size, size), 0)
    return mask(row // SUBLANES + tall * (row % SUBLANES) == iota((size, size), 1))


def half(left, right):
    return jnp.where(iota(left.shape, 1) < LANES // 2, left, right)


def swap(block):
    return pltpu.roll(block, LANES // 2, 1)


def unpaired(block):
    tall = block.shape[0] // 2
    top, low = block[:tall], block[tall:]
    return half(top, swap(low)), half(swap(top), low)


def holds(layer_row, modules, first):
    slots = layer_row.shape[1]
    if first:
        layer_row = jnp.concatenate([layer_row[:, first:], layer_row[:, :first]], axis=1)
    return mask(iota((modules, slots), 0) == layer_row)


def pack(layer_hbm, query_hbm, cand_hbm, out_ref, layer_ref, query_ref, cand_ref, wide, sems):
    arrivals = [
        pltpu.make_async_copy(source, target, sems.at[i])
        for i, (source, target) in enumerate(
            ((layer_hbm, layer_ref), (query_hbm, query_ref), (cand_hbm, cand_ref))
        )
    ]
    for arrival in arrivals:
        arrival.start()
    arrivals[0].wait()
    modules, flat = query_ref.shape[1:]
    slots, height, _ = out_ref.shape
    tall = flat // LANES
    step = height + 1
    one_hot = holds(layer_ref[...], modules, firsts(slots)[0])
    sources = [(query_ref, r) for r in range(query_ref.shape[0])] + [(cand_ref, r) for r in range(cand_ref.shape[0])]
    for r, (ref, row) in enumerate(sources):
        if row == 0:
            arrivals[1 if ref is query_ref else 2].wait()
        by_slot = dot(one_hot, ref[row], ((0,), (0,)))
        for j in range(tall):
            wide[pl.ds(r * tall + j, slots, stride=step), :] = by_slot[:, j * LANES : (j + 1) * LANES]
    for k in range(slots):
        out_ref[k] = wide[pl.ds(k * step, height), :].astype(bf16)


def upright(row, count):
    shape = (count, row.shape[1])
    return jnp.sum(jnp.where(iota(shape, 0) == iota(shape, 1), row, 0.0), axis=1, keepdims=True)


def prepare(
    length_ref, layer_ref, out_basis_ref, in_basis_ref, eigen_ref, rows_ref, lists_ref, after_ref,
    enter_ref, outer_ref, inner_ref, factor_ref, gather_ref, holds_ref, chosen_ref,
):
    del after_ref
    out_basis, in_basis = out_basis_ref[...], in_basis_ref[...]
    side = out_basis.shape[0]
    tall = side // 2
    size = enter_ref.shape[0]
    order = mask(iota((side, side), 1) == 2 * (iota((side, side), 0) % tall) + iota((side, side), 0) // tall)
    basis = dot(dot(order, out_basis).astype(bf16), order, ((1,), (1,))).astype(bf16)
    spread = mask(iota((size, side), 0) % side == iota((size, side), 1))
    row, column = iota((size, size), 0) // side, iota((size, size), 1) // side
    outer = dot(dot(spread, basis).astype(bf16), spread, ((1,), (1,)))
    inner = dot(dot(spread, in_basis).astype(bf16), spread, ((1,), (1,)))
    outer_ref[...] = jnp.where(row == column, outer, 0.0).astype(bf16)
    inner_ref[...] = jnp.where(row == column, inner, 0.0).astype(bf16)
    enter_ref[...] = jnp.where(row == 2 * (column % 2) + column // 2, inner, 0.0).astype(bf16)
    eigen = eigen_ref[...]
    turned = swap(eigen)
    factor_ref[...] = 1.0 / (jnp.concatenate([half(eigen, turned), half(turned, eigen)], axis=0) + damping)
    gather_ref[...] = gather_rows(tall)
    modules, slots = holds_ref.shape
    holds_ref[...] = holds(layer_ref[...], modules, firsts(slots)[1])

    count = rows_ref.shape[1]
    lists = lists_ref[...]
    longest = lists.shape[1]
    rows = upright(rows_ref[...].astype(f32), count)
    place = jnp.sum(jnp.where(iota((count, longest), 0) == lists, rows, 0.0), axis=0, keepdims=True)
    place = jnp.where(iota((1, longest), 1) < length_ref[0], place.astype(jnp.int32), -1)
    chosen_ref[...] = (iota((count, longest), 0) == place).astype(f32)


def work(moved_ref, enter_ref, outer_ref, inner_ref, factor_ref, gather_ref, out_ref, tails):
    sources, height, _ = moved_ref.shape
    _, send, _ = out_ref.shape
    size = enter_ref.shape[0]
    side, tall = size // 4, size // SUBLANES
    per = height // tall - 1
    count = sources * per
    pairs = sources // 2
    stacks = pairs // 4
    arrive, leave = firsts(sources)
    places = [(d - leave) % sources for d in order_of(sources, arrive)]
    outer, inner, gather = outer_ref[...], inner_ref[...], gather_ref[...]
    factor = factor_ref[...]

    queries = [jnp.concatenate([moved_ref[2 * p, :tall, :], moved_ref[2 * p + 1, :tall, :]], axis=1) for p in range(pairs)]
    entered = dot(jnp.concatenate(queries, axis=0), enter_ref[...]).astype(bf16)
    columns = []
    for t in range(stacks):
        tiles = []
        for p in range(4 * t, 4 * t + 4):
            rows = entered[p * tall : (p + 1) * tall]
            tiles += [rows[:, :LANES], rows[:, LANES:]]
        columns.append(jnp.concatenate(tiles, axis=0))
    rotated = dot(outer, jnp.concatenate(columns, axis=1), ((0,), (0,)))
    tile = jnp.concatenate([jnp.concatenate([factor] * 4, axis=0)] * 2, axis=1)
    scaled = [
        (rotated[:, t * LANES : (t + 2) * LANES] * tile).astype(bf16) for t in range(0, stacks, 2)
    ]
    returned = dot(jnp.concatenate(scaled, axis=0), inner, ((1,), (1,))).astype(bf16)
    returned = jnp.concatenate([returned[t * size : (t + 1) * size] for t in range(stacks // 2)], axis=1)
    precond = dot(outer, returned).astype(bf16).astype(f32)

    homes = [None] * sources
    for p in range(pairs):
        t, u = p // 4, p % 4
        block = precond[u * side : (u + 1) * side, t * LANES : (t + 1) * LANES]
        homes[places[2 * p]], homes[places[2 * p + 1]] = unpaired(block)

    def flat(blocks):
        groups = [
            jnp.concatenate(blocks[g : g + SUBLANES], axis=0).astype(bf16) for g in range(0, len(blocks), SUBLANES)
        ]
        turned = dot(gather, jnp.concatenate(groups, axis=1))
        return jnp.concatenate(
            [
                jnp.concatenate(
                    [
                        turned[j * SUBLANES : (j + 1) * SUBLANES, g * LANES : (g + 1) * LANES]
                        for g in range(len(groups))
                    ],
                    axis=0,
                ).astype(bf16)
                for j in range(tall)
            ],
            axis=1,
        )

    cands = [
        moved_ref[(d - arrive) % sources, (1 + c) * tall : (2 + c) * tall, :]
        for d in range(sources)
        for c in range(per)
    ]
    rest = dot(flat(homes), flat(cands), ((1,), (1,)))
    wide = -(-count // LANES)
    if wide * LANES > count:
        rest = jnp.concatenate([rest, jnp.zeros((sources, wide * LANES - count), f32)], axis=1)
    tail = send - tall
    tails[...] = jnp.zeros_like(tails)
    for k in range(PIECES):
        piece = rest.astype(bf16).astype(f32)
        rest = rest - piece
        for t in range(wide):
            tails[pl.ds(k * wide + t, sources, stride=tail), :] = piece[:, t * LANES : (t + 1) * LANES]
    for k in range(sources):
        out_ref[k] = jnp.concatenate([homes[k], tails[k * tail : (k + 1) * tail, :]], axis=0).astype(bf16)


def finish(home_ref, holds_ref, chosen_ref, precond_ref, scores_ref, wide):
    slots, send, _ = home_ref.shape
    _, flat = precond_ref.shape[1:]
    count = chosen_ref.shape[0]
    tall = flat // LANES
    step = send + 1
    for k in range(slots):
        wide[pl.ds(k * step, send), :] = home_ref[k].astype(f32)
    by_slot = jnp.concatenate([wide[pl.ds(j, slots, stride=step), :].astype(bf16) for j in range(tall)], axis=1)
    precond_ref[0] = dot(holds_ref[...], by_slot).astype(bf16)
    groups = -(-count // LANES)
    parts = []
    for t in range(groups):
        pieces = [wide[pl.ds(tall + k * groups + t, slots, stride=step), :] for k in range(PIECES)]
        parts.append(jnp.sum((pieces[2] + pieces[1]) + pieces[0], axis=0, keepdims=True))
    dense = parts[0] if groups == 1 else jnp.concatenate(parts, axis=1)
    scores_ref[...] = jnp.sum(
        jnp.where(chosen_ref[...] > 0.0, upright(dense, count), 0.0), axis=0, keepdims=True
    )


HBM = pl.BlockSpec(memory_space=pltpu.HBM)
ANY = pl.BlockSpec(memory_space=pl.ANY)
SMEM = pl.BlockSpec(memory_space=pltpu.SMEM)
VMEM = pl.BlockSpec(memory_space=pltpu.VMEM)
PARAMS = pltpu.CompilerParams(vmem_limit_bytes=40 * 1024 * 1024)


def body(
    query_grads,
    cand_grads,
    basis_out,
    basis_in,
    eigvals,
    layer_map,
    cand_rows,
    cand_lists,
    list_lengths,
):
    own, modules, flat = query_grads.shape
    per = cand_grads.shape[0]
    slots = layer_map.shape[0]
    layer_row = layer_map.reshape(1, slots)
    tall = flat // LANES
    side = basis_out.shape[1]
    size = SUBLANES * tall
    count = cand_rows.shape[0]
    height = (own + per) * tall
    send = tall + -(-PIECES * -(-count // LANES) // SUBLANES) * SUBLANES

    def in_hbm(x):
        return pltpu.with_memory_space_constraint(x, pltpu.HBM)

    def swap_over(x, first):
        groups = [order_of(slots, first)]
        return lax.all_to_all(x, "shard", split_axis=0, concat_axis=0, tiled=True, axis_index_groups=groups)

    packed = pl.pallas_call(
        pack,
        out_shape=jax.ShapeDtypeStruct((slots, height, LANES), bf16),
        in_specs=[HBM] * 3,
        out_specs=VMEM,
        scratch_shapes=[
            pltpu.VMEM(layer_row.shape, jnp.int32),
            pltpu.VMEM(query_grads.shape, bf16),
            pltpu.VMEM(cand_grads.shape, bf16),
            pltpu.VMEM((slots * (height + 1), LANES), f32),
            pltpu.SemaphoreType.DMA((3,)),
        ],
        compiler_params=PARAMS,
        name="pack",
    )(in_hbm(layer_row), in_hbm(query_grads), in_hbm(cand_grads))
    square = jax.ShapeDtypeStruct((size, size), bf16)
    enter, outer, inner, factor, gather, held, chosen = pl.pallas_call(
        prepare,
        out_shape=(
            square,
            square,
            square,
            jax.ShapeDtypeStruct((side, LANES), f32),
            square,
            jax.ShapeDtypeStruct((modules, slots), bf16),
            jax.ShapeDtypeStruct((count, cand_lists.shape[1]), f32),
        ),
        in_specs=[SMEM] + [VMEM] * 6 + [ANY],
        out_specs=[VMEM] * 7,
        compiler_params=PARAMS,
        name="prepare",
    )(
        list_lengths,
        layer_row,
        basis_out.reshape(basis_out.shape[1:]),
        basis_in.reshape(basis_in.shape[1:]),
        eigvals.reshape(tall, LANES),
        cand_rows.reshape(1, count),
        cand_lists,
        packed,
    )
    moved = swap_over(packed, firsts(slots)[0])
    homes = pl.pallas_call(
        work,
        out_shape=jax.ShapeDtypeStruct((slots, send, LANES), bf16),
        in_specs=[VMEM] * 6,
        out_specs=VMEM,
        scratch_shapes=[pltpu.VMEM((slots * (send - tall), LANES), f32)],
        compiler_params=PARAMS,
        name="work",
    )(moved, enter, outer, inner, factor, gather)
    home = swap_over(homes, firsts(slots)[1])
    return pl.pallas_call(
        finish,
        out_shape=(
            jax.ShapeDtypeStruct(query_grads.shape, bf16),
            jax.ShapeDtypeStruct(cand_lists.shape, f32),
        ),
        in_specs=[VMEM] * 3,
        out_specs=(VMEM, VMEM),
        scratch_shapes=[pltpu.VMEM((slots * (send + 1), LANES), f32)],
        compiler_params=PARAMS,
        name="finish",
    )(home, held, chosen)


def solution(mesh):
    return jax.shard_map(
        body,
        mesh=mesh,
        in_specs=(
            P(("groups", "shard"), None, None),
            P(("groups", "shard"), None, None),
            P("shard", None, None),
            P("shard", None, None),
            P("shard", None),
            P(),
            P("groups"),
            P(("groups", "shard"), None),
            P(("groups", "shard")),
        ),
        out_specs=(P(("groups", "shard"), None, None), P(("groups", "shard"), None)),
        check_vma=False,
    )
```

```python
import jax
import jax.numpy as jnp
from jax import lax
from jax.experimental import pallas as pl
from jax.experimental.pallas import tpu as pltpu
from jax.sharding import PartitionSpec as P

damping = 0.1
LANES = 128
SUBLANES = 8
PIECES = 3
f32, bf16 = jnp.float32, jnp.bfloat16


def iota(shape, axis):
    return lax.broadcasted_iota(jnp.int32, shape, axis)


def dot(a, b, dims=((1,), (0,))):
    return lax.dot_general(a, b, (dims, ((), ())), preferred_element_type=f32)


def mask(condition):
    return condition.astype(f32).astype(bf16)


def order_of(slots, first):
    return [(first + k) % slots for k in range(slots)]


def firsts(slots):
    return slots * 5 // 8, slots * 5 // 8


def gather_rows(tall):
    size = SUBLANES * tall
    row = iota((size, size), 0)
    return mask(row // SUBLANES + tall * (row % SUBLANES) == iota((size, size), 1))


def half(left, right):
    return jnp.where(iota(left.shape, 1) < LANES // 2, left, right)


def swap(block):
    return pltpu.roll(block, LANES // 2, 1)


def unpaired(block):
    tall = block.shape[0] // 2
    top, low = block[:tall], block[tall:]
    return half(top, swap(low)), half(swap(top), low)


def holds(layer_row, modules, first):
    slots = layer_row.shape[1]
    if first:
        layer_row = jnp.concatenate([layer_row[:, first:], layer_row[:, :first]], axis=1)
    return mask(iota((modules, slots), 0) == layer_row)


def pack(layer_hbm, query_hbm, cand_hbm, out_ref, layer_ref, query_ref, cand_ref, wide, sems):
    arrivals = [
        pltpu.make_async_copy(source, target, sems.at[i])
        for i, (source, target) in enumerate(
            ((layer_hbm, layer_ref), (query_hbm, query_ref), (cand_hbm, cand_ref))
        )
    ]
    for arrival in arrivals:
        arrival.start()
    modules, flat = query_ref.shape[1:]
    slots, height, _ = out_ref.shape
    tall = flat // LANES
    slot, module = iota((slots, modules), 0), iota((slots, modules), 1)
    arrivals[0].wait()
    one_hot = jnp.zeros((slots, modules), f32)
    for k, s in enumerate(order_of(slots, firsts(slots)[0])):
        one_hot = jnp.where((slot == k) & (module == layer_ref[s]), 1.0, one_hot)
    one_hot = one_hot.astype(bf16)
    r = 0
    for arrival, ref in zip(arrivals[1:], (query_ref, cand_ref)):
        arrival.wait()
        for row in range(ref.shape[0]):
            by_slot = dot(one_hot, ref[row])
            for j in range(tall):
                wide[pl.ds(r * tall + j, slots, stride=height), :] = by_slot[:, j * LANES : (j + 1) * LANES]
            r += 1
    for k in range(slots):
        out_ref[k] = wide[k * height : (k + 1) * height, :].astype(bf16)


def upright(row, count):
    shape = (count, row.shape[1])
    return jnp.sum(jnp.where(iota(shape, 0) == iota(shape, 1), row, 0.0), axis=1, keepdims=True)


def prepare(
    length_ref, layer_ref, out_basis_ref, in_basis_ref, eigen_ref, rows_ref, lists_ref, after_ref,
    enter_ref, outer_ref, inner_ref, factor_ref, gather_ref, holds_ref, chosen_ref,
):
    del after_ref
    out_basis, in_basis = out_basis_ref[...], in_basis_ref[...]
    side = out_basis.shape[0]
    tall = side // 2
    size = enter_ref.shape[0]
    order = mask(iota((side, side), 1) == 2 * (iota((side, side), 0) % tall) + iota((side, side), 0) // tall)
    basis = dot(dot(order, out_basis).astype(bf16), order, ((1,), (1,))).astype(bf16)
    spread = mask(iota((size, side), 0) % side == iota((size, side), 1))
    row, column = iota((size, size), 0) // side, iota((size, size), 1) // side
    outer = dot(dot(spread, basis).astype(bf16), spread, ((1,), (1,)))
    inner = dot(dot(spread, in_basis).astype(bf16), spread, ((1,), (1,)))
    outer_ref[...] = jnp.where(row == column, outer, 0.0).astype(bf16)
    inner_ref[...] = jnp.where(row == column, inner, 0.0).astype(bf16)
    enter_ref[...] = jnp.where(row == 2 * (column % 2) + column // 2, inner, 0.0).astype(bf16)
    eigen = eigen_ref[...]
    turned = swap(eigen)
    factor_ref[...] = 1.0 / (jnp.concatenate([half(eigen, turned), half(turned, eigen)], axis=0) + damping)
    gather_ref[...] = gather_rows(tall)
    modules, slots = holds_ref.shape
    holds_ref[...] = holds(layer_ref[...], modules, firsts(slots)[1])

    count = rows_ref.shape[1]
    lists = lists_ref[...]
    longest = lists.shape[1]
    rows = upright(rows_ref[...].astype(f32), count)
    place = jnp.sum(jnp.where(iota((count, longest), 0) == lists, rows, 0.0), axis=0, keepdims=True)
    place = jnp.where(iota((1, longest), 1) < length_ref[0], place.astype(jnp.int32), -1)
    chosen_ref[...] = (iota((count, longest), 0) == place).astype(f32)


def work(moved_ref, enter_ref, outer_ref, inner_ref, factor_ref, gather_ref, out_ref, tails):
    sources, height, _ = moved_ref.shape
    _, send, _ = out_ref.shape
    size = enter_ref.shape[0]
    side, tall = size // 4, size // SUBLANES
    per = height // tall - 1
    count = sources * per
    pairs = sources // 2
    stacks = pairs // 4
    arrive, leave = firsts(sources)
    places = [(d - leave) % sources for d in order_of(sources, arrive)]
    outer, inner, gather = outer_ref[...], inner_ref[...], gather_ref[...]
    factor = factor_ref[...]

    queries = [jnp.concatenate([moved_ref[2 * p, :tall, :], moved_ref[2 * p + 1, :tall, :]], axis=1) for p in range(pairs)]
    entered = dot(jnp.concatenate(queries, axis=0), enter_ref[...]).astype(bf16)
    columns = []
    for t in range(stacks):
        tiles = []
        for p in range(4 * t, 4 * t + 4):
            rows = entered[p * tall : (p + 1) * tall]
            tiles += [rows[:, :LANES], rows[:, LANES:]]
        columns.append(jnp.concatenate(tiles, axis=0))
    rotated = dot(outer, jnp.concatenate(columns, axis=1), ((0,), (0,)))
    tile = jnp.concatenate([jnp.concatenate([factor] * 4, axis=0)] * 2, axis=1)
    scaled = [
        (rotated[:, t * LANES : (t + 2) * LANES] * tile).astype(bf16) for t in range(0, stacks, 2)
    ]
    returned = dot(jnp.concatenate(scaled, axis=0), inner, ((1,), (1,))).astype(bf16)
    returned = jnp.concatenate([returned[t * size : (t + 1) * size] for t in range(stacks // 2)], axis=1)
    precond = dot(outer, returned).astype(bf16).astype(f32)

    homes = [None] * sources
    for p in range(pairs):
        t, u = p // 4, p % 4
        block = precond[u * side : (u + 1) * side, t * LANES : (t + 1) * LANES]
        homes[places[2 * p]], homes[places[2 * p + 1]] = unpaired(block)

    def flat(blocks):
        groups = [
            jnp.concatenate(blocks[g : g + SUBLANES], axis=0).astype(bf16) for g in range(0, len(blocks), SUBLANES)
        ]
        turned = dot(gather, jnp.concatenate(groups, axis=1))
        return jnp.concatenate(
            [
                jnp.concatenate(
                    [
                        turned[j * SUBLANES : (j + 1) * SUBLANES, g * LANES : (g + 1) * LANES]
                        for g in range(len(groups))
                    ],
                    axis=0,
                ).astype(bf16)
                for j in range(tall)
            ],
            axis=1,
        )

    cands = [
        moved_ref[(d - arrive) % sources, (1 + c) * tall : (2 + c) * tall, :]
        for d in range(sources)
        for c in range(per)
    ]
    rest = dot(flat(homes), flat(cands), ((1,), (1,)))
    wide = -(-count // LANES)
    if wide * LANES > count:
        rest = jnp.concatenate([rest, jnp.zeros((sources, wide * LANES - count), f32)], axis=1)
    tail = send - tall
    tails[...] = jnp.zeros_like(tails)
    for k in range(PIECES):
        piece = rest.astype(bf16).astype(f32)
        rest = rest - piece
        for t in range(wide):
            tails[pl.ds(k * wide + t, sources, stride=tail), :] = piece[:, t * LANES : (t + 1) * LANES]
    for k in range(sources):
        out_ref[k] = jnp.concatenate([homes[k], tails[k * tail : (k + 1) * tail, :]], axis=0).astype(bf16)


def finish(home_ref, holds_ref, chosen_ref, precond_ref, scores_ref, wide):
    slots, send, _ = home_ref.shape
    _, flat = precond_ref.shape[1:]
    count = chosen_ref.shape[0]
    tall = flat // LANES
    step = send + 1
    for k in range(slots):
        wide[pl.ds(k * step, send), :] = home_ref[k].astype(f32)
    by_slot = jnp.concatenate([wide[pl.ds(j, slots, stride=step), :].astype(bf16) for j in range(tall)], axis=1)
    precond_ref[0] = dot(holds_ref[...], by_slot).astype(bf16)
    groups = -(-count // LANES)
    parts = []
    for t in range(groups):
        pieces = [wide[pl.ds(tall + k * groups + t, slots, stride=step), :] for k in range(PIECES)]
        parts.append(jnp.sum((pieces[2] + pieces[1]) + pieces[0], axis=0, keepdims=True))
    dense = parts[0] if groups == 1 else jnp.concatenate(parts, axis=1)
    scores_ref[...] = jnp.sum(
        jnp.where(chosen_ref[...] > 0.0, upright(dense, count), 0.0), axis=0, keepdims=True
    )


HBM = pl.BlockSpec(memory_space=pltpu.HBM)
ANY = pl.BlockSpec(memory_space=pl.ANY)
SMEM = pl.BlockSpec(memory_space=pltpu.SMEM)
VMEM = pl.BlockSpec(memory_space=pltpu.VMEM)
PARAMS = pltpu.CompilerParams(vmem_limit_bytes=40 * 1024 * 1024)


def body(
    query_grads,
    cand_grads,
    basis_out,
    basis_in,
    eigvals,
    layer_map,
    cand_rows,
    cand_lists,
    list_lengths,
):
    own, modules, flat = query_grads.shape
    per = cand_grads.shape[0]
    slots = layer_map.shape[0]
    layer_row = layer_map.reshape(1, slots)
    tall = flat // LANES
    side = basis_out.shape[1]
    size = SUBLANES * tall
    count = cand_rows.shape[0]
    height = (own + per) * tall
    send = tall + -(-PIECES * -(-count // LANES) // SUBLANES) * SUBLANES

    def in_hbm(x):
        return pltpu.with_memory_space_constraint(x, pltpu.HBM)

    def swap_over(x, first):
        groups = [order_of(slots, first)]
        return lax.all_to_all(x, "shard", split_axis=0, concat_axis=0, tiled=True, axis_index_groups=groups)

    packed = pl.pallas_call(
        pack,
        out_shape=jax.ShapeDtypeStruct((slots, height, LANES), bf16),
        in_specs=[HBM] * 3,
        out_specs=VMEM,
        scratch_shapes=[
            pltpu.SMEM(layer_map.shape, jnp.int32),
            pltpu.VMEM(query_grads.shape, bf16),
            pltpu.VMEM(cand_grads.shape, bf16),
            pltpu.VMEM((slots * height, LANES), f32),
            pltpu.SemaphoreType.DMA((3,)),
        ],
        compiler_params=PARAMS,
        name="pack",
    )(in_hbm(layer_map), in_hbm(query_grads), in_hbm(cand_grads))
    square = jax.ShapeDtypeStruct((size, size), bf16)
    enter, outer, inner, factor, gather, held, chosen = pl.pallas_call(
        prepare,
        out_shape=(
            square,
            square,
            square,
            jax.ShapeDtypeStruct((side, LANES), f32),
            square,
            jax.ShapeDtypeStruct((modules, slots), bf16),
            jax.ShapeDtypeStruct((count, cand_lists.shape[1]), f32),
        ),
        in_specs=[SMEM] + [VMEM] * 6 + [ANY],
        out_specs=[VMEM] * 7,
        compiler_params=PARAMS,
        name="prepare",
    )(
        list_lengths,
        layer_row,
        basis_out.reshape(basis_out.shape[1:]),
        basis_in.reshape(basis_in.shape[1:]),
        eigvals.reshape(tall, LANES),
        cand_rows.reshape(1, count),
        cand_lists,
        packed,
    )
    moved = swap_over(packed, firsts(slots)[0])
    homes = pl.pallas_call(
        work,
        out_shape=jax.ShapeDtypeStruct((slots, send, LANES), bf16),
        in_specs=[VMEM] * 6,
        out_specs=VMEM,
        scratch_shapes=[pltpu.VMEM((slots * (send - tall), LANES), f32)],
        compiler_params=PARAMS,
        name="work",
    )(moved, enter, outer, inner, factor, gather)
    home = swap_over(homes, firsts(slots)[1])
    return pl.pallas_call(
        finish,
        out_shape=(
            jax.ShapeDtypeStruct(query_grads.shape, bf16),
            jax.ShapeDtypeStruct(cand_lists.shape, f32),
        ),
        in_specs=[VMEM] * 3,
        out_specs=(VMEM, VMEM),
        scratch_shapes=[pltpu.VMEM((slots * (send + 1), LANES), f32)],
        compiler_params=PARAMS,
        name="finish",
    )(home, held, chosen)


def solution(mesh):
    return jax.shard_map(
        body,
        mesh=mesh,
        in_specs=(
            P(("groups", "shard"), None, None),
            P(("groups", "shard"), None, None),
            P("shard", None, None),
            P("shard", None, None),
            P("shard", None),
            P(),
            P("groups"),
            P(("groups", "shard"), None),
            P(("groups", "shard")),
        ),
        out_specs=(P(("groups", "shard"), None, None), P(("groups", "shard"), None)),
        check_vma=False,
    )
```

```python
import jax
import jax.numpy as jnp
from jax import lax
from jax.experimental import pallas as pl
from jax.experimental.pallas import tpu as pltpu
from jax.sharding import PartitionSpec as P

damping = 0.1
LANES = 128
SUBLANES = 8
PIECES = 3
f32, bf16 = jnp.float32, jnp.bfloat16


def iota(shape, axis):
    return lax.broadcasted_iota(jnp.int32, shape, axis)


def dot(a, b, dims=((1,), (0,))):
    return lax.dot_general(a, b, (dims, ((), ())), preferred_element_type=f32)


def mask(condition):
    return condition.astype(f32).astype(bf16)


def order_of(slots, first):
    return [(first + k) % slots for k in range(slots)]


def firsts(slots):
    return slots // 2, slots * 5 // 8


def gather_rows(tall):
    size = SUBLANES * tall
    row = iota((size, size), 0)
    return mask(row // SUBLANES + tall * (row % SUBLANES) == iota((size, size), 1))


def half(left, right):
    return jnp.where(iota(left.shape, 1) < LANES // 2, left, right)


def swap(block):
    return pltpu.roll(block, LANES // 2, 1)


def unpaired(block):
    tall = block.shape[0] // 2
    top, low = block[:tall], block[tall:]
    return half(top, swap(low)), half(swap(top), low)


def holds(layer_row, modules, first):
    slots = layer_row.shape[1]
    if first:
        layer_row = jnp.concatenate([layer_row[:, first:], layer_row[:, :first]], axis=1)
    return mask(iota((modules, slots), 0) == layer_row)


def pack(layer_hbm, query_hbm, cand_hbm, out_ref, layer_ref, query_ref, cand_ref, wide, sems):
    sources = [(query_hbm, query_ref, r) for r in range(query_ref.shape[0])]
    sources += [(cand_hbm, cand_ref, r) for r in range(cand_ref.shape[0])]
    first = pltpu.make_async_copy(layer_hbm, layer_ref, sems.at[len(sources)])
    first.start()
    arrivals = [
        pltpu.make_async_copy(hbm.at[row], ref.at[row], sems.at[i]) for i, (hbm, ref, row) in enumerate(sources)
    ]
    for arrival in arrivals:
        arrival.start()
    first.wait()
    modules, flat = query_ref.shape[1:]
    slots, height, _ = out_ref.shape
    tall = flat // LANES
    step = height + 1
    one_hot = holds(layer_ref[...], modules, firsts(slots)[0])
    for r, (_, ref, row) in enumerate(sources):
        arrivals[r].wait()
        by_slot = dot(one_hot, ref[row], ((0,), (0,)))
        for j in range(tall):
            wide[pl.ds(r * tall + j, slots, stride=step), :] = by_slot[:, j * LANES : (j + 1) * LANES]
    for k in range(slots):
        out_ref[k] = wide[pl.ds(k * step, height), :].astype(bf16)


def upright(row, count):
    shape = (count, row.shape[1])
    return jnp.sum(jnp.where(iota(shape, 0) == iota(shape, 1), row, 0.0), axis=1, keepdims=True)


def prepare(
    length_ref, layer_ref, out_basis_ref, in_basis_ref, eigen_ref, rows_ref, lists_ref, after_ref,
    enter_ref, outer_ref, inner_ref, factor_ref, gather_ref, holds_ref, chosen_ref,
):
    del after_ref
    out_basis, in_basis = out_basis_ref[...], in_basis_ref[...]
    side = out_basis.shape[0]
    tall = side // 2
    size = enter_ref.shape[0]
    order = mask(iota((side, side), 1) == 2 * (iota((side, side), 0) % tall) + iota((side, side), 0) // tall)
    basis = dot(dot(order, out_basis).astype(bf16), order, ((1,), (1,))).astype(bf16)
    spread = mask(iota((size, side), 0) % side == iota((size, side), 1))
    row, column = iota((size, size), 0) // side, iota((size, size), 1) // side
    outer = dot(dot(spread, basis).astype(bf16), spread, ((1,), (1,)))
    inner = dot(dot(spread, in_basis).astype(bf16), spread, ((1,), (1,)))
    outer_ref[...] = jnp.where(row == column, outer, 0.0).astype(bf16)
    inner_ref[...] = jnp.where(row == column, inner, 0.0).astype(bf16)
    enter_ref[...] = jnp.where(row == 2 * (column % 2) + column // 2, inner, 0.0).astype(bf16)
    eigen = eigen_ref[...]
    turned = swap(eigen)
    factor_ref[...] = 1.0 / (jnp.concatenate([half(eigen, turned), half(turned, eigen)], axis=0) + damping)
    gather_ref[...] = gather_rows(tall)
    modules, slots = holds_ref.shape
    holds_ref[...] = holds(layer_ref[...], modules, firsts(slots)[1])

    count = rows_ref.shape[1]
    lists = lists_ref[...]
    longest = lists.shape[1]
    rows = upright(rows_ref[...].astype(f32), count)
    place = jnp.sum(jnp.where(iota((count, longest), 0) == lists, rows, 0.0), axis=0, keepdims=True)
    place = jnp.where(iota((1, longest), 1) < length_ref[0], place.astype(jnp.int32), -1)
    chosen_ref[...] = (iota((count, longest), 0) == place).astype(f32)


def work(moved_ref, enter_ref, outer_ref, inner_ref, factor_ref, gather_ref, out_ref, tails):
    sources, height, _ = moved_ref.shape
    _, send, _ = out_ref.shape
    size = enter_ref.shape[0]
    side, tall = size // 4, size // SUBLANES
    per = height // tall - 1
    count = sources * per
    pairs = sources // 2
    stacks = pairs // 4
    arrive, leave = firsts(sources)
    places = [(d - leave) % sources for d in order_of(sources, arrive)]
    outer, inner, gather = outer_ref[...], inner_ref[...], gather_ref[...]
    factor = factor_ref[...]

    queries = [jnp.concatenate([moved_ref[2 * p, :tall, :], moved_ref[2 * p + 1, :tall, :]], axis=1) for p in range(pairs)]
    entered = dot(jnp.concatenate(queries, axis=0), enter_ref[...]).astype(bf16)
    columns = []
    for t in range(stacks):
        tiles = []
        for p in range(4 * t, 4 * t + 4):
            rows = entered[p * tall : (p + 1) * tall]
            tiles += [rows[:, :LANES], rows[:, LANES:]]
        columns.append(jnp.concatenate(tiles, axis=0))
    rotated = dot(outer, jnp.concatenate(columns, axis=1), ((0,), (0,)))
    tile = jnp.concatenate([jnp.concatenate([factor] * 4, axis=0)] * 2, axis=1)
    scaled = [
        (rotated[:, t * LANES : (t + 2) * LANES] * tile).astype(bf16) for t in range(0, stacks, 2)
    ]
    returned = dot(jnp.concatenate(scaled, axis=0), inner, ((1,), (1,))).astype(bf16)
    returned = jnp.concatenate([returned[t * size : (t + 1) * size] for t in range(stacks // 2)], axis=1)
    precond = dot(outer, returned).astype(bf16).astype(f32)

    homes = [None] * sources
    for p in range(pairs):
        t, u = p // 4, p % 4
        block = precond[u * side : (u + 1) * side, t * LANES : (t + 1) * LANES]
        homes[places[2 * p]], homes[places[2 * p + 1]] = unpaired(block)

    def flat(blocks):
        groups = [
            jnp.concatenate(blocks[g : g + SUBLANES], axis=0).astype(bf16) for g in range(0, len(blocks), SUBLANES)
        ]
        turned = dot(gather, jnp.concatenate(groups, axis=1))
        return jnp.concatenate(
            [
                jnp.concatenate(
                    [
                        turned[j * SUBLANES : (j + 1) * SUBLANES, g * LANES : (g + 1) * LANES]
                        for g in range(len(groups))
                    ],
                    axis=0,
                ).astype(bf16)
                for j in range(tall)
            ],
            axis=1,
        )

    cands = [
        moved_ref[(d - arrive) % sources, (1 + c) * tall : (2 + c) * tall, :]
        for d in range(sources)
        for c in range(per)
    ]
    rest = dot(flat(homes), flat(cands), ((1,), (1,)))
    wide = -(-count // LANES)
    if wide * LANES > count:
        rest = jnp.concatenate([rest, jnp.zeros((sources, wide * LANES - count), f32)], axis=1)
    tail = send - tall
    tails[...] = jnp.zeros_like(tails)
    for k in range(PIECES):
        piece = rest.astype(bf16).astype(f32)
        rest = rest - piece
        for t in range(wide):
            tails[pl.ds(k * wide + t, sources, stride=tail), :] = piece[:, t * LANES : (t + 1) * LANES]
    for k in range(sources):
        out_ref[k] = jnp.concatenate([homes[k], tails[k * tail : (k + 1) * tail, :]], axis=0).astype(bf16)


def finish(home_ref, holds_ref, chosen_ref, precond_ref, scores_ref, wide):
    slots, send, _ = home_ref.shape
    _, flat = precond_ref.shape[1:]
    count = chosen_ref.shape[0]
    tall = flat // LANES
    step = send + 1
    for k in range(slots):
        wide[pl.ds(k * step, send), :] = home_ref[k].astype(f32)
    by_slot = jnp.concatenate([wide[pl.ds(j, slots, stride=step), :].astype(bf16) for j in range(tall)], axis=1)
    precond_ref[0] = dot(holds_ref[...], by_slot).astype(bf16)
    groups = -(-count // LANES)
    parts = []
    for t in range(groups):
        pieces = [wide[pl.ds(tall + k * groups + t, slots, stride=step), :] for k in range(PIECES)]
        parts.append(jnp.sum((pieces[2] + pieces[1]) + pieces[0], axis=0, keepdims=True))
    dense = parts[0] if groups == 1 else jnp.concatenate(parts, axis=1)
    scores_ref[...] = jnp.sum(
        jnp.where(chosen_ref[...] > 0.0, upright(dense, count), 0.0), axis=0, keepdims=True
    )


HBM = pl.BlockSpec(memory_space=pltpu.HBM)
ANY = pl.BlockSpec(memory_space=pl.ANY)
SMEM = pl.BlockSpec(memory_space=pltpu.SMEM)
VMEM = pl.BlockSpec(memory_space=pltpu.VMEM)
PARAMS = pltpu.CompilerParams(vmem_limit_bytes=40 * 1024 * 1024)


def body(
    query_grads,
    cand_grads,
    basis_out,
    basis_in,
    eigvals,
    layer_map,
    cand_rows,
    cand_lists,
    list_lengths,
):
    own, modules, flat = query_grads.shape
    per = cand_grads.shape[0]
    slots = layer_map.shape[0]
    layer_row = layer_map.reshape(1, slots)
    tall = flat // LANES
    side = basis_out.shape[1]
    size = SUBLANES * tall
    count = cand_rows.shape[0]
    height = (own + per) * tall
    send = tall + -(-PIECES * -(-count // LANES) // SUBLANES) * SUBLANES

    def in_hbm(x):
        return pltpu.with_memory_space_constraint(x, pltpu.HBM)

    def swap_over(x, first):
        groups = [order_of(slots, first)]
        return lax.all_to_all(x, "shard", split_axis=0, concat_axis=0, tiled=True, axis_index_groups=groups)

    packed = pl.pallas_call(
        pack,
        out_shape=jax.ShapeDtypeStruct((slots, height, LANES), bf16),
        in_specs=[HBM] * 3,
        out_specs=VMEM,
        scratch_shapes=[
            pltpu.VMEM(layer_row.shape, jnp.int32),
            pltpu.VMEM(query_grads.shape, bf16),
            pltpu.VMEM(cand_grads.shape, bf16),
            pltpu.VMEM((slots * (height + 1), LANES), f32),
            pltpu.SemaphoreType.DMA((own + per + 1,)),
        ],
        compiler_params=PARAMS,
        name="pack",
    )(in_hbm(layer_row), in_hbm(query_grads), in_hbm(cand_grads))
    square = jax.ShapeDtypeStruct((size, size), bf16)
    enter, outer, inner, factor, gather, held, chosen = pl.pallas_call(
        prepare,
        out_shape=(
            square,
            square,
            square,
            jax.ShapeDtypeStruct((side, LANES), f32),
            square,
            jax.ShapeDtypeStruct((modules, slots), bf16),
            jax.ShapeDtypeStruct((count, cand_lists.shape[1]), f32),
        ),
        in_specs=[SMEM] + [VMEM] * 6 + [ANY],
        out_specs=[VMEM] * 7,
        compiler_params=PARAMS,
        name="prepare",
    )(
        list_lengths,
        layer_row,
        basis_out.reshape(basis_out.shape[1:]),
        basis_in.reshape(basis_in.shape[1:]),
        eigvals.reshape(tall, LANES),
        cand_rows.reshape(1, count),
        cand_lists,
        packed,
    )
    moved = swap_over(packed, firsts(slots)[0])
    homes = pl.pallas_call(
        work,
        out_shape=jax.ShapeDtypeStruct((slots, send, LANES), bf16),
        in_specs=[VMEM] * 6,
        out_specs=VMEM,
        scratch_shapes=[pltpu.VMEM((slots * (send - tall), LANES), f32)],
        compiler_params=PARAMS,
        name="work",
    )(moved, enter, outer, inner, factor, gather)
    home = swap_over(homes, firsts(slots)[1])
    return pl.pallas_call(
        finish,
        out_shape=(
            jax.ShapeDtypeStruct(query_grads.shape, bf16),
            jax.ShapeDtypeStruct(cand_lists.shape, f32),
        ),
        in_specs=[VMEM] * 3,
        out_specs=(VMEM, VMEM),
        scratch_shapes=[pltpu.VMEM((slots * (send + 1), LANES), f32)],
        compiler_params=PARAMS,
        name="finish",
    )(home, held, chosen)


def solution(mesh):
    return jax.shard_map(
        body,
        mesh=mesh,
        in_specs=(
            P(("groups", "shard"), None, None),
            P(("groups", "shard"), None, None),
            P("shard", None, None),
            P("shard", None, None),
            P("shard", None),
            P(),
            P("groups"),
            P(("groups", "shard"), None),
            P(("groups", "shard")),
        ),
        out_specs=(P(("groups", "shard"), None, None), P(("groups", "shard"), None)),
        check_vma=False,
    )
```

```python
import jax
import jax.numpy as jnp
from jax import lax
from jax.experimental import pallas as pl
from jax.experimental.pallas import tpu as pltpu
from jax.sharding import PartitionSpec as P

damping = 0.1
LANES = 128
SUBLANES = 8
PIECES = 3
f32, bf16 = jnp.float32, jnp.bfloat16


def iota(shape, axis):
    return lax.broadcasted_iota(jnp.int32, shape, axis)


def dot(a, b, dims=((1,), (0,))):
    return lax.dot_general(a, b, (dims, ((), ())), preferred_element_type=f32)


def mask(condition):
    return condition.astype(f32).astype(bf16)


def order_of(slots, first):
    return [(first + k) % slots for k in range(slots)]


def firsts(slots):
    return slots // 2, slots * 5 // 8


def gather_rows(tall):
    size = SUBLANES * tall
    row = iota((size, size), 0)
    return mask(row // SUBLANES + tall * (row % SUBLANES) == iota((size, size), 1))


def half(left, right):
    return jnp.where(iota(left.shape, 1) < LANES // 2, left, right)


def swap(block):
    return pltpu.roll(block, LANES // 2, 1)


def unpaired(block):
    tall = block.shape[0] // 2
    top, low = block[:tall], block[tall:]
    return half(top, swap(low)), half(swap(top), low)


def holds(layer_row, modules, first):
    slots = layer_row.shape[1]
    if first:
        layer_row = jnp.concatenate([layer_row[:, first:], layer_row[:, :first]], axis=1)
    return mask(iota((modules, slots), 0) == layer_row)


def pack(layer_hbm, query_hbm, cand_hbm, out_ref, layer_ref, query_ref, cand_ref, wide, sems):
    sources = [(query_hbm, query_ref, r) for r in range(query_ref.shape[0])]
    sources += [(cand_hbm, cand_ref, r) for r in range(cand_ref.shape[0])]
    first = pltpu.make_async_copy(layer_hbm, layer_ref, sems.at[len(sources)])
    first.start()
    arrivals = [
        pltpu.make_async_copy(hbm.at[row], ref.at[row], sems.at[i]) for i, (hbm, ref, row) in enumerate(sources)
    ]
    for arrival in arrivals:
        arrival.start()
    first.wait()
    modules, flat = query_ref.shape[1:]
    slots, height, _ = out_ref.shape
    tall = flat // LANES
    step = height + 1
    one_hot = holds(layer_ref[...], modules, firsts(slots)[0])
    for r, (_, ref, row) in enumerate(sources):
        arrivals[r].wait()
        by_slot = dot(one_hot, ref[row], ((0,), (0,)))
        for j in range(tall):
            wide[pl.ds(r * tall + j, slots, stride=step), :] = by_slot[:, j * LANES : (j + 1) * LANES]
    for k in range(slots):
        out_ref[k] = wide[pl.ds(k * step, height), :].astype(bf16)


def upright(row, count):
    shape = (count, row.shape[1])
    return jnp.sum(jnp.where(iota(shape, 0) == iota(shape, 1), row, 0.0), axis=1, keepdims=True)


def prepare(
    length_ref, layer_ref, out_basis_ref, in_basis_ref, eigen_ref, rows_ref, lists_ref, after_ref,
    enter_ref, outer_ref, turned_ref, back_ref, factor_ref, gather_ref, holds_ref, chosen_ref,
):
    del after_ref
    out_basis, in_basis = out_basis_ref[...], in_basis_ref[...]
    side = out_basis.shape[0]
    tall = side // 2
    size = enter_ref.shape[0]
    order = mask(iota((side, side), 1) == 2 * (iota((side, side), 0) % tall) + iota((side, side), 0) // tall)
    basis = dot(dot(order, out_basis).astype(bf16), order, ((1,), (1,))).astype(bf16)
    spread = mask(iota((size, side), 0) % side == iota((size, side), 1))
    row, column = iota((size, size), 0) // side, iota((size, size), 1) // side
    outer = dot(dot(spread, basis).astype(bf16), spread, ((1,), (1,)))
    inner = dot(dot(spread, in_basis).astype(bf16), spread, ((1,), (1,)))
    outer = jnp.where(row == column, outer, 0.0)
    outer_ref[...] = outer.astype(bf16)
    turned_ref[...] = outer.T.astype(bf16)
    back_ref[...] = jnp.where(row == column, inner, 0.0).T.astype(bf16)
    enter_ref[...] = jnp.where(row == 2 * (column % 2) + column // 2, inner, 0.0).astype(bf16)
    eigen = eigen_ref[...]
    turned = swap(eigen)
    factor_ref[...] = 1.0 / (jnp.concatenate([half(eigen, turned), half(turned, eigen)], axis=0) + damping)
    gather_ref[...] = gather_rows(tall)
    modules, slots = holds_ref.shape
    holds_ref[...] = holds(layer_ref[...], modules, firsts(slots)[1])

    count = rows_ref.shape[1]
    lists = lists_ref[...]
    longest = lists.shape[1]
    rows = upright(rows_ref[...].astype(f32), count)
    place = jnp.sum(jnp.where(iota((count, longest), 0) == lists, rows, 0.0), axis=0, keepdims=True)
    place = jnp.where(iota((1, longest), 1) < length_ref[0], place.astype(jnp.int32), -1)
    chosen_ref[...] = (iota((count, longest), 0) == place).astype(f32)


def work(moved_ref, enter_ref, outer_ref, turned_ref, back_ref, factor_ref, gather_ref, out_ref, tails):
    sources, height, _ = moved_ref.shape
    _, send, _ = out_ref.shape
    size = enter_ref.shape[0]
    side, tall = size // 4, size // SUBLANES
    per = height // tall - 1
    count = sources * per
    pairs = sources // 2
    stacks = pairs // 4
    arrive, leave = firsts(sources)
    places = [(d - leave) % sources for d in order_of(sources, arrive)]
    gather = gather_ref[...]
    factor = factor_ref[...]

    queries = [jnp.concatenate([moved_ref[2 * p, :tall, :], moved_ref[2 * p + 1, :tall, :]], axis=1) for p in range(pairs)]
    entered = dot(jnp.concatenate(queries, axis=0), enter_ref[...]).astype(bf16)
    columns = []
    for t in range(stacks):
        tiles = []
        for p in range(4 * t, 4 * t + 4):
            rows = entered[p * tall : (p + 1) * tall]
            tiles += [rows[:, :LANES], rows[:, LANES:]]
        columns.append(jnp.concatenate(tiles, axis=0))
    rotated = dot(turned_ref[...], jnp.concatenate(columns, axis=1))
    tile = jnp.concatenate([jnp.concatenate([factor] * 4, axis=0)] * 2, axis=1)
    scaled = [
        (rotated[:, t * LANES : (t + 2) * LANES] * tile).astype(bf16) for t in range(0, stacks, 2)
    ]
    returned = dot(jnp.concatenate(scaled, axis=0), back_ref[...]).astype(bf16)
    returned = jnp.concatenate([returned[t * size : (t + 1) * size] for t in range(stacks // 2)], axis=1)
    precond = dot(outer_ref[...], returned).astype(bf16).astype(f32)

    homes = [None] * sources
    for p in range(pairs):
        t, u = p // 4, p % 4
        block = precond[u * side : (u + 1) * side, t * LANES : (t + 1) * LANES]
        homes[places[2 * p]], homes[places[2 * p + 1]] = unpaired(block)

    def flat(blocks):
        groups = [
            jnp.concatenate(blocks[g : g + SUBLANES], axis=0).astype(bf16) for g in range(0, len(blocks), SUBLANES)
        ]
        turned = dot(gather, jnp.concatenate(groups, axis=1))
        return jnp.concatenate(
            [
                jnp.concatenate(
                    [
                        turned[j * SUBLANES : (j + 1) * SUBLANES, g * LANES : (g + 1) * LANES]
                        for g in range(len(groups))
                    ],
                    axis=0,
                ).astype(bf16)
                for j in range(tall)
            ],
            axis=1,
        )

    cands = [
        moved_ref[(d - arrive) % sources, (1 + c) * tall : (2 + c) * tall, :]
        for d in range(sources)
        for c in range(per)
    ]
    rest = dot(flat(homes), flat(cands), ((1,), (1,)))
    wide = -(-count // LANES)
    if wide * LANES > count:
        rest = jnp.concatenate([rest, jnp.zeros((sources, wide * LANES - count), f32)], axis=1)
    tail = send - tall
    tails[...] = jnp.zeros_like(tails)
    for k in range(PIECES):
        piece = rest.astype(bf16).astype(f32)
        rest = rest - piece
        for t in range(wide):
            tails[pl.ds(k * wide + t, sources, stride=tail), :] = piece[:, t * LANES : (t + 1) * LANES]
    for k in range(sources):
        out_ref[k] = jnp.concatenate([homes[k], tails[k * tail : (k + 1) * tail, :]], axis=0).astype(bf16)


def finish(home_ref, holds_ref, chosen_ref, precond_ref, scores_ref, wide):
    slots, send, _ = home_ref.shape
    _, flat = precond_ref.shape[1:]
    count = chosen_ref.shape[0]
    tall = flat // LANES
    step = send + 1
    for k in range(slots):
        wide[pl.ds(k * step, send), :] = home_ref[k].astype(f32)
    by_slot = jnp.concatenate([wide[pl.ds(j, slots, stride=step), :].astype(bf16) for j in range(tall)], axis=1)
    precond_ref[0] = dot(holds_ref[...], by_slot).astype(bf16)
    groups = -(-count // LANES)
    parts = []
    for t in range(groups):
        pieces = [wide[pl.ds(tall + k * groups + t, slots, stride=step), :] for k in range(PIECES)]
        parts.append(jnp.sum((pieces[2] + pieces[1]) + pieces[0], axis=0, keepdims=True))
    dense = parts[0] if groups == 1 else jnp.concatenate(parts, axis=1)
    scores_ref[...] = jnp.sum(
        jnp.where(chosen_ref[...] > 0.0, upright(dense, count), 0.0), axis=0, keepdims=True
    )


HBM = pl.BlockSpec(memory_space=pltpu.HBM)
ANY = pl.BlockSpec(memory_space=pl.ANY)
SMEM = pl.BlockSpec(memory_space=pltpu.SMEM)
VMEM = pl.BlockSpec(memory_space=pltpu.VMEM)
PARAMS = pltpu.CompilerParams(vmem_limit_bytes=40 * 1024 * 1024)


def body(
    query_grads,
    cand_grads,
    basis_out,
    basis_in,
    eigvals,
    layer_map,
    cand_rows,
    cand_lists,
    list_lengths,
):
    own, modules, flat = query_grads.shape
    per = cand_grads.shape[0]
    slots = layer_map.shape[0]
    layer_row = layer_map.reshape(1, slots)
    tall = flat // LANES
    side = basis_out.shape[1]
    size = SUBLANES * tall
    count = cand_rows.shape[0]
    height = (own + per) * tall
    send = tall + -(-PIECES * -(-count // LANES) // SUBLANES) * SUBLANES

    def in_hbm(x):
        return pltpu.with_memory_space_constraint(x, pltpu.HBM)

    def swap_over(x, first):
        groups = [order_of(slots, first)]
        return lax.all_to_all(x, "shard", split_axis=0, concat_axis=0, tiled=True, axis_index_groups=groups)

    packed = pl.pallas_call(
        pack,
        out_shape=jax.ShapeDtypeStruct((slots, height, LANES), bf16),
        in_specs=[HBM] * 3,
        out_specs=VMEM,
        scratch_shapes=[
            pltpu.VMEM(layer_row.shape, jnp.int32),
            pltpu.VMEM(query_grads.shape, bf16),
            pltpu.VMEM(cand_grads.shape, bf16),
            pltpu.VMEM((slots * (height + 1), LANES), f32),
            pltpu.SemaphoreType.DMA((own + per + 1,)),
        ],
        compiler_params=PARAMS,
        name="pack",
    )(in_hbm(layer_row), in_hbm(query_grads), in_hbm(cand_grads))
    square = jax.ShapeDtypeStruct((size, size), bf16)
    enter, outer, turned, back, factor, gather, held, chosen = pl.pallas_call(
        prepare,
        out_shape=(
            square,
            square,
            square,
            square,
            jax.ShapeDtypeStruct((side, LANES), f32),
            square,
            jax.ShapeDtypeStruct((modules, slots), bf16),
            jax.ShapeDtypeStruct((count, cand_lists.shape[1]), f32),
        ),
        in_specs=[SMEM] + [VMEM] * 6 + [ANY],
        out_specs=[VMEM] * 8,
        compiler_params=PARAMS,
        name="prepare",
    )(
        list_lengths,
        layer_row,
        basis_out.reshape(basis_out.shape[1:]),
        basis_in.reshape(basis_in.shape[1:]),
        eigvals.reshape(tall, LANES),
        cand_rows.reshape(1, count),
        cand_lists,
        packed,
    )
    moved = swap_over(packed, firsts(slots)[0])
    homes = pl.pallas_call(
        work,
        out_shape=jax.ShapeDtypeStruct((slots, send, LANES), bf16),
        in_specs=[VMEM] * 7,
        out_specs=VMEM,
        scratch_shapes=[pltpu.VMEM((slots * (send - tall), LANES), f32)],
        compiler_params=PARAMS,
        name="work",
    )(moved, enter, outer, turned, back, factor, gather)
    home = swap_over(homes, firsts(slots)[1])
    return pl.pallas_call(
        finish,
        out_shape=(
            jax.ShapeDtypeStruct(query_grads.shape, bf16),
            jax.ShapeDtypeStruct(cand_lists.shape, f32),
        ),
        in_specs=[VMEM] * 3,
        out_specs=(VMEM, VMEM),
        scratch_shapes=[pltpu.VMEM((slots * (send + 1), LANES), f32)],
        compiler_params=PARAMS,
        name="finish",
    )(home, held, chosen)


def solution(mesh):
    return jax.shard_map(
        body,
        mesh=mesh,
        in_specs=(
            P(("groups", "shard"), None, None),
            P(("groups", "shard"), None, None),
            P("shard", None, None),
            P("shard", None, None),
            P("shard", None),
            P(),
            P("groups"),
            P(("groups", "shard"), None),
            P(("groups", "shard")),
        ),
        out_specs=(P(("groups", "shard"), None, None), P(("groups", "shard"), None)),
        check_vma=False,
    )
```

```python
import jax
import jax.numpy as jnp
from jax import lax
from jax.experimental import pallas as pl
from jax.experimental.pallas import tpu as pltpu
from jax.sharding import PartitionSpec as P

damping = 0.1
LANES = 128
SUBLANES = 8
PIECES = 3
f32, bf16 = jnp.float32, jnp.bfloat16


def iota(shape, axis):
    return lax.broadcasted_iota(jnp.int32, shape, axis)


def dot(a, b, dims=((1,), (0,))):
    return lax.dot_general(a, b, (dims, ((), ())), preferred_element_type=f32)


def mask(condition):
    return condition.astype(f32).astype(bf16)


def order_of(slots, first):
    return [(first + k) % slots for k in range(slots)]


def firsts(slots):
    return slots * 5 // 8, slots * 5 // 8


def gather_rows(tall):
    size = SUBLANES * tall
    row = iota((size, size), 0)
    return mask(row // SUBLANES + tall * (row % SUBLANES) == iota((size, size), 1))


def half(left, right):
    return jnp.where(iota(left.shape, 1) < LANES // 2, left, right)


def swap(block):
    return pltpu.roll(block, LANES // 2, 1)


def unpaired(block):
    tall = block.shape[0] // 2
    top, low = block[:tall], block[tall:]
    return half(top, swap(low)), half(swap(top), low)


def holds(layer_row, modules, first):
    slots = layer_row.shape[1]
    if first:
        layer_row = jnp.concatenate([layer_row[:, first:], layer_row[:, :first]], axis=1)
    return mask(iota((modules, slots), 0) == layer_row)


def block_bases(out_basis, in_basis, eigen):
    side = out_basis.shape[0]
    tall = side // 2
    size = 4 * side

    def spread(basis):
        wide = jnp.concatenate([basis] * 4, axis=1)
        return jnp.concatenate([wide] * 4, axis=0)

    row, column = iota((size, size), 0) // side, iota((size, size), 1) // side
    turn = mask(iota((side, side), 1) == 2 * (iota((side, side), 0) % tall) + iota((side, side), 0) // tall)
    bases = spread(dot(dot(turn, out_basis).astype(bf16), turn, ((1,), (1,))))
    outer = jnp.where(row == column, bases, 0.0).astype(bf16)
    bases = spread(in_basis.astype(f32))
    enter = jnp.where(row == 2 * (column % 2) + column // 2, bases, 0.0).astype(bf16)
    inner = jnp.where(row == column, bases, 0.0).astype(bf16)
    turned = swap(eigen)
    factor = 1.0 / (jnp.concatenate([half(eigen, turned), half(turned, eigen)], axis=0) + damping)
    return enter, outer, inner, factor


def pack(
    length_ref, layer_hbm, out_basis_hbm, in_basis_hbm, eigen_hbm, query_hbm, cand_hbm,
    out_ref, enter_ref, outer_ref, inner_ref, factor_ref, gather_ref, holds_ref, limit_ref,
    layer_ref, out_basis_ref, in_basis_ref, eigen_ref, query_ref, cand_ref, wide, sems,
):
    arrivals = [
        pltpu.make_async_copy(source, target, sems.at[i])
        for i, (source, target) in enumerate(
            (
                (layer_hbm, layer_ref),
                (out_basis_hbm, out_basis_ref),
                (in_basis_hbm, in_basis_ref),
                (eigen_hbm, eigen_ref),
                (query_hbm, query_ref),
                (cand_hbm, cand_ref),
            )
        )
    ]
    for arrival in arrivals:
        arrival.start()
    modules, flat = query_ref.shape[1:]
    slots, height, _ = out_ref.shape
    tall = flat // LANES
    step = height + 1
    gather_ref[...] = gather_rows(tall)
    limit_ref[...] = jnp.full(limit_ref.shape, length_ref[0])
    for arrival in arrivals[:4]:
        arrival.wait()
    one_hot = holds(layer_ref[...], modules, firsts(slots)[0])
    holds_ref[...] = holds(layer_ref[...], modules, firsts(slots)[1])
    enter_ref[...], outer_ref[...], inner_ref[...], factor_ref[...] = block_bases(
        out_basis_ref[...], in_basis_ref[...], eigen_ref[...]
    )
    r = 0
    for arrival, ref in zip(arrivals[4:], (query_ref, cand_ref)):
        arrival.wait()
        for row in range(ref.shape[0]):
            by_slot = dot(one_hot, ref[row], ((0,), (0,)))
            for j in range(tall):
                wide[pl.ds(r * tall + j, slots, stride=step), :] = by_slot[:, j * LANES : (j + 1) * LANES]
            r += 1
    for k in range(slots):
        out_ref[k] = wide[pl.ds(k * step, height), :].astype(bf16)


def upright(row, count):
    shape = (count, row.shape[1])
    return jnp.sum(jnp.where(iota(shape, 0) == iota(shape, 1), row, 0.0), axis=1, keepdims=True)


def work(
    moved_ref, enter_ref, outer_ref, inner_ref, factor_ref, gather_ref, limit_ref, rows_hbm, lists_hbm,
    out_ref, chosen_ref, tails, rows_ref, lists_ref, sems,
):
    arrivals = [
        pltpu.make_async_copy(rows_hbm, rows_ref, sems.at[0]),
        pltpu.make_async_copy(lists_hbm, lists_ref, sems.at[1]),
    ]
    for arrival in arrivals:
        arrival.start()
    sources, height, _ = moved_ref.shape
    _, send, _ = out_ref.shape
    size = enter_ref.shape[0]
    side, tall = size // 4, size // SUBLANES
    per = height // tall - 1
    count = sources * per
    pairs = sources // 2
    stacks = pairs // 4
    arrive, leave = firsts(sources)
    places = [(d - leave) % sources for d in order_of(sources, arrive)]
    outer, inner, gather = outer_ref[...], inner_ref[...], gather_ref[...]
    factor = factor_ref[...]

    queries = [jnp.concatenate([moved_ref[2 * p, :tall, :], moved_ref[2 * p + 1, :tall, :]], axis=1) for p in range(pairs)]
    entered = dot(jnp.concatenate(queries, axis=0), enter_ref[...]).astype(bf16)
    columns = []
    for t in range(stacks):
        tiles = []
        for p in range(4 * t, 4 * t + 4):
            rows = entered[p * tall : (p + 1) * tall]
            tiles += [rows[:, :LANES], rows[:, LANES:]]
        columns.append(jnp.concatenate(tiles, axis=0))
    rotated = dot(outer, jnp.concatenate(columns, axis=1), ((0,), (0,)))
    tile = jnp.concatenate([jnp.concatenate([factor] * 4, axis=0)] * 2, axis=1)
    scaled = [
        (rotated[:, t * LANES : (t + 2) * LANES] * tile).astype(bf16) for t in range(0, stacks, 2)
    ]
    returned = dot(jnp.concatenate(scaled, axis=0), inner, ((1,), (1,))).astype(bf16)
    returned = jnp.concatenate([returned[t * size : (t + 1) * size] for t in range(stacks // 2)], axis=1)
    precond = dot(outer, returned).astype(bf16).astype(f32)

    homes = [None] * sources
    for p in range(pairs):
        t, u = p // 4, p % 4
        block = precond[u * side : (u + 1) * side, t * LANES : (t + 1) * LANES]
        homes[places[2 * p]], homes[places[2 * p + 1]] = unpaired(block)

    def flat(blocks):
        groups = [
            jnp.concatenate(blocks[g : g + SUBLANES], axis=0).astype(bf16) for g in range(0, len(blocks), SUBLANES)
        ]
        turned = dot(gather, jnp.concatenate(groups, axis=1))
        return jnp.concatenate(
            [
                jnp.concatenate(
                    [
                        turned[j * SUBLANES : (j + 1) * SUBLANES, g * LANES : (g + 1) * LANES]
                        for g in range(len(groups))
                    ],
                    axis=0,
                ).astype(bf16)
                for j in range(tall)
            ],
            axis=1,
        )

    cands = [
        moved_ref[(d - arrive) % sources, (1 + c) * tall : (2 + c) * tall, :]
        for d in range(sources)
        for c in range(per)
    ]
    rest = dot(flat(homes), flat(cands), ((1,), (1,)))
    wide = -(-count // LANES)
    if wide * LANES > count:
        rest = jnp.concatenate([rest, jnp.zeros((sources, wide * LANES - count), f32)], axis=1)
    tail = send - tall
    tails[...] = jnp.zeros_like(tails)
    for k in range(PIECES):
        piece = rest.astype(bf16).astype(f32)
        rest = rest - piece
        for t in range(wide):
            tails[pl.ds(k * wide + t, sources, stride=tail), :] = piece[:, t * LANES : (t + 1) * LANES]
    for k in range(sources):
        out_ref[k] = jnp.concatenate([homes[k], tails[k * tail : (k + 1) * tail, :]], axis=0).astype(bf16)

    for arrival in arrivals:
        arrival.wait()
    lists = lists_ref[...]
    longest = lists.shape[1]
    rows = upright(rows_ref[...].astype(f32), count)
    place = jnp.sum(jnp.where(iota((count, longest), 0) == lists, rows, 0.0), axis=0, keepdims=True)
    place = jnp.where(iota((1, longest), 1) < limit_ref[:, :1], place.astype(jnp.int32), -1)
    chosen_ref[...] = (iota((count, longest), 0) == place).astype(f32)


def finish(home_ref, holds_ref, chosen_ref, precond_ref, scores_ref, wide):
    slots, send, _ = home_ref.shape
    _, flat = precond_ref.shape[1:]
    count = chosen_ref.shape[0]
    tall = flat // LANES
    step = send + 1
    for k in range(slots):
        wide[pl.ds(k * step, send), :] = home_ref[k].astype(f32)
    by_slot = jnp.concatenate([wide[pl.ds(j, slots, stride=step), :].astype(bf16) for j in range(tall)], axis=1)
    precond_ref[0] = dot(holds_ref[...], by_slot).astype(bf16)
    groups = -(-count // LANES)
    parts = []
    for t in range(groups):
        pieces = [wide[pl.ds(tall + k * groups + t, slots, stride=step), :] for k in range(PIECES)]
        parts.append(jnp.sum((pieces[2] + pieces[1]) + pieces[0], axis=0, keepdims=True))
    dense = parts[0] if groups == 1 else jnp.concatenate(parts, axis=1)
    scores_ref[...] = jnp.sum(
        jnp.where(chosen_ref[...] > 0.0, upright(dense, count), 0.0), axis=0, keepdims=True
    )


SMEM = pl.BlockSpec(memory_space=pltpu.SMEM)
HBM = pl.BlockSpec(memory_space=pltpu.HBM)
VMEM = pl.BlockSpec(memory_space=pltpu.VMEM)
PARAMS = pltpu.CompilerParams(vmem_limit_bytes=40 * 1024 * 1024)


def body(
    query_grads,
    cand_grads,
    basis_out,
    basis_in,
    eigvals,
    layer_map,
    cand_rows,
    cand_lists,
    list_lengths,
):
    own, modules, flat = query_grads.shape
    per = cand_grads.shape[0]
    slots = layer_map.shape[0]
    tall = flat // LANES
    side = basis_out.shape[1]
    size = SUBLANES * tall
    count = cand_rows.shape[0]
    height = (own + per) * tall
    send = tall + -(-PIECES * -(-count // LANES) // SUBLANES) * SUBLANES

    def in_hbm(x):
        return pltpu.with_memory_space_constraint(x, pltpu.HBM)

    def swap_over(x, first):
        groups = [order_of(slots, first)]
        return lax.all_to_all(x, "shard", split_axis=0, concat_axis=0, tiled=True, axis_index_groups=groups)

    square = pltpu.VMEM((size, size), bf16)
    operands = (
        layer_map.reshape(1, slots),
        basis_out.reshape(basis_out.shape[1:]),
        basis_in.reshape(basis_in.shape[1:]),
        eigvals.reshape(tall, LANES),
        query_grads,
        cand_grads,
    )
    packed, enter, outer, inner, factor, gather, held, limit = pl.pallas_call(
        pack,
        out_shape=(
            pltpu.VMEM((slots, height, LANES), bf16),
            square,
            square,
            square,
            pltpu.VMEM((side, LANES), f32),
            square,
            pltpu.VMEM((modules, slots), bf16),
            pltpu.VMEM((1, LANES), jnp.int32),
        ),
        in_specs=[SMEM] + [HBM] * len(operands),
        out_specs=[VMEM] * 8,
        scratch_shapes=[pltpu.VMEM(x.shape, x.dtype) for x in operands]
        + [pltpu.VMEM((slots * (height + 1), LANES), f32), pltpu.SemaphoreType.DMA((len(operands),))],
        compiler_params=PARAMS,
        name="pack",
    )(list_lengths, *(in_hbm(x) for x in operands))
    moved = swap_over(packed, firsts(slots)[0])
    small = (cand_rows.reshape(1, count), cand_lists)
    homes, chosen = pl.pallas_call(
        work,
        out_shape=(
            jax.ShapeDtypeStruct((slots, send, LANES), bf16),
            jax.ShapeDtypeStruct((count, cand_lists.shape[1]), f32),
        ),
        in_specs=[VMEM] * 7 + [HBM] * 2,
        out_specs=[VMEM] * 2,
        scratch_shapes=[pltpu.VMEM((slots * (send - tall), LANES), f32)]
        + [pltpu.VMEM(x.shape, jnp.int32) for x in small]
        + [pltpu.SemaphoreType.DMA((2,))],
        compiler_params=PARAMS,
        name="work",
    )(moved, enter, outer, inner, factor, gather, limit, *(in_hbm(x) for x in small))
    home = swap_over(homes, firsts(slots)[1])
    return pl.pallas_call(
        finish,
        out_shape=(
            jax.ShapeDtypeStruct(query_grads.shape, bf16),
            jax.ShapeDtypeStruct(cand_lists.shape, f32),
        ),
        in_specs=[VMEM] * 3,
        out_specs=(VMEM, VMEM),
        scratch_shapes=[pltpu.VMEM((slots * (send + 1), LANES), f32)],
        compiler_params=PARAMS,
        name="finish",
    )(home, held, chosen)


def solution(mesh):
    return jax.shard_map(
        body,
        mesh=mesh,
        in_specs=(
            P(("groups", "shard"), None, None),
            P(("groups", "shard"), None, None),
            P("shard", None, None),
            P("shard", None, None),
            P("shard", None),
            P(),
            P("groups"),
            P(("groups", "shard"), None),
            P(("groups", "shard")),
        ),
        out_specs=(P(("groups", "shard"), None, None), P(("groups", "shard"), None)),
        check_vma=False,
    )
```

```python
import jax
import jax.numpy as jnp
from jax import lax
from jax.experimental import pallas as pl
from jax.experimental.pallas import tpu as pltpu
from jax.sharding import PartitionSpec as P

damping = 0.1
LANES = 128
SUBLANES = 8
PIECES = 3
f32, bf16 = jnp.float32, jnp.bfloat16


def iota(shape, axis):
    return lax.broadcasted_iota(jnp.int32, shape, axis)


def dot(a, b, dims=((1,), (0,))):
    return lax.dot_general(a, b, (dims, ((), ())), preferred_element_type=f32)


def mask(condition):
    return condition.astype(f32).astype(bf16)


def order_of(slots, first):
    return [(first + k) % slots for k in range(slots)]


def firsts(slots):
    return slots * 5 // 8, slots * 5 // 8


def gather_rows(tall):
    size = SUBLANES * tall
    row = iota((size, size), 0)
    return mask(row // SUBLANES + tall * (row % SUBLANES) == iota((size, size), 1))


def half(left, right):
    return jnp.where(iota(left.shape, 1) < LANES // 2, left, right)


def swap(block):
    return pltpu.roll(block, LANES // 2, 1)


def unpaired(block):
    tall = block.shape[0] // 2
    top, low = block[:tall], block[tall:]
    return half(top, swap(low)), half(swap(top), low)


def holds(layer_row, modules, first):
    slots = layer_row.shape[1]
    if first:
        layer_row = jnp.concatenate([layer_row[:, first:], layer_row[:, :first]], axis=1)
    return mask(iota((modules, slots), 0) == layer_row)


def block_bases(out_basis, in_basis, eigen):
    side = out_basis.shape[0]
    tall = side // 2
    size = 4 * side

    def spread(basis):
        wide = jnp.concatenate([basis] * 4, axis=1)
        return jnp.concatenate([wide] * 4, axis=0)

    row, column = iota((size, size), 0) // side, iota((size, size), 1) // side
    turn = mask(iota((side, side), 1) == 2 * (iota((side, side), 0) % tall) + iota((side, side), 0) // tall)
    bases = spread(dot(dot(turn, out_basis).astype(bf16), turn, ((1,), (1,))))
    outer = jnp.where(row == column, bases, 0.0).astype(bf16)
    bases = spread(in_basis.astype(f32))
    enter = jnp.where(row == 2 * (column % 2) + column // 2, bases, 0.0).astype(bf16)
    inner = jnp.where(row == column, bases, 0.0).astype(bf16)
    turned = swap(eigen)
    factor = 1.0 / (jnp.concatenate([half(eigen, turned), half(turned, eigen)], axis=0) + damping)
    return enter, outer, inner, factor


def pack(
    length_ref, query_hbm, cand_hbm, layer_hbm, out_basis_hbm, in_basis_hbm, eigen_hbm, rows_hbm, lists_hbm,
    out_ref, enter_ref, outer_ref, inner_ref, factor_ref, gather_ref, holds_ref, chosen_ref,
    query_ref, cand_ref, layer_ref, out_basis_ref, in_basis_ref, eigen_ref, rows_ref, lists_ref, wide, sems,
):
    arrivals = [
        pltpu.make_async_copy(source, target, sems.at[i])
        for i, (source, target) in enumerate(
            (
                (query_hbm, query_ref),
                (cand_hbm, cand_ref),
                (layer_hbm, layer_ref),
                (out_basis_hbm, out_basis_ref),
                (in_basis_hbm, in_basis_ref),
                (eigen_hbm, eigen_ref),
                (rows_hbm, rows_ref),
                (lists_hbm, lists_ref),
            )
        )
    ]
    for arrival in arrivals:
        arrival.start()
    modules, flat = query_ref.shape[1:]
    slots, height, _ = out_ref.shape
    tall = flat // LANES
    step = height + 1
    gather_ref[...] = gather_rows(tall)
    for arrival in arrivals[2:]:
        arrival.wait()
    one_hot = holds(layer_ref[...], modules, firsts(slots)[0])
    holds_ref[...] = holds(layer_ref[...], modules, firsts(slots)[1])
    enter_ref[...], outer_ref[...], inner_ref[...], factor_ref[...] = block_bases(
        out_basis_ref[...], in_basis_ref[...], eigen_ref[...]
    )
    lists = lists_ref[...]
    count, longest = rows_ref.shape[1], lists.shape[1]
    rows = upright(rows_ref[...].astype(f32), count)
    place = jnp.sum(jnp.where(iota((count, longest), 0) == lists, rows, 0.0), axis=0, keepdims=True)
    place = jnp.where(iota((1, longest), 1) < length_ref[0], place.astype(jnp.int32), -1)
    chosen_ref[...] = (iota((count, longest), 0) == place).astype(f32)
    r = 0
    for arrival, ref in zip(arrivals, (query_ref, cand_ref)):
        arrival.wait()
        for row in range(ref.shape[0]):
            by_slot = dot(one_hot, ref[row], ((0,), (0,)))
            for j in range(tall):
                wide[pl.ds(r * tall + j, slots, stride=step), :] = by_slot[:, j * LANES : (j + 1) * LANES]
            r += 1
    for k in range(slots):
        out_ref[k] = wide[pl.ds(k * step, height), :].astype(bf16)


def upright(row, count):
    shape = (count, row.shape[1])
    return jnp.sum(jnp.where(iota(shape, 0) == iota(shape, 1), row, 0.0), axis=1, keepdims=True)


def work(moved_ref, enter_ref, outer_ref, inner_ref, factor_ref, gather_ref, out_ref, tails):
    sources, height, _ = moved_ref.shape
    _, send, _ = out_ref.shape
    size = enter_ref.shape[0]
    side, tall = size // 4, size // SUBLANES
    per = height // tall - 1
    count = sources * per
    pairs = sources // 2
    stacks = pairs // 4
    arrive, leave = firsts(sources)
    places = [(d - leave) % sources for d in order_of(sources, arrive)]
    outer, inner, gather = outer_ref[...], inner_ref[...], gather_ref[...]
    factor = factor_ref[...]

    queries = [jnp.concatenate([moved_ref[2 * p, :tall, :], moved_ref[2 * p + 1, :tall, :]], axis=1) for p in range(pairs)]
    entered = dot(jnp.concatenate(queries, axis=0), enter_ref[...]).astype(bf16)
    columns = []
    for t in range(stacks):
        tiles = []
        for p in range(4 * t, 4 * t + 4):
            rows = entered[p * tall : (p + 1) * tall]
            tiles += [rows[:, :LANES], rows[:, LANES:]]
        columns.append(jnp.concatenate(tiles, axis=0))
    rotated = dot(outer, jnp.concatenate(columns, axis=1), ((0,), (0,)))
    tile = jnp.concatenate([jnp.concatenate([factor] * 4, axis=0)] * 2, axis=1)
    scaled = [
        (rotated[:, t * LANES : (t + 2) * LANES] * tile).astype(bf16) for t in range(0, stacks, 2)
    ]
    returned = dot(jnp.concatenate(scaled, axis=0), inner, ((1,), (1,))).astype(bf16)
    returned = jnp.concatenate([returned[t * size : (t + 1) * size] for t in range(stacks // 2)], axis=1)
    precond = dot(outer, returned).astype(bf16).astype(f32)

    homes = [None] * sources
    for p in range(pairs):
        t, u = p // 4, p % 4
        block = precond[u * side : (u + 1) * side, t * LANES : (t + 1) * LANES]
        homes[places[2 * p]], homes[places[2 * p + 1]] = unpaired(block)

    def flat(blocks):
        groups = [
            jnp.concatenate(blocks[g : g + SUBLANES], axis=0).astype(bf16) for g in range(0, len(blocks), SUBLANES)
        ]
        turned = dot(gather, jnp.concatenate(groups, axis=1))
        return jnp.concatenate(
            [
                jnp.concatenate(
                    [
                        turned[j * SUBLANES : (j + 1) * SUBLANES, g * LANES : (g + 1) * LANES]
                        for g in range(len(groups))
                    ],
                    axis=0,
                ).astype(bf16)
                for j in range(tall)
            ],
            axis=1,
        )

    cands = [
        moved_ref[(d - arrive) % sources, (1 + c) * tall : (2 + c) * tall, :]
        for d in range(sources)
        for c in range(per)
    ]
    rest = dot(flat(homes), flat(cands), ((1,), (1,)))
    wide = -(-count // LANES)
    if wide * LANES > count:
        rest = jnp.concatenate([rest, jnp.zeros((sources, wide * LANES - count), f32)], axis=1)
    tail = send - tall
    tails[...] = jnp.zeros_like(tails)
    for k in range(PIECES):
        piece = rest.astype(bf16).astype(f32)
        rest = rest - piece
        for t in range(wide):
            tails[pl.ds(k * wide + t, sources, stride=tail), :] = piece[:, t * LANES : (t + 1) * LANES]
    for k in range(sources):
        out_ref[k] = jnp.concatenate([homes[k], tails[k * tail : (k + 1) * tail, :]], axis=0).astype(bf16)


def finish(home_ref, holds_ref, chosen_ref, precond_ref, scores_ref, wide):
    slots, send, _ = home_ref.shape
    _, flat = precond_ref.shape[1:]
    count = chosen_ref.shape[0]
    tall = flat // LANES
    step = send + 1
    for k in range(slots):
        wide[pl.ds(k * step, send), :] = home_ref[k].astype(f32)
    by_slot = jnp.concatenate([wide[pl.ds(j, slots, stride=step), :].astype(bf16) for j in range(tall)], axis=1)
    precond_ref[0] = dot(holds_ref[...], by_slot).astype(bf16)
    groups = -(-count // LANES)
    parts = []
    for t in range(groups):
        pieces = [wide[pl.ds(tall + k * groups + t, slots, stride=step), :] for k in range(PIECES)]
        parts.append(jnp.sum((pieces[2] + pieces[1]) + pieces[0], axis=0, keepdims=True))
    dense = parts[0] if groups == 1 else jnp.concatenate(parts, axis=1)
    scores_ref[...] = jnp.sum(
        jnp.where(chosen_ref[...] > 0.0, upright(dense, count), 0.0), axis=0, keepdims=True
    )


SMEM = pl.BlockSpec(memory_space=pltpu.SMEM)
HBM = pl.BlockSpec(memory_space=pltpu.HBM)
VMEM = pl.BlockSpec(memory_space=pltpu.VMEM)
PARAMS = pltpu.CompilerParams(vmem_limit_bytes=40 * 1024 * 1024)


def body(
    query_grads,
    cand_grads,
    basis_out,
    basis_in,
    eigvals,
    layer_map,
    cand_rows,
    cand_lists,
    list_lengths,
):
    own, modules, flat = query_grads.shape
    per = cand_grads.shape[0]
    slots = layer_map.shape[0]
    tall = flat // LANES
    side = basis_out.shape[1]
    size = SUBLANES * tall
    count = cand_rows.shape[0]
    height = (own + per) * tall
    send = tall + -(-PIECES * -(-count // LANES) // SUBLANES) * SUBLANES

    def in_hbm(x):
        return pltpu.with_memory_space_constraint(x, pltpu.HBM)

    def swap_over(x, first):
        groups = [order_of(slots, first)]
        return lax.all_to_all(x, "shard", split_axis=0, concat_axis=0, tiled=True, axis_index_groups=groups)

    square = pltpu.VMEM((size, size), bf16)
    operands = (
        query_grads,
        cand_grads,
        layer_map.reshape(1, slots),
        basis_out.reshape(basis_out.shape[1:]),
        basis_in.reshape(basis_in.shape[1:]),
        eigvals.reshape(tall, LANES),
        cand_rows.reshape(1, count),
        cand_lists,
    )
    packed, enter, outer, inner, factor, gather, held, chosen = pl.pallas_call(
        pack,
        out_shape=(
            pltpu.VMEM((slots, height, LANES), bf16),
            square,
            square,
            square,
            pltpu.VMEM((side, LANES), f32),
            square,
            pltpu.VMEM((modules, slots), bf16),
            pltpu.VMEM((count, cand_lists.shape[1]), f32),
        ),
        in_specs=[SMEM] + [HBM] * len(operands),
        out_specs=[VMEM] * 8,
        scratch_shapes=[pltpu.VMEM(x.shape, x.dtype) for x in operands]
        + [pltpu.VMEM((slots * (height + 1), LANES), f32), pltpu.SemaphoreType.DMA((len(operands),))],
        compiler_params=PARAMS,
        name="pack",
    )(list_lengths, *(in_hbm(x) for x in operands))
    moved = swap_over(packed, firsts(slots)[0])
    homes = pl.pallas_call(
        work,
        out_shape=jax.ShapeDtypeStruct((slots, send, LANES), bf16),
        in_specs=[VMEM] * 6,
        out_specs=VMEM,
        scratch_shapes=[pltpu.VMEM((slots * (send - tall), LANES), f32)],
        compiler_params=PARAMS,
        name="work",
    )(moved, enter, outer, inner, factor, gather)
    home = swap_over(homes, firsts(slots)[1])
    return pl.pallas_call(
        finish,
        out_shape=(
            jax.ShapeDtypeStruct(query_grads.shape, bf16),
            jax.ShapeDtypeStruct(cand_lists.shape, f32),
        ),
        in_specs=[VMEM] * 3,
        out_specs=(VMEM, VMEM),
        scratch_shapes=[pltpu.VMEM((slots * (send + 1), LANES), f32)],
        compiler_params=PARAMS,
        name="finish",
    )(home, held, chosen)


def solution(mesh):
    return jax.shard_map(
        body,
        mesh=mesh,
        in_specs=(
            P(("groups", "shard"), None, None),
            P(("groups", "shard"), None, None),
            P("shard", None, None),
            P("shard", None, None),
            P("shard", None),
            P(),
            P("groups"),
            P(("groups", "shard"), None),
            P(("groups", "shard")),
        ),
        out_specs=(P(("groups", "shard"), None, None), P(("groups", "shard"), None)),
        check_vma=False,
    )
```

```python
import jax
import jax.numpy as jnp
from jax import lax
from jax.experimental import pallas as pl
from jax.experimental.pallas import tpu as pltpu
from jax.sharding import PartitionSpec as P

damping = 0.1
LANES = 128
SUBLANES = 8
PIECES = 3
f32, bf16 = jnp.float32, jnp.bfloat16


def iota(shape, axis):
    return lax.broadcasted_iota(jnp.int32, shape, axis)


def dot(a, b, dims=((1,), (0,))):
    return lax.dot_general(a, b, (dims, ((), ())), preferred_element_type=f32)


def mask(condition):
    return condition.astype(f32).astype(bf16)


def order_of(slots, first):
    return [(first - k) % slots for k in range(slots)]


def firsts(slots):
    return slots * 5 // 8, slots * 5 // 8


def gather_rows(tall):
    size = SUBLANES * tall
    row = iota((size, size), 0)
    return mask(row // SUBLANES + tall * (row % SUBLANES) == iota((size, size), 1))


def half(left, right):
    return jnp.where(iota(left.shape, 1) < LANES // 2, left, right)


def swap(block):
    return pltpu.roll(block, LANES // 2, 1)


def unpaired(block):
    tall = block.shape[0] // 2
    top, low = block[:tall], block[tall:]
    return half(top, swap(low)), half(swap(top), low)


def holds(layer_row, modules, first):
    slots = layer_row.shape[1]
    placed = mask(iota((slots, slots), 0) == (first + slots - iota((slots, slots), 1)) % slots)
    return dot(mask(iota((modules, slots), 0) == layer_row), placed).astype(bf16)


def block_bases(out_basis, in_basis, eigen):
    side = out_basis.shape[0]
    tall = side // 2
    size = 4 * side

    def spread(basis):
        wide = jnp.concatenate([basis] * 4, axis=1)
        return jnp.concatenate([wide] * 4, axis=0)

    row, column = iota((size, size), 0) // side, iota((size, size), 1) // side
    turn = mask(iota((side, side), 1) == 2 * (iota((side, side), 0) % tall) + iota((side, side), 0) // tall)
    bases = spread(dot(dot(turn, out_basis).astype(bf16), turn, ((1,), (1,))))
    outer = jnp.where(row == column, bases, 0.0).astype(bf16)
    bases = spread(in_basis.astype(f32))
    enter = jnp.where(row == 2 * (column % 2) + column // 2, bases, 0.0).astype(bf16)
    inner = jnp.where(row == column, bases, 0.0).astype(bf16)
    turned = swap(eigen)
    factor = 1.0 / (jnp.concatenate([half(eigen, turned), half(turned, eigen)], axis=0) + damping)
    return enter, outer, inner, factor


def pack(
    length_ref, query_hbm, cand_hbm, layer_hbm, out_basis_hbm, in_basis_hbm, eigen_hbm, rows_hbm, lists_hbm,
    out_ref, enter_ref, outer_ref, inner_ref, factor_ref, gather_ref, holds_ref, chosen_ref,
    query_ref, cand_ref, layer_ref, out_basis_ref, in_basis_ref, eigen_ref, rows_ref, lists_ref, wide, sems,
):
    arrivals = [
        pltpu.make_async_copy(source, target, sems.at[i])
        for i, (source, target) in enumerate(
            (
                (query_hbm, query_ref),
                (cand_hbm, cand_ref),
                (layer_hbm, layer_ref),
                (out_basis_hbm, out_basis_ref),
                (in_basis_hbm, in_basis_ref),
                (eigen_hbm, eigen_ref),
                (rows_hbm, rows_ref),
                (lists_hbm, lists_ref),
            )
        )
    ]
    for arrival in arrivals:
        arrival.start()
    modules, flat = query_ref.shape[1:]
    slots, height, _ = out_ref.shape
    tall = flat // LANES
    step = height + 1
    gather_ref[...] = gather_rows(tall)
    for arrival in arrivals[2:]:
        arrival.wait()
    one_hot = holds(layer_ref[...], modules, firsts(slots)[0])
    holds_ref[...] = holds(layer_ref[...], modules, firsts(slots)[1])
    enter_ref[...], outer_ref[...], inner_ref[...], factor_ref[...] = block_bases(
        out_basis_ref[...], in_basis_ref[...], eigen_ref[...]
    )
    lists = lists_ref[...]
    count, longest = rows_ref.shape[1], lists.shape[1]
    rows = upright(rows_ref[...].astype(f32), count)
    place = jnp.sum(jnp.where(iota((count, longest), 0) == lists, rows, 0.0), axis=0, keepdims=True)
    place = jnp.where(iota((1, longest), 1) < length_ref[0], place.astype(jnp.int32), -1)
    chosen_ref[...] = (iota((count, longest), 0) == place).astype(f32)
    r = 0
    for arrival, ref in zip(arrivals, (query_ref, cand_ref)):
        arrival.wait()
        for row in range(ref.shape[0]):
            by_slot = dot(one_hot, ref[row], ((0,), (0,)))
            for j in range(tall):
                wide[pl.ds(r * tall + j, slots, stride=step), :] = by_slot[:, j * LANES : (j + 1) * LANES]
            r += 1
    for k in range(slots):
        out_ref[k] = wide[pl.ds(k * step, height), :].astype(bf16)


def upright(row, count):
    shape = (count, row.shape[1])
    return jnp.sum(jnp.where(iota(shape, 0) == iota(shape, 1), row, 0.0), axis=1, keepdims=True)


def work(moved_ref, enter_ref, outer_ref, inner_ref, factor_ref, gather_ref, out_ref, tails):
    sources, height, _ = moved_ref.shape
    _, send, _ = out_ref.shape
    size = enter_ref.shape[0]
    side, tall = size // 4, size // SUBLANES
    per = height // tall - 1
    count = sources * per
    pairs = sources // 2
    stacks = pairs // 4
    arrive, leave = firsts(sources)
    order = order_of(sources, arrive)
    places = [order_of(sources, leave).index(d) for d in order]
    outer, inner, gather = outer_ref[...], inner_ref[...], gather_ref[...]
    factor = factor_ref[...]

    queries = [jnp.concatenate([moved_ref[2 * p, :tall, :], moved_ref[2 * p + 1, :tall, :]], axis=1) for p in range(pairs)]
    entered = dot(jnp.concatenate(queries, axis=0), enter_ref[...]).astype(bf16)
    columns = []
    for t in range(stacks):
        tiles = []
        for p in range(4 * t, 4 * t + 4):
            rows = entered[p * tall : (p + 1) * tall]
            tiles += [rows[:, :LANES], rows[:, LANES:]]
        columns.append(jnp.concatenate(tiles, axis=0))
    rotated = dot(outer, jnp.concatenate(columns, axis=1), ((0,), (0,)))
    tile = jnp.concatenate([jnp.concatenate([factor] * 4, axis=0)] * 2, axis=1)
    scaled = [
        (rotated[:, t * LANES : (t + 2) * LANES] * tile).astype(bf16) for t in range(0, stacks, 2)
    ]
    returned = dot(jnp.concatenate(scaled, axis=0), inner, ((1,), (1,))).astype(bf16)
    returned = jnp.concatenate([returned[t * size : (t + 1) * size] for t in range(stacks // 2)], axis=1)
    precond = dot(outer, returned).astype(bf16).astype(f32)

    homes = [None] * sources
    for p in range(pairs):
        t, u = p // 4, p % 4
        block = precond[u * side : (u + 1) * side, t * LANES : (t + 1) * LANES]
        homes[places[2 * p]], homes[places[2 * p + 1]] = unpaired(block)

    def flat(blocks):
        groups = [
            jnp.concatenate(blocks[g : g + SUBLANES], axis=0).astype(bf16) for g in range(0, len(blocks), SUBLANES)
        ]
        turned = dot(gather, jnp.concatenate(groups, axis=1))
        return jnp.concatenate(
            [
                jnp.concatenate(
                    [
                        turned[j * SUBLANES : (j + 1) * SUBLANES, g * LANES : (g + 1) * LANES]
                        for g in range(len(groups))
                    ],
                    axis=0,
                ).astype(bf16)
                for j in range(tall)
            ],
            axis=1,
        )

    cands = [
        moved_ref[order.index(d), (1 + c) * tall : (2 + c) * tall, :]
        for d in range(sources)
        for c in range(per)
    ]
    rest = dot(flat(homes), flat(cands), ((1,), (1,)))
    wide = -(-count // LANES)
    if wide * LANES > count:
        rest = jnp.concatenate([rest, jnp.zeros((sources, wide * LANES - count), f32)], axis=1)
    tail = send - tall
    tails[...] = jnp.zeros_like(tails)
    for k in range(PIECES):
        piece = rest.astype(bf16).astype(f32)
        rest = rest - piece
        for t in range(wide):
            tails[pl.ds(k * wide + t, sources, stride=tail), :] = piece[:, t * LANES : (t + 1) * LANES]
    for k in range(sources):
        out_ref[k] = jnp.concatenate([homes[k], tails[k * tail : (k + 1) * tail, :]], axis=0).astype(bf16)


def finish(home_ref, holds_ref, chosen_ref, precond_ref, scores_ref, wide):
    slots, send, _ = home_ref.shape
    _, flat = precond_ref.shape[1:]
    count = chosen_ref.shape[0]
    tall = flat // LANES
    step = send + 1
    for k in range(slots):
        wide[pl.ds(k * step, send), :] = home_ref[k].astype(f32)
    by_slot = jnp.concatenate([wide[pl.ds(j, slots, stride=step), :].astype(bf16) for j in range(tall)], axis=1)
    precond_ref[0] = dot(holds_ref[...], by_slot).astype(bf16)
    groups = -(-count // LANES)
    parts = []
    for t in range(groups):
        pieces = [wide[pl.ds(tall + k * groups + t, slots, stride=step), :] for k in range(PIECES)]
        parts.append(jnp.sum((pieces[2] + pieces[1]) + pieces[0], axis=0, keepdims=True))
    dense = parts[0] if groups == 1 else jnp.concatenate(parts, axis=1)
    scores_ref[...] = jnp.sum(
        jnp.where(chosen_ref[...] > 0.0, upright(dense, count), 0.0), axis=0, keepdims=True
    )


SMEM = pl.BlockSpec(memory_space=pltpu.SMEM)
HBM = pl.BlockSpec(memory_space=pltpu.HBM)
VMEM = pl.BlockSpec(memory_space=pltpu.VMEM)
PARAMS = pltpu.CompilerParams(vmem_limit_bytes=40 * 1024 * 1024)


def body(
    query_grads,
    cand_grads,
    basis_out,
    basis_in,
    eigvals,
    layer_map,
    cand_rows,
    cand_lists,
    list_lengths,
):
    own, modules, flat = query_grads.shape
    per = cand_grads.shape[0]
    slots = layer_map.shape[0]
    tall = flat // LANES
    side = basis_out.shape[1]
    size = SUBLANES * tall
    count = cand_rows.shape[0]
    height = (own + per) * tall
    send = tall + -(-PIECES * -(-count // LANES) // SUBLANES) * SUBLANES

    def in_hbm(x):
        return pltpu.with_memory_space_constraint(x, pltpu.HBM)

    def swap_over(x, first):
        groups = [order_of(slots, first)]
        return lax.all_to_all(x, "shard", split_axis=0, concat_axis=0, tiled=True, axis_index_groups=groups)

    square = pltpu.VMEM((size, size), bf16)
    operands = (
        query_grads,
        cand_grads,
        layer_map.reshape(1, slots),
        basis_out.reshape(basis_out.shape[1:]),
        basis_in.reshape(basis_in.shape[1:]),
        eigvals.reshape(tall, LANES),
        cand_rows.reshape(1, count),
        cand_lists,
    )
    packed, enter, outer, inner, factor, gather, held, chosen = pl.pallas_call(
        pack,
        out_shape=(
            pltpu.VMEM((slots, height, LANES), bf16),
            square,
            square,
            square,
            pltpu.VMEM((side, LANES), f32),
            square,
            pltpu.VMEM((modules, slots), bf16),
            pltpu.VMEM((count, cand_lists.shape[1]), f32),
        ),
        in_specs=[SMEM] + [HBM] * len(operands),
        out_specs=[VMEM] * 8,
        scratch_shapes=[pltpu.VMEM(x.shape, x.dtype) for x in operands]
        + [pltpu.VMEM((slots * (height + 1), LANES), f32), pltpu.SemaphoreType.DMA((len(operands),))],
        compiler_params=PARAMS,
        name="pack",
    )(list_lengths, *(in_hbm(x) for x in operands))
    moved = swap_over(packed, firsts(slots)[0])
    homes = pl.pallas_call(
        work,
        out_shape=jax.ShapeDtypeStruct((slots, send, LANES), bf16),
        in_specs=[VMEM] * 6,
        out_specs=VMEM,
        scratch_shapes=[pltpu.VMEM((slots * (send - tall), LANES), f32)],
        compiler_params=PARAMS,
        name="work",
    )(moved, enter, outer, inner, factor, gather)
    home = swap_over(homes, firsts(slots)[1])
    return pl.pallas_call(
        finish,
        out_shape=(
            jax.ShapeDtypeStruct(query_grads.shape, bf16),
            jax.ShapeDtypeStruct(cand_lists.shape, f32),
        ),
        in_specs=[VMEM] * 3,
        out_specs=(VMEM, VMEM),
        scratch_shapes=[pltpu.VMEM((slots * (send + 1), LANES), f32)],
        compiler_params=PARAMS,
        name="finish",
    )(home, held, chosen)


def solution(mesh):
    return jax.shard_map(
        body,
        mesh=mesh,
        in_specs=(
            P(("groups", "shard"), None, None),
            P(("groups", "shard"), None, None),
            P("shard", None, None),
            P("shard", None, None),
            P("shard", None),
            P(),
            P("groups"),
            P(("groups", "shard"), None),
            P(("groups", "shard")),
        ),
        out_specs=(P(("groups", "shard"), None, None), P(("groups", "shard"), None)),
        check_vma=False,
    )
```

```python
import jax
import jax.numpy as jnp
from jax import lax
from jax.experimental import pallas as pl
from jax.experimental.pallas import tpu as pltpu
from jax.sharding import PartitionSpec as P

damping = 0.1
LANES = 128
SUBLANES = 8
PIECES = 3
f32, bf16 = jnp.float32, jnp.bfloat16


def iota(shape, axis):
    return lax.broadcasted_iota(jnp.int32, shape, axis)


def dot(a, b, dims=((1,), (0,))):
    return lax.dot_general(a, b, (dims, ((), ())), preferred_element_type=f32)


def mask(condition):
    return condition.astype(f32).astype(bf16)


def order_of(slots, first):
    return [(first - k) % slots for k in range(slots)]


def firsts(slots):
    return slots * 5 // 8, slots // 2


def gather_rows(tall):
    size = SUBLANES * tall
    row = iota((size, size), 0)
    return mask(row // SUBLANES + tall * (row % SUBLANES) == iota((size, size), 1))


def half(left, right):
    return jnp.where(iota(left.shape, 1) < LANES // 2, left, right)


def swap(block):
    return pltpu.roll(block, LANES // 2, 1)


def unpaired(block):
    tall = block.shape[0] // 2
    top, low = block[:tall], block[tall:]
    return half(top, swap(low)), half(swap(top), low)


def holds(layer_row, modules, first):
    slots = layer_row.shape[1]
    placed = mask(iota((slots, slots), 0) == (first + slots - iota((slots, slots), 1)) % slots)
    return dot(mask(iota((modules, slots), 0) == layer_row), placed).astype(bf16)


def block_bases(out_basis, in_basis, eigen):
    side = out_basis.shape[0]
    tall = side // 2
    size = 4 * side

    def spread(basis):
        wide = jnp.concatenate([basis] * 4, axis=1)
        return jnp.concatenate([wide] * 4, axis=0)

    row, column = iota((size, size), 0) // side, iota((size, size), 1) // side
    turn = mask(iota((side, side), 1) == 2 * (iota((side, side), 0) % tall) + iota((side, side), 0) // tall)
    bases = spread(dot(dot(turn, out_basis).astype(bf16), turn, ((1,), (1,))))
    outer = jnp.where(row == column, bases, 0.0).astype(bf16)
    bases = spread(in_basis.astype(f32))
    enter = jnp.where(row == 2 * (column % 2) + column // 2, bases, 0.0).astype(bf16)
    inner = jnp.where(row == column, bases, 0.0).astype(bf16)
    turned = swap(eigen)
    factor = 1.0 / (jnp.concatenate([half(eigen, turned), half(turned, eigen)], axis=0) + damping)
    return enter, outer, inner, factor


def pack(
    length_ref, query_hbm, cand_hbm, layer_hbm, out_basis_hbm, in_basis_hbm, eigen_hbm, rows_hbm, lists_hbm,
    out_ref, enter_ref, outer_ref, inner_ref, factor_ref, gather_ref, holds_ref, chosen_ref,
    query_ref, cand_ref, layer_ref, out_basis_ref, in_basis_ref, eigen_ref, rows_ref, lists_ref, wide, sems,
):
    arrivals = [
        pltpu.make_async_copy(source, target, sems.at[i])
        for i, (source, target) in enumerate(
            (
                (query_hbm, query_ref),
                (cand_hbm, cand_ref),
                (layer_hbm, layer_ref),
                (out_basis_hbm, out_basis_ref),
                (in_basis_hbm, in_basis_ref),
                (eigen_hbm, eigen_ref),
                (rows_hbm, rows_ref),
                (lists_hbm, lists_ref),
            )
        )
    ]
    for arrival in arrivals:
        arrival.start()
    modules, flat = query_ref.shape[1:]
    slots, height, _ = out_ref.shape
    tall = flat // LANES
    step = height + 1
    gather_ref[...] = gather_rows(tall)
    for arrival in arrivals[2:]:
        arrival.wait()
    one_hot = holds(layer_ref[...], modules, firsts(slots)[0])
    holds_ref[...] = holds(layer_ref[...], modules, firsts(slots)[1])
    enter_ref[...], outer_ref[...], inner_ref[...], factor_ref[...] = block_bases(
        out_basis_ref[...], in_basis_ref[...], eigen_ref[...]
    )
    lists = lists_ref[...]
    count, longest = rows_ref.shape[1], lists.shape[1]
    rows = upright(rows_ref[...].astype(f32), count)
    place = jnp.sum(jnp.where(iota((count, longest), 0) == lists, rows, 0.0), axis=0, keepdims=True)
    place = jnp.where(iota((1, longest), 1) < length_ref[0], place.astype(jnp.int32), -1)
    chosen_ref[...] = (iota((count, longest), 0) == place).astype(f32)
    r = 0
    for arrival, ref in zip(arrivals, (query_ref, cand_ref)):
        arrival.wait()
        for row in range(ref.shape[0]):
            by_slot = dot(one_hot, ref[row], ((0,), (0,)))
            for j in range(tall):
                wide[pl.ds(r * tall + j, slots, stride=step), :] = by_slot[:, j * LANES : (j + 1) * LANES]
            r += 1
    for k in range(slots):
        out_ref[k] = wide[pl.ds(k * step, height), :].astype(bf16)


def upright(row, count):
    shape = (count, row.shape[1])
    return jnp.sum(jnp.where(iota(shape, 0) == iota(shape, 1), row, 0.0), axis=1, keepdims=True)


def work(moved_ref, enter_ref, outer_ref, inner_ref, factor_ref, gather_ref, out_ref, tails):
    sources, height, _ = moved_ref.shape
    _, send, _ = out_ref.shape
    size = enter_ref.shape[0]
    side, tall = size // 4, size // SUBLANES
    per = height // tall - 1
    count = sources * per
    pairs = sources // 2
    stacks = pairs // 4
    arrive, leave = firsts(sources)
    order = order_of(sources, arrive)
    places = [order_of(sources, leave).index(d) for d in order]
    outer, inner, gather = outer_ref[...], inner_ref[...], gather_ref[...]
    factor = factor_ref[...]

    queries = [jnp.concatenate([moved_ref[2 * p, :tall, :], moved_ref[2 * p + 1, :tall, :]], axis=1) for p in range(pairs)]
    entered = dot(jnp.concatenate(queries, axis=0), enter_ref[...]).astype(bf16)
    columns = []
    for t in range(stacks):
        tiles = []
        for p in range(4 * t, 4 * t + 4):
            rows = entered[p * tall : (p + 1) * tall]
            tiles += [rows[:, :LANES], rows[:, LANES:]]
        columns.append(jnp.concatenate(tiles, axis=0))
    rotated = dot(outer, jnp.concatenate(columns, axis=1), ((0,), (0,)))
    tile = jnp.concatenate([jnp.concatenate([factor] * 4, axis=0)] * 2, axis=1)
    scaled = [
        (rotated[:, t * LANES : (t + 2) * LANES] * tile).astype(bf16) for t in range(0, stacks, 2)
    ]
    returned = dot(jnp.concatenate(scaled, axis=0), inner, ((1,), (1,))).astype(bf16)
    returned = jnp.concatenate([returned[t * size : (t + 1) * size] for t in range(stacks // 2)], axis=1)
    precond = dot(outer, returned).astype(bf16).astype(f32)

    homes = [None] * sources
    for p in range(pairs):
        t, u = p // 4, p % 4
        block = precond[u * side : (u + 1) * side, t * LANES : (t + 1) * LANES]
        homes[places[2 * p]], homes[places[2 * p + 1]] = unpaired(block)

    def flat(blocks):
        groups = [
            jnp.concatenate(blocks[g : g + SUBLANES], axis=0).astype(bf16) for g in range(0, len(blocks), SUBLANES)
        ]
        turned = dot(gather, jnp.concatenate(groups, axis=1))
        return jnp.concatenate(
            [
                jnp.concatenate(
                    [
                        turned[j * SUBLANES : (j + 1) * SUBLANES, g * LANES : (g + 1) * LANES]
                        for g in range(len(groups))
                    ],
                    axis=0,
                ).astype(bf16)
                for j in range(tall)
            ],
            axis=1,
        )

    cands = [
        moved_ref[order.index(d), (1 + c) * tall : (2 + c) * tall, :]
        for d in range(sources)
        for c in range(per)
    ]
    rest = dot(flat(homes), flat(cands), ((1,), (1,)))
    wide = -(-count // LANES)
    if wide * LANES > count:
        rest = jnp.concatenate([rest, jnp.zeros((sources, wide * LANES - count), f32)], axis=1)
    tail = send - tall
    tails[...] = jnp.zeros_like(tails)
    for k in range(PIECES):
        piece = rest.astype(bf16).astype(f32)
        rest = rest - piece
        for t in range(wide):
            tails[pl.ds(k * wide + t, sources, stride=tail), :] = piece[:, t * LANES : (t + 1) * LANES]
    for k in range(sources):
        out_ref[k] = jnp.concatenate([homes[k], tails[k * tail : (k + 1) * tail, :]], axis=0).astype(bf16)


def finish(home_ref, holds_ref, chosen_ref, precond_ref, scores_ref, wide):
    slots, send, _ = home_ref.shape
    _, flat = precond_ref.shape[1:]
    count = chosen_ref.shape[0]
    tall = flat // LANES
    step = send + 1
    for k in range(slots):
        wide[pl.ds(k * step, send), :] = home_ref[k].astype(f32)
    by_slot = jnp.concatenate([wide[pl.ds(j, slots, stride=step), :].astype(bf16) for j in range(tall)], axis=1)
    precond_ref[0] = dot(holds_ref[...], by_slot).astype(bf16)
    groups = -(-count // LANES)
    parts = []
    for t in range(groups):
        pieces = [wide[pl.ds(tall + k * groups + t, slots, stride=step), :] for k in range(PIECES)]
        parts.append(jnp.sum((pieces[2] + pieces[1]) + pieces[0], axis=0, keepdims=True))
    dense = parts[0] if groups == 1 else jnp.concatenate(parts, axis=1)
    scores_ref[...] = jnp.sum(
        jnp.where(chosen_ref[...] > 0.0, upright(dense, count), 0.0), axis=0, keepdims=True
    )


SMEM = pl.BlockSpec(memory_space=pltpu.SMEM)
HBM = pl.BlockSpec(memory_space=pltpu.HBM)
VMEM = pl.BlockSpec(memory_space=pltpu.VMEM)
PARAMS = pltpu.CompilerParams(vmem_limit_bytes=40 * 1024 * 1024)


def body(
    query_grads,
    cand_grads,
    basis_out,
    basis_in,
    eigvals,
    layer_map,
    cand_rows,
    cand_lists,
    list_lengths,
):
    own, modules, flat = query_grads.shape
    per = cand_grads.shape[0]
    slots = layer_map.shape[0]
    tall = flat // LANES
    side = basis_out.shape[1]
    size = SUBLANES * tall
    count = cand_rows.shape[0]
    height = (own + per) * tall
    send = tall + -(-PIECES * -(-count // LANES) // SUBLANES) * SUBLANES

    def in_hbm(x):
        return pltpu.with_memory_space_constraint(x, pltpu.HBM)

    def swap_over(x, first):
        groups = [order_of(slots, first)]
        return lax.all_to_all(x, "shard", split_axis=0, concat_axis=0, tiled=True, axis_index_groups=groups)

    square = pltpu.VMEM((size, size), bf16)
    operands = (
        query_grads,
        cand_grads,
        layer_map.reshape(1, slots),
        basis_out.reshape(basis_out.shape[1:]),
        basis_in.reshape(basis_in.shape[1:]),
        eigvals.reshape(tall, LANES),
        cand_rows.reshape(1, count),
        cand_lists,
    )
    packed, enter, outer, inner, factor, gather, held, chosen = pl.pallas_call(
        pack,
        out_shape=(
            pltpu.VMEM((slots, height, LANES), bf16),
            square,
            square,
            square,
            pltpu.VMEM((side, LANES), f32),
            square,
            pltpu.VMEM((modules, slots), bf16),
            pltpu.VMEM((count, cand_lists.shape[1]), f32),
        ),
        in_specs=[SMEM] + [HBM] * len(operands),
        out_specs=[VMEM] * 8,
        scratch_shapes=[pltpu.VMEM(x.shape, x.dtype) for x in operands]
        + [pltpu.VMEM((slots * (height + 1), LANES), f32), pltpu.SemaphoreType.DMA((len(operands),))],
        compiler_params=PARAMS,
        name="pack",
    )(list_lengths, *(in_hbm(x) for x in operands))
    moved = swap_over(packed, firsts(slots)[0])
    homes = pl.pallas_call(
        work,
        out_shape=jax.ShapeDtypeStruct((slots, send, LANES), bf16),
        in_specs=[VMEM] * 6,
        out_specs=VMEM,
        scratch_shapes=[pltpu.VMEM((slots * (send - tall), LANES), f32)],
        compiler_params=PARAMS,
        name="work",
    )(moved, enter, outer, inner, factor, gather)
    home = swap_over(homes, firsts(slots)[1])
    return pl.pallas_call(
        finish,
        out_shape=(
            jax.ShapeDtypeStruct(query_grads.shape, bf16),
            jax.ShapeDtypeStruct(cand_lists.shape, f32),
        ),
        in_specs=[VMEM] * 3,
        out_specs=(VMEM, VMEM),
        scratch_shapes=[pltpu.VMEM((slots * (send + 1), LANES), f32)],
        compiler_params=PARAMS,
        name="finish",
    )(home, held, chosen)


def solution(mesh):
    return jax.shard_map(
        body,
        mesh=mesh,
        in_specs=(
            P(("groups", "shard"), None, None),
            P(("groups", "shard"), None, None),
            P("shard", None, None),
            P("shard", None, None),
            P("shard", None),
            P(),
            P("groups"),
            P(("groups", "shard"), None),
            P(("groups", "shard")),
        ),
        out_specs=(P(("groups", "shard"), None, None), P(("groups", "shard"), None)),
        check_vma=False,
    )
```

```python
import jax
import jax.numpy as jnp
from jax import lax
from jax.experimental import pallas as pl
from jax.experimental.pallas import tpu as pltpu
from jax.sharding import PartitionSpec as P

damping = 0.1
LANES = 128
SUBLANES = 8
PIECES = 3
f32, bf16 = jnp.float32, jnp.bfloat16


def iota(shape, axis):
    return lax.broadcasted_iota(jnp.int32, shape, axis)


def dot(a, b, dims=((1,), (0,))):
    return lax.dot_general(a, b, (dims, ((), ())), preferred_element_type=f32)


def mask(condition):
    return condition.astype(f32).astype(bf16)


def ring(place, slots):
    core, middle = place % 2, slots // 2
    up = 4 * (place // 2) + core
    down = 2 * (middle - 1 - 2 * ((place - middle) // 2)) + core
    if isinstance(place, int):
        return up if place < middle else down
    return jnp.where(place < middle, up, down)


def order_of(slots, first):
    start = [ring(k, slots) for k in range(slots)].index(first)
    return [ring((start + k) % slots, slots) for k in range(slots)]


def firsts(slots):
    return slots * 5 // 8, slots * 5 // 8


def gather_rows(tall):
    size = SUBLANES * tall
    row = iota((size, size), 0)
    return mask(row // SUBLANES + tall * (row % SUBLANES) == iota((size, size), 1))


def half(left, right):
    return jnp.where(iota(left.shape, 1) < LANES // 2, left, right)


def swap(block):
    return pltpu.roll(block, LANES // 2, 1)


def unpaired(block):
    tall = block.shape[0] // 2
    top, low = block[:tall], block[tall:]
    return half(top, swap(low)), half(swap(top), low)


def holds(layer_row, modules, first):
    slots = layer_row.shape[1]
    start = [ring(k, slots) for k in range(slots)].index(first)
    placed = mask(iota((slots, slots), 0) == ring((start + iota((slots, slots), 1)) % slots, slots))
    return dot(mask(iota((modules, slots), 0) == layer_row), placed).astype(bf16)


def block_bases(out_basis, in_basis, eigen):
    side = out_basis.shape[0]
    tall = side // 2
    size = 4 * side

    def spread(basis):
        wide = jnp.concatenate([basis] * 4, axis=1)
        return jnp.concatenate([wide] * 4, axis=0)

    row, column = iota((size, size), 0) // side, iota((size, size), 1) // side
    turn = mask(iota((side, side), 1) == 2 * (iota((side, side), 0) % tall) + iota((side, side), 0) // tall)
    bases = spread(dot(dot(turn, out_basis).astype(bf16), turn, ((1,), (1,))))
    outer = jnp.where(row == column, bases, 0.0).astype(bf16)
    bases = spread(in_basis.astype(f32))
    enter = jnp.where(row == 2 * (column % 2) + column // 2, bases, 0.0).astype(bf16)
    inner = jnp.where(row == column, bases, 0.0).astype(bf16)
    turned = swap(eigen)
    factor = 1.0 / (jnp.concatenate([half(eigen, turned), half(turned, eigen)], axis=0) + damping)
    return enter, outer, inner, factor


def pack(
    length_ref, query_hbm, cand_hbm, layer_hbm, out_basis_hbm, in_basis_hbm, eigen_hbm, rows_hbm, lists_hbm,
    out_ref, enter_ref, outer_ref, inner_ref, factor_ref, gather_ref, holds_ref, chosen_ref,
    query_ref, cand_ref, layer_ref, out_basis_ref, in_basis_ref, eigen_ref, rows_ref, lists_ref, wide, sems,
):
    arrivals = [
        pltpu.make_async_copy(source, target, sems.at[i])
        for i, (source, target) in enumerate(
            (
                (query_hbm, query_ref),
                (cand_hbm, cand_ref),
                (layer_hbm, layer_ref),
                (out_basis_hbm, out_basis_ref),
                (in_basis_hbm, in_basis_ref),
                (eigen_hbm, eigen_ref),
                (rows_hbm, rows_ref),
                (lists_hbm, lists_ref),
            )
        )
    ]
    for arrival in arrivals:
        arrival.start()
    modules, flat = query_ref.shape[1:]
    slots, height, _ = out_ref.shape
    tall = flat // LANES
    step = height + 1
    gather_ref[...] = gather_rows(tall)
    for arrival in arrivals[2:]:
        arrival.wait()
    one_hot = holds(layer_ref[...], modules, firsts(slots)[0])
    holds_ref[...] = holds(layer_ref[...], modules, firsts(slots)[1])
    enter_ref[...], outer_ref[...], inner_ref[...], factor_ref[...] = block_bases(
        out_basis_ref[...], in_basis_ref[...], eigen_ref[...]
    )
    lists = lists_ref[...]
    count, longest = rows_ref.shape[1], lists.shape[1]
    rows = upright(rows_ref[...].astype(f32), count)
    place = jnp.sum(jnp.where(iota((count, longest), 0) == lists, rows, 0.0), axis=0, keepdims=True)
    place = jnp.where(iota((1, longest), 1) < length_ref[0], place.astype(jnp.int32), -1)
    chosen_ref[...] = (iota((count, longest), 0) == place).astype(f32)
    r = 0
    for arrival, ref in zip(arrivals, (query_ref, cand_ref)):
        arrival.wait()
        for row in range(ref.shape[0]):
            by_slot = dot(one_hot, ref[row], ((0,), (0,)))
            for j in range(tall):
                wide[pl.ds(r * tall + j, slots, stride=step), :] = by_slot[:, j * LANES : (j + 1) * LANES]
            r += 1
    for k in range(slots):
        out_ref[k] = wide[pl.ds(k * step, height), :].astype(bf16)


def upright(row, count):
    shape = (count, row.shape[1])
    return jnp.sum(jnp.where(iota(shape, 0) == iota(shape, 1), row, 0.0), axis=1, keepdims=True)


def work(moved_ref, enter_ref, outer_ref, inner_ref, factor_ref, gather_ref, out_ref, tails):
    sources, height, _ = moved_ref.shape
    _, send, _ = out_ref.shape
    size = enter_ref.shape[0]
    side, tall = size // 4, size // SUBLANES
    per = height // tall - 1
    count = sources * per
    pairs = sources // 2
    stacks = pairs // 4
    arrive, leave = firsts(sources)
    order = order_of(sources, arrive)
    places = [order_of(sources, leave).index(d) for d in order]
    outer, inner, gather = outer_ref[...], inner_ref[...], gather_ref[...]
    factor = factor_ref[...]

    queries = [jnp.concatenate([moved_ref[2 * p, :tall, :], moved_ref[2 * p + 1, :tall, :]], axis=1) for p in range(pairs)]
    entered = dot(jnp.concatenate(queries, axis=0), enter_ref[...]).astype(bf16)
    columns = []
    for t in range(stacks):
        tiles = []
        for p in range(4 * t, 4 * t + 4):
            rows = entered[p * tall : (p + 1) * tall]
            tiles += [rows[:, :LANES], rows[:, LANES:]]
        columns.append(jnp.concatenate(tiles, axis=0))
    rotated = dot(outer, jnp.concatenate(columns, axis=1), ((0,), (0,)))
    tile = jnp.concatenate([jnp.concatenate([factor] * 4, axis=0)] * 2, axis=1)
    scaled = [
        (rotated[:, t * LANES : (t + 2) * LANES] * tile).astype(bf16) for t in range(0, stacks, 2)
    ]
    returned = dot(jnp.concatenate(scaled, axis=0), inner, ((1,), (1,))).astype(bf16)
    returned = jnp.concatenate([returned[t * size : (t + 1) * size] for t in range(stacks // 2)], axis=1)
    precond = dot(outer, returned).astype(bf16).astype(f32)

    homes = [None] * sources
    for p in range(pairs):
        t, u = p // 4, p % 4
        block = precond[u * side : (u + 1) * side, t * LANES : (t + 1) * LANES]
        homes[places[2 * p]], homes[places[2 * p + 1]] = unpaired(block)

    def flat(blocks):
        groups = [
            jnp.concatenate(blocks[g : g + SUBLANES], axis=0).astype(bf16) for g in range(0, len(blocks), SUBLANES)
        ]
        turned = dot(gather, jnp.concatenate(groups, axis=1))
        return jnp.concatenate(
            [
                jnp.concatenate(
                    [
                        turned[j * SUBLANES : (j + 1) * SUBLANES, g * LANES : (g + 1) * LANES]
                        for g in range(len(groups))
                    ],
                    axis=0,
                ).astype(bf16)
                for j in range(tall)
            ],
            axis=1,
        )

    cands = [
        moved_ref[order.index(d), (1 + c) * tall : (2 + c) * tall, :]
        for d in range(sources)
        for c in range(per)
    ]
    rest = dot(flat(homes), flat(cands), ((1,), (1,)))
    wide = -(-count // LANES)
    if wide * LANES > count:
        rest = jnp.concatenate([rest, jnp.zeros((sources, wide * LANES - count), f32)], axis=1)
    tail = send - tall
    tails[...] = jnp.zeros_like(tails)
    for k in range(PIECES):
        piece = rest.astype(bf16).astype(f32)
        rest = rest - piece
        for t in range(wide):
            tails[pl.ds(k * wide + t, sources, stride=tail), :] = piece[:, t * LANES : (t + 1) * LANES]
    for k in range(sources):
        out_ref[k] = jnp.concatenate([homes[k], tails[k * tail : (k + 1) * tail, :]], axis=0).astype(bf16)


def finish(home_ref, holds_ref, chosen_ref, precond_ref, scores_ref, wide):
    slots, send, _ = home_ref.shape
    _, flat = precond_ref.shape[1:]
    count = chosen_ref.shape[0]
    tall = flat // LANES
    step = send + 1
    for k in range(slots):
        wide[pl.ds(k * step, send), :] = home_ref[k].astype(f32)
    by_slot = jnp.concatenate([wide[pl.ds(j, slots, stride=step), :].astype(bf16) for j in range(tall)], axis=1)
    precond_ref[0] = dot(holds_ref[...], by_slot).astype(bf16)
    groups = -(-count // LANES)
    parts = []
    for t in range(groups):
        pieces = [wide[pl.ds(tall + k * groups + t, slots, stride=step), :] for k in range(PIECES)]
        parts.append(jnp.sum((pieces[2] + pieces[1]) + pieces[0], axis=0, keepdims=True))
    dense = parts[0] if groups == 1 else jnp.concatenate(parts, axis=1)
    scores_ref[...] = jnp.sum(
        jnp.where(chosen_ref[...] > 0.0, upright(dense, count), 0.0), axis=0, keepdims=True
    )


SMEM = pl.BlockSpec(memory_space=pltpu.SMEM)
HBM = pl.BlockSpec(memory_space=pltpu.HBM)
VMEM = pl.BlockSpec(memory_space=pltpu.VMEM)
PARAMS = pltpu.CompilerParams(vmem_limit_bytes=40 * 1024 * 1024)


def body(
    query_grads,
    cand_grads,
    basis_out,
    basis_in,
    eigvals,
    layer_map,
    cand_rows,
    cand_lists,
    list_lengths,
):
    own, modules, flat = query_grads.shape
    per = cand_grads.shape[0]
    slots = layer_map.shape[0]
    tall = flat // LANES
    side = basis_out.shape[1]
    size = SUBLANES * tall
    count = cand_rows.shape[0]
    height = (own + per) * tall
    send = tall + -(-PIECES * -(-count // LANES) // SUBLANES) * SUBLANES

    def in_hbm(x):
        return pltpu.with_memory_space_constraint(x, pltpu.HBM)

    def swap_over(x, first):
        groups = [order_of(slots, first)]
        return lax.all_to_all(x, "shard", split_axis=0, concat_axis=0, tiled=True, axis_index_groups=groups)

    square = pltpu.VMEM((size, size), bf16)
    operands = (
        query_grads,
        cand_grads,
        layer_map.reshape(1, slots),
        basis_out.reshape(basis_out.shape[1:]),
        basis_in.reshape(basis_in.shape[1:]),
        eigvals.reshape(tall, LANES),
        cand_rows.reshape(1, count),
        cand_lists,
    )
    packed, enter, outer, inner, factor, gather, held, chosen = pl.pallas_call(
        pack,
        out_shape=(
            pltpu.VMEM((slots, height, LANES), bf16),
            square,
            square,
            square,
            pltpu.VMEM((side, LANES), f32),
            square,
            pltpu.VMEM((modules, slots), bf16),
            pltpu.VMEM((count, cand_lists.shape[1]), f32),
        ),
        in_specs=[SMEM] + [HBM] * len(operands),
        out_specs=[VMEM] * 8,
        scratch_shapes=[pltpu.VMEM(x.shape, x.dtype) for x in operands]
        + [pltpu.VMEM((slots * (height + 1), LANES), f32), pltpu.SemaphoreType.DMA((len(operands),))],
        compiler_params=PARAMS,
        name="pack",
    )(list_lengths, *(in_hbm(x) for x in operands))
    moved = swap_over(packed, firsts(slots)[0])
    homes = pl.pallas_call(
        work,
        out_shape=jax.ShapeDtypeStruct((slots, send, LANES), bf16),
        in_specs=[VMEM] * 6,
        out_specs=VMEM,
        scratch_shapes=[pltpu.VMEM((slots * (send - tall), LANES), f32)],
        compiler_params=PARAMS,
        name="work",
    )(moved, enter, outer, inner, factor, gather)
    home = swap_over(homes, firsts(slots)[1])
    return pl.pallas_call(
        finish,
        out_shape=(
            jax.ShapeDtypeStruct(query_grads.shape, bf16),
            jax.ShapeDtypeStruct(cand_lists.shape, f32),
        ),
        in_specs=[VMEM] * 3,
        out_specs=(VMEM, VMEM),
        scratch_shapes=[pltpu.VMEM((slots * (send + 1), LANES), f32)],
        compiler_params=PARAMS,
        name="finish",
    )(home, held, chosen)


def solution(mesh):
    return jax.shard_map(
        body,
        mesh=mesh,
        in_specs=(
            P(("groups", "shard"), None, None),
            P(("groups", "shard"), None, None),
            P("shard", None, None),
            P("shard", None, None),
            P("shard", None),
            P(),
            P("groups"),
            P(("groups", "shard"), None),
            P(("groups", "shard")),
        ),
        out_specs=(P(("groups", "shard"), None, None), P(("groups", "shard"), None)),
        check_vma=False,
    )
```

```python
import jax
import jax.numpy as jnp
from jax import lax
from jax.experimental import pallas as pl
from jax.experimental.pallas import tpu as pltpu
from jax.sharding import PartitionSpec as P

damping = 0.1
LANES = 128
SUBLANES = 8
PIECES = 3
STRIDE = 7
f32, bf16 = jnp.float32, jnp.bfloat16


def iota(shape, axis):
    return lax.broadcasted_iota(jnp.int32, shape, axis)


def dot(a, b, dims=((1,), (0,))):
    return lax.dot_general(a, b, (dims, ((), ())), preferred_element_type=f32)


def mask(condition):
    return condition.astype(f32).astype(bf16)


def ring(place, slots):
    core, middle = place % 2, slots // 2
    up = 4 * (place // 2) + core
    down = 2 * (middle - 1 - 2 * ((place - middle) // 2)) + core
    if isinstance(place, int):
        return up if place < middle else down
    return jnp.where(place < middle, up, down)


def order_of(slots, first):
    start = [ring(k, slots) for k in range(slots)].index(first)
    return [ring((start + STRIDE * k) % slots, slots) for k in range(slots)]


def firsts(slots):
    return slots * 5 // 8, slots * 5 // 8


def gather_rows(tall):
    size = SUBLANES * tall
    row = iota((size, size), 0)
    return mask(row // SUBLANES + tall * (row % SUBLANES) == iota((size, size), 1))


def half(left, right):
    return jnp.where(iota(left.shape, 1) < LANES // 2, left, right)


def swap(block):
    return pltpu.roll(block, LANES // 2, 1)


def unpaired(block):
    tall = block.shape[0] // 2
    top, low = block[:tall], block[tall:]
    return half(top, swap(low)), half(swap(top), low)


def holds(layer_row, modules, first):
    slots = layer_row.shape[1]
    start = [ring(k, slots) for k in range(slots)].index(first)
    placed = mask(iota((slots, slots), 0) == ring((start + STRIDE * iota((slots, slots), 1)) % slots, slots))
    return dot(mask(iota((modules, slots), 0) == layer_row), placed).astype(bf16)


def block_bases(out_basis, in_basis, eigen):
    side = out_basis.shape[0]
    tall = side // 2
    size = 4 * side

    def spread(basis):
        wide = jnp.concatenate([basis] * 4, axis=1)
        return jnp.concatenate([wide] * 4, axis=0)

    row, column = iota((size, size), 0) // side, iota((size, size), 1) // side
    turn = mask(iota((side, side), 1) == 2 * (iota((side, side), 0) % tall) + iota((side, side), 0) // tall)
    bases = spread(dot(dot(turn, out_basis).astype(bf16), turn, ((1,), (1,))))
    outer = jnp.where(row == column, bases, 0.0).astype(bf16)
    bases = spread(in_basis.astype(f32))
    enter = jnp.where(row == 2 * (column % 2) + column // 2, bases, 0.0).astype(bf16)
    inner = jnp.where(row == column, bases, 0.0).astype(bf16)
    turned = swap(eigen)
    factor = 1.0 / (jnp.concatenate([half(eigen, turned), half(turned, eigen)], axis=0) + damping)
    return enter, outer, inner, factor


def pack(
    length_ref, query_hbm, cand_hbm, layer_hbm, out_basis_hbm, in_basis_hbm, eigen_hbm, rows_hbm, lists_hbm,
    out_ref, enter_ref, outer_ref, inner_ref, factor_ref, gather_ref, holds_ref, chosen_ref,
    query_ref, cand_ref, layer_ref, out_basis_ref, in_basis_ref, eigen_ref, rows_ref, lists_ref, wide, sems,
):
    arrivals = [
        pltpu.make_async_copy(source, target, sems.at[i])
        for i, (source, target) in enumerate(
            (
                (query_hbm, query_ref),
                (cand_hbm, cand_ref),
                (layer_hbm, layer_ref),
                (out_basis_hbm, out_basis_ref),
                (in_basis_hbm, in_basis_ref),
                (eigen_hbm, eigen_ref),
                (rows_hbm, rows_ref),
                (lists_hbm, lists_ref),
            )
        )
    ]
    for arrival in arrivals:
        arrival.start()
    modules, flat = query_ref.shape[1:]
    slots, height, _ = out_ref.shape
    tall = flat // LANES
    step = height + 1
    gather_ref[...] = gather_rows(tall)
    for arrival in arrivals[2:]:
        arrival.wait()
    one_hot = holds(layer_ref[...], modules, firsts(slots)[0])
    holds_ref[...] = holds(layer_ref[...], modules, firsts(slots)[1])
    enter_ref[...], outer_ref[...], inner_ref[...], factor_ref[...] = block_bases(
        out_basis_ref[...], in_basis_ref[...], eigen_ref[...]
    )
    lists = lists_ref[...]
    count, longest = rows_ref.shape[1], lists.shape[1]
    rows = upright(rows_ref[...].astype(f32), count)
    place = jnp.sum(jnp.where(iota((count, longest), 0) == lists, rows, 0.0), axis=0, keepdims=True)
    place = jnp.where(iota((1, longest), 1) < length_ref[0], place.astype(jnp.int32), -1)
    chosen_ref[...] = (iota((count, longest), 0) == place).astype(f32)
    r = 0
    for arrival, ref in zip(arrivals, (query_ref, cand_ref)):
        arrival.wait()
        for row in range(ref.shape[0]):
            by_slot = dot(one_hot, ref[row], ((0,), (0,)))
            for j in range(tall):
                wide[pl.ds(r * tall + j, slots, stride=step), :] = by_slot[:, j * LANES : (j + 1) * LANES]
            r += 1
    for k in range(slots):
        out_ref[k] = wide[pl.ds(k * step, height), :].astype(bf16)


def upright(row, count):
    shape = (count, row.shape[1])
    return jnp.sum(jnp.where(iota(shape, 0) == iota(shape, 1), row, 0.0), axis=1, keepdims=True)


def work(moved_ref, enter_ref, outer_ref, inner_ref, factor_ref, gather_ref, out_ref, tails):
    sources, height, _ = moved_ref.shape
    _, send, _ = out_ref.shape
    size = enter_ref.shape[0]
    side, tall = size // 4, size // SUBLANES
    per = height // tall - 1
    count = sources * per
    pairs = sources // 2
    stacks = pairs // 4
    arrive, leave = firsts(sources)
    order = order_of(sources, arrive)
    places = [order_of(sources, leave).index(d) for d in order]
    outer, inner, gather = outer_ref[...], inner_ref[...], gather_ref[...]
    factor = factor_ref[...]

    queries = [jnp.concatenate([moved_ref[2 * p, :tall, :], moved_ref[2 * p + 1, :tall, :]], axis=1) for p in range(pairs)]
    entered = dot(jnp.concatenate(queries, axis=0), enter_ref[...]).astype(bf16)
    columns = []
    for t in range(stacks):
        tiles = []
        for p in range(4 * t, 4 * t + 4):
            rows = entered[p * tall : (p + 1) * tall]
            tiles += [rows[:, :LANES], rows[:, LANES:]]
        columns.append(jnp.concatenate(tiles, axis=0))
    rotated = dot(outer, jnp.concatenate(columns, axis=1), ((0,), (0,)))
    tile = jnp.concatenate([jnp.concatenate([factor] * 4, axis=0)] * 2, axis=1)
    scaled = [
        (rotated[:, t * LANES : (t + 2) * LANES] * tile).astype(bf16) for t in range(0, stacks, 2)
    ]
    returned = dot(jnp.concatenate(scaled, axis=0), inner, ((1,), (1,))).astype(bf16)
    returned = jnp.concatenate([returned[t * size : (t + 1) * size] for t in range(stacks // 2)], axis=1)
    precond = dot(outer, returned).astype(bf16).astype(f32)

    homes = [None] * sources
    for p in range(pairs):
        t, u = p // 4, p % 4
        block = precond[u * side : (u + 1) * side, t * LANES : (t + 1) * LANES]
        homes[places[2 * p]], homes[places[2 * p + 1]] = unpaired(block)

    def flat(blocks):
        groups = [
            jnp.concatenate(blocks[g : g + SUBLANES], axis=0).astype(bf16) for g in range(0, len(blocks), SUBLANES)
        ]
        turned = dot(gather, jnp.concatenate(groups, axis=1))
        return jnp.concatenate(
            [
                jnp.concatenate(
                    [
                        turned[j * SUBLANES : (j + 1) * SUBLANES, g * LANES : (g + 1) * LANES]
                        for g in range(len(groups))
                    ],
                    axis=0,
                ).astype(bf16)
                for j in range(tall)
            ],
            axis=1,
        )

    cands = [
        moved_ref[order.index(d), (1 + c) * tall : (2 + c) * tall, :]
        for d in range(sources)
        for c in range(per)
    ]
    rest = dot(flat(homes), flat(cands), ((1,), (1,)))
    wide = -(-count // LANES)
    if wide * LANES > count:
        rest = jnp.concatenate([rest, jnp.zeros((sources, wide * LANES - count), f32)], axis=1)
    tail = send - tall
    tails[...] = jnp.zeros_like(tails)
    for k in range(PIECES):
        piece = rest.astype(bf16).astype(f32)
        rest = rest - piece
        for t in range(wide):
            tails[pl.ds(k * wide + t, sources, stride=tail), :] = piece[:, t * LANES : (t + 1) * LANES]
    for k in range(sources):
        out_ref[k] = jnp.concatenate([homes[k], tails[k * tail : (k + 1) * tail, :]], axis=0).astype(bf16)


def finish(home_ref, holds_ref, chosen_ref, precond_ref, scores_ref, wide):
    slots, send, _ = home_ref.shape
    _, flat = precond_ref.shape[1:]
    count = chosen_ref.shape[0]
    tall = flat // LANES
    step = send + 1
    for k in range(slots):
        wide[pl.ds(k * step, send), :] = home_ref[k].astype(f32)
    by_slot = jnp.concatenate([wide[pl.ds(j, slots, stride=step), :].astype(bf16) for j in range(tall)], axis=1)
    precond_ref[0] = dot(holds_ref[...], by_slot).astype(bf16)
    groups = -(-count // LANES)
    parts = []
    for t in range(groups):
        pieces = [wide[pl.ds(tall + k * groups + t, slots, stride=step), :] for k in range(PIECES)]
        parts.append(jnp.sum((pieces[2] + pieces[1]) + pieces[0], axis=0, keepdims=True))
    dense = parts[0] if groups == 1 else jnp.concatenate(parts, axis=1)
    scores_ref[...] = jnp.sum(
        jnp.where(chosen_ref[...] > 0.0, upright(dense, count), 0.0), axis=0, keepdims=True
    )


SMEM = pl.BlockSpec(memory_space=pltpu.SMEM)
HBM = pl.BlockSpec(memory_space=pltpu.HBM)
VMEM = pl.BlockSpec(memory_space=pltpu.VMEM)
PARAMS = pltpu.CompilerParams(vmem_limit_bytes=40 * 1024 * 1024)


def body(
    query_grads,
    cand_grads,
    basis_out,
    basis_in,
    eigvals,
    layer_map,
    cand_rows,
    cand_lists,
    list_lengths,
):
    own, modules, flat = query_grads.shape
    per = cand_grads.shape[0]
    slots = layer_map.shape[0]
    tall = flat // LANES
    side = basis_out.shape[1]
    size = SUBLANES * tall
    count = cand_rows.shape[0]
    height = (own + per) * tall
    send = tall + -(-PIECES * -(-count // LANES) // SUBLANES) * SUBLANES

    def in_hbm(x):
        return pltpu.with_memory_space_constraint(x, pltpu.HBM)

    def swap_over(x, first):
        groups = [order_of(slots, first)]
        return lax.all_to_all(x, "shard", split_axis=0, concat_axis=0, tiled=True, axis_index_groups=groups)

    square = pltpu.VMEM((size, size), bf16)
    operands = (
        query_grads,
        cand_grads,
        layer_map.reshape(1, slots),
        basis_out.reshape(basis_out.shape[1:]),
        basis_in.reshape(basis_in.shape[1:]),
        eigvals.reshape(tall, LANES),
        cand_rows.reshape(1, count),
        cand_lists,
    )
    packed, enter, outer, inner, factor, gather, held, chosen = pl.pallas_call(
        pack,
        out_shape=(
            pltpu.VMEM((slots, height, LANES), bf16),
            square,
            square,
            square,
            pltpu.VMEM((side, LANES), f32),
            square,
            pltpu.VMEM((modules, slots), bf16),
            pltpu.VMEM((count, cand_lists.shape[1]), f32),
        ),
        in_specs=[SMEM] + [HBM] * len(operands),
        out_specs=[VMEM] * 8,
        scratch_shapes=[pltpu.VMEM(x.shape, x.dtype) for x in operands]
        + [pltpu.VMEM((slots * (height + 1), LANES), f32), pltpu.SemaphoreType.DMA((len(operands),))],
        compiler_params=PARAMS,
        name="pack",
    )(list_lengths, *(in_hbm(x) for x in operands))
    moved = swap_over(packed, firsts(slots)[0])
    homes = pl.pallas_call(
        work,
        out_shape=jax.ShapeDtypeStruct((slots, send, LANES), bf16),
        in_specs=[VMEM] * 6,
        out_specs=VMEM,
        scratch_shapes=[pltpu.VMEM((slots * (send - tall), LANES), f32)],
        compiler_params=PARAMS,
        name="work",
    )(moved, enter, outer, inner, factor, gather)
    home = swap_over(homes, firsts(slots)[1])
    return pl.pallas_call(
        finish,
        out_shape=(
            jax.ShapeDtypeStruct(query_grads.shape, bf16),
            jax.ShapeDtypeStruct(cand_lists.shape, f32),
        ),
        in_specs=[VMEM] * 3,
        out_specs=(VMEM, VMEM),
        scratch_shapes=[pltpu.VMEM((slots * (send + 1), LANES), f32)],
        compiler_params=PARAMS,
        name="finish",
    )(home, held, chosen)


def solution(mesh):
    return jax.shard_map(
        body,
        mesh=mesh,
        in_specs=(
            P(("groups", "shard"), None, None),
            P(("groups", "shard"), None, None),
            P("shard", None, None),
            P("shard", None, None),
            P("shard", None),
            P(),
            P("groups"),
            P(("groups", "shard"), None),
            P(("groups", "shard")),
        ),
        out_specs=(P(("groups", "shard"), None, None), P(("groups", "shard"), None)),
        check_vma=False,
    )
```

```python
import jax
import jax.numpy as jnp
from jax import lax
from jax.experimental import pallas as pl
from jax.experimental.pallas import tpu as pltpu
from jax.sharding import PartitionSpec as P

damping = 0.1
LANES = 128
SUBLANES = 8
PIECES = 3
f32, bf16 = jnp.float32, jnp.bfloat16


def iota(shape, axis):
    return lax.broadcasted_iota(jnp.int32, shape, axis)


def dot(a, b, dims=((1,), (0,))):
    return lax.dot_general(a, b, (dims, ((), ())), preferred_element_type=f32)


def mask(condition):
    return condition.astype(f32).astype(bf16)


def ring(place, slots):
    core, middle = place % 2, slots // 2
    up = 4 * (place // 2) + core
    down = 2 * (middle - 1 - 2 * ((place - middle) // 2)) + core
    if isinstance(place, int):
        return up if place < middle else down
    return jnp.where(place < middle, up, down)


def order_of(slots, first, stride):
    start = [ring(k, slots) for k in range(slots)].index(first)
    return [ring((start + stride * k) % slots, slots) for k in range(slots)]


def orders(slots):
    return (slots * 5 // 8, 7), (slots * 5 // 8, 1)


def gather_rows(tall):
    size = SUBLANES * tall
    row = iota((size, size), 0)
    return mask(row // SUBLANES + tall * (row % SUBLANES) == iota((size, size), 1))


def half(left, right):
    return jnp.where(iota(left.shape, 1) < LANES // 2, left, right)


def swap(block):
    return pltpu.roll(block, LANES // 2, 1)


def unpaired(block):
    tall = block.shape[0] // 2
    top, low = block[:tall], block[tall:]
    return half(top, swap(low)), half(swap(top), low)


def holds(layer_row, modules, first, stride):
    slots = layer_row.shape[1]
    start = [ring(k, slots) for k in range(slots)].index(first)
    placed = mask(iota((slots, slots), 0) == ring((start + stride * iota((slots, slots), 1)) % slots, slots))
    return dot(mask(iota((modules, slots), 0) == layer_row), placed).astype(bf16)


def block_bases(out_basis, in_basis, eigen):
    side = out_basis.shape[0]
    tall = side // 2
    size = 4 * side

    def spread(basis):
        wide = jnp.concatenate([basis] * 4, axis=1)
        return jnp.concatenate([wide] * 4, axis=0)

    row, column = iota((size, size), 0) // side, iota((size, size), 1) // side
    turn = mask(iota((side, side), 1) == 2 * (iota((side, side), 0) % tall) + iota((side, side), 0) // tall)
    bases = spread(dot(dot(turn, out_basis).astype(bf16), turn, ((1,), (1,))))
    outer = jnp.where(row == column, bases, 0.0).astype(bf16)
    bases = spread(in_basis.astype(f32))
    enter = jnp.where(row == 2 * (column % 2) + column // 2, bases, 0.0).astype(bf16)
    inner = jnp.where(row == column, bases, 0.0).astype(bf16)
    turned = swap(eigen)
    factor = 1.0 / (jnp.concatenate([half(eigen, turned), half(turned, eigen)], axis=0) + damping)
    return enter, outer, inner, factor


def pack(
    length_ref, query_hbm, cand_hbm, layer_hbm, out_basis_hbm, in_basis_hbm, eigen_hbm, rows_hbm, lists_hbm,
    out_ref, enter_ref, outer_ref, inner_ref, factor_ref, gather_ref, holds_ref, chosen_ref,
    query_ref, cand_ref, layer_ref, out_basis_ref, in_basis_ref, eigen_ref, rows_ref, lists_ref, wide, sems,
):
    arrivals = [
        pltpu.make_async_copy(source, target, sems.at[i])
        for i, (source, target) in enumerate(
            (
                (query_hbm, query_ref),
                (cand_hbm, cand_ref),
                (layer_hbm, layer_ref),
                (out_basis_hbm, out_basis_ref),
                (in_basis_hbm, in_basis_ref),
                (eigen_hbm, eigen_ref),
                (rows_hbm, rows_ref),
                (lists_hbm, lists_ref),
            )
        )
    ]
    for arrival in arrivals:
        arrival.start()
    modules, flat = query_ref.shape[1:]
    slots, height, _ = out_ref.shape
    tall = flat // LANES
    step = height + 1
    gather_ref[...] = gather_rows(tall)
    for arrival in arrivals[2:]:
        arrival.wait()
    one_hot = holds(layer_ref[...], modules, *orders(slots)[0])
    holds_ref[...] = holds(layer_ref[...], modules, *orders(slots)[1])
    enter_ref[...], outer_ref[...], inner_ref[...], factor_ref[...] = block_bases(
        out_basis_ref[...], in_basis_ref[...], eigen_ref[...]
    )
    lists = lists_ref[...]
    count, longest = rows_ref.shape[1], lists.shape[1]
    rows = upright(rows_ref[...].astype(f32), count)
    place = jnp.sum(jnp.where(iota((count, longest), 0) == lists, rows, 0.0), axis=0, keepdims=True)
    place = jnp.where(iota((1, longest), 1) < length_ref[0], place.astype(jnp.int32), -1)
    chosen_ref[...] = (iota((count, longest), 0) == place).astype(f32)
    r = 0
    for arrival, ref in zip(arrivals, (query_ref, cand_ref)):
        arrival.wait()
        for row in range(ref.shape[0]):
            by_slot = dot(one_hot, ref[row], ((0,), (0,)))
            for j in range(tall):
                wide[pl.ds(r * tall + j, slots, stride=step), :] = by_slot[:, j * LANES : (j + 1) * LANES]
            r += 1
    for k in range(slots):
        out_ref[k] = wide[pl.ds(k * step, height), :].astype(bf16)


def upright(row, count):
    shape = (count, row.shape[1])
    return jnp.sum(jnp.where(iota(shape, 0) == iota(shape, 1), row, 0.0), axis=1, keepdims=True)


def work(moved_ref, enter_ref, outer_ref, inner_ref, factor_ref, gather_ref, out_ref, tails):
    sources, height, _ = moved_ref.shape
    _, send, _ = out_ref.shape
    size = enter_ref.shape[0]
    side, tall = size // 4, size // SUBLANES
    per = height // tall - 1
    count = sources * per
    pairs = sources // 2
    stacks = pairs // 4
    order, later = (order_of(sources, *each) for each in orders(sources))
    places = [later.index(d) for d in order]
    outer, inner, gather = outer_ref[...], inner_ref[...], gather_ref[...]
    factor = factor_ref[...]

    queries = [jnp.concatenate([moved_ref[2 * p, :tall, :], moved_ref[2 * p + 1, :tall, :]], axis=1) for p in range(pairs)]
    entered = dot(jnp.concatenate(queries, axis=0), enter_ref[...]).astype(bf16)
    columns = []
    for t in range(stacks):
        tiles = []
        for p in range(4 * t, 4 * t + 4):
            rows = entered[p * tall : (p + 1) * tall]
            tiles += [rows[:, :LANES], rows[:, LANES:]]
        columns.append(jnp.concatenate(tiles, axis=0))
    rotated = dot(outer, jnp.concatenate(columns, axis=1), ((0,), (0,)))
    tile = jnp.concatenate([jnp.concatenate([factor] * 4, axis=0)] * 2, axis=1)
    scaled = [
        (rotated[:, t * LANES : (t + 2) * LANES] * tile).astype(bf16) for t in range(0, stacks, 2)
    ]
    returned = dot(jnp.concatenate(scaled, axis=0), inner, ((1,), (1,))).astype(bf16)
    returned = jnp.concatenate([returned[t * size : (t + 1) * size] for t in range(stacks // 2)], axis=1)
    precond = dot(outer, returned).astype(bf16).astype(f32)

    homes = [None] * sources
    for p in range(pairs):
        t, u = p // 4, p % 4
        block = precond[u * side : (u + 1) * side, t * LANES : (t + 1) * LANES]
        homes[places[2 * p]], homes[places[2 * p + 1]] = unpaired(block)

    def flat(blocks):
        groups = [
            jnp.concatenate(blocks[g : g + SUBLANES], axis=0).astype(bf16) for g in range(0, len(blocks), SUBLANES)
        ]
        turned = dot(gather, jnp.concatenate(groups, axis=1))
        return jnp.concatenate(
            [
                jnp.concatenate(
                    [
                        turned[j * SUBLANES : (j + 1) * SUBLANES, g * LANES : (g + 1) * LANES]
                        for g in range(len(groups))
                    ],
                    axis=0,
                ).astype(bf16)
                for j in range(tall)
            ],
            axis=1,
        )

    cands = [
        moved_ref[order.index(d), (1 + c) * tall : (2 + c) * tall, :]
        for d in range(sources)
        for c in range(per)
    ]
    rest = dot(flat(homes), flat(cands), ((1,), (1,)))
    wide = -(-count // LANES)
    if wide * LANES > count:
        rest = jnp.concatenate([rest, jnp.zeros((sources, wide * LANES - count), f32)], axis=1)
    tail = send - tall
    tails[...] = jnp.zeros_like(tails)
    for k in range(PIECES):
        piece = rest.astype(bf16).astype(f32)
        rest = rest - piece
        for t in range(wide):
            tails[pl.ds(k * wide + t, sources, stride=tail), :] = piece[:, t * LANES : (t + 1) * LANES]
    for k in range(sources):
        out_ref[k] = jnp.concatenate([homes[k], tails[k * tail : (k + 1) * tail, :]], axis=0).astype(bf16)


def finish(home_ref, holds_ref, chosen_ref, precond_ref, scores_ref, wide):
    slots, send, _ = home_ref.shape
    _, flat = precond_ref.shape[1:]
    count = chosen_ref.shape[0]
    tall = flat // LANES
    step = send + 1
    for k in range(slots):
        wide[pl.ds(k * step, send), :] = home_ref[k].astype(f32)
    by_slot = jnp.concatenate([wide[pl.ds(j, slots, stride=step), :].astype(bf16) for j in range(tall)], axis=1)
    precond_ref[0] = dot(holds_ref[...], by_slot).astype(bf16)
    groups = -(-count // LANES)
    parts = []
    for t in range(groups):
        pieces = [wide[pl.ds(tall + k * groups + t, slots, stride=step), :] for k in range(PIECES)]
        parts.append(jnp.sum((pieces[2] + pieces[1]) + pieces[0], axis=0, keepdims=True))
    dense = parts[0] if groups == 1 else jnp.concatenate(parts, axis=1)
    scores_ref[...] = jnp.sum(
        jnp.where(chosen_ref[...] > 0.0, upright(dense, count), 0.0), axis=0, keepdims=True
    )


SMEM = pl.BlockSpec(memory_space=pltpu.SMEM)
HBM = pl.BlockSpec(memory_space=pltpu.HBM)
VMEM = pl.BlockSpec(memory_space=pltpu.VMEM)
PARAMS = pltpu.CompilerParams(vmem_limit_bytes=40 * 1024 * 1024)


def body(
    query_grads,
    cand_grads,
    basis_out,
    basis_in,
    eigvals,
    layer_map,
    cand_rows,
    cand_lists,
    list_lengths,
):
    own, modules, flat = query_grads.shape
    per = cand_grads.shape[0]
    slots = layer_map.shape[0]
    tall = flat // LANES
    side = basis_out.shape[1]
    size = SUBLANES * tall
    count = cand_rows.shape[0]
    height = (own + per) * tall
    send = tall + -(-PIECES * -(-count // LANES) // SUBLANES) * SUBLANES

    def in_hbm(x):
        return pltpu.with_memory_space_constraint(x, pltpu.HBM)

    def swap_over(x, first, stride):
        groups = [order_of(slots, first, stride)]
        return lax.all_to_all(x, "shard", split_axis=0, concat_axis=0, tiled=True, axis_index_groups=groups)

    square = pltpu.VMEM((size, size), bf16)
    operands = (
        query_grads,
        cand_grads,
        layer_map.reshape(1, slots),
        basis_out.reshape(basis_out.shape[1:]),
        basis_in.reshape(basis_in.shape[1:]),
        eigvals.reshape(tall, LANES),
        cand_rows.reshape(1, count),
        cand_lists,
    )
    packed, enter, outer, inner, factor, gather, held, chosen = pl.pallas_call(
        pack,
        out_shape=(
            pltpu.VMEM((slots, height, LANES), bf16),
            square,
            square,
            square,
            pltpu.VMEM((side, LANES), f32),
            square,
            pltpu.VMEM((modules, slots), bf16),
            pltpu.VMEM((count, cand_lists.shape[1]), f32),
        ),
        in_specs=[SMEM] + [HBM] * len(operands),
        out_specs=[VMEM] * 8,
        scratch_shapes=[pltpu.VMEM(x.shape, x.dtype) for x in operands]
        + [pltpu.VMEM((slots * (height + 1), LANES), f32), pltpu.SemaphoreType.DMA((len(operands),))],
        compiler_params=PARAMS,
        name="pack",
    )(list_lengths, *(in_hbm(x) for x in operands))
    moved = swap_over(packed, *orders(slots)[0])
    homes = pl.pallas_call(
        work,
        out_shape=jax.ShapeDtypeStruct((slots, send, LANES), bf16),
        in_specs=[VMEM] * 6,
        out_specs=VMEM,
        scratch_shapes=[pltpu.VMEM((slots * (send - tall), LANES), f32)],
        compiler_params=PARAMS,
        name="work",
    )(moved, enter, outer, inner, factor, gather)
    home = swap_over(homes, *orders(slots)[1])
    return pl.pallas_call(
        finish,
        out_shape=(
            jax.ShapeDtypeStruct(query_grads.shape, bf16),
            jax.ShapeDtypeStruct(cand_lists.shape, f32),
        ),
        in_specs=[VMEM] * 3,
        out_specs=(VMEM, VMEM),
        scratch_shapes=[pltpu.VMEM((slots * (send + 1), LANES), f32)],
        compiler_params=PARAMS,
        name="finish",
    )(home, held, chosen)


def solution(mesh):
    return jax.shard_map(
        body,
        mesh=mesh,
        in_specs=(
            P(("groups", "shard"), None, None),
            P(("groups", "shard"), None, None),
            P("shard", None, None),
            P("shard", None, None),
            P("shard", None),
            P(),
            P("groups"),
            P(("groups", "shard"), None),
            P(("groups", "shard")),
        ),
        out_specs=(P(("groups", "shard"), None, None), P(("groups", "shard"), None)),
        check_vma=False,
    )
```

```python
import jax
import jax.numpy as jnp
from jax import lax
from jax.experimental import pallas as pl
from jax.experimental.pallas import tpu as pltpu
from jax.sharding import PartitionSpec as P

damping = 0.1
LANES = 128
SUBLANES = 8
PIECES = 3
f32, bf16 = jnp.float32, jnp.bfloat16


def iota(shape, axis):
    return lax.broadcasted_iota(jnp.int32, shape, axis)


def dot(a, b, dims=((1,), (0,))):
    return lax.dot_general(a, b, (dims, ((), ())), preferred_element_type=f32)


def mask(condition):
    return condition.astype(f32).astype(bf16)


def ring(place, slots):
    core, middle = place % 2, slots // 2
    up = 4 * (place // 2) + core
    down = 2 * (middle - 1 - 2 * ((place - middle) // 2)) + core
    if isinstance(place, int):
        return up if place < middle else down
    return jnp.where(place < middle, up, down)


def order_of(slots, first, stride):
    start = [ring(k, slots) for k in range(slots)].index(first)
    return [ring((start + stride * k) % slots, slots) for k in range(slots)]


def orders(slots):
    return (slots * 5 // 8, 3), (slots * 5 // 8, slots - 1)


def gather_rows(tall):
    size = SUBLANES * tall
    row = iota((size, size), 0)
    return mask(row // SUBLANES + tall * (row % SUBLANES) == iota((size, size), 1))


def half(left, right):
    return jnp.where(iota(left.shape, 1) < LANES // 2, left, right)


def swap(block):
    return pltpu.roll(block, LANES // 2, 1)


def unpaired(block):
    tall = block.shape[0] // 2
    top, low = block[:tall], block[tall:]
    return half(top, swap(low)), half(swap(top), low)


def holds(layer_row, modules, first, stride):
    slots = layer_row.shape[1]
    start = [ring(k, slots) for k in range(slots)].index(first)
    placed = mask(iota((slots, slots), 0) == ring((start + stride * iota((slots, slots), 1)) % slots, slots))
    return dot(mask(iota((modules, slots), 0) == layer_row), placed).astype(bf16)


def block_bases(out_basis, in_basis, eigen):
    side = out_basis.shape[0]
    tall = side // 2
    size = 4 * side

    def spread(basis):
        wide = jnp.concatenate([basis] * 4, axis=1)
        return jnp.concatenate([wide] * 4, axis=0)

    row, column = iota((size, size), 0) // side, iota((size, size), 1) // side
    turn = mask(iota((side, side), 1) == 2 * (iota((side, side), 0) % tall) + iota((side, side), 0) // tall)
    bases = spread(dot(dot(turn, out_basis).astype(bf16), turn, ((1,), (1,))))
    outer = jnp.where(row == column, bases, 0.0).astype(bf16)
    bases = spread(in_basis.astype(f32))
    enter = jnp.where(row == 2 * (column % 2) + column // 2, bases, 0.0).astype(bf16)
    inner = jnp.where(row == column, bases, 0.0).astype(bf16)
    turned = swap(eigen)
    factor = 1.0 / (jnp.concatenate([half(eigen, turned), half(turned, eigen)], axis=0) + damping)
    return enter, outer, inner, factor


def pack(
    length_ref, query_hbm, cand_hbm, layer_hbm, out_basis_hbm, in_basis_hbm, eigen_hbm, rows_hbm, lists_hbm,
    out_ref, enter_ref, outer_ref, inner_ref, factor_ref, gather_ref, holds_ref, chosen_ref,
    query_ref, cand_ref, layer_ref, out_basis_ref, in_basis_ref, eigen_ref, rows_ref, lists_ref, wide, sems,
):
    arrivals = [
        pltpu.make_async_copy(source, target, sems.at[i])
        for i, (source, target) in enumerate(
            (
                (query_hbm, query_ref),
                (cand_hbm, cand_ref),
                (layer_hbm, layer_ref),
                (out_basis_hbm, out_basis_ref),
                (in_basis_hbm, in_basis_ref),
                (eigen_hbm, eigen_ref),
                (rows_hbm, rows_ref),
                (lists_hbm, lists_ref),
            )
        )
    ]
    for arrival in arrivals:
        arrival.start()
    modules, flat = query_ref.shape[1:]
    slots, height, _ = out_ref.shape
    tall = flat // LANES
    step = height + 1
    gather_ref[...] = gather_rows(tall)
    for arrival in arrivals[2:]:
        arrival.wait()
    one_hot = holds(layer_ref[...], modules, *orders(slots)[0])
    holds_ref[...] = holds(layer_ref[...], modules, *orders(slots)[1])
    enter_ref[...], outer_ref[...], inner_ref[...], factor_ref[...] = block_bases(
        out_basis_ref[...], in_basis_ref[...], eigen_ref[...]
    )
    lists = lists_ref[...]
    count, longest = rows_ref.shape[1], lists.shape[1]
    rows = upright(rows_ref[...].astype(f32), count)
    place = jnp.sum(jnp.where(iota((count, longest), 0) == lists, rows, 0.0), axis=0, keepdims=True)
    place = jnp.where(iota((1, longest), 1) < length_ref[0], place.astype(jnp.int32), -1)
    chosen_ref[...] = (iota((count, longest), 0) == place).astype(f32)
    r = 0
    for arrival, ref in zip(arrivals, (query_ref, cand_ref)):
        arrival.wait()
        for row in range(ref.shape[0]):
            by_slot = dot(one_hot, ref[row], ((0,), (0,)))
            for j in range(tall):
                wide[pl.ds(r * tall + j, slots, stride=step), :] = by_slot[:, j * LANES : (j + 1) * LANES]
            r += 1
    for k in range(slots):
        out_ref[k] = wide[pl.ds(k * step, height), :].astype(bf16)


def upright(row, count):
    shape = (count, row.shape[1])
    return jnp.sum(jnp.where(iota(shape, 0) == iota(shape, 1), row, 0.0), axis=1, keepdims=True)


def work(moved_ref, enter_ref, outer_ref, inner_ref, factor_ref, gather_ref, out_ref, tails):
    sources, height, _ = moved_ref.shape
    _, send, _ = out_ref.shape
    size = enter_ref.shape[0]
    side, tall = size // 4, size // SUBLANES
    per = height // tall - 1
    count = sources * per
    pairs = sources // 2
    stacks = pairs // 4
    order, later = (order_of(sources, *each) for each in orders(sources))
    places = [later.index(d) for d in order]
    outer, inner, gather = outer_ref[...], inner_ref[...], gather_ref[...]
    factor = factor_ref[...]

    queries = [jnp.concatenate([moved_ref[2 * p, :tall, :], moved_ref[2 * p + 1, :tall, :]], axis=1) for p in range(pairs)]
    entered = dot(jnp.concatenate(queries, axis=0), enter_ref[...]).astype(bf16)
    columns = []
    for t in range(stacks):
        tiles = []
        for p in range(4 * t, 4 * t + 4):
            rows = entered[p * tall : (p + 1) * tall]
            tiles += [rows[:, :LANES], rows[:, LANES:]]
        columns.append(jnp.concatenate(tiles, axis=0))
    rotated = dot(outer, jnp.concatenate(columns, axis=1), ((0,), (0,)))
    tile = jnp.concatenate([jnp.concatenate([factor] * 4, axis=0)] * 2, axis=1)
    scaled = [
        (rotated[:, t * LANES : (t + 2) * LANES] * tile).astype(bf16) for t in range(0, stacks, 2)
    ]
    returned = dot(jnp.concatenate(scaled, axis=0), inner, ((1,), (1,))).astype(bf16)
    returned = jnp.concatenate([returned[t * size : (t + 1) * size] for t in range(stacks // 2)], axis=1)
    precond = dot(outer, returned).astype(bf16).astype(f32)

    homes = [None] * sources
    for p in range(pairs):
        t, u = p // 4, p % 4
        block = precond[u * side : (u + 1) * side, t * LANES : (t + 1) * LANES]
        homes[places[2 * p]], homes[places[2 * p + 1]] = unpaired(block)

    def flat(blocks):
        groups = [
            jnp.concatenate(blocks[g : g + SUBLANES], axis=0).astype(bf16) for g in range(0, len(blocks), SUBLANES)
        ]
        turned = dot(gather, jnp.concatenate(groups, axis=1))
        return jnp.concatenate(
            [
                jnp.concatenate(
                    [
                        turned[j * SUBLANES : (j + 1) * SUBLANES, g * LANES : (g + 1) * LANES]
                        for g in range(len(groups))
                    ],
                    axis=0,
                ).astype(bf16)
                for j in range(tall)
            ],
            axis=1,
        )

    cands = [
        moved_ref[order.index(d), (1 + c) * tall : (2 + c) * tall, :]
        for d in range(sources)
        for c in range(per)
    ]
    rest = dot(flat(homes), flat(cands), ((1,), (1,)))
    wide = -(-count // LANES)
    if wide * LANES > count:
        rest = jnp.concatenate([rest, jnp.zeros((sources, wide * LANES - count), f32)], axis=1)
    tail = send - tall
    tails[...] = jnp.zeros_like(tails)
    for k in range(PIECES):
        piece = rest.astype(bf16).astype(f32)
        rest = rest - piece
        for t in range(wide):
            tails[pl.ds(k * wide + t, sources, stride=tail), :] = piece[:, t * LANES : (t + 1) * LANES]
    for k in range(sources):
        out_ref[k] = jnp.concatenate([homes[k], tails[k * tail : (k + 1) * tail, :]], axis=0).astype(bf16)


def finish(home_ref, holds_ref, chosen_ref, precond_ref, scores_ref, wide):
    slots, send, _ = home_ref.shape
    _, flat = precond_ref.shape[1:]
    count = chosen_ref.shape[0]
    tall = flat // LANES
    step = send + 1
    for k in range(slots):
        wide[pl.ds(k * step, send), :] = home_ref[k].astype(f32)
    by_slot = jnp.concatenate([wide[pl.ds(j, slots, stride=step), :].astype(bf16) for j in range(tall)], axis=1)
    precond_ref[0] = dot(holds_ref[...], by_slot).astype(bf16)
    groups = -(-count // LANES)
    parts = []
    for t in range(groups):
        pieces = [wide[pl.ds(tall + k * groups + t, slots, stride=step), :] for k in range(PIECES)]
        parts.append(jnp.sum((pieces[2] + pieces[1]) + pieces[0], axis=0, keepdims=True))
    dense = parts[0] if groups == 1 else jnp.concatenate(parts, axis=1)
    scores_ref[...] = jnp.sum(
        jnp.where(chosen_ref[...] > 0.0, upright(dense, count), 0.0), axis=0, keepdims=True
    )


SMEM = pl.BlockSpec(memory_space=pltpu.SMEM)
HBM = pl.BlockSpec(memory_space=pltpu.HBM)
VMEM = pl.BlockSpec(memory_space=pltpu.VMEM)
PARAMS = pltpu.CompilerParams(vmem_limit_bytes=40 * 1024 * 1024)


def body(
    query_grads,
    cand_grads,
    basis_out,
    basis_in,
    eigvals,
    layer_map,
    cand_rows,
    cand_lists,
    list_lengths,
):
    own, modules, flat = query_grads.shape
    per = cand_grads.shape[0]
    slots = layer_map.shape[0]
    tall = flat // LANES
    side = basis_out.shape[1]
    size = SUBLANES * tall
    count = cand_rows.shape[0]
    height = (own + per) * tall
    send = tall + -(-PIECES * -(-count // LANES) // SUBLANES) * SUBLANES

    def in_hbm(x):
        return pltpu.with_memory_space_constraint(x, pltpu.HBM)

    def swap_over(x, first, stride):
        groups = [order_of(slots, first, stride)]
        return lax.all_to_all(x, "shard", split_axis=0, concat_axis=0, tiled=True, axis_index_groups=groups)

    square = pltpu.VMEM((size, size), bf16)
    operands = (
        query_grads,
        cand_grads,
        layer_map.reshape(1, slots),
        basis_out.reshape(basis_out.shape[1:]),
        basis_in.reshape(basis_in.shape[1:]),
        eigvals.reshape(tall, LANES),
        cand_rows.reshape(1, count),
        cand_lists,
    )
    packed, enter, outer, inner, factor, gather, held, chosen = pl.pallas_call(
        pack,
        out_shape=(
            pltpu.VMEM((slots, height, LANES), bf16),
            square,
            square,
            square,
            pltpu.VMEM((side, LANES), f32),
            square,
            pltpu.VMEM((modules, slots), bf16),
            pltpu.VMEM((count, cand_lists.shape[1]), f32),
        ),
        in_specs=[SMEM] + [HBM] * len(operands),
        out_specs=[VMEM] * 8,
        scratch_shapes=[pltpu.VMEM(x.shape, x.dtype) for x in operands]
        + [pltpu.VMEM((slots * (height + 1), LANES), f32), pltpu.SemaphoreType.DMA((len(operands),))],
        compiler_params=PARAMS,
        name="pack",
    )(list_lengths, *(in_hbm(x) for x in operands))
    moved = swap_over(packed, *orders(slots)[0])
    homes = pl.pallas_call(
        work,
        out_shape=jax.ShapeDtypeStruct((slots, send, LANES), bf16),
        in_specs=[VMEM] * 6,
        out_specs=VMEM,
        scratch_shapes=[pltpu.VMEM((slots * (send - tall), LANES), f32)],
        compiler_params=PARAMS,
        name="work",
    )(moved, enter, outer, inner, factor, gather)
    home = swap_over(homes, *orders(slots)[1])
    return pl.pallas_call(
        finish,
        out_shape=(
            jax.ShapeDtypeStruct(query_grads.shape, bf16),
            jax.ShapeDtypeStruct(cand_lists.shape, f32),
        ),
        in_specs=[VMEM] * 3,
        out_specs=(VMEM, VMEM),
        scratch_shapes=[pltpu.VMEM((slots * (send + 1), LANES), f32)],
        compiler_params=PARAMS,
        name="finish",
    )(home, held, chosen)


def solution(mesh):
    return jax.shard_map(
        body,
        mesh=mesh,
        in_specs=(
            P(("groups", "shard"), None, None),
            P(("groups", "shard"), None, None),
            P("shard", None, None),
            P("shard", None, None),
            P("shard", None),
            P(),
            P("groups"),
            P(("groups", "shard"), None),
            P(("groups", "shard")),
        ),
        out_specs=(P(("groups", "shard"), None, None), P(("groups", "shard"), None)),
        check_vma=False,
    )
```

```python
import jax
import jax.numpy as jnp
from jax import lax
from jax.experimental import pallas as pl
from jax.experimental.pallas import tpu as pltpu
from jax.sharding import PartitionSpec as P

damping = 0.1
LANES = 128
SUBLANES = 8
PIECES = 3
f32, bf16 = jnp.float32, jnp.bfloat16


def iota(shape, axis):
    return lax.broadcasted_iota(jnp.int32, shape, axis)


def dot(a, b, dims=((1,), (0,))):
    return lax.dot_general(a, b, (dims, ((), ())), preferred_element_type=f32)


def mask(condition):
    return condition.astype(f32).astype(bf16)


def ring(place, slots):
    core, middle = place % 2, slots // 2
    up = 4 * (place // 2) + core
    down = 2 * (middle - 1 - 2 * ((place - middle) // 2)) + core
    if isinstance(place, int):
        return up if place < middle else down
    return jnp.where(place < middle, up, down)


def order_of(slots, first, stride):
    start = [ring(k, slots) for k in range(slots)].index(first)
    return [ring((start + stride * k) % slots, slots) for k in range(slots)]


def orders(slots):
    return (slots * 5 // 8, 7), (slots * 5 // 8, slots - 1)


def gather_rows(tall):
    size = SUBLANES * tall
    row = iota((size, size), 0)
    return mask(row // SUBLANES + tall * (row % SUBLANES) == iota((size, size), 1))


def half(left, right):
    return jnp.where(iota(left.shape, 1) < LANES // 2, left, right)


def swap(block):
    return pltpu.roll(block, LANES // 2, 1)


def unpaired(block):
    tall = block.shape[0] // 2
    top, low = block[:tall], block[tall:]
    return half(top, swap(low)), half(swap(top), low)


def holds(layer_row, modules, first, stride):
    slots = layer_row.shape[1]
    start = [ring(k, slots) for k in range(slots)].index(first)
    placed = mask(iota((slots, slots), 0) == ring((start + stride * iota((slots, slots), 1)) % slots, slots))
    return dot(mask(iota((modules, slots), 0) == layer_row), placed).astype(bf16)


def block_bases(out_basis, in_basis, eigen):
    side = out_basis.shape[0]
    tall = side // 2
    size = 4 * side

    def spread(basis):
        wide = jnp.concatenate([basis] * 4, axis=1)
        return jnp.concatenate([wide] * 4, axis=0)

    row, column = iota((size, size), 0) // side, iota((size, size), 1) // side
    turn = mask(iota((side, side), 1) == 2 * (iota((side, side), 0) % tall) + iota((side, side), 0) // tall)
    bases = spread(dot(dot(turn, out_basis).astype(bf16), turn, ((1,), (1,))))
    outer = jnp.where(row == column, bases, 0.0).astype(bf16)
    bases = spread(in_basis.astype(f32))
    enter = jnp.where(row == 2 * (column % 2) + column // 2, bases, 0.0).astype(bf16)
    inner = jnp.where(row == column, bases, 0.0).astype(bf16)
    turned = swap(eigen)
    factor = 1.0 / (jnp.concatenate([half(eigen, turned), half(turned, eigen)], axis=0) + damping)
    return enter, outer, inner, factor


def pack(
    length_ref, query_hbm, cand_hbm, layer_hbm, out_basis_hbm, in_basis_hbm, eigen_hbm, rows_hbm, lists_hbm,
    out_ref, enter_ref, outer_ref, inner_ref, factor_ref, gather_ref, holds_ref, chosen_ref,
    query_ref, cand_ref, layer_ref, out_basis_ref, in_basis_ref, eigen_ref, rows_ref, lists_ref, wide, sems,
):
    arrivals = [
        pltpu.make_async_copy(source, target, sems.at[i])
        for i, (source, target) in enumerate(
            (
                (query_hbm, query_ref),
                (cand_hbm, cand_ref),
                (layer_hbm, layer_ref),
                (out_basis_hbm, out_basis_ref),
                (in_basis_hbm, in_basis_ref),
                (eigen_hbm, eigen_ref),
                (rows_hbm, rows_ref),
                (lists_hbm, lists_ref),
            )
        )
    ]
    for arrival in arrivals:
        arrival.start()
    modules, flat = query_ref.shape[1:]
    slots, height, _ = out_ref.shape
    tall = flat // LANES
    step = height + 1
    gather_ref[...] = gather_rows(tall)
    for arrival in arrivals[2:]:
        arrival.wait()
    one_hot = holds(layer_ref[...], modules, *orders(slots)[0])
    holds_ref[...] = holds(layer_ref[...], modules, *orders(slots)[1])
    enter_ref[...], outer_ref[...], inner_ref[...], factor_ref[...] = block_bases(
        out_basis_ref[...], in_basis_ref[...], eigen_ref[...]
    )
    lists = lists_ref[...]
    count, longest = rows_ref.shape[1], lists.shape[1]
    rows = upright(rows_ref[...].astype(f32), count)
    place = jnp.sum(jnp.where(iota((count, longest), 0) == lists, rows, 0.0), axis=0, keepdims=True)
    place = jnp.where(iota((1, longest), 1) < length_ref[0], place.astype(jnp.int32), -1)
    chosen_ref[...] = (iota((count, longest), 0) == place).astype(f32)
    r = 0
    for arrival, ref in zip(arrivals, (query_ref, cand_ref)):
        arrival.wait()
        for row in range(ref.shape[0]):
            by_slot = dot(one_hot, ref[row], ((0,), (0,)))
            for j in range(tall):
                wide[pl.ds(r * tall + j, slots, stride=step), :] = by_slot[:, j * LANES : (j + 1) * LANES]
            r += 1
    for k in range(slots):
        out_ref[k] = wide[pl.ds(k * step, height), :].astype(bf16)


def upright(row, count):
    shape = (count, row.shape[1])
    return jnp.sum(jnp.where(iota(shape, 0) == iota(shape, 1), row, 0.0), axis=1, keepdims=True)


def work(moved_ref, enter_ref, outer_ref, inner_ref, factor_ref, gather_ref, out_ref, tails):
    sources, height, _ = moved_ref.shape
    _, send, _ = out_ref.shape
    size = enter_ref.shape[0]
    side, tall = size // 4, size // SUBLANES
    per = height // tall - 1
    count = sources * per
    pairs = sources // 2
    stacks = pairs // 4
    order, later = (order_of(sources, *each) for each in orders(sources))
    places = [later.index(d) for d in order]
    outer, inner, gather = outer_ref[...], inner_ref[...], gather_ref[...]
    factor = factor_ref[...]

    queries = [jnp.concatenate([moved_ref[2 * p, :tall, :], moved_ref[2 * p + 1, :tall, :]], axis=1) for p in range(pairs)]
    entered = dot(jnp.concatenate(queries, axis=0), enter_ref[...]).astype(bf16)
    columns = []
    for t in range(stacks):
        tiles = []
        for p in range(4 * t, 4 * t + 4):
            rows = entered[p * tall : (p + 1) * tall]
            tiles += [rows[:, :LANES], rows[:, LANES:]]
        columns.append(jnp.concatenate(tiles, axis=0))
    rotated = dot(outer, jnp.concatenate(columns, axis=1), ((0,), (0,)))
    tile = jnp.concatenate([jnp.concatenate([factor] * 4, axis=0)] * 2, axis=1)
    scaled = [
        (rotated[:, t * LANES : (t + 2) * LANES] * tile).astype(bf16) for t in range(0, stacks, 2)
    ]
    returned = dot(jnp.concatenate(scaled, axis=0), inner, ((1,), (1,))).astype(bf16)
    returned = jnp.concatenate([returned[t * size : (t + 1) * size] for t in range(stacks // 2)], axis=1)
    precond = dot(outer, returned).astype(bf16).astype(f32)

    homes = [None] * sources
    for p in range(pairs):
        t, u = p // 4, p % 4
        block = precond[u * side : (u + 1) * side, t * LANES : (t + 1) * LANES]
        homes[places[2 * p]], homes[places[2 * p + 1]] = unpaired(block)

    def flat(blocks):
        groups = [
            jnp.concatenate(blocks[g : g + SUBLANES], axis=0).astype(bf16) for g in range(0, len(blocks), SUBLANES)
        ]
        turned = dot(gather, jnp.concatenate(groups, axis=1))
        return jnp.concatenate(
            [
                jnp.concatenate(
                    [
                        turned[j * SUBLANES : (j + 1) * SUBLANES, g * LANES : (g + 1) * LANES]
                        for g in range(len(groups))
                    ],
                    axis=0,
                ).astype(bf16)
                for j in range(tall)
            ],
            axis=1,
        )

    cands = [
        moved_ref[order.index(d), (1 + c) * tall : (2 + c) * tall, :]
        for d in range(sources)
        for c in range(per)
    ]
    rest = dot(flat(homes), flat(cands), ((1,), (1,)))
    wide = -(-count // LANES)
    if wide * LANES > count:
        rest = jnp.concatenate([rest, jnp.zeros((sources, wide * LANES - count), f32)], axis=1)
    tail = send - tall
    tails[...] = jnp.zeros_like(tails)
    for k in range(PIECES):
        piece = rest.astype(bf16).astype(f32)
        rest = rest - piece
        for t in range(wide):
            tails[pl.ds(k * wide + t, sources, stride=tail), :] = piece[:, t * LANES : (t + 1) * LANES]
    for k in range(sources):
        out_ref[k] = jnp.concatenate([homes[k], tails[k * tail : (k + 1) * tail, :]], axis=0).astype(bf16)


def finish(home_ref, holds_ref, chosen_ref, precond_ref, scores_ref, wide):
    slots, send, _ = home_ref.shape
    _, flat = precond_ref.shape[1:]
    count = chosen_ref.shape[0]
    tall = flat // LANES
    step = send + 1
    for k in range(slots):
        wide[pl.ds(k * step, send), :] = home_ref[k].astype(f32)
    by_slot = jnp.concatenate([wide[pl.ds(j, slots, stride=step), :].astype(bf16) for j in range(tall)], axis=1)
    precond_ref[0] = dot(holds_ref[...], by_slot).astype(bf16)
    groups = -(-count // LANES)
    parts = []
    for t in range(groups):
        pieces = [wide[pl.ds(tall + k * groups + t, slots, stride=step), :] for k in range(PIECES)]
        parts.append(jnp.sum((pieces[2] + pieces[1]) + pieces[0], axis=0, keepdims=True))
    dense = parts[0] if groups == 1 else jnp.concatenate(parts, axis=1)
    scores_ref[...] = jnp.sum(
        jnp.where(chosen_ref[...] > 0.0, upright(dense, count), 0.0), axis=0, keepdims=True
    )


SMEM = pl.BlockSpec(memory_space=pltpu.SMEM)
HBM = pl.BlockSpec(memory_space=pltpu.HBM)
VMEM = pl.BlockSpec(memory_space=pltpu.VMEM)
PARAMS = pltpu.CompilerParams(vmem_limit_bytes=40 * 1024 * 1024)


def body(
    query_grads,
    cand_grads,
    basis_out,
    basis_in,
    eigvals,
    layer_map,
    cand_rows,
    cand_lists,
    list_lengths,
):
    own, modules, flat = query_grads.shape
    per = cand_grads.shape[0]
    slots = layer_map.shape[0]
    tall = flat // LANES
    side = basis_out.shape[1]
    size = SUBLANES * tall
    count = cand_rows.shape[0]
    height = (own + per) * tall
    send = tall + -(-PIECES * -(-count // LANES) // SUBLANES) * SUBLANES

    def in_hbm(x):
        return pltpu.with_memory_space_constraint(x, pltpu.HBM)

    def swap_over(x, first, stride):
        groups = [order_of(slots, first, stride)]
        return lax.all_to_all(x, "shard", split_axis=0, concat_axis=0, tiled=True, axis_index_groups=groups)

    square = pltpu.VMEM((size, size), bf16)
    operands = (
        query_grads,
        cand_grads,
        layer_map.reshape(1, slots),
        basis_out.reshape(basis_out.shape[1:]),
        basis_in.reshape(basis_in.shape[1:]),
        eigvals.reshape(tall, LANES),
        cand_rows.reshape(1, count),
        cand_lists,
    )
    packed, enter, outer, inner, factor, gather, held, chosen = pl.pallas_call(
        pack,
        out_shape=(
            pltpu.VMEM((slots, height, LANES), bf16),
            square,
            square,
            square,
            pltpu.VMEM((side, LANES), f32),
            square,
            pltpu.VMEM((modules, slots), bf16),
            pltpu.VMEM((count, cand_lists.shape[1]), f32),
        ),
        in_specs=[SMEM] + [HBM] * len(operands),
        out_specs=[VMEM] * 8,
        scratch_shapes=[pltpu.VMEM(x.shape, x.dtype) for x in operands]
        + [pltpu.VMEM((slots * (height + 1), LANES), f32), pltpu.SemaphoreType.DMA((len(operands),))],
        compiler_params=PARAMS,
        name="pack",
    )(list_lengths, *(in_hbm(x) for x in operands))
    moved = swap_over(packed, *orders(slots)[0])
    homes = pl.pallas_call(
        work,
        out_shape=jax.ShapeDtypeStruct((slots, send, LANES), bf16),
        in_specs=[VMEM] * 6,
        out_specs=VMEM,
        scratch_shapes=[pltpu.VMEM((slots * (send - tall), LANES), f32)],
        compiler_params=PARAMS,
        name="work",
    )(moved, enter, outer, inner, factor, gather)
    home = swap_over(homes, *orders(slots)[1])
    return pl.pallas_call(
        finish,
        out_shape=(
            jax.ShapeDtypeStruct(query_grads.shape, bf16),
            jax.ShapeDtypeStruct(cand_lists.shape, f32),
        ),
        in_specs=[VMEM] * 3,
        out_specs=(VMEM, VMEM),
        scratch_shapes=[pltpu.VMEM((slots * (send + 1), LANES), f32)],
        compiler_params=PARAMS,
        name="finish",
    )(home, held, chosen)


def solution(mesh):
    return jax.shard_map(
        body,
        mesh=mesh,
        in_specs=(
            P(("groups", "shard"), None, None),
            P(("groups", "shard"), None, None),
            P("shard", None, None),
            P("shard", None, None),
            P("shard", None),
            P(),
            P("groups"),
            P(("groups", "shard"), None),
            P(("groups", "shard")),
        ),
        out_specs=(P(("groups", "shard"), None, None), P(("groups", "shard"), None)),
        check_vma=False,
    )
```

```python
import jax
import jax.numpy as jnp
from jax import lax
from jax.experimental import pallas as pl
from jax.experimental.pallas import tpu as pltpu
from jax.sharding import PartitionSpec as P

damping = 0.1
LANES = 128
SUBLANES = 8
PIECES = 3
f32, bf16 = jnp.float32, jnp.bfloat16


def iota(shape, axis):
    return lax.broadcasted_iota(jnp.int32, shape, axis)


def dot(a, b, dims=((1,), (0,))):
    return lax.dot_general(a, b, (dims, ((), ())), preferred_element_type=f32)


def mask(condition):
    return condition.astype(f32).astype(bf16)


def ring(place, slots):
    core, middle = place % 2, slots // 2
    up = 4 * (place // 2) + core
    down = 2 * (middle - 1 - 2 * ((place - middle) // 2)) + core
    if isinstance(place, int):
        return up if place < middle else down
    return jnp.where(place < middle, up, down)


def order_of(slots, first, stride):
    start = [ring(k, slots) for k in range(slots)].index(first)
    return [ring((start + stride * k) % slots, slots) for k in range(slots)]


def orders(slots):
    return (slots * 5 // 8, slots - 7), (slots * 5 // 8, slots - 1)


def gather_rows(tall):
    size = SUBLANES * tall
    row = iota((size, size), 0)
    return mask(row // SUBLANES + tall * (row % SUBLANES) == iota((size, size), 1))


def half(left, right):
    return jnp.where(iota(left.shape, 1) < LANES // 2, left, right)


def swap(block):
    return pltpu.roll(block, LANES // 2, 1)


def unpaired(block):
    tall = block.shape[0] // 2
    top, low = block[:tall], block[tall:]
    return half(top, swap(low)), half(swap(top), low)


def holds(layer_row, modules, first, stride):
    slots = layer_row.shape[1]
    start = [ring(k, slots) for k in range(slots)].index(first)
    placed = mask(iota((slots, slots), 0) == ring((start + stride * iota((slots, slots), 1)) % slots, slots))
    return dot(mask(iota((modules, slots), 0) == layer_row), placed).astype(bf16)


def block_bases(out_basis, in_basis, eigen):
    side = out_basis.shape[0]
    tall = side // 2
    size = 4 * side

    def spread(basis):
        wide = jnp.concatenate([basis] * 4, axis=1)
        return jnp.concatenate([wide] * 4, axis=0)

    row, column = iota((size, size), 0) // side, iota((size, size), 1) // side
    turn = mask(iota((side, side), 1) == 2 * (iota((side, side), 0) % tall) + iota((side, side), 0) // tall)
    bases = spread(dot(dot(turn, out_basis).astype(bf16), turn, ((1,), (1,))))
    outer = jnp.where(row == column, bases, 0.0).astype(bf16)
    bases = spread(in_basis.astype(f32))
    enter = jnp.where(row == 2 * (column % 2) + column // 2, bases, 0.0).astype(bf16)
    inner = jnp.where(row == column, bases, 0.0).astype(bf16)
    turned = swap(eigen)
    factor = 1.0 / (jnp.concatenate([half(eigen, turned), half(turned, eigen)], axis=0) + damping)
    return enter, outer, inner, factor


def pack(
    length_ref, query_hbm, cand_hbm, layer_hbm, out_basis_hbm, in_basis_hbm, eigen_hbm, rows_hbm, lists_hbm,
    out_ref, enter_ref, outer_ref, inner_ref, factor_ref, gather_ref, holds_ref, chosen_ref,
    query_ref, cand_ref, layer_ref, out_basis_ref, in_basis_ref, eigen_ref, rows_ref, lists_ref, wide, sems,
):
    arrivals = [
        pltpu.make_async_copy(source, target, sems.at[i])
        for i, (source, target) in enumerate(
            (
                (query_hbm, query_ref),
                (cand_hbm, cand_ref),
                (layer_hbm, layer_ref),
                (out_basis_hbm, out_basis_ref),
                (in_basis_hbm, in_basis_ref),
                (eigen_hbm, eigen_ref),
                (rows_hbm, rows_ref),
                (lists_hbm, lists_ref),
            )
        )
    ]
    for arrival in arrivals:
        arrival.start()
    modules, flat = query_ref.shape[1:]
    slots, height, _ = out_ref.shape
    tall = flat // LANES
    step = height + 1
    gather_ref[...] = gather_rows(tall)
    for arrival in arrivals[2:]:
        arrival.wait()
    one_hot = holds(layer_ref[...], modules, *orders(slots)[0])
    holds_ref[...] = holds(layer_ref[...], modules, *orders(slots)[1])
    enter_ref[...], outer_ref[...], inner_ref[...], factor_ref[...] = block_bases(
        out_basis_ref[...], in_basis_ref[...], eigen_ref[...]
    )
    lists = lists_ref[...]
    count, longest = rows_ref.shape[1], lists.shape[1]
    rows = upright(rows_ref[...].astype(f32), count)
    place = jnp.sum(jnp.where(iota((count, longest), 0) == lists, rows, 0.0), axis=0, keepdims=True)
    place = jnp.where(iota((1, longest), 1) < length_ref[0], place.astype(jnp.int32), -1)
    chosen_ref[...] = (iota((count, longest), 0) == place).astype(f32)
    r = 0
    for arrival, ref in zip(arrivals, (query_ref, cand_ref)):
        arrival.wait()
        for row in range(ref.shape[0]):
            by_slot = dot(one_hot, ref[row], ((0,), (0,)))
            for j in range(tall):
                wide[pl.ds(r * tall + j, slots, stride=step), :] = by_slot[:, j * LANES : (j + 1) * LANES]
            r += 1
    for k in range(slots):
        out_ref[k] = wide[pl.ds(k * step, height), :].astype(bf16)


def upright(row, count):
    shape = (count, row.shape[1])
    return jnp.sum(jnp.where(iota(shape, 0) == iota(shape, 1), row, 0.0), axis=1, keepdims=True)


def work(moved_ref, enter_ref, outer_ref, inner_ref, factor_ref, gather_ref, out_ref, tails):
    sources, height, _ = moved_ref.shape
    _, send, _ = out_ref.shape
    size = enter_ref.shape[0]
    side, tall = size // 4, size // SUBLANES
    per = height // tall - 1
    count = sources * per
    pairs = sources // 2
    stacks = pairs // 4
    order, later = (order_of(sources, *each) for each in orders(sources))
    places = [later.index(d) for d in order]
    outer, inner, gather = outer_ref[...], inner_ref[...], gather_ref[...]
    factor = factor_ref[...]

    queries = [jnp.concatenate([moved_ref[2 * p, :tall, :], moved_ref[2 * p + 1, :tall, :]], axis=1) for p in range(pairs)]
    entered = dot(jnp.concatenate(queries, axis=0), enter_ref[...]).astype(bf16)
    columns = []
    for t in range(stacks):
        tiles = []
        for p in range(4 * t, 4 * t + 4):
            rows = entered[p * tall : (p + 1) * tall]
            tiles += [rows[:, :LANES], rows[:, LANES:]]
        columns.append(jnp.concatenate(tiles, axis=0))
    rotated = dot(outer, jnp.concatenate(columns, axis=1), ((0,), (0,)))
    tile = jnp.concatenate([jnp.concatenate([factor] * 4, axis=0)] * 2, axis=1)
    scaled = [
        (rotated[:, t * LANES : (t + 2) * LANES] * tile).astype(bf16) for t in range(0, stacks, 2)
    ]
    returned = dot(jnp.concatenate(scaled, axis=0), inner, ((1,), (1,))).astype(bf16)
    returned = jnp.concatenate([returned[t * size : (t + 1) * size] for t in range(stacks // 2)], axis=1)
    precond = dot(outer, returned).astype(bf16).astype(f32)

    homes = [None] * sources
    for p in range(pairs):
        t, u = p // 4, p % 4
        block = precond[u * side : (u + 1) * side, t * LANES : (t + 1) * LANES]
        homes[places[2 * p]], homes[places[2 * p + 1]] = unpaired(block)

    def flat(blocks):
        groups = [
            jnp.concatenate(blocks[g : g + SUBLANES], axis=0).astype(bf16) for g in range(0, len(blocks), SUBLANES)
        ]
        turned = dot(gather, jnp.concatenate(groups, axis=1))
        return jnp.concatenate(
            [
                jnp.concatenate(
                    [
                        turned[j * SUBLANES : (j + 1) * SUBLANES, g * LANES : (g + 1) * LANES]
                        for g in range(len(groups))
                    ],
                    axis=0,
                ).astype(bf16)
                for j in range(tall)
            ],
            axis=1,
        )

    cands = [
        moved_ref[order.index(d), (1 + c) * tall : (2 + c) * tall, :]
        for d in range(sources)
        for c in range(per)
    ]
    rest = dot(flat(homes), flat(cands), ((1,), (1,)))
    wide = -(-count // LANES)
    if wide * LANES > count:
        rest = jnp.concatenate([rest, jnp.zeros((sources, wide * LANES - count), f32)], axis=1)
    tail = send - tall
    tails[...] = jnp.zeros_like(tails)
    for k in range(PIECES):
        piece = rest.astype(bf16).astype(f32)
        rest = rest - piece
        for t in range(wide):
            tails[pl.ds(k * wide + t, sources, stride=tail), :] = piece[:, t * LANES : (t + 1) * LANES]
    for k in range(sources):
        out_ref[k] = jnp.concatenate([homes[k], tails[k * tail : (k + 1) * tail, :]], axis=0).astype(bf16)


def finish(home_ref, holds_ref, chosen_ref, precond_ref, scores_ref, wide):
    slots, send, _ = home_ref.shape
    _, flat = precond_ref.shape[1:]
    count = chosen_ref.shape[0]
    tall = flat // LANES
    step = send + 1
    for k in range(slots):
        wide[pl.ds(k * step, send), :] = home_ref[k].astype(f32)
    by_slot = jnp.concatenate([wide[pl.ds(j, slots, stride=step), :].astype(bf16) for j in range(tall)], axis=1)
    precond_ref[0] = dot(holds_ref[...], by_slot).astype(bf16)
    groups = -(-count // LANES)
    parts = []
    for t in range(groups):
        pieces = [wide[pl.ds(tall + k * groups + t, slots, stride=step), :] for k in range(PIECES)]
        parts.append(jnp.sum((pieces[2] + pieces[1]) + pieces[0], axis=0, keepdims=True))
    dense = parts[0] if groups == 1 else jnp.concatenate(parts, axis=1)
    scores_ref[...] = jnp.sum(
        jnp.where(chosen_ref[...] > 0.0, upright(dense, count), 0.0), axis=0, keepdims=True
    )


SMEM = pl.BlockSpec(memory_space=pltpu.SMEM)
HBM = pl.BlockSpec(memory_space=pltpu.HBM)
VMEM = pl.BlockSpec(memory_space=pltpu.VMEM)
PARAMS = pltpu.CompilerParams(vmem_limit_bytes=40 * 1024 * 1024)


def body(
    query_grads,
    cand_grads,
    basis_out,
    basis_in,
    eigvals,
    layer_map,
    cand_rows,
    cand_lists,
    list_lengths,
):
    own, modules, flat = query_grads.shape
    per = cand_grads.shape[0]
    slots = layer_map.shape[0]
    tall = flat // LANES
    side = basis_out.shape[1]
    size = SUBLANES * tall
    count = cand_rows.shape[0]
    height = (own + per) * tall
    send = tall + -(-PIECES * -(-count // LANES) // SUBLANES) * SUBLANES

    def in_hbm(x):
        return pltpu.with_memory_space_constraint(x, pltpu.HBM)

    def swap_over(x, first, stride):
        groups = [order_of(slots, first, stride)]
        return lax.all_to_all(x, "shard", split_axis=0, concat_axis=0, tiled=True, axis_index_groups=groups)

    square = pltpu.VMEM((size, size), bf16)
    operands = (
        query_grads,
        cand_grads,
        layer_map.reshape(1, slots),
        basis_out.reshape(basis_out.shape[1:]),
        basis_in.reshape(basis_in.shape[1:]),
        eigvals.reshape(tall, LANES),
        cand_rows.reshape(1, count),
        cand_lists,
    )
    packed, enter, outer, inner, factor, gather, held, chosen = pl.pallas_call(
        pack,
        out_shape=(
            pltpu.VMEM((slots, height, LANES), bf16),
            square,
            square,
            square,
            pltpu.VMEM((side, LANES), f32),
            square,
            pltpu.VMEM((modules, slots), bf16),
            pltpu.VMEM((count, cand_lists.shape[1]), f32),
        ),
        in_specs=[SMEM] + [HBM] * len(operands),
        out_specs=[VMEM] * 8,
        scratch_shapes=[pltpu.VMEM(x.shape, x.dtype) for x in operands]
        + [pltpu.VMEM((slots * (height + 1), LANES), f32), pltpu.SemaphoreType.DMA((len(operands),))],
        compiler_params=PARAMS,
        name="pack",
    )(list_lengths, *(in_hbm(x) for x in operands))
    moved = swap_over(packed, *orders(slots)[0])
    homes = pl.pallas_call(
        work,
        out_shape=jax.ShapeDtypeStruct((slots, send, LANES), bf16),
        in_specs=[VMEM] * 6,
        out_specs=VMEM,
        scratch_shapes=[pltpu.VMEM((slots * (send - tall), LANES), f32)],
        compiler_params=PARAMS,
        name="work",
    )(moved, enter, outer, inner, factor, gather)
    home = swap_over(homes, *orders(slots)[1])
    return pl.pallas_call(
        finish,
        out_shape=(
            jax.ShapeDtypeStruct(query_grads.shape, bf16),
            jax.ShapeDtypeStruct(cand_lists.shape, f32),
        ),
        in_specs=[VMEM] * 3,
        out_specs=(VMEM, VMEM),
        scratch_shapes=[pltpu.VMEM((slots * (send + 1), LANES), f32)],
        compiler_params=PARAMS,
        name="finish",
    )(home, held, chosen)


def solution(mesh):
    return jax.shard_map(
        body,
        mesh=mesh,
        in_specs=(
            P(("groups", "shard"), None, None),
            P(("groups", "shard"), None, None),
            P("shard", None, None),
            P("shard", None, None),
            P("shard", None),
            P(),
            P("groups"),
            P(("groups", "shard"), None),
            P(("groups", "shard")),
        ),
        out_specs=(P(("groups", "shard"), None, None), P(("groups", "shard"), None)),
        check_vma=False,
    )
```

```python
import jax
import jax.numpy as jnp
from jax import lax
from jax.experimental import pallas as pl
from jax.experimental.pallas import tpu as pltpu
from jax.sharding import PartitionSpec as P

damping = 0.1
LANES = 128
SUBLANES = 8
PIECES = 3
f32, bf16 = jnp.float32, jnp.bfloat16


def iota(shape, axis):
    return lax.broadcasted_iota(jnp.int32, shape, axis)


def dot(a, b, dims=((1,), (0,))):
    return lax.dot_general(a, b, (dims, ((), ())), preferred_element_type=f32)


def mask(condition):
    return condition.astype(f32).astype(bf16)


def ring(place, slots):
    core, middle = place % 2, slots // 2
    up = 4 * (place // 2) + core
    down = 2 * (middle - 1 - 2 * ((place - middle) // 2)) + core
    if isinstance(place, int):
        return up if place < middle else down
    return jnp.where(place < middle, up, down)


def order_of(slots, first, stride):
    start = [ring(k, slots) for k in range(slots)].index(first)
    return [ring((start + stride * k) % slots, slots) for k in range(slots)]


def orders(slots):
    return (slots * 5 // 8, slots - 7), (slots // 2, slots - 1)


def gather_rows(tall):
    size = SUBLANES * tall
    row = iota((size, size), 0)
    return mask(row // SUBLANES + tall * (row % SUBLANES) == iota((size, size), 1))


def half(left, right):
    return jnp.where(iota(left.shape, 1) < LANES // 2, left, right)


def swap(block):
    return pltpu.roll(block, LANES // 2, 1)


def unpaired(block):
    tall = block.shape[0] // 2
    top, low = block[:tall], block[tall:]
    return half(top, swap(low)), half(swap(top), low)


def holds(layer_row, modules, first, stride):
    slots = layer_row.shape[1]
    start = [ring(k, slots) for k in range(slots)].index(first)
    placed = mask(iota((slots, slots), 0) == ring((start + stride * iota((slots, slots), 1)) % slots, slots))
    return dot(mask(iota((modules, slots), 0) == layer_row), placed).astype(bf16)


def block_bases(out_basis, in_basis, eigen):
    side = out_basis.shape[0]
    tall = side // 2
    size = 4 * side

    def spread(basis):
        wide = jnp.concatenate([basis] * 4, axis=1)
        return jnp.concatenate([wide] * 4, axis=0)

    row, column = iota((size, size), 0) // side, iota((size, size), 1) // side
    turn = mask(iota((side, side), 1) == 2 * (iota((side, side), 0) % tall) + iota((side, side), 0) // tall)
    bases = spread(dot(dot(turn, out_basis).astype(bf16), turn, ((1,), (1,))))
    outer = jnp.where(row == column, bases, 0.0).astype(bf16)
    bases = spread(in_basis.astype(f32))
    enter = jnp.where(row == 2 * (column % 2) + column // 2, bases, 0.0).astype(bf16)
    inner = jnp.where(row == column, bases, 0.0).astype(bf16)
    turned = swap(eigen)
    factor = 1.0 / (jnp.concatenate([half(eigen, turned), half(turned, eigen)], axis=0) + damping)
    return enter, outer, inner, factor


def pack(
    length_ref, query_hbm, cand_hbm, layer_hbm, out_basis_hbm, in_basis_hbm, eigen_hbm, rows_hbm, lists_hbm,
    out_ref, enter_ref, outer_ref, inner_ref, factor_ref, gather_ref, holds_ref, chosen_ref,
    query_ref, cand_ref, layer_ref, out_basis_ref, in_basis_ref, eigen_ref, rows_ref, lists_ref, wide, sems,
):
    arrivals = [
        pltpu.make_async_copy(source, target, sems.at[i])
        for i, (source, target) in enumerate(
            (
                (query_hbm, query_ref),
                (cand_hbm, cand_ref),
                (layer_hbm, layer_ref),
                (out_basis_hbm, out_basis_ref),
                (in_basis_hbm, in_basis_ref),
                (eigen_hbm, eigen_ref),
                (rows_hbm, rows_ref),
                (lists_hbm, lists_ref),
            )
        )
    ]
    for arrival in arrivals:
        arrival.start()
    modules, flat = query_ref.shape[1:]
    slots, height, _ = out_ref.shape
    tall = flat // LANES
    step = height + 1
    gather_ref[...] = gather_rows(tall)
    for arrival in arrivals[2:]:
        arrival.wait()
    one_hot = holds(layer_ref[...], modules, *orders(slots)[0])
    holds_ref[...] = holds(layer_ref[...], modules, *orders(slots)[1])
    enter_ref[...], outer_ref[...], inner_ref[...], factor_ref[...] = block_bases(
        out_basis_ref[...], in_basis_ref[...], eigen_ref[...]
    )
    lists = lists_ref[...]
    count, longest = rows_ref.shape[1], lists.shape[1]
    rows = upright(rows_ref[...].astype(f32), count)
    place = jnp.sum(jnp.where(iota((count, longest), 0) == lists, rows, 0.0), axis=0, keepdims=True)
    place = jnp.where(iota((1, longest), 1) < length_ref[0], place.astype(jnp.int32), -1)
    chosen_ref[...] = (iota((count, longest), 0) == place).astype(f32)
    r = 0
    for arrival, ref in zip(arrivals, (query_ref, cand_ref)):
        arrival.wait()
        for row in range(ref.shape[0]):
            by_slot = dot(one_hot, ref[row], ((0,), (0,)))
            for j in range(tall):
                wide[pl.ds(r * tall + j, slots, stride=step), :] = by_slot[:, j * LANES : (j + 1) * LANES]
            r += 1
    for k in range(slots):
        out_ref[k] = wide[pl.ds(k * step, height), :].astype(bf16)


def upright(row, count):
    shape = (count, row.shape[1])
    return jnp.sum(jnp.where(iota(shape, 0) == iota(shape, 1), row, 0.0), axis=1, keepdims=True)


def work(moved_ref, enter_ref, outer_ref, inner_ref, factor_ref, gather_ref, out_ref, tails):
    sources, height, _ = moved_ref.shape
    _, send, _ = out_ref.shape
    size = enter_ref.shape[0]
    side, tall = size // 4, size // SUBLANES
    per = height // tall - 1
    count = sources * per
    pairs = sources // 2
    stacks = pairs // 4
    order, later = (order_of(sources, *each) for each in orders(sources))
    places = [later.index(d) for d in order]
    outer, inner, gather = outer_ref[...], inner_ref[...], gather_ref[...]
    factor = factor_ref[...]

    queries = [jnp.concatenate([moved_ref[2 * p, :tall, :], moved_ref[2 * p + 1, :tall, :]], axis=1) for p in range(pairs)]
    entered = dot(jnp.concatenate(queries, axis=0), enter_ref[...]).astype(bf16)
    columns = []
    for t in range(stacks):
        tiles = []
        for p in range(4 * t, 4 * t + 4):
            rows = entered[p * tall : (p + 1) * tall]
            tiles += [rows[:, :LANES], rows[:, LANES:]]
        columns.append(jnp.concatenate(tiles, axis=0))
    rotated = dot(outer, jnp.concatenate(columns, axis=1), ((0,), (0,)))
    tile = jnp.concatenate([jnp.concatenate([factor] * 4, axis=0)] * 2, axis=1)
    scaled = [
        (rotated[:, t * LANES : (t + 2) * LANES] * tile).astype(bf16) for t in range(0, stacks, 2)
    ]
    returned = dot(jnp.concatenate(scaled, axis=0), inner, ((1,), (1,))).astype(bf16)
    returned = jnp.concatenate([returned[t * size : (t + 1) * size] for t in range(stacks // 2)], axis=1)
    precond = dot(outer, returned).astype(bf16).astype(f32)

    homes = [None] * sources
    for p in range(pairs):
        t, u = p // 4, p % 4
        block = precond[u * side : (u + 1) * side, t * LANES : (t + 1) * LANES]
        homes[places[2 * p]], homes[places[2 * p + 1]] = unpaired(block)

    def flat(blocks):
        groups = [
            jnp.concatenate(blocks[g : g + SUBLANES], axis=0).astype(bf16) for g in range(0, len(blocks), SUBLANES)
        ]
        turned = dot(gather, jnp.concatenate(groups, axis=1))
        return jnp.concatenate(
            [
                jnp.concatenate(
                    [
                        turned[j * SUBLANES : (j + 1) * SUBLANES, g * LANES : (g + 1) * LANES]
                        for g in range(len(groups))
                    ],
                    axis=0,
                ).astype(bf16)
                for j in range(tall)
            ],
            axis=1,
        )

    cands = [
        moved_ref[order.index(d), (1 + c) * tall : (2 + c) * tall, :]
        for d in range(sources)
        for c in range(per)
    ]
    rest = dot(flat(homes), flat(cands), ((1,), (1,)))
    wide = -(-count // LANES)
    if wide * LANES > count:
        rest = jnp.concatenate([rest, jnp.zeros((sources, wide * LANES - count), f32)], axis=1)
    tail = send - tall
    tails[...] = jnp.zeros_like(tails)
    for k in range(PIECES):
        piece = rest.astype(bf16).astype(f32)
        rest = rest - piece
        for t in range(wide):
            tails[pl.ds(k * wide + t, sources, stride=tail), :] = piece[:, t * LANES : (t + 1) * LANES]
    for k in range(sources):
        out_ref[k] = jnp.concatenate([homes[k], tails[k * tail : (k + 1) * tail, :]], axis=0).astype(bf16)


def finish(home_ref, holds_ref, chosen_ref, precond_ref, scores_ref, wide):
    slots, send, _ = home_ref.shape
    _, flat = precond_ref.shape[1:]
    count = chosen_ref.shape[0]
    tall = flat // LANES
    step = send + 1
    for k in range(slots):
        wide[pl.ds(k * step, send), :] = home_ref[k].astype(f32)
    by_slot = jnp.concatenate([wide[pl.ds(j, slots, stride=step), :].astype(bf16) for j in range(tall)], axis=1)
    precond_ref[0] = dot(holds_ref[...], by_slot).astype(bf16)
    groups = -(-count // LANES)
    parts = []
    for t in range(groups):
        pieces = [wide[pl.ds(tall + k * groups + t, slots, stride=step), :] for k in range(PIECES)]
        parts.append(jnp.sum((pieces[2] + pieces[1]) + pieces[0], axis=0, keepdims=True))
    dense = parts[0] if groups == 1 else jnp.concatenate(parts, axis=1)
    scores_ref[...] = jnp.sum(
        jnp.where(chosen_ref[...] > 0.0, upright(dense, count), 0.0), axis=0, keepdims=True
    )


SMEM = pl.BlockSpec(memory_space=pltpu.SMEM)
HBM = pl.BlockSpec(memory_space=pltpu.HBM)
VMEM = pl.BlockSpec(memory_space=pltpu.VMEM)
PARAMS = pltpu.CompilerParams(vmem_limit_bytes=40 * 1024 * 1024)


def body(
    query_grads,
    cand_grads,
    basis_out,
    basis_in,
    eigvals,
    layer_map,
    cand_rows,
    cand_lists,
    list_lengths,
):
    own, modules, flat = query_grads.shape
    per = cand_grads.shape[0]
    slots = layer_map.shape[0]
    tall = flat // LANES
    side = basis_out.shape[1]
    size = SUBLANES * tall
    count = cand_rows.shape[0]
    height = (own + per) * tall
    send = tall + -(-PIECES * -(-count // LANES) // SUBLANES) * SUBLANES

    def in_hbm(x):
        return pltpu.with_memory_space_constraint(x, pltpu.HBM)

    def swap_over(x, first, stride):
        groups = [order_of(slots, first, stride)]
        return lax.all_to_all(x, "shard", split_axis=0, concat_axis=0, tiled=True, axis_index_groups=groups)

    square = pltpu.VMEM((size, size), bf16)
    operands = (
        query_grads,
        cand_grads,
        layer_map.reshape(1, slots),
        basis_out.reshape(basis_out.shape[1:]),
        basis_in.reshape(basis_in.shape[1:]),
        eigvals.reshape(tall, LANES),
        cand_rows.reshape(1, count),
        cand_lists,
    )
    packed, enter, outer, inner, factor, gather, held, chosen = pl.pallas_call(
        pack,
        out_shape=(
            pltpu.VMEM((slots, height, LANES), bf16),
            square,
            square,
            square,
            pltpu.VMEM((side, LANES), f32),
            square,
            pltpu.VMEM((modules, slots), bf16),
            pltpu.VMEM((count, cand_lists.shape[1]), f32),
        ),
        in_specs=[SMEM] + [HBM] * len(operands),
        out_specs=[VMEM] * 8,
        scratch_shapes=[pltpu.VMEM(x.shape, x.dtype) for x in operands]
        + [pltpu.VMEM((slots * (height + 1), LANES), f32), pltpu.SemaphoreType.DMA((len(operands),))],
        compiler_params=PARAMS,
        name="pack",
    )(list_lengths, *(in_hbm(x) for x in operands))
    moved = swap_over(packed, *orders(slots)[0])
    homes = pl.pallas_call(
        work,
        out_shape=jax.ShapeDtypeStruct((slots, send, LANES), bf16),
        in_specs=[VMEM] * 6,
        out_specs=VMEM,
        scratch_shapes=[pltpu.VMEM((slots * (send - tall), LANES), f32)],
        compiler_params=PARAMS,
        name="work",
    )(moved, enter, outer, inner, factor, gather)
    home = swap_over(homes, *orders(slots)[1])
    return pl.pallas_call(
        finish,
        out_shape=(
            jax.ShapeDtypeStruct(query_grads.shape, bf16),
            jax.ShapeDtypeStruct(cand_lists.shape, f32),
        ),
        in_specs=[VMEM] * 3,
        out_specs=(VMEM, VMEM),
        scratch_shapes=[pltpu.VMEM((slots * (send + 1), LANES), f32)],
        compiler_params=PARAMS,
        name="finish",
    )(home, held, chosen)


def solution(mesh):
    return jax.shard_map(
        body,
        mesh=mesh,
        in_specs=(
            P(("groups", "shard"), None, None),
            P(("groups", "shard"), None, None),
            P("shard", None, None),
            P("shard", None, None),
            P("shard", None),
            P(),
            P("groups"),
            P(("groups", "shard"), None),
            P(("groups", "shard")),
        ),
        out_specs=(P(("groups", "shard"), None, None), P(("groups", "shard"), None)),
        check_vma=False,
    )
```

```python
import jax
import jax.numpy as jnp
from jax import lax
from jax.experimental import pallas as pl
from jax.experimental.pallas import tpu as pltpu
from jax.sharding import PartitionSpec as P

damping = 0.1
LANES = 128
SUBLANES = 8
PIECES = 3
f32, bf16 = jnp.float32, jnp.bfloat16


def iota(shape, axis):
    return lax.broadcasted_iota(jnp.int32, shape, axis)


def dot(a, b, dims=((1,), (0,))):
    return lax.dot_general(a, b, (dims, ((), ())), preferred_element_type=f32)


def mask(condition):
    return condition.astype(f32).astype(bf16)


def ring(place, slots):
    core, middle = place % 2, slots // 2
    up = 4 * (place // 2) + core
    down = 2 * (middle - 1 - 2 * ((place - middle) // 2)) + core
    if isinstance(place, int):
        return up if place < middle else down
    return jnp.where(place < middle, up, down)


def order_of(slots, first, stride):
    start = [ring(k, slots) for k in range(slots)].index(first)
    return [ring((start + stride * k) % slots, slots) for k in range(slots)]


def orders(slots):
    return (slots * 5 // 8, slots - 7), (slots - 2, slots - 1)


def gather_rows(tall):
    size = SUBLANES * tall
    row = iota((size, size), 0)
    return mask(row // SUBLANES + tall * (row % SUBLANES) == iota((size, size), 1))


def half(left, right):
    return jnp.where(iota(left.shape, 1) < LANES // 2, left, right)


def swap(block):
    return pltpu.roll(block, LANES // 2, 1)


def unpaired(block):
    tall = block.shape[0] // 2
    top, low = block[:tall], block[tall:]
    return half(top, swap(low)), half(swap(top), low)


def holds(layer_row, modules, first, stride):
    slots = layer_row.shape[1]
    start = [ring(k, slots) for k in range(slots)].index(first)
    placed = mask(iota((slots, slots), 0) == ring((start + stride * iota((slots, slots), 1)) % slots, slots))
    return dot(mask(iota((modules, slots), 0) == layer_row), placed).astype(bf16)


def block_bases(out_basis, in_basis, eigen):
    side = out_basis.shape[0]
    tall = side // 2
    size = 4 * side

    def spread(basis):
        wide = jnp.concatenate([basis] * 4, axis=1)
        return jnp.concatenate([wide] * 4, axis=0)

    row, column = iota((size, size), 0) // side, iota((size, size), 1) // side
    turn = mask(iota((side, side), 1) == 2 * (iota((side, side), 0) % tall) + iota((side, side), 0) // tall)
    bases = spread(dot(dot(turn, out_basis).astype(bf16), turn, ((1,), (1,))))
    outer = jnp.where(row == column, bases, 0.0).astype(bf16)
    bases = spread(in_basis.astype(f32))
    enter = jnp.where(row == 2 * (column % 2) + column // 2, bases, 0.0).astype(bf16)
    inner = jnp.where(row == column, bases, 0.0).astype(bf16)
    turned = swap(eigen)
    factor = 1.0 / (jnp.concatenate([half(eigen, turned), half(turned, eigen)], axis=0) + damping)
    return enter, outer, inner, factor


def pack(
    length_ref, query_hbm, cand_hbm, layer_hbm, out_basis_hbm, in_basis_hbm, eigen_hbm, rows_hbm, lists_hbm,
    out_ref, enter_ref, outer_ref, inner_ref, factor_ref, gather_ref, holds_ref, chosen_ref,
    query_ref, cand_ref, layer_ref, out_basis_ref, in_basis_ref, eigen_ref, rows_ref, lists_ref, wide, sems,
):
    arrivals = [
        pltpu.make_async_copy(source, target, sems.at[i])
        for i, (source, target) in enumerate(
            (
                (query_hbm, query_ref),
                (cand_hbm, cand_ref),
                (layer_hbm, layer_ref),
                (out_basis_hbm, out_basis_ref),
                (in_basis_hbm, in_basis_ref),
                (eigen_hbm, eigen_ref),
                (rows_hbm, rows_ref),
                (lists_hbm, lists_ref),
            )
        )
    ]
    for arrival in arrivals:
        arrival.start()
    modules, flat = query_ref.shape[1:]
    slots, height, _ = out_ref.shape
    tall = flat // LANES
    step = height + 1
    gather_ref[...] = gather_rows(tall)
    for arrival in arrivals[2:]:
        arrival.wait()
    one_hot = holds(layer_ref[...], modules, *orders(slots)[0])
    holds_ref[...] = holds(layer_ref[...], modules, *orders(slots)[1])
    enter_ref[...], outer_ref[...], inner_ref[...], factor_ref[...] = block_bases(
        out_basis_ref[...], in_basis_ref[...], eigen_ref[...]
    )
    lists = lists_ref[...]
    count, longest = rows_ref.shape[1], lists.shape[1]
    rows = upright(rows_ref[...].astype(f32), count)
    place = jnp.sum(jnp.where(iota((count, longest), 0) == lists, rows, 0.0), axis=0, keepdims=True)
    place = jnp.where(iota((1, longest), 1) < length_ref[0], place.astype(jnp.int32), -1)
    chosen_ref[...] = (iota((count, longest), 0) == place).astype(f32)
    r = 0
    for arrival, ref in zip(arrivals, (query_ref, cand_ref)):
        arrival.wait()
        for row in range(ref.shape[0]):
            by_slot = dot(one_hot, ref[row], ((0,), (0,)))
            for j in range(tall):
                wide[pl.ds(r * tall + j, slots, stride=step), :] = by_slot[:, j * LANES : (j + 1) * LANES]
            r += 1
    for k in range(slots):
        out_ref[k] = wide[pl.ds(k * step, height), :].astype(bf16)


def upright(row, count):
    shape = (count, row.shape[1])
    return jnp.sum(jnp.where(iota(shape, 0) == iota(shape, 1), row, 0.0), axis=1, keepdims=True)


def work(moved_ref, enter_ref, outer_ref, inner_ref, factor_ref, gather_ref, out_ref, tails):
    sources, height, _ = moved_ref.shape
    _, send, _ = out_ref.shape
    size = enter_ref.shape[0]
    side, tall = size // 4, size // SUBLANES
    per = height // tall - 1
    count = sources * per
    pairs = sources // 2
    stacks = pairs // 4
    order, later = (order_of(sources, *each) for each in orders(sources))
    places = [later.index(d) for d in order]
    outer, inner, gather = outer_ref[...], inner_ref[...], gather_ref[...]
    factor = factor_ref[...]

    queries = [jnp.concatenate([moved_ref[2 * p, :tall, :], moved_ref[2 * p + 1, :tall, :]], axis=1) for p in range(pairs)]
    entered = dot(jnp.concatenate(queries, axis=0), enter_ref[...]).astype(bf16)
    columns = []
    for t in range(stacks):
        tiles = []
        for p in range(4 * t, 4 * t + 4):
            rows = entered[p * tall : (p + 1) * tall]
            tiles += [rows[:, :LANES], rows[:, LANES:]]
        columns.append(jnp.concatenate(tiles, axis=0))
    rotated = dot(outer, jnp.concatenate(columns, axis=1), ((0,), (0,)))
    tile = jnp.concatenate([jnp.concatenate([factor] * 4, axis=0)] * 2, axis=1)
    scaled = [
        (rotated[:, t * LANES : (t + 2) * LANES] * tile).astype(bf16) for t in range(0, stacks, 2)
    ]
    returned = dot(jnp.concatenate(scaled, axis=0), inner, ((1,), (1,))).astype(bf16)
    returned = jnp.concatenate([returned[t * size : (t + 1) * size] for t in range(stacks // 2)], axis=1)
    precond = dot(outer, returned).astype(bf16).astype(f32)

    homes = [None] * sources
    for p in range(pairs):
        t, u = p // 4, p % 4
        block = precond[u * side : (u + 1) * side, t * LANES : (t + 1) * LANES]
        homes[places[2 * p]], homes[places[2 * p + 1]] = unpaired(block)

    def flat(blocks):
        groups = [
            jnp.concatenate(blocks[g : g + SUBLANES], axis=0).astype(bf16) for g in range(0, len(blocks), SUBLANES)
        ]
        turned = dot(gather, jnp.concatenate(groups, axis=1))
        return jnp.concatenate(
            [
                jnp.concatenate(
                    [
                        turned[j * SUBLANES : (j + 1) * SUBLANES, g * LANES : (g + 1) * LANES]
                        for g in range(len(groups))
                    ],
                    axis=0,
                ).astype(bf16)
                for j in range(tall)
            ],
            axis=1,
        )

    cands = [
        moved_ref[order.index(d), (1 + c) * tall : (2 + c) * tall, :]
        for d in range(sources)
        for c in range(per)
    ]
    rest = dot(flat(homes), flat(cands), ((1,), (1,)))
    wide = -(-count // LANES)
    if wide * LANES > count:
        rest = jnp.concatenate([rest, jnp.zeros((sources, wide * LANES - count), f32)], axis=1)
    tail = send - tall
    tails[...] = jnp.zeros_like(tails)
    for k in range(PIECES):
        piece = rest.astype(bf16).astype(f32)
        rest = rest - piece
        for t in range(wide):
            tails[pl.ds(k * wide + t, sources, stride=tail), :] = piece[:, t * LANES : (t + 1) * LANES]
    for k in range(sources):
        out_ref[k] = jnp.concatenate([homes[k], tails[k * tail : (k + 1) * tail, :]], axis=0).astype(bf16)


def finish(home_ref, holds_ref, chosen_ref, precond_ref, scores_ref, wide):
    slots, send, _ = home_ref.shape
    _, flat = precond_ref.shape[1:]
    count = chosen_ref.shape[0]
    tall = flat // LANES
    step = send + 1
    for k in range(slots):
        wide[pl.ds(k * step, send), :] = home_ref[k].astype(f32)
    by_slot = jnp.concatenate([wide[pl.ds(j, slots, stride=step), :].astype(bf16) for j in range(tall)], axis=1)
    precond_ref[0] = dot(holds_ref[...], by_slot).astype(bf16)
    groups = -(-count // LANES)
    parts = []
    for t in range(groups):
        pieces = [wide[pl.ds(tall + k * groups + t, slots, stride=step), :] for k in range(PIECES)]
        parts.append(jnp.sum((pieces[2] + pieces[1]) + pieces[0], axis=0, keepdims=True))
    dense = parts[0] if groups == 1 else jnp.concatenate(parts, axis=1)
    scores_ref[...] = jnp.sum(
        jnp.where(chosen_ref[...] > 0.0, upright(dense, count), 0.0), axis=0, keepdims=True
    )


SMEM = pl.BlockSpec(memory_space=pltpu.SMEM)
HBM = pl.BlockSpec(memory_space=pltpu.HBM)
VMEM = pl.BlockSpec(memory_space=pltpu.VMEM)
PARAMS = pltpu.CompilerParams(vmem_limit_bytes=40 * 1024 * 1024)


def body(
    query_grads,
    cand_grads,
    basis_out,
    basis_in,
    eigvals,
    layer_map,
    cand_rows,
    cand_lists,
    list_lengths,
):
    own, modules, flat = query_grads.shape
    per = cand_grads.shape[0]
    slots = layer_map.shape[0]
    tall = flat // LANES
    side = basis_out.shape[1]
    size = SUBLANES * tall
    count = cand_rows.shape[0]
    height = (own + per) * tall
    send = tall + -(-PIECES * -(-count // LANES) // SUBLANES) * SUBLANES

    def in_hbm(x):
        return pltpu.with_memory_space_constraint(x, pltpu.HBM)

    def swap_over(x, first, stride):
        groups = [order_of(slots, first, stride)]
        return lax.all_to_all(x, "shard", split_axis=0, concat_axis=0, tiled=True, axis_index_groups=groups)

    square = pltpu.VMEM((size, size), bf16)
    operands = (
        query_grads,
        cand_grads,
        layer_map.reshape(1, slots),
        basis_out.reshape(basis_out.shape[1:]),
        basis_in.reshape(basis_in.shape[1:]),
        eigvals.reshape(tall, LANES),
        cand_rows.reshape(1, count),
        cand_lists,
    )
    packed, enter, outer, inner, factor, gather, held, chosen = pl.pallas_call(
        pack,
        out_shape=(
            pltpu.VMEM((slots, height, LANES), bf16),
            square,
            square,
            square,
            pltpu.VMEM((side, LANES), f32),
            square,
            pltpu.VMEM((modules, slots), bf16),
            pltpu.VMEM((count, cand_lists.shape[1]), f32),
        ),
        in_specs=[SMEM] + [HBM] * len(operands),
        out_specs=[VMEM] * 8,
        scratch_shapes=[pltpu.VMEM(x.shape, x.dtype) for x in operands]
        + [pltpu.VMEM((slots * (height + 1), LANES), f32), pltpu.SemaphoreType.DMA((len(operands),))],
        compiler_params=PARAMS,
        name="pack",
    )(list_lengths, *(in_hbm(x) for x in operands))
    moved = swap_over(packed, *orders(slots)[0])
    homes = pl.pallas_call(
        work,
        out_shape=jax.ShapeDtypeStruct((slots, send, LANES), bf16),
        in_specs=[VMEM] * 6,
        out_specs=VMEM,
        scratch_shapes=[pltpu.VMEM((slots * (send - tall), LANES), f32)],
        compiler_params=PARAMS,
        name="work",
    )(moved, enter, outer, inner, factor, gather)
    home = swap_over(homes, *orders(slots)[1])
    return pl.pallas_call(
        finish,
        out_shape=(
            jax.ShapeDtypeStruct(query_grads.shape, bf16),
            jax.ShapeDtypeStruct(cand_lists.shape, f32),
        ),
        in_specs=[VMEM] * 3,
        out_specs=(VMEM, VMEM),
        scratch_shapes=[pltpu.VMEM((slots * (send + 1), LANES), f32)],
        compiler_params=PARAMS,
        name="finish",
    )(home, held, chosen)


def solution(mesh):
    return jax.shard_map(
        body,
        mesh=mesh,
        in_specs=(
            P(("groups", "shard"), None, None),
            P(("groups", "shard"), None, None),
            P("shard", None, None),
            P("shard", None, None),
            P("shard", None),
            P(),
            P("groups"),
            P(("groups", "shard"), None),
            P(("groups", "shard")),
        ),
        out_specs=(P(("groups", "shard"), None, None), P(("groups", "shard"), None)),
        check_vma=False,
    )
```

```python
import jax
import jax.numpy as jnp
from jax import lax
from jax.experimental import pallas as pl
from jax.experimental.pallas import tpu as pltpu
from jax.sharding import PartitionSpec as P

damping = 0.1
LANES = 128
SUBLANES = 8
PIECES = 3
f32, bf16 = jnp.float32, jnp.bfloat16


def iota(shape, axis):
    return lax.broadcasted_iota(jnp.int32, shape, axis)


def dot(a, b, dims=((1,), (0,))):
    return lax.dot_general(a, b, (dims, ((), ())), preferred_element_type=f32)


def mask(condition):
    return condition.astype(f32).astype(bf16)


def ring(place, slots):
    core, middle = place % 2, slots // 2
    up = 4 * (place // 2) + core
    down = 2 * (middle - 1 - 2 * ((place - middle) // 2)) + core
    if isinstance(place, int):
        return up if place < middle else down
    return jnp.where(place < middle, up, down)


def order_of(slots, first, stride):
    start = [ring(k, slots) for k in range(slots)].index(first)
    return [ring((start + stride * k) % slots, slots) for k in range(slots)]


def orders(slots):
    return (slots - 2, slots - 7), (slots * 5 // 8, slots - 1)


def gather_rows(tall):
    size = SUBLANES * tall
    row = iota((size, size), 0)
    return mask(row // SUBLANES + tall * (row % SUBLANES) == iota((size, size), 1))


def half(left, right):
    return jnp.where(iota(left.shape, 1) < LANES // 2, left, right)


def swap(block):
    return pltpu.roll(block, LANES // 2, 1)


def unpaired(block):
    tall = block.shape[0] // 2
    top, low = block[:tall], block[tall:]
    return half(top, swap(low)), half(swap(top), low)


def holds(layer_row, modules, first, stride):
    slots = layer_row.shape[1]
    start = [ring(k, slots) for k in range(slots)].index(first)
    placed = mask(iota((slots, slots), 0) == ring((start + stride * iota((slots, slots), 1)) % slots, slots))
    return dot(mask(iota((modules, slots), 0) == layer_row), placed).astype(bf16)


def block_bases(out_basis, in_basis, eigen):
    side = out_basis.shape[0]
    tall = side // 2
    size = 4 * side

    def spread(basis):
        wide = jnp.concatenate([basis] * 4, axis=1)
        return jnp.concatenate([wide] * 4, axis=0)

    row, column = iota((size, size), 0) // side, iota((size, size), 1) // side
    turn = mask(iota((side, side), 1) == 2 * (iota((side, side), 0) % tall) + iota((side, side), 0) // tall)
    bases = spread(dot(dot(turn, out_basis).astype(bf16), turn, ((1,), (1,))))
    outer = jnp.where(row == column, bases, 0.0).astype(bf16)
    bases = spread(in_basis.astype(f32))
    enter = jnp.where(row == 2 * (column % 2) + column // 2, bases, 0.0).astype(bf16)
    inner = jnp.where(row == column, bases, 0.0).astype(bf16)
    turned = swap(eigen)
    factor = 1.0 / (jnp.concatenate([half(eigen, turned), half(turned, eigen)], axis=0) + damping)
    return enter, outer, inner, factor


def pack(
    length_ref, query_hbm, cand_hbm, layer_hbm, out_basis_hbm, in_basis_hbm, eigen_hbm, rows_hbm, lists_hbm,
    out_ref, enter_ref, outer_ref, inner_ref, factor_ref, gather_ref, holds_ref, chosen_ref,
    query_ref, cand_ref, layer_ref, out_basis_ref, in_basis_ref, eigen_ref, rows_ref, lists_ref, wide, sems,
):
    arrivals = [
        pltpu.make_async_copy(source, target, sems.at[i])
        for i, (source, target) in enumerate(
            (
                (query_hbm, query_ref),
                (cand_hbm, cand_ref),
                (layer_hbm, layer_ref),
                (out_basis_hbm, out_basis_ref),
                (in_basis_hbm, in_basis_ref),
                (eigen_hbm, eigen_ref),
                (rows_hbm, rows_ref),
                (lists_hbm, lists_ref),
            )
        )
    ]
    for arrival in arrivals:
        arrival.start()
    modules, flat = query_ref.shape[1:]
    slots, height, _ = out_ref.shape
    tall = flat // LANES
    step = height + 1
    gather_ref[...] = gather_rows(tall)
    for arrival in arrivals[2:]:
        arrival.wait()
    one_hot = holds(layer_ref[...], modules, *orders(slots)[0])
    holds_ref[...] = holds(layer_ref[...], modules, *orders(slots)[1])
    enter_ref[...], outer_ref[...], inner_ref[...], factor_ref[...] = block_bases(
        out_basis_ref[...], in_basis_ref[...], eigen_ref[...]
    )
    lists = lists_ref[...]
    count, longest = rows_ref.shape[1], lists.shape[1]
    rows = upright(rows_ref[...].astype(f32), count)
    place = jnp.sum(jnp.where(iota((count, longest), 0) == lists, rows, 0.0), axis=0, keepdims=True)
    place = jnp.where(iota((1, longest), 1) < length_ref[0], place.astype(jnp.int32), -1)
    chosen_ref[...] = (iota((count, longest), 0) == place).astype(f32)
    r = 0
    for arrival, ref in zip(arrivals, (query_ref, cand_ref)):
        arrival.wait()
        for row in range(ref.shape[0]):
            by_slot = dot(one_hot, ref[row], ((0,), (0,)))
            for j in range(tall):
                wide[pl.ds(r * tall + j, slots, stride=step), :] = by_slot[:, j * LANES : (j + 1) * LANES]
            r += 1
    for k in range(slots):
        out_ref[k] = wide[pl.ds(k * step, height), :].astype(bf16)


def upright(row, count):
    shape = (count, row.shape[1])
    return jnp.sum(jnp.where(iota(shape, 0) == iota(shape, 1), row, 0.0), axis=1, keepdims=True)


def work(moved_ref, enter_ref, outer_ref, inner_ref, factor_ref, gather_ref, out_ref, tails):
    sources, height, _ = moved_ref.shape
    _, send, _ = out_ref.shape
    size = enter_ref.shape[0]
    side, tall = size // 4, size // SUBLANES
    per = height // tall - 1
    count = sources * per
    pairs = sources // 2
    stacks = pairs // 4
    order, later = (order_of(sources, *each) for each in orders(sources))
    places = [later.index(d) for d in order]
    outer, inner, gather = outer_ref[...], inner_ref[...], gather_ref[...]
    factor = factor_ref[...]

    queries = [jnp.concatenate([moved_ref[2 * p, :tall, :], moved_ref[2 * p + 1, :tall, :]], axis=1) for p in range(pairs)]
    entered = dot(jnp.concatenate(queries, axis=0), enter_ref[...]).astype(bf16)
    columns = []
    for t in range(stacks):
        tiles = []
        for p in range(4 * t, 4 * t + 4):
            rows = entered[p * tall : (p + 1) * tall]
            tiles += [rows[:, :LANES], rows[:, LANES:]]
        columns.append(jnp.concatenate(tiles, axis=0))
    rotated = dot(outer, jnp.concatenate(columns, axis=1), ((0,), (0,)))
    tile = jnp.concatenate([jnp.concatenate([factor] * 4, axis=0)] * 2, axis=1)
    scaled = [
        (rotated[:, t * LANES : (t + 2) * LANES] * tile).astype(bf16) for t in range(0, stacks, 2)
    ]
    returned = dot(jnp.concatenate(scaled, axis=0), inner, ((1,), (1,))).astype(bf16)
    returned = jnp.concatenate([returned[t * size : (t + 1) * size] for t in range(stacks // 2)], axis=1)
    precond = dot(outer, returned).astype(bf16).astype(f32)

    homes = [None] * sources
    for p in range(pairs):
        t, u = p // 4, p % 4
        block = precond[u * side : (u + 1) * side, t * LANES : (t + 1) * LANES]
        homes[places[2 * p]], homes[places[2 * p + 1]] = unpaired(block)

    def flat(blocks):
        groups = [
            jnp.concatenate(blocks[g : g + SUBLANES], axis=0).astype(bf16) for g in range(0, len(blocks), SUBLANES)
        ]
        turned = dot(gather, jnp.concatenate(groups, axis=1))
        return jnp.concatenate(
            [
                jnp.concatenate(
                    [
                        turned[j * SUBLANES : (j + 1) * SUBLANES, g * LANES : (g + 1) * LANES]
                        for g in range(len(groups))
                    ],
                    axis=0,
                ).astype(bf16)
                for j in range(tall)
            ],
            axis=1,
        )

    cands = [
        moved_ref[order.index(d), (1 + c) * tall : (2 + c) * tall, :]
        for d in range(sources)
        for c in range(per)
    ]
    rest = dot(flat(homes), flat(cands), ((1,), (1,)))
    wide = -(-count // LANES)
    if wide * LANES > count:
        rest = jnp.concatenate([rest, jnp.zeros((sources, wide * LANES - count), f32)], axis=1)
    tail = send - tall
    tails[...] = jnp.zeros_like(tails)
    for k in range(PIECES):
        piece = rest.astype(bf16).astype(f32)
        rest = rest - piece
        for t in range(wide):
            tails[pl.ds(k * wide + t, sources, stride=tail), :] = piece[:, t * LANES : (t + 1) * LANES]
    for k in range(sources):
        out_ref[k] = jnp.concatenate([homes[k], tails[k * tail : (k + 1) * tail, :]], axis=0).astype(bf16)


def finish(home_ref, holds_ref, chosen_ref, precond_ref, scores_ref, wide):
    slots, send, _ = home_ref.shape
    _, flat = precond_ref.shape[1:]
    count = chosen_ref.shape[0]
    tall = flat // LANES
    step = send + 1
    for k in range(slots):
        wide[pl.ds(k * step, send), :] = home_ref[k].astype(f32)
    by_slot = jnp.concatenate([wide[pl.ds(j, slots, stride=step), :].astype(bf16) for j in range(tall)], axis=1)
    precond_ref[0] = dot(holds_ref[...], by_slot).astype(bf16)
    groups = -(-count // LANES)
    parts = []
    for t in range(groups):
        pieces = [wide[pl.ds(tall + k * groups + t, slots, stride=step), :] for k in range(PIECES)]
        parts.append(jnp.sum((pieces[2] + pieces[1]) + pieces[0], axis=0, keepdims=True))
    dense = parts[0] if groups == 1 else jnp.concatenate(parts, axis=1)
    scores_ref[...] = jnp.sum(
        jnp.where(chosen_ref[...] > 0.0, upright(dense, count), 0.0), axis=0, keepdims=True
    )


SMEM = pl.BlockSpec(memory_space=pltpu.SMEM)
HBM = pl.BlockSpec(memory_space=pltpu.HBM)
VMEM = pl.BlockSpec(memory_space=pltpu.VMEM)
PARAMS = pltpu.CompilerParams(vmem_limit_bytes=40 * 1024 * 1024)


def body(
    query_grads,
    cand_grads,
    basis_out,
    basis_in,
    eigvals,
    layer_map,
    cand_rows,
    cand_lists,
    list_lengths,
):
    own, modules, flat = query_grads.shape
    per = cand_grads.shape[0]
    slots = layer_map.shape[0]
    tall = flat // LANES
    side = basis_out.shape[1]
    size = SUBLANES * tall
    count = cand_rows.shape[0]
    height = (own + per) * tall
    send = tall + -(-PIECES * -(-count // LANES) // SUBLANES) * SUBLANES

    def in_hbm(x):
        return pltpu.with_memory_space_constraint(x, pltpu.HBM)

    def swap_over(x, first, stride):
        groups = [order_of(slots, first, stride)]
        return lax.all_to_all(x, "shard", split_axis=0, concat_axis=0, tiled=True, axis_index_groups=groups)

    square = pltpu.VMEM((size, size), bf16)
    operands = (
        query_grads,
        cand_grads,
        layer_map.reshape(1, slots),
        basis_out.reshape(basis_out.shape[1:]),
        basis_in.reshape(basis_in.shape[1:]),
        eigvals.reshape(tall, LANES),
        cand_rows.reshape(1, count),
        cand_lists,
    )
    packed, enter, outer, inner, factor, gather, held, chosen = pl.pallas_call(
        pack,
        out_shape=(
            pltpu.VMEM((slots, height, LANES), bf16),
            square,
            square,
            square,
            pltpu.VMEM((side, LANES), f32),
            square,
            pltpu.VMEM((modules, slots), bf16),
            pltpu.VMEM((count, cand_lists.shape[1]), f32),
        ),
        in_specs=[SMEM] + [HBM] * len(operands),
        out_specs=[VMEM] * 8,
        scratch_shapes=[pltpu.VMEM(x.shape, x.dtype) for x in operands]
        + [pltpu.VMEM((slots * (height + 1), LANES), f32), pltpu.SemaphoreType.DMA((len(operands),))],
        compiler_params=PARAMS,
        name="pack",
    )(list_lengths, *(in_hbm(x) for x in operands))
    moved = swap_over(packed, *orders(slots)[0])
    homes = pl.pallas_call(
        work,
        out_shape=jax.ShapeDtypeStruct((slots, send, LANES), bf16),
        in_specs=[VMEM] * 6,
        out_specs=VMEM,
        scratch_shapes=[pltpu.VMEM((slots * (send - tall), LANES), f32)],
        compiler_params=PARAMS,
        name="work",
    )(moved, enter, outer, inner, factor, gather)
    home = swap_over(homes, *orders(slots)[1])
    return pl.pallas_call(
        finish,
        out_shape=(
            jax.ShapeDtypeStruct(query_grads.shape, bf16),
            jax.ShapeDtypeStruct(cand_lists.shape, f32),
        ),
        in_specs=[VMEM] * 3,
        out_specs=(VMEM, VMEM),
        scratch_shapes=[pltpu.VMEM((slots * (send + 1), LANES), f32)],
        compiler_params=PARAMS,
        name="finish",
    )(home, held, chosen)


def solution(mesh):
    return jax.shard_map(
        body,
        mesh=mesh,
        in_specs=(
            P(("groups", "shard"), None, None),
            P(("groups", "shard"), None, None),
            P("shard", None, None),
            P("shard", None, None),
            P("shard", None),
            P(),
            P("groups"),
            P(("groups", "shard"), None),
            P(("groups", "shard")),
        ),
        out_specs=(P(("groups", "shard"), None, None), P(("groups", "shard"), None)),
        check_vma=False,
    )
```

```python
import jax
import jax.numpy as jnp
from jax import lax
from jax.experimental import pallas as pl
from jax.experimental.pallas import tpu as pltpu
from jax.sharding import PartitionSpec as P

damping = 0.1
LANES = 128
SUBLANES = 8
PIECES = 3
f32, bf16 = jnp.float32, jnp.bfloat16


def iota(shape, axis):
    return lax.broadcasted_iota(jnp.int32, shape, axis)


def dot(a, b, dims=((1,), (0,))):
    return lax.dot_general(a, b, (dims, ((), ())), preferred_element_type=f32)


def mask(condition):
    return condition.astype(f32).astype(bf16)


def ring(place, slots):
    core, middle = place % 2, slots // 2
    up = 4 * (place // 2) + core
    down = 2 * (middle - 1 - 2 * ((place - middle) // 2)) + core
    if isinstance(place, int):
        return up if place < middle else down
    return jnp.where(place < middle, up, down)


def order_of(slots, first, stride):
    start = [ring(k, slots) for k in range(slots)].index(first)
    return [ring((start + stride * k) % slots, slots) for k in range(slots)]


def orders(slots):
    return (slots // 2, slots - 7), (slots * 5 // 8, slots - 1)


def gather_rows(tall):
    size = SUBLANES * tall
    row = iota((size, size), 0)
    return mask(row // SUBLANES + tall * (row % SUBLANES) == iota((size, size), 1))


def half(left, right):
    return jnp.where(iota(left.shape, 1) < LANES // 2, left, right)


def swap(block):
    return pltpu.roll(block, LANES // 2, 1)


def unpaired(block):
    tall = block.shape[0] // 2
    top, low = block[:tall], block[tall:]
    return half(top, swap(low)), half(swap(top), low)


def holds(layer_row, modules, first, stride):
    slots = layer_row.shape[1]
    start = [ring(k, slots) for k in range(slots)].index(first)
    placed = mask(iota((slots, slots), 0) == ring((start + stride * iota((slots, slots), 1)) % slots, slots))
    return dot(mask(iota((modules, slots), 0) == layer_row), placed).astype(bf16)


def block_bases(out_basis, in_basis, eigen):
    side = out_basis.shape[0]
    tall = side // 2
    size = 4 * side

    def spread(basis):
        wide = jnp.concatenate([basis] * 4, axis=1)
        return jnp.concatenate([wide] * 4, axis=0)

    row, column = iota((size, size), 0) // side, iota((size, size), 1) // side
    turn = mask(iota((side, side), 1) == 2 * (iota((side, side), 0) % tall) + iota((side, side), 0) // tall)
    bases = spread(dot(dot(turn, out_basis).astype(bf16), turn, ((1,), (1,))))
    outer = jnp.where(row == column, bases, 0.0).astype(bf16)
    bases = spread(in_basis.astype(f32))
    enter = jnp.where(row == 2 * (column % 2) + column // 2, bases, 0.0).astype(bf16)
    inner = jnp.where(row == column, bases, 0.0).astype(bf16)
    turned = swap(eigen)
    factor = 1.0 / (jnp.concatenate([half(eigen, turned), half(turned, eigen)], axis=0) + damping)
    return enter, outer, inner, factor


def pack(
    length_ref, query_hbm, cand_hbm, layer_hbm, out_basis_hbm, in_basis_hbm, eigen_hbm, rows_hbm, lists_hbm,
    out_ref, enter_ref, outer_ref, inner_ref, factor_ref, gather_ref, holds_ref, chosen_ref,
    query_ref, cand_ref, layer_ref, out_basis_ref, in_basis_ref, eigen_ref, rows_ref, lists_ref, wide, sems,
):
    arrivals = [
        pltpu.make_async_copy(source, target, sems.at[i])
        for i, (source, target) in enumerate(
            (
                (query_hbm, query_ref),
                (cand_hbm, cand_ref),
                (layer_hbm, layer_ref),
                (out_basis_hbm, out_basis_ref),
                (in_basis_hbm, in_basis_ref),
                (eigen_hbm, eigen_ref),
                (rows_hbm, rows_ref),
                (lists_hbm, lists_ref),
            )
        )
    ]
    for arrival in arrivals:
        arrival.start()
    modules, flat = query_ref.shape[1:]
    slots, height, _ = out_ref.shape
    tall = flat // LANES
    step = height + 1
    gather_ref[...] = gather_rows(tall)
    for arrival in arrivals[2:]:
        arrival.wait()
    one_hot = holds(layer_ref[...], modules, *orders(slots)[0])
    holds_ref[...] = holds(layer_ref[...], modules, *orders(slots)[1])
    enter_ref[...], outer_ref[...], inner_ref[...], factor_ref[...] = block_bases(
        out_basis_ref[...], in_basis_ref[...], eigen_ref[...]
    )
    lists = lists_ref[...]
    count, longest = rows_ref.shape[1], lists.shape[1]
    rows = upright(rows_ref[...].astype(f32), count)
    place = jnp.sum(jnp.where(iota((count, longest), 0) == lists, rows, 0.0), axis=0, keepdims=True)
    place = jnp.where(iota((1, longest), 1) < length_ref[0], place.astype(jnp.int32), -1)
    chosen_ref[...] = (iota((count, longest), 0) == place).astype(f32)
    r = 0
    for arrival, ref in zip(arrivals, (query_ref, cand_ref)):
        arrival.wait()
        for row in range(ref.shape[0]):
            by_slot = dot(one_hot, ref[row], ((0,), (0,)))
            for j in range(tall):
                wide[pl.ds(r * tall + j, slots, stride=step), :] = by_slot[:, j * LANES : (j + 1) * LANES]
            r += 1
    for k in range(slots):
        out_ref[k] = wide[pl.ds(k * step, height), :].astype(bf16)


def upright(row, count):
    shape = (count, row.shape[1])
    return jnp.sum(jnp.where(iota(shape, 0) == iota(shape, 1), row, 0.0), axis=1, keepdims=True)


def work(moved_ref, enter_ref, outer_ref, inner_ref, factor_ref, gather_ref, out_ref, tails):
    sources, height, _ = moved_ref.shape
    _, send, _ = out_ref.shape
    size = enter_ref.shape[0]
    side, tall = size // 4, size // SUBLANES
    per = height // tall - 1
    count = sources * per
    pairs = sources // 2
    stacks = pairs // 4
    order, later = (order_of(sources, *each) for each in orders(sources))
    places = [later.index(d) for d in order]
    outer, inner, gather = outer_ref[...], inner_ref[...], gather_ref[...]
    factor = factor_ref[...]

    queries = [jnp.concatenate([moved_ref[2 * p, :tall, :], moved_ref[2 * p + 1, :tall, :]], axis=1) for p in range(pairs)]
    entered = dot(jnp.concatenate(queries, axis=0), enter_ref[...]).astype(bf16)
    columns = []
    for t in range(stacks):
        tiles = []
        for p in range(4 * t, 4 * t + 4):
            rows = entered[p * tall : (p + 1) * tall]
            tiles += [rows[:, :LANES], rows[:, LANES:]]
        columns.append(jnp.concatenate(tiles, axis=0))
    rotated = dot(outer, jnp.concatenate(columns, axis=1), ((0,), (0,)))
    tile = jnp.concatenate([jnp.concatenate([factor] * 4, axis=0)] * 2, axis=1)
    scaled = [
        (rotated[:, t * LANES : (t + 2) * LANES] * tile).astype(bf16) for t in range(0, stacks, 2)
    ]
    returned = dot(jnp.concatenate(scaled, axis=0), inner, ((1,), (1,))).astype(bf16)
    returned = jnp.concatenate([returned[t * size : (t + 1) * size] for t in range(stacks // 2)], axis=1)
    precond = dot(outer, returned).astype(bf16).astype(f32)

    homes = [None] * sources
    for p in range(pairs):
        t, u = p // 4, p % 4
        block = precond[u * side : (u + 1) * side, t * LANES : (t + 1) * LANES]
        homes[places[2 * p]], homes[places[2 * p + 1]] = unpaired(block)

    def flat(blocks):
        groups = [
            jnp.concatenate(blocks[g : g + SUBLANES], axis=0).astype(bf16) for g in range(0, len(blocks), SUBLANES)
        ]
        turned = dot(gather, jnp.concatenate(groups, axis=1))
        return jnp.concatenate(
            [
                jnp.concatenate(
                    [
                        turned[j * SUBLANES : (j + 1) * SUBLANES, g * LANES : (g + 1) * LANES]
                        for g in range(len(groups))
                    ],
                    axis=0,
                ).astype(bf16)
                for j in range(tall)
            ],
            axis=1,
        )

    cands = [
        moved_ref[order.index(d), (1 + c) * tall : (2 + c) * tall, :]
        for d in range(sources)
        for c in range(per)
    ]
    rest = dot(flat(homes), flat(cands), ((1,), (1,)))
    wide = -(-count // LANES)
    if wide * LANES > count:
        rest = jnp.concatenate([rest, jnp.zeros((sources, wide * LANES - count), f32)], axis=1)
    tail = send - tall
    tails[...] = jnp.zeros_like(tails)
    for k in range(PIECES):
        piece = rest.astype(bf16).astype(f32)
        rest = rest - piece
        for t in range(wide):
            tails[pl.ds(k * wide + t, sources, stride=tail), :] = piece[:, t * LANES : (t + 1) * LANES]
    for k in range(sources):
        out_ref[k] = jnp.concatenate([homes[k], tails[k * tail : (k + 1) * tail, :]], axis=0).astype(bf16)


def finish(home_ref, holds_ref, chosen_ref, precond_ref, scores_ref, wide):
    slots, send, _ = home_ref.shape
    _, flat = precond_ref.shape[1:]
    count = chosen_ref.shape[0]
    tall = flat // LANES
    step = send + 1
    for k in range(slots):
        wide[pl.ds(k * step, send), :] = home_ref[k].astype(f32)
    by_slot = jnp.concatenate([wide[pl.ds(j, slots, stride=step), :].astype(bf16) for j in range(tall)], axis=1)
    precond_ref[0] = dot(holds_ref[...], by_slot).astype(bf16)
    groups = -(-count // LANES)
    parts = []
    for t in range(groups):
        pieces = [wide[pl.ds(tall + k * groups + t, slots, stride=step), :] for k in range(PIECES)]
        parts.append(jnp.sum((pieces[2] + pieces[1]) + pieces[0], axis=0, keepdims=True))
    dense = parts[0] if groups == 1 else jnp.concatenate(parts, axis=1)
    scores_ref[...] = jnp.sum(
        jnp.where(chosen_ref[...] > 0.0, upright(dense, count), 0.0), axis=0, keepdims=True
    )


SMEM = pl.BlockSpec(memory_space=pltpu.SMEM)
HBM = pl.BlockSpec(memory_space=pltpu.HBM)
VMEM = pl.BlockSpec(memory_space=pltpu.VMEM)
PARAMS = pltpu.CompilerParams(vmem_limit_bytes=40 * 1024 * 1024)


def body(
    query_grads,
    cand_grads,
    basis_out,
    basis_in,
    eigvals,
    layer_map,
    cand_rows,
    cand_lists,
    list_lengths,
):
    own, modules, flat = query_grads.shape
    per = cand_grads.shape[0]
    slots = layer_map.shape[0]
    tall = flat // LANES
    side = basis_out.shape[1]
    size = SUBLANES * tall
    count = cand_rows.shape[0]
    height = (own + per) * tall
    send = tall + -(-PIECES * -(-count // LANES) // SUBLANES) * SUBLANES

    def in_hbm(x):
        return pltpu.with_memory_space_constraint(x, pltpu.HBM)

    def swap_over(x, first, stride):
        groups = [order_of(slots, first, stride)]
        return lax.all_to_all(x, "shard", split_axis=0, concat_axis=0, tiled=True, axis_index_groups=groups)

    square = pltpu.VMEM((size, size), bf16)
    operands = (
        query_grads,
        cand_grads,
        layer_map.reshape(1, slots),
        basis_out.reshape(basis_out.shape[1:]),
        basis_in.reshape(basis_in.shape[1:]),
        eigvals.reshape(tall, LANES),
        cand_rows.reshape(1, count),
        cand_lists,
    )
    packed, enter, outer, inner, factor, gather, held, chosen = pl.pallas_call(
        pack,
        out_shape=(
            pltpu.VMEM((slots, height, LANES), bf16),
            square,
            square,
            square,
            pltpu.VMEM((side, LANES), f32),
            square,
            pltpu.VMEM((modules, slots), bf16),
            pltpu.VMEM((count, cand_lists.shape[1]), f32),
        ),
        in_specs=[SMEM] + [HBM] * len(operands),
        out_specs=[VMEM] * 8,
        scratch_shapes=[pltpu.VMEM(x.shape, x.dtype) for x in operands]
        + [pltpu.VMEM((slots * (height + 1), LANES), f32), pltpu.SemaphoreType.DMA((len(operands),))],
        compiler_params=PARAMS,
        name="pack",
    )(list_lengths, *(in_hbm(x) for x in operands))
    moved = swap_over(packed, *orders(slots)[0])
    homes = pl.pallas_call(
        work,
        out_shape=jax.ShapeDtypeStruct((slots, send, LANES), bf16),
        in_specs=[VMEM] * 6,
        out_specs=VMEM,
        scratch_shapes=[pltpu.VMEM((slots * (send - tall), LANES), f32)],
        compiler_params=PARAMS,
        name="work",
    )(moved, enter, outer, inner, factor, gather)
    home = swap_over(homes, *orders(slots)[1])
    return pl.pallas_call(
        finish,
        out_shape=(
            jax.ShapeDtypeStruct(query_grads.shape, bf16),
            jax.ShapeDtypeStruct(cand_lists.shape, f32),
        ),
        in_specs=[VMEM] * 3,
        out_specs=(VMEM, VMEM),
        scratch_shapes=[pltpu.VMEM((slots * (send + 1), LANES), f32)],
        compiler_params=PARAMS,
        name="finish",
    )(home, held, chosen)


def solution(mesh):
    return jax.shard_map(
        body,
        mesh=mesh,
        in_specs=(
            P(("groups", "shard"), None, None),
            P(("groups", "shard"), None, None),
            P("shard", None, None),
            P("shard", None, None),
            P("shard", None),
            P(),
            P("groups"),
            P(("groups", "shard"), None),
            P(("groups", "shard")),
        ),
        out_specs=(P(("groups", "shard"), None, None), P(("groups", "shard"), None)),
        check_vma=False,
    )
```

```python
import jax
import jax.numpy as jnp
from jax import lax
from jax.experimental import pallas as pl
from jax.experimental.pallas import tpu as pltpu
from jax.sharding import PartitionSpec as P

damping = 0.1
LANES = 128
SUBLANES = 8
PIECES = 3
f32, bf16 = jnp.float32, jnp.bfloat16


def iota(shape, axis):
    return lax.broadcasted_iota(jnp.int32, shape, axis)


def dot(a, b, dims=((1,), (0,))):
    return lax.dot_general(a, b, (dims, ((), ())), preferred_element_type=f32)


def mask(condition):
    return condition.astype(f32).astype(bf16)


def ring(place, slots):
    core, middle = place % 2, slots // 2
    up = 4 * (place // 2) + core
    down = 2 * (middle - 1 - 2 * ((place - middle) // 2)) + core
    if isinstance(place, int):
        return up if place < middle else down
    return jnp.where(place < middle, up, down)


def order_of(slots, first, stride):
    start = [ring(k, slots) for k in range(slots)].index(first)
    return [ring((start + stride * k) % slots, slots) for k in range(slots)]


def orders(slots):
    return (slots * 5 // 8, slots - 5), (slots * 5 // 8, slots - 1)


def gather_rows(tall):
    size = SUBLANES * tall
    row = iota((size, size), 0)
    return mask(row // SUBLANES + tall * (row % SUBLANES) == iota((size, size), 1))


def half(left, right):
    return jnp.where(iota(left.shape, 1) < LANES // 2, left, right)


def swap(block):
    return pltpu.roll(block, LANES // 2, 1)


def unpaired(block):
    tall = block.shape[0] // 2
    top, low = block[:tall], block[tall:]
    return half(top, swap(low)), half(swap(top), low)


def holds(layer_row, modules, first, stride):
    slots = layer_row.shape[1]
    start = [ring(k, slots) for k in range(slots)].index(first)
    placed = mask(iota((slots, slots), 0) == ring((start + stride * iota((slots, slots), 1)) % slots, slots))
    return dot(mask(iota((modules, slots), 0) == layer_row), placed).astype(bf16)


def block_bases(out_basis, in_basis, eigen):
    side = out_basis.shape[0]
    tall = side // 2
    size = 4 * side

    def spread(basis):
        wide = jnp.concatenate([basis] * 4, axis=1)
        return jnp.concatenate([wide] * 4, axis=0)

    row, column = iota((size, size), 0) // side, iota((size, size), 1) // side
    turn = mask(iota((side, side), 1) == 2 * (iota((side, side), 0) % tall) + iota((side, side), 0) // tall)
    bases = spread(dot(dot(turn, out_basis).astype(bf16), turn, ((1,), (1,))))
    outer = jnp.where(row == column, bases, 0.0).astype(bf16)
    bases = spread(in_basis.astype(f32))
    enter = jnp.where(row == 2 * (column % 2) + column // 2, bases, 0.0).astype(bf16)
    inner = jnp.where(row == column, bases, 0.0).astype(bf16)
    turned = swap(eigen)
    factor = 1.0 / (jnp.concatenate([half(eigen, turned), half(turned, eigen)], axis=0) + damping)
    return enter, outer, inner, factor


def pack(
    length_ref, query_hbm, cand_hbm, layer_hbm, out_basis_hbm, in_basis_hbm, eigen_hbm, rows_hbm, lists_hbm,
    out_ref, enter_ref, outer_ref, inner_ref, factor_ref, gather_ref, holds_ref, chosen_ref,
    query_ref, cand_ref, layer_ref, out_basis_ref, in_basis_ref, eigen_ref, rows_ref, lists_ref, wide, sems,
):
    arrivals = [
        pltpu.make_async_copy(source, target, sems.at[i])
        for i, (source, target) in enumerate(
            (
                (query_hbm, query_ref),
                (cand_hbm, cand_ref),
                (layer_hbm, layer_ref),
                (out_basis_hbm, out_basis_ref),
                (in_basis_hbm, in_basis_ref),
                (eigen_hbm, eigen_ref),
                (rows_hbm, rows_ref),
                (lists_hbm, lists_ref),
            )
        )
    ]
    for arrival in arrivals:
        arrival.start()
    modules, flat = query_ref.shape[1:]
    slots, height, _ = out_ref.shape
    tall = flat // LANES
    step = height + 1
    gather_ref[...] = gather_rows(tall)
    for arrival in arrivals[2:]:
        arrival.wait()
    one_hot = holds(layer_ref[...], modules, *orders(slots)[0])
    holds_ref[...] = holds(layer_ref[...], modules, *orders(slots)[1])
    enter_ref[...], outer_ref[...], inner_ref[...], factor_ref[...] = block_bases(
        out_basis_ref[...], in_basis_ref[...], eigen_ref[...]
    )
    lists = lists_ref[...]
    count, longest = rows_ref.shape[1], lists.shape[1]
    rows = upright(rows_ref[...].astype(f32), count)
    place = jnp.sum(jnp.where(iota((count, longest), 0) == lists, rows, 0.0), axis=0, keepdims=True)
    place = jnp.where(iota((1, longest), 1) < length_ref[0], place.astype(jnp.int32), -1)
    chosen_ref[...] = (iota((count, longest), 0) == place).astype(f32)
    r = 0
    for arrival, ref in zip(arrivals, (query_ref, cand_ref)):
        arrival.wait()
        for row in range(ref.shape[0]):
            by_slot = dot(one_hot, ref[row], ((0,), (0,)))
            for j in range(tall):
                wide[pl.ds(r * tall + j, slots, stride=step), :] = by_slot[:, j * LANES : (j + 1) * LANES]
            r += 1
    for k in range(slots):
        out_ref[k] = wide[pl.ds(k * step, height), :].astype(bf16)


def upright(row, count):
    shape = (count, row.shape[1])
    return jnp.sum(jnp.where(iota(shape, 0) == iota(shape, 1), row, 0.0), axis=1, keepdims=True)


def work(moved_ref, enter_ref, outer_ref, inner_ref, factor_ref, gather_ref, out_ref, tails):
    sources, height, _ = moved_ref.shape
    _, send, _ = out_ref.shape
    size = enter_ref.shape[0]
    side, tall = size // 4, size // SUBLANES
    per = height // tall - 1
    count = sources * per
    pairs = sources // 2
    stacks = pairs // 4
    order, later = (order_of(sources, *each) for each in orders(sources))
    places = [later.index(d) for d in order]
    outer, inner, gather = outer_ref[...], inner_ref[...], gather_ref[...]
    factor = factor_ref[...]

    queries = [jnp.concatenate([moved_ref[2 * p, :tall, :], moved_ref[2 * p + 1, :tall, :]], axis=1) for p in range(pairs)]
    entered = dot(jnp.concatenate(queries, axis=0), enter_ref[...]).astype(bf16)
    columns = []
    for t in range(stacks):
        tiles = []
        for p in range(4 * t, 4 * t + 4):
            rows = entered[p * tall : (p + 1) * tall]
            tiles += [rows[:, :LANES], rows[:, LANES:]]
        columns.append(jnp.concatenate(tiles, axis=0))
    rotated = dot(outer, jnp.concatenate(columns, axis=1), ((0,), (0,)))
    tile = jnp.concatenate([jnp.concatenate([factor] * 4, axis=0)] * 2, axis=1)
    scaled = [
        (rotated[:, t * LANES : (t + 2) * LANES] * tile).astype(bf16) for t in range(0, stacks, 2)
    ]
    returned = dot(jnp.concatenate(scaled, axis=0), inner, ((1,), (1,))).astype(bf16)
    returned = jnp.concatenate([returned[t * size : (t + 1) * size] for t in range(stacks // 2)], axis=1)
    precond = dot(outer, returned).astype(bf16).astype(f32)

    homes = [None] * sources
    for p in range(pairs):
        t, u = p // 4, p % 4
        block = precond[u * side : (u + 1) * side, t * LANES : (t + 1) * LANES]
        homes[places[2 * p]], homes[places[2 * p + 1]] = unpaired(block)

    def flat(blocks):
        groups = [
            jnp.concatenate(blocks[g : g + SUBLANES], axis=0).astype(bf16) for g in range(0, len(blocks), SUBLANES)
        ]
        turned = dot(gather, jnp.concatenate(groups, axis=1))
        return jnp.concatenate(
            [
                jnp.concatenate(
                    [
                        turned[j * SUBLANES : (j + 1) * SUBLANES, g * LANES : (g + 1) * LANES]
                        for g in range(len(groups))
                    ],
                    axis=0,
                ).astype(bf16)
                for j in range(tall)
            ],
            axis=1,
        )

    cands = [
        moved_ref[order.index(d), (1 + c) * tall : (2 + c) * tall, :]
        for d in range(sources)
        for c in range(per)
    ]
    rest = dot(flat(homes), flat(cands), ((1,), (1,)))
    wide = -(-count // LANES)
    if wide * LANES > count:
        rest = jnp.concatenate([rest, jnp.zeros((sources, wide * LANES - count), f32)], axis=1)
    tail = send - tall
    tails[...] = jnp.zeros_like(tails)
    for k in range(PIECES):
        piece = rest.astype(bf16).astype(f32)
        rest = rest - piece
        for t in range(wide):
            tails[pl.ds(k * wide + t, sources, stride=tail), :] = piece[:, t * LANES : (t + 1) * LANES]
    for k in range(sources):
        out_ref[k] = jnp.concatenate([homes[k], tails[k * tail : (k + 1) * tail, :]], axis=0).astype(bf16)


def finish(home_ref, holds_ref, chosen_ref, precond_ref, scores_ref, wide):
    slots, send, _ = home_ref.shape
    _, flat = precond_ref.shape[1:]
    count = chosen_ref.shape[0]
    tall = flat // LANES
    step = send + 1
    for k in range(slots):
        wide[pl.ds(k * step, send), :] = home_ref[k].astype(f32)
    by_slot = jnp.concatenate([wide[pl.ds(j, slots, stride=step), :].astype(bf16) for j in range(tall)], axis=1)
    precond_ref[0] = dot(holds_ref[...], by_slot).astype(bf16)
    groups = -(-count // LANES)
    parts = []
    for t in range(groups):
        pieces = [wide[pl.ds(tall + k * groups + t, slots, stride=step), :] for k in range(PIECES)]
        parts.append(jnp.sum((pieces[2] + pieces[1]) + pieces[0], axis=0, keepdims=True))
    dense = parts[0] if groups == 1 else jnp.concatenate(parts, axis=1)
    scores_ref[...] = jnp.sum(
        jnp.where(chosen_ref[...] > 0.0, upright(dense, count), 0.0), axis=0, keepdims=True
    )


SMEM = pl.BlockSpec(memory_space=pltpu.SMEM)
HBM = pl.BlockSpec(memory_space=pltpu.HBM)
VMEM = pl.BlockSpec(memory_space=pltpu.VMEM)
PARAMS = pltpu.CompilerParams(vmem_limit_bytes=40 * 1024 * 1024)


def body(
    query_grads,
    cand_grads,
    basis_out,
    basis_in,
    eigvals,
    layer_map,
    cand_rows,
    cand_lists,
    list_lengths,
):
    own, modules, flat = query_grads.shape
    per = cand_grads.shape[0]
    slots = layer_map.shape[0]
    tall = flat // LANES
    side = basis_out.shape[1]
    size = SUBLANES * tall
    count = cand_rows.shape[0]
    height = (own + per) * tall
    send = tall + -(-PIECES * -(-count // LANES) // SUBLANES) * SUBLANES

    def in_hbm(x):
        return pltpu.with_memory_space_constraint(x, pltpu.HBM)

    def swap_over(x, first, stride):
        groups = [order_of(slots, first, stride)]
        return lax.all_to_all(x, "shard", split_axis=0, concat_axis=0, tiled=True, axis_index_groups=groups)

    square = pltpu.VMEM((size, size), bf16)
    operands = (
        query_grads,
        cand_grads,
        layer_map.reshape(1, slots),
        basis_out.reshape(basis_out.shape[1:]),
        basis_in.reshape(basis_in.shape[1:]),
        eigvals.reshape(tall, LANES),
        cand_rows.reshape(1, count),
        cand_lists,
    )
    packed, enter, outer, inner, factor, gather, held, chosen = pl.pallas_call(
        pack,
        out_shape=(
            pltpu.VMEM((slots, height, LANES), bf16),
            square,
            square,
            square,
            pltpu.VMEM((side, LANES), f32),
            square,
            pltpu.VMEM((modules, slots), bf16),
            pltpu.VMEM((count, cand_lists.shape[1]), f32),
        ),
        in_specs=[SMEM] + [HBM] * len(operands),
        out_specs=[VMEM] * 8,
        scratch_shapes=[pltpu.VMEM(x.shape, x.dtype) for x in operands]
        + [pltpu.VMEM((slots * (height + 1), LANES), f32), pltpu.SemaphoreType.DMA((len(operands),))],
        compiler_params=PARAMS,
        name="pack",
    )(list_lengths, *(in_hbm(x) for x in operands))
    moved = swap_over(packed, *orders(slots)[0])
    homes = pl.pallas_call(
        work,
        out_shape=jax.ShapeDtypeStruct((slots, send, LANES), bf16),
        in_specs=[VMEM] * 6,
        out_specs=VMEM,
        scratch_shapes=[pltpu.VMEM((slots * (send - tall), LANES), f32)],
        compiler_params=PARAMS,
        name="work",
    )(moved, enter, outer, inner, factor, gather)
    home = swap_over(homes, *orders(slots)[1])
    return pl.pallas_call(
        finish,
        out_shape=(
            jax.ShapeDtypeStruct(query_grads.shape, bf16),
            jax.ShapeDtypeStruct(cand_lists.shape, f32),
        ),
        in_specs=[VMEM] * 3,
        out_specs=(VMEM, VMEM),
        scratch_shapes=[pltpu.VMEM((slots * (send + 1), LANES), f32)],
        compiler_params=PARAMS,
        name="finish",
    )(home, held, chosen)


def solution(mesh):
    return jax.shard_map(
        body,
        mesh=mesh,
        in_specs=(
            P(("groups", "shard"), None, None),
            P(("groups", "shard"), None, None),
            P("shard", None, None),
            P("shard", None, None),
            P("shard", None),
            P(),
            P("groups"),
            P(("groups", "shard"), None),
            P(("groups", "shard")),
        ),
        out_specs=(P(("groups", "shard"), None, None), P(("groups", "shard"), None)),
        check_vma=False,
    )
```
